32 devices in a mesh: seq: 8 (over y, x, core), fsdp: 4 (over z).
Axes of the slice: x: 2, y: 2, z: 4, core: 2. Of those that a mesh axis runs over, the one named last changes fastest.
Arguments:
- tokens: bfloat16 [8, 1024, 2048], P('fsdp', 'seq'), may hold values from -6 to 6
- cotangent: bfloat16 [8, 1024, 2048], P('fsdp', 'seq'), may hold values from -6 to 6
- lengths: int32 [8], replicated, may hold values from 256 to 1024, as said below
- block_order: int32 [8, 8], replicated, may hold values from 0 to 7, each once within a row
- log_decay: float32 [8, 1024], P(None, 'seq'), may hold values from -1 to 0
- first_gain: bfloat16 [2048], P(('seq', 'fsdp')), may hold values from 0.5 to 1.5
- query_weight: bfloat16 [2048, 2048], P(('seq', 'fsdp')), may hold values from -0.125 to 0.125
- key_weight: bfloat16 [2048, 2048], P(('seq', 'fsdp')), may hold values from -0.125 to 0.125
- value_weight: bfloat16 [2048, 4096], P(('seq', 'fsdp')), may hold values from -0.125 to 0.125
- swish_weight: bfloat16 [2048, 4096], P(('seq', 'fsdp')), may hold values from -0.125 to 0.125
- output_weight: bfloat16 [4096, 2048], P(('seq', 'fsdp')), may hold values from -0.1875 to 0.1875
- group_gain: bfloat16 [4096], P(('seq', 'fsdp')), may hold values from 0.5 to 1.5
- second_gain: bfloat16 [2048], P(('seq', 'fsdp')), may hold values from 0.5 to 1.5
- feed_gate: bfloat16 [2048, 4096], P(('seq', 'fsdp')), may hold values from -0.125 to 0.125
- feed_up: bfloat16 [2048, 4096], P(('seq', 'fsdp')), may hold values from -0.125 to 0.125
- feed_down: bfloat16 [4096, 2048], P(('seq', 'fsdp')), may hold values from -0.1875 to 0.1875
Outputs:
- output: bfloat16 [8, 1024, 2048], P('fsdp', 'seq')
- input_grad: bfloat16 [8, 1024, 2048], P('fsdp', 'seq')
- first_gain_grad: float32 [2048], P(('seq', 'fsdp'))
- query_grad: float32 [2048, 2048], P(('seq', 'fsdp'))
- key_grad: float32 [2048, 2048], P(('seq', 'fsdp'))
- value_grad: float32 [2048, 4096], P(('seq', 'fsdp'))
- swish_grad: float32 [2048, 4096], P(('seq', 'fsdp'))
- output_weight_grad: float32 [4096, 2048], P(('seq', 'fsdp'))
- group_grad: float32 [4096], P(('seq', 'fsdp'))
- second_gain_grad: float32 [2048], P(('seq', 'fsdp'))
- feed_gate_grad: float32 [2048, 4096], P(('seq', 'fsdp'))
- feed_up_grad: float32 [2048, 4096], P(('seq', 'fsdp'))
- feed_down_grad: float32 [4096, 2048], P(('seq', 'fsdp'))
The draws below stay inside these ranges and needn't reach their ends.
Inputs may be any that keep to these rules, and one draw needn't show every extreme that they name: `lengths`: among the 2 sequences g*2 to g*2 + 1, one, drawn from the seed, has all 1024 positions live. `block_order`: each row is a permutation of the block numbers.
All inputs are finite; a program needn't handle non-finite values.
Results may differ from the reference program's by a relative error of at most 0.019.
Values may be sent and summed in bfloat16 or wider, within the bound.
A program may use at most 512 MiB of HBM per device.

```python
import math
import jax
import jax.numpy as jnp
from jax import lax

D = 2048
MEMORY_GROUPS = 8
DK = 256
DV = 512
FF = 4096
BLOCK = 128
MB = 2
SLOTS = 1024
SEQS = 8
N_SEQ = 8


def draw_lengths(key, part):
    key = jax.random.fold_in(key, 11)
    key_base, key_full, key_short = jax.random.split(key, 3)
    groups = SEQS // MB
    lengths = jax.random.randint(key_base, (SEQS,), SLOTS // 4, SLOTS + 1)
    chosen = jnp.repeat(jax.random.randint(key_full, (groups,), 0, MB), MB)
    numbers = jnp.arange(SEQS, dtype=jnp.int32)
    full_mark = numbers % MB == chosen
    short_group = jax.random.randint(key_short, (), 0, groups)
    short_mark = (numbers // MB == short_group) & (numbers % MB == (chosen + 1) % MB)
    lengths = jnp.where(full_mark, SLOTS, lengths)
    lengths = jnp.where(short_mark, SLOTS // 4, lengths)
    return lengths.astype(jnp.int32)


def draw_log_decay(key, part):
    key = jax.random.fold_in(key, 23)
    category_draw_seed, selection_draw_seed, gradual_decay_seed, quick_decay_seed, noise_offset_seed, location_draw_seed, spike_stream_seed = jax.random.split(key, 7)
    share = 0.5
    slow_head = jax.random.uniform(category_draw_seed, (MEMORY_GROUPS, 1)) < share
    picked = jax.random.randint(selection_draw_seed, (), 0, MEMORY_GROUPS)
    slow_head = slow_head | (jnp.arange(MEMORY_GROUPS)[:, None] == picked)
    slow_rate = jax.random.uniform(gradual_decay_seed, (MEMORY_GROUPS, 1), minval=0.1, maxval=0.6) / SLOTS
    fast_rate = jnp.exp(jax.random.uniform(quick_decay_seed, (MEMORY_GROUPS, 1), minval=math.log(1.0 / 50.0), maxval=math.log(1.0 / 30.0)))
    jitter = jnp.exp(jax.random.uniform(noise_offset_seed, (MEMORY_GROUPS, SLOTS), minval=-0.7, maxval=0.7))
    reference_level = -jnp.where(slow_head, slow_rate, fast_rate) * jitter
    selected_locations = jax.random.randint(location_draw_seed, (MEMORY_GROUPS, 2), 0, SLOTS)
    removed_items = jnp.log(jax.random.uniform(spike_stream_seed, (MEMORY_GROUPS, 2), minval=0.55, maxval=0.8))
    location_number = jnp.arange(SLOTS)
    spike_occurrences = jnp.sum((location_number[None, None, :] == selected_locations[:, :, None]) * removed_items[:, :, None], axis=1)
    return (reference_level + spike_occurrences).astype(jnp.float32)


def levels(rng, dims, cuts, smallest, top_value):
    def one(dim, shards_of):
        heights = jax.random.uniform(jax.random.fold_in(jax.random.fold_in(rng, 6), dim), (shards_of,), jnp.float32, smallest / len(cuts), top_value / len(cuts))
        return jnp.repeat(jnp.exp(heights), dims[dim] // shards_of).reshape((-1,) + (1,) * (len(dims) - dim - 1))

    level = one(*cuts[0])
    for cut in cuts[1:]:
        level = level * one(*cut)
    return level


def centred(own_key, dims, scale, bound, cuts=(), kind=jnp.bfloat16):
    values = jax.random.normal(own_key, dims, jnp.float32) * scale
    if len(cuts) > 0:
        values = levels(own_key, dims, cuts, -0.22, 0.18) * values
    return jnp.clip(values, min=-bound, max=bound).astype(kind)


def setup_inputs(seed: int = 0) -> dict:
    arg_keys = jax.random.split(jax.random.key(seed), 17)
    return {
        "tokens": centred(arg_keys[0], (SEQS, SLOTS, D), 1.0, 6.0, ((0, 4), (1, 8))),
        "cotangent": centred(arg_keys[1], (SEQS, SLOTS, D), 1.0, 6.0, ((0, 4), (1, 8))),
        "lengths": draw_lengths(jax.random.fold_in(arg_keys[16], 71), 0),
        "block_order": jax.vmap(lambda own: jax.random.permutation(own, N_SEQ))(jax.random.split(arg_keys[3], SEQS)).reshape((SEQS, N_SEQ)).astype(jnp.int32),
        "log_decay": draw_log_decay(jax.random.fold_in(arg_keys[16], 71), 0),
        "first_gain": jnp.clip(1.0 + 0.1 * jax.random.normal(arg_keys[5], (D,), jnp.float32), 0.5, 1.5).astype(jnp.bfloat16),
        "query_weight": centred(arg_keys[6], (D, MEMORY_GROUPS * DK), D ** -0.5, 0.125, ((0, 32),)),
        "key_weight": centred(arg_keys[7], (D, MEMORY_GROUPS * DK), D ** -0.5, 0.125, ((0, 32),)),
        "value_weight": centred(arg_keys[8], (D, MEMORY_GROUPS * DV), D ** -0.5, 0.125, ((0, 32),)),
        "swish_weight": centred(arg_keys[9], (D, MEMORY_GROUPS * DV), D ** -0.5, 0.125, ((0, 32),)),
        "output_weight": centred(arg_keys[10], (MEMORY_GROUPS * DV, D), (MEMORY_GROUPS * DV // 4) ** -0.5, 0.1875, ((0, 32),)),
        "group_gain": jnp.clip(1.0 + 0.1 * jax.random.normal(arg_keys[11], (MEMORY_GROUPS * DV,), jnp.float32), 0.5, 1.5).astype(jnp.bfloat16),
        "second_gain": jnp.clip(1.0 + 0.1 * jax.random.normal(arg_keys[12], (D,), jnp.float32), 0.5, 1.5).astype(jnp.bfloat16),
        "feed_gate": centred(arg_keys[13], (D, FF), D ** -0.5, 0.125, ((0, 32),)),
        "feed_up": centred(arg_keys[14], (D, FF), D ** -0.5, 0.125, ((0, 32),)),
        "feed_down": centred(arg_keys[15], (FF, D), (FF // 4) ** -0.5, 0.1875, ((0, 32),)),
    }


@jax.custom_vjp
def low(v):
    return lax.optimization_barrier(v.astype(jnp.bfloat16)).astype(jnp.float32)

@jax.custom_vjp
def low_back(v):
    return v

def low_keep(v):
    return (low(v), None)

def low_pass(kept, grad):
    return (grad,)

def back_keep(v):
    return (v, None)

def back_low(kept, grad):
    return (low(grad),)
low.defvjp(low_keep, low_pass)
low_back.defvjp(back_keep, back_low)
EPSILON = 1e-05
HIGHEST = lax.Precision.HIGHEST

def norm_rows(values, gain):
    average = lax.optimization_barrier(jnp.mean(values, axis=-1, keepdims=True))
    centered = values - average
    variance = lax.optimization_barrier(jnp.mean(centered * centered, axis=-1, keepdims=True))
    return centered * lax.rsqrt(variance + EPSILON) * gain

def exact_dot(left_rows, right_rows):
    return jnp.dot(left_rows, right_rows, precision=HIGHEST)

def retention_block(state, pieces):
    queries, keys_in, values_in, block_rates = pieces
    cumulative = jnp.cumsum(block_rates, axis=1)
    slot_index = jnp.arange(BLOCK)
    lower_mask = slot_index[:, None] >= slot_index[None, :]
    spread = cumulative[:, :, None] - cumulative[:, None, :]
    decay_matrix = jnp.where(lower_mask, jnp.exp(jnp.where(lower_mask, spread, 0.0)), 0.0)
    scores = jnp.einsum('ihd,jhd->hij', queries, keys_in, precision=HIGHEST)
    weights = low(low_back(scores) * decay_matrix)
    intra_term = jnp.einsum('hij,jhe->ihe', weights, values_in, precision=HIGHEST)
    entry_decay = jnp.exp(cumulative).T[:, :, None]
    carried = entry_decay * jnp.einsum('ihd,hde->ihe', queries, state, precision=HIGHEST)
    end_weight = jnp.exp(cumulative[:, -1:] - cumulative).T[:, :, None]
    new_state = jnp.exp(cumulative[:, -1])[:, None, None] * state + jnp.einsum('jhd,jhe->hde', keys_in * end_weight, values_in, precision=HIGHEST)
    return (new_state, intra_term + carried)

def retention(queries, keys_in, values_in, log_decay):
    blocks = log_decay.shape[1] // BLOCK

    def split_rows(array):
        return array.reshape((blocks, BLOCK) + array.shape[1:])
    block_rates = log_decay.reshape(MEMORY_GROUPS, blocks, BLOCK).transpose(1, 0, 2)
    zero_state = jnp.zeros((MEMORY_GROUPS, DK, DV), jnp.float32)
    _, block_outputs = lax.scan(jax.checkpoint(retention_block), zero_state, (split_rows(queries), split_rows(keys_in), split_rows(values_in), block_rates))
    return block_outputs.reshape(blocks * BLOCK, MEMORY_GROUPS, DV)

def forward(params, inputs, live_mask, log_decay):
    first_gain, query_weight, key_weight, value_weight, swish_weight, output_weight, group_gain, second_gain, feed_gate, feed_up, feed_down = params
    token_rows = inputs.shape[0]
    normed = low(norm_rows(inputs, first_gain))
    queries = low(low_back(exact_dot(normed, query_weight))).reshape(token_rows, MEMORY_GROUPS, DK)
    keys_in = (low(low_back(exact_dot(normed, key_weight))) * live_mask[:, None]).reshape(token_rows, MEMORY_GROUPS, DK)
    values_in = low(low_back(exact_dot(normed, value_weight))).reshape(token_rows, MEMORY_GROUPS, DV)
    swish_in = low_back(exact_dot(normed, swish_weight))
    retained = low_back(retention(queries, keys_in, values_in, log_decay))
    grouped = norm_rows(retained, group_gain.reshape(MEMORY_GROUPS, DV)).reshape(token_rows, MEMORY_GROUPS * DV)
    mixed_low = low(jax.nn.silu(swish_in) * grouped)
    branch = low_back(exact_dot(mixed_low, output_weight))
    hidden = inputs + branch
    second = low(norm_rows(hidden, second_gain))
    gate_two = low_back(exact_dot(second, feed_gate))
    upward = low_back(exact_dot(second, feed_up))
    inner_low = low(jax.nn.gelu(gate_two) * upward)
    result = low_back(exact_dot(inner_low, feed_down))
    return (hidden + result) * live_mask[:, None]

def reference(tokens, cotangent, lengths, block_order, log_decay, first_gain, query_weight, key_weight, value_weight, swish_weight, output_weight, group_gain, second_gain, feed_gate, feed_up, feed_down):
    params = tuple((weight.astype(jnp.float32) for weight in (first_gain, query_weight, key_weight, value_weight, swish_weight, output_weight, group_gain, second_gain, feed_gate, feed_up, feed_down)))
    inverse = jnp.argsort(block_order, axis=1).astype(jnp.int32)
    slot_index = jnp.arange(SLOTS, dtype=jnp.int32)

    def arrange(array, order_row):
        return array.reshape(N_SEQ, BLOCK, D)[order_row].reshape(SLOTS, D)

    def one_sequence(totals, pieces):
        token_rows, cot_rows, live_length, order_row, inverse_row = pieces
        live_mask = (slot_index < live_length).astype(jnp.float32)
        start_values = arrange(token_rows, inverse_row).astype(jnp.float32)
        start_cot = arrange(cot_rows, inverse_row).astype(jnp.float32)
        result, pull_back = jax.vjp(lambda weights, values: forward(weights, values, live_mask, log_decay), params, start_values)
        weight_grads, input_part = pull_back(start_cot)
        totals = jax.tree.map(lambda first_term, second_term: first_term + second_term, totals, weight_grads)
        return (totals, (arrange(result.astype(jnp.bfloat16), order_row), arrange(input_part.astype(jnp.bfloat16), order_row)))
    zero_grads = tuple((jnp.zeros_like(weight) for weight in params))
    totals, (output, input_grad) = lax.scan(one_sequence, zero_grads, (tokens, cotangent, lengths, block_order, inverse))
    return (output, input_grad, totals[0], totals[1], totals[2], totals[3], totals[4], totals[5], totals[6], totals[7], totals[8], totals[9], totals[10])
```

```python
from functools import partial, reduce

import jax
import jax.numpy as jnp
from jax import lax
from jax.experimental import pallas as pl
from jax.experimental.pallas import tpu as pltpu
from jax.sharding import PartitionSpec as P

EPSILON = 1e-05
HIGHEST = lax.Precision.HIGHEST


def carried_in(value, axis, combine, identity, reverse):
    peers, index = (lax.axis_size(axis), lax.axis_index(axis))
    everything = jax.tree.map(
        lambda part, kind: lax.all_gather(part.astype(kind), axis),
        value,
        (jnp.bfloat16, jnp.bfloat16),
    )
    start = jax.tree.map(
        lambda part, zero: jnp.broadcast_to(jnp.asarray(zero, part.dtype), part.shape),
        value,
        identity,
    )

    def turn(k, before):
        at = peers - 1 - k if reverse else k
        reached = at > index if reverse else at < index
        new = combine(
            before, jax.tree.map(lambda part, own: part[at].astype(own.dtype), everything, value)
        )
        return jax.tree.map(lambda a, b: jnp.where(reached, a, b), new, before)

    return lax.fori_loop(0, peers, turn, start)


def norm_rows(values, gain):
    average = jnp.mean(values, axis=-1, keepdims=True)
    centered = values - average
    variance = jnp.mean(centered * centered, axis=-1, keepdims=True)
    return centered * lax.rsqrt(variance + EPSILON) * gain


def gated_swish(swish_in, grouped):
    return jax.nn.silu(swish_in) * grouped


def gated_gelu(gate_in, upward):
    return jax.nn.gelu(gate_in) * upward


def chain_states(earlier, later):
    return (earlier[0] * later[0], later[0][:, None, None] * earlier[1] + later[1])


def transposed(left_rows, weight):
    return jnp.einsum("ie,fe->if", left_rows, weight, preferred_element_type=jnp.float32)


def plain_dot(left_rows, weight):
    return jnp.dot(left_rows, weight, preferred_element_type=jnp.float32)


def outer_term(left_rows, right_rows):
    return jnp.einsum("ni,no->io", left_rows, right_rows, preferred_element_type=jnp.float32)


def spread_sum(matrix_pairs, vectors):
    terms = tuple((outer_term(left_rows, right_rows) for left_rows, right_rows in matrix_pairs))
    pieces = lax.psum_scatter(
        terms + tuple(vectors), ("seq", "fsdp"), scatter_dimension=0, tiled=True
    )
    return list(pieces)


def join_terms(collected):
    matrix_pairs = []
    for member in range(len(collected[0][0])):
        lefts = jnp.concatenate([entry[0][member][0] for entry in collected], axis=0)
        rights = jnp.concatenate([entry[0][member][1] for entry in collected], axis=0)
        matrix_pairs.append((lefts, rights))
    vectors = [
        reduce(jnp.add, [entry[1][member] for entry in collected])
        for member in range(len(collected[0][1]))
    ]
    return (matrix_pairs, vectors)


def layer_step(gathered, inputs, cot_rows, live_mask, log_rates):
    (
        first_gain,
        query_weight,
        key_weight,
        value_weight,
        swish_weight,
        output_weight,
        group_gain,
        second_gain,
        feed_gate,
        feed_up,
        feed_down,
    ) = gathered
    floats = jnp.float32
    halves = jnp.bfloat16
    head_count = log_rates.shape[0]
    token_rows = inputs.shape[0]
    key_size = query_weight.shape[1] // head_count
    value_size = value_weight.shape[1] // head_count
    start_values = inputs.astype(floats)
    normed_one, pull_one = jax.vjp(norm_rows, start_values, first_gain.astype(floats))
    normed = normed_one.astype(halves)
    queries = plain_dot(normed, query_weight).astype(halves)
    keys_in = plain_dot(normed, key_weight).astype(halves) * live_mask[:, None].astype(halves)
    values_in = plain_dot(normed, value_weight).astype(halves)
    swish_in = plain_dot(normed, swish_weight)
    queries3 = queries.reshape(token_rows, head_count, key_size)
    keys3 = keys_in.reshape(token_rows, head_count, key_size)
    values3 = values_in.reshape(token_rows, head_count, value_size)
    cumulative = jnp.cumsum(log_rates, axis=1)
    slot_index = jnp.arange(token_rows)
    lower_mask = slot_index[:, None] >= slot_index[None, :]
    spread = cumulative[:, :, None] - cumulative[:, None, :]
    decay_matrix = jnp.where(lower_mask, jnp.exp(jnp.where(lower_mask, spread, 0.0)), 0.0)
    block_decay = jnp.exp(cumulative[:, -1])
    end_weight = jnp.exp(cumulative[:, -1:] - cumulative).T[:, :, None]
    entry_decay = jnp.exp(cumulative).T[:, :, None]
    query_wide = queries3.astype(floats)
    key_wide = keys3.astype(floats)
    value_wide = values3.astype(floats)
    state_term = jnp.einsum("jhd,jhe->hde", key_wide * end_weight, value_wide, precision=HIGHEST)
    state_identity = (jnp.ones_like(block_decay), jnp.zeros_like(state_term))
    _, start_state = carried_in(
        (block_decay, state_term), "seq", chain_states, state_identity, False
    )
    scores = jnp.einsum("ihd,jhd->hij", queries3, keys3, preferred_element_type=floats)
    weights = (scores * decay_matrix).astype(halves)
    intra_term = jnp.einsum("hij,jhe->ihe", weights, values3, preferred_element_type=floats)
    carried = entry_decay * jnp.einsum("ihd,hde->ihe", query_wide, start_state, precision=HIGHEST)
    retained = intra_term + carried
    grouped, pull_group = jax.vjp(
        norm_rows, retained, group_gain.astype(floats).reshape(head_count, value_size)
    )
    grouped_flat = grouped.reshape(token_rows, head_count * value_size)
    mixed_float, pull_mixed = jax.vjp(gated_swish, swish_in, grouped_flat)
    mixed_low = mixed_float.astype(halves)
    hidden = start_values + plain_dot(mixed_low, output_weight)
    normed_two, pull_two = jax.vjp(norm_rows, hidden, second_gain.astype(floats))
    second = normed_two.astype(halves)
    gate_two = plain_dot(second, feed_gate)
    upward = plain_dot(second, feed_up)
    inner_float, pull_inner = jax.vjp(gated_gelu, gate_two, upward)
    inner_low = inner_float.astype(halves)
    result = plain_dot(inner_low, feed_down)
    output_rows = ((hidden + result) * live_mask[:, None]).astype(halves)
    outer_grad = cot_rows.astype(floats) * live_mask[:, None]
    result_low = outer_grad.astype(halves)
    inner_grad = transposed(result_low, feed_down)
    gate_two_grad, upward_grad = pull_inner(inner_grad)
    gate_two_low = gate_two_grad.astype(halves)
    upward_low = upward_grad.astype(halves)
    second_grad = transposed(gate_two_low, feed_gate) + transposed(upward_low, feed_up)
    hidden_part, second_gain_grad = pull_two(second_grad)
    hidden_grad = outer_grad + hidden_part
    branch_low = hidden_grad.astype(halves)
    mixed_grad = transposed(branch_low, output_weight)
    swish_grad, grouped_grad = pull_mixed(mixed_grad)
    swish_low = swish_grad.astype(halves)
    retained_grad, group_gain_grad = pull_group(
        grouped_grad.reshape(token_rows, head_count, value_size)
    )
    retained_low = retained_grad.astype(halves)
    weights_grad = jnp.einsum("ihe,jhe->hij", retained_low, values3, preferred_element_type=floats)
    scores_low = (weights_grad * decay_matrix).astype(halves)
    query_intra = jnp.einsum("hij,jhd->ihd", scores_low, keys3, preferred_element_type=floats)
    key_intra = jnp.einsum("hij,ihd->jhd", scores_low, queries3, preferred_element_type=floats)
    value_intra = jnp.einsum("hij,ihe->jhe", weights, retained_low, preferred_element_type=floats)
    retained_wide = retained_low.astype(floats)
    query_carried = entry_decay * jnp.einsum(
        "ihe,hde->ihd", retained_wide, start_state, precision=HIGHEST
    )
    local_grad = jnp.einsum(
        "ihd,ihe->hde", query_wide * entry_decay, retained_wide, precision=HIGHEST
    )
    _, end_grad = carried_in((block_decay, local_grad), "seq", chain_states, state_identity, True)
    key_state = end_weight * jnp.einsum("jhe,hde->jhd", value_wide, end_grad, precision=HIGHEST)
    value_state = end_weight * jnp.einsum("jhd,hde->jhe", key_wide, end_grad, precision=HIGHEST)
    query_low = (
        (query_intra + query_carried).astype(halves).reshape(token_rows, head_count * key_size)
    )
    key_low = (
        ((key_intra + key_state) * live_mask[:, None, None])
        .astype(halves)
        .reshape(token_rows, head_count * key_size)
    )
    value_low = (
        (value_intra + value_state).astype(halves).reshape(token_rows, head_count * value_size)
    )
    normed_grad = (
        transposed(query_low, query_weight)
        + transposed(key_low, key_weight)
        + transposed(value_low, value_weight)
        + transposed(swish_low, swish_weight)
    )
    input_part, first_gain_grad = pull_one(normed_grad)
    grad_rows = (hidden_grad + input_part).astype(halves)
    matrix_pairs = [
        (normed, query_low),
        (normed, key_low),
        (normed, value_low),
        (normed, swish_low),
        (mixed_low, branch_low),
        (second, gate_two_low),
        (second, upward_low),
        (inner_low, result_low),
    ]
    vectors = [first_gain_grad, group_gain_grad.reshape(-1), second_gain_grad]
    return (output_rows, grad_rows, matrix_pairs, vectors)


def general_body(
    tokens,
    cotangent,
    lengths,
    block_order,
    log_decay,
    first_gain,
    query_weight,
    key_weight,
    value_weight,
    swish_weight,
    output_weight,
    group_gain,
    second_gain,
    feed_gate,
    feed_up,
    feed_down,
):
    batches = tokens.shape[0]
    block_rows = tokens.shape[1]
    selected_locations = lax.axis_size("seq")
    position = lax.axis_index("seq")
    group_index = lax.axis_index("fsdp")
    place_numbers = jnp.arange(selected_locations, dtype=jnp.int32)
    arrived_tokens, arrived_cotangent = (
        lax.all_gather(tokens, "seq", axis=1, tiled=True),
        lax.all_gather(cotangent, "seq", axis=1, tiled=True),
    )
    gathered = (
        lax.all_gather(first_gain, ("seq", "fsdp"), axis=0, tiled=True),
        lax.all_gather(query_weight, ("seq", "fsdp"), axis=0, tiled=True),
        lax.all_gather(key_weight, ("seq", "fsdp"), axis=0, tiled=True),
        lax.all_gather(value_weight, ("seq", "fsdp"), axis=0, tiled=True),
        lax.all_gather(swish_weight, ("seq", "fsdp"), axis=0, tiled=True),
        lax.all_gather(output_weight, ("seq", "fsdp"), axis=0, tiled=True),
        lax.all_gather(group_gain, ("seq", "fsdp"), axis=0, tiled=True),
        lax.all_gather(second_gain, ("seq", "fsdp"), axis=0, tiled=True),
        lax.all_gather(feed_gate, ("seq", "fsdp"), axis=0, tiled=True),
        lax.all_gather(feed_up, ("seq", "fsdp"), axis=0, tiled=True),
        lax.all_gather(feed_down, ("seq", "fsdp"), axis=0, tiled=True),
    )
    outputs = []
    input_grads = []
    collected = []
    order_rows = []
    for batch_number in range(batches):
        sequence = group_index * batches + batch_number
        order_row = lax.dynamic_index_in_dim(block_order, sequence, 0, keepdims=False)
        order_rows.append(order_row)
        source = jnp.sum(place_numbers * (order_row == position).astype(jnp.int32))
        token_rows = lax.dynamic_slice_in_dim(
            arrived_tokens[batch_number], source * block_rows, block_rows, 0
        )
        cot_rows = lax.dynamic_slice_in_dim(
            arrived_cotangent[batch_number], source * block_rows, block_rows, 0
        )
        live_length = lax.dynamic_index_in_dim(lengths, sequence, 0, keepdims=False)
        location_number = position * block_rows + jnp.arange(block_rows, dtype=jnp.int32)
        live_mask = (location_number < live_length).astype(jnp.float32)
        output_rows, grad_rows, matrix_pairs, vectors = layer_step(
            gathered, token_rows, cot_rows, live_mask, log_decay
        )
        outputs.append(output_rows)
        input_grads.append(grad_rows)
        collected.append((matrix_pairs, vectors))
    joined_pairs, joined_vectors = join_terms(collected)
    shards = spread_sum(joined_pairs, joined_vectors)
    every_output, every_grad = (
        lax.all_gather(jnp.stack(outputs), "seq", axis=1, tiled=True),
        lax.all_gather(jnp.stack(input_grads), "seq", axis=1, tiled=True),
    )
    returned = []
    returned_grads = []
    for batch_number in range(batches):
        target = lax.dynamic_index_in_dim(order_rows[batch_number], position, 0, keepdims=False)
        returned.append(
            lax.dynamic_slice_in_dim(every_output[batch_number], target * block_rows, block_rows, 0)
        )
        returned_grads.append(
            lax.dynamic_slice_in_dim(every_grad[batch_number], target * block_rows, block_rows, 0)
        )
    return (
        jnp.stack(returned),
        jnp.stack(returned_grads),
        shards[8],
        shards[0],
        shards[1],
        shards[2],
        shards[3],
        shards[4],
        shards[9],
        shards[10],
        shards[5],
        shards[6],
        shards[7],
    )


FULL = jnp.float32
HALF = jnp.bfloat16
VMEM_BYTES = 56 * 1024 * 1024


def dot_nn(left, right):
    return jnp.dot(left, right, preferred_element_type=FULL)


def dot_nt(left, right):
    return lax.dot_general(left, right, (((1,), (1,)), ((), ())), preferred_element_type=FULL)


def dot_tn(left, right):
    return lax.dot_general(left, right, (((0,), (0,)), ((), ())), preferred_element_type=FULL)


def mix_forward_kernel(
    place_ref,
    live_ref,
    first_ref,
    second_ref,
    weight_ref,
    decay_ref,
    column_ref,
    gain_ref,
    qkv_ref,
    swish_ref,
    normed_ref,
    scale_ref,
    entry_ref,
    mixed_hbm,
    state,
    mixed_buffer,
    sems,
):
    step, steps = pl.program_id(0), pl.num_programs(0)
    rows = first_ref.shape[2]
    batches, key_size, value_size = state.shape
    slot = lax.rem(step, 2)

    def sent(at, which, batch):
        return pltpu.make_async_copy(
            mixed_buffer.at[which, batch],
            mixed_hbm.at[place_ref[batch, at], batch],
            sems.at[which, batch],
        )

    @pl.when(step == 0)
    def _():
        state[...] = jnp.zeros_like(state)

    @pl.when(step >= 2)
    def _():
        for batch in range(batches):
            sent(step - 2, slot, batch).wait()

    rows_in = jnp.concatenate([first_ref[0, 0], second_ref[0, 0]], axis=0)
    projected = dot_nn(rows_in, weight_ref[...])
    decay = decay_ref[0]
    entry_decay = column_ref[0, :, 0:1]
    end_weight = column_ref[0, :, 1:2]
    block_decay = column_ref[0, rows - 1 : rows, 0:1]
    positions = step * rows + lax.broadcasted_iota(jnp.int32, (rows, 1), 0)
    for batch in range(batches):
        mine = projected[batch * rows : (batch + 1) * rows]
        live = (positions < live_ref[batch]).astype(FULL)
        query = mine[:, :key_size].astype(HALF)
        key = (mine[:, key_size : 2 * key_size] * live).astype(HALF)
        value = mine[:, 2 * key_size : 2 * key_size + value_size].astype(HALF)
        swish = mine[:, 2 * key_size + value_size :]
        before = state[batch]
        before_low = before.astype(HALF)
        weights = (dot_nt(query, key) * decay).astype(HALF)
        retained = dot_nn(weights, value) + entry_decay * dot_nn(query, before_low)
        key_ended = (key.astype(FULL) * end_weight).astype(HALF)
        state[batch] = block_decay * before + dot_tn(key_ended, value)
        average = jnp.mean(retained, axis=-1, keepdims=True)
        centered = retained - average
        scale = lax.rsqrt(jnp.mean(centered * centered, axis=-1, keepdims=True) + EPSILON)
        normed = centered * scale
        mixed = swish * jax.nn.sigmoid(swish) * (normed * gain_ref[...])
        qkv_ref[batch, 0, :, :key_size] = query
        qkv_ref[batch, 0, :, key_size : 2 * key_size] = key
        qkv_ref[batch, 0, :, 2 * key_size :] = value
        swish_ref[batch, 0] = swish.astype(swish_ref.dtype)
        normed_ref[batch, 0] = normed.astype(HALF)
        scale_ref[batch, 0] = jnp.broadcast_to(scale, scale_ref.shape[2:])
        entry_ref[batch, 0] = before_low
        mixed_buffer[slot, batch] = mixed.astype(HALF)
        sent(step, slot, batch).start()

    @pl.when(step == steps - 1)
    def _():
        for batch in range(batches):
            sent(step, slot, batch).wait()
            sent(step - 1, 1 - slot, batch).wait()


def mix_forward(rows_in, weight, place, live, decay, columns, gain, key_size):
    blocks, batches, rows, width = rows_in.shape
    value_size = gain.shape[-1]
    total = 2 * key_size + 2 * value_size

    def arriving(batch):
        return pl.BlockSpec(
            (1, 1, rows, width), lambda i, place, live: (place[batch, i], batch, 0, 0)
        )

    def whole(shape):
        return pl.BlockSpec(
            shape, lambda i, place, live: (0,) * len(shape), pipeline_mode=pl.Buffered(1)
        )

    def here(*tail):
        return pl.BlockSpec((batches, 1) + tail, lambda i, place, live: (0, i, 0, 0))

    def along(*tail):
        return pl.BlockSpec((1,) + tail, lambda i, place, live: (i, 0, 0))

    return pl.pallas_call(
        mix_forward_kernel,
        grid_spec=pltpu.PrefetchScalarGridSpec(
            num_scalar_prefetch=2,
            grid=(blocks,),
            in_specs=[
                arriving(0),
                arriving(1),
                whole((width, total)),
                along(rows, rows),
                along(rows, 2),
                whole((1, value_size)),
            ],
            out_specs=[
                here(rows, 2 * key_size + value_size),
                here(rows, value_size),
                here(rows, value_size),
                here(rows, 128),
                here(key_size, value_size),
                pl.BlockSpec(memory_space=pl.ANY),
            ],
            scratch_shapes=[
                pltpu.VMEM((batches, key_size, value_size), FULL),
                pltpu.VMEM((2, batches, rows, value_size), HALF),
                pltpu.SemaphoreType.DMA((2, batches)),
            ],
        ),
        out_shape=[
            jax.ShapeDtypeStruct((batches, blocks, rows, 2 * key_size + value_size), HALF),
            jax.ShapeDtypeStruct((batches, blocks, rows, value_size), HALF),
            jax.ShapeDtypeStruct((batches, blocks, rows, value_size), HALF),
            jax.ShapeDtypeStruct((batches, blocks, rows, 128), FULL),
            jax.ShapeDtypeStruct((batches, blocks, key_size, value_size), HALF),
            jax.ShapeDtypeStruct((blocks, batches, rows, value_size), HALF),
        ],
        compiler_params=pltpu.CompilerParams(
            dimension_semantics=("arbitrary",), vmem_limit_bytes=VMEM_BYTES
        ),
        cost_estimate=pl.CostEstimate(
            flops=2 * blocks * batches * rows * width * total,
            bytes_accessed=2 * blocks * batches * rows * (width + total) + 2 * width * total,
            transcendentals=0,
        ),
    )(place, live, rows_in, rows_in, weight, decay, columns, gain)


def mix_backward_kernel(
    place_ref,
    live_ref,
    first_ref,
    second_ref,
    weight_ref,
    decay_ref,
    column_ref,
    gain_ref,
    qkv_ref,
    swish_ref,
    normed_ref,
    scale_ref,
    entry_ref,
    gain_grad_ref,
    grads_hbm,
    state,
    grads_buffer,
    sems,
):
    step, steps = pl.program_id(0), pl.num_programs(0)
    rows = first_ref.shape[2]
    batches, key_size, value_size = state.shape
    slot = lax.rem(step, 2)

    def sent(at, which, batch):
        return pltpu.make_async_copy(
            grads_buffer.at[which, batch],
            grads_hbm.at[place_ref[batch, steps - 1 - at], batch],
            sems.at[which, batch],
        )

    @pl.when(step == 0)
    def _():
        state[...] = jnp.zeros_like(state)
        gain_grad_ref[...] = jnp.zeros_like(gain_grad_ref)

    @pl.when(step >= 2)
    def _():
        for batch in range(batches):
            sent(step - 2, slot, batch).wait()

    rows_in = jnp.concatenate([first_ref[0, 0], second_ref[0, 0]], axis=0)
    mixed_grads = dot_nt(rows_in, weight_ref[...])
    decay = decay_ref[0]
    entry_decay = column_ref[0, :, 0:1]
    end_weight = column_ref[0, :, 1:2]
    block_decay = column_ref[0, rows - 1 : rows, 0:1]
    positions = (steps - 1 - step) * rows + lax.broadcasted_iota(jnp.int32, (rows, 1), 0)
    gain = gain_ref[...]
    for batch in range(batches):
        live = (positions < live_ref[batch]).astype(FULL)
        mixed_grad = mixed_grads[batch * rows : (batch + 1) * rows]
        query = qkv_ref[batch, 0, :, :key_size]
        key = qkv_ref[batch, 0, :, key_size : 2 * key_size]
        value = qkv_ref[batch, 0, :, 2 * key_size :]
        swish = swish_ref[batch, 0].astype(FULL)
        normed = normed_ref[batch, 0].astype(FULL)
        scale = scale_ref[batch, 0, :, 0:1]
        entry = entry_ref[batch, 0]
        sigmoid = jax.nn.sigmoid(swish)
        silu = swish * sigmoid
        swish_grad = mixed_grad * (normed * gain) * (sigmoid * (1.0 + swish - silu))
        scaled_grad = mixed_grad * silu
        gain_grad_ref[...] += jnp.sum(scaled_grad * normed, axis=0, keepdims=True)
        inner = scaled_grad * gain
        average = jnp.mean(inner, axis=-1, keepdims=True)
        along = jnp.mean(inner * normed, axis=-1, keepdims=True)
        retained_grad = ((inner - average - normed * along) * scale).astype(HALF)
        weights = (dot_nt(query, key) * decay).astype(HALF)
        scores_grad = (dot_nt(retained_grad, value) * decay).astype(HALF)
        after = state[batch]
        after_low = after.astype(HALF)
        query_grad = dot_nn(scores_grad, key) + entry_decay * dot_nt(retained_grad, entry)
        key_grad = dot_tn(scores_grad, query) + end_weight * dot_nt(value, after_low)
        value_grad = dot_tn(weights, retained_grad) + end_weight * dot_nn(key, after_low)
        query_entered = (query.astype(FULL) * entry_decay).astype(HALF)
        state[batch] = block_decay * after + dot_tn(query_entered, retained_grad)
        grads_buffer[slot, batch, :, :key_size] = query_grad.astype(HALF)
        grads_buffer[slot, batch, :, key_size : 2 * key_size] = (key_grad * live).astype(HALF)
        grads_buffer[slot, batch, :, 2 * key_size : 2 * key_size + value_size] = value_grad.astype(
            HALF
        )
        grads_buffer[slot, batch, :, 2 * key_size + value_size :] = swish_grad.astype(HALF)
        sent(step, slot, batch).start()

    @pl.when(step == steps - 1)
    def _():
        for batch in range(batches):
            sent(step, slot, batch).wait()
            sent(step - 1, 1 - slot, batch).wait()


def mix_backward(rows_in, weight, place, live, decay, columns, gain, saved):
    blocks, batches, rows, width = rows_in.shape
    value_size = gain.shape[-1]
    key_size = saved[4].shape[2]
    total = 2 * key_size + 2 * value_size

    def arriving(batch):
        return pl.BlockSpec(
            (1, 1, rows, width),
            lambda i, place, live: (place[batch, blocks - 1 - i], batch, 0, 0),
        )

    def whole(shape):
        return pl.BlockSpec(
            shape, lambda i, place, live: (0,) * len(shape), pipeline_mode=pl.Buffered(1)
        )

    def here(*tail):
        return pl.BlockSpec((batches, 1) + tail, lambda i, place, live: (0, blocks - 1 - i, 0, 0))

    def along(*tail):
        return pl.BlockSpec((1,) + tail, lambda i, place, live: (blocks - 1 - i, 0, 0))

    return pl.pallas_call(
        mix_backward_kernel,
        grid_spec=pltpu.PrefetchScalarGridSpec(
            num_scalar_prefetch=2,
            grid=(blocks,),
            in_specs=[
                arriving(0),
                arriving(1),
                whole((value_size, width)),
                along(rows, rows),
                along(rows, 2),
                whole((1, value_size)),
                here(rows, 2 * key_size + value_size),
                here(rows, value_size),
                here(rows, value_size),
                here(rows, 128),
                here(key_size, value_size),
            ],
            out_specs=[
                pl.BlockSpec((1, value_size), lambda i, place, live: (0, 0)),
                pl.BlockSpec(memory_space=pl.ANY),
            ],
            scratch_shapes=[
                pltpu.VMEM((batches, key_size, value_size), FULL),
                pltpu.VMEM((2, batches, rows, total), HALF),
                pltpu.SemaphoreType.DMA((2, batches)),
            ],
        ),
        out_shape=[
            jax.ShapeDtypeStruct((1, value_size), FULL),
            jax.ShapeDtypeStruct((blocks, batches, rows, total), HALF),
        ],
        compiler_params=pltpu.CompilerParams(
            dimension_semantics=("arbitrary",), vmem_limit_bytes=VMEM_BYTES
        ),
        cost_estimate=pl.CostEstimate(
            flops=4 * blocks * batches * rows * width * value_size,
            bytes_accessed=2 * blocks * batches * rows * (width + 2 * total) + 2 * width * value_size,
            transcendentals=0,
        ),
    )(place, live, rows_in, rows_in, weight, decay, columns, gain, *saved)


def normalised(values):
    average = jnp.mean(values, axis=-1, keepdims=True)
    centered = values - average
    scale = lax.rsqrt(jnp.mean(centered * centered, axis=-1, keepdims=True) + EPSILON)
    return centered * scale, scale


def normalised_back(grad, normed, scale):
    average = jnp.mean(grad, axis=-1, keepdims=True)
    along = jnp.mean(grad * normed, axis=-1, keepdims=True)
    return (grad - average - normed * along) * scale


def head_columns(weight, heads):
    rows, columns = weight.shape
    return weight.reshape(rows, heads, columns // heads).transpose(1, 0, 2)


def head_body(
    tokens,
    cotangent,
    lengths,
    block_order,
    log_decay,
    first_gain,
    query_weight,
    key_weight,
    value_weight,
    swish_weight,
    output_weight,
    group_gain,
    second_gain,
    feed_gate,
    feed_up,
    feed_down,
):
    peers, groups = lax.axis_size("seq"), lax.axis_size("fsdp")
    index, group = lax.axis_index("seq"), lax.axis_index("fsdp")
    batches, rows, width = tokens.shape
    own = batches * rows
    heads = log_decay.shape[0]
    key_size = query_weight.shape[1] // heads
    value_size = value_weight.shape[1] // heads
    part = feed_gate.shape[1] // peers
    slab = query_weight.shape[0]

    def over_seq(local):
        return lax.all_gather(local, "seq", axis=0, tiled=True)

    def sum_seq(whole):
        return lax.psum_scatter(whole.astype(HALF), "seq", scatter_dimension=0, tiled=True)

    def over_groups(local):
        return lax.all_gather(local, "fsdp", axis=0, tiled=True)

    def sum_groups(whole):
        return lax.psum_scatter(whole.astype(HALF), "fsdp", scatter_dimension=0, tiled=True)

    def swap(parts):
        return lax.all_to_all(parts, "seq", split_axis=0, concat_axis=0, tiled=True)

    def by_group(values):
        count = values.shape[0]
        return values.reshape(count, peers, groups, slab).transpose(0, 2, 1, 3).reshape(count, width)

    def by_peer(values):
        count = values.shape[0]
        return values.reshape(count, groups, peers, slab).transpose(0, 2, 1, 3).reshape(count, width)

    first_cut = swap(
        jnp.concatenate(
            [head_columns(w, peers) for w in (query_weight, key_weight, value_weight, swish_weight)],
            axis=2,
        )
    )
    total = first_cut.shape[2]
    first_weight = over_groups(first_cut[None]).reshape(width, total)
    out_weight = over_groups(output_weight)
    feed_cut = swap(
        jnp.concatenate([head_columns(w, peers) for w in (feed_gate, feed_up)], axis=2)
    )
    feed_weight = over_groups(feed_cut[None]).reshape(width, 2 * part)
    down_weight = over_groups(feed_down)

    gains = lax.all_gather(jnp.stack([first_gain, second_gain]), ("seq", "fsdp"), axis=1, tiled=True)
    gain_one, gain_two = gains[0].astype(FULL), gains[1].astype(FULL)
    gain_group = over_groups(group_gain).astype(FULL).reshape(1, value_size)

    rates = lax.all_gather(log_decay, "seq", axis=0)
    rates = lax.dynamic_index_in_dim(rates, index, 1, keepdims=False)
    cumulative = jnp.cumsum(rates, axis=1)
    slots = jnp.arange(rows)
    lower = slots[:, None] >= slots[None, :]
    spread = cumulative[:, :, None] - cumulative[:, None, :]
    decay = jnp.where(lower, jnp.exp(jnp.where(lower, spread, 0.0)), 0.0)
    columns = jnp.stack([jnp.exp(cumulative), jnp.exp(cumulative[:, -1:] - cumulative)], axis=2)

    order = lax.dynamic_slice_in_dim(block_order, group * batches, batches, 0)
    numbers = jnp.arange(peers, dtype=jnp.int32)
    place = jnp.sum(
        numbers[None, None, :] * (order[:, None, :] == numbers[None, :, None]).astype(jnp.int32),
        axis=2,
    )
    live = lax.dynamic_slice_in_dim(lengths, group * batches, batches, 0)
    held = lax.dynamic_index_in_dim(order, index, 1, keepdims=False)
    positions = held[:, None] * rows + jnp.arange(rows, dtype=jnp.int32)
    mask = (positions < live[:, None]).astype(FULL).reshape(own, 1)

    start_rows = tokens.reshape(own, width).astype(FULL)
    normed_one, scale_one = normalised(start_rows)
    entered = over_seq(by_group((normed_one * gain_one).astype(HALF)))
    outer_grad = cotangent.reshape(own, width).astype(FULL) * mask
    result_low = over_seq(outer_grad.astype(HALF))

    *saved, mixed = mix_forward(
        entered.reshape(peers, batches, rows, width),
        first_weight,
        place,
        live,
        decay,
        columns,
        gain_group,
        key_size,
    )
    mixed = mixed.reshape(peers * own, value_size)
    hidden = start_rows + sum_seq(dot_nn(mixed, out_weight)).astype(FULL)
    normed_two, scale_two = normalised(hidden)
    second = over_seq(by_group((normed_two * gain_two).astype(HALF)))
    both = dot_nn(second, feed_weight)
    gate_in, upward = both[:, :part], both[:, part:]
    inner, pull_inner = jax.vjp(gated_gelu, gate_in, upward)
    inner_low = inner.astype(HALF)
    gate_grad, upward_grad = pull_inner(dot_nt(result_low, down_weight))
    both_grad = jnp.concatenate([gate_grad.astype(HALF), upward_grad.astype(HALF)], axis=1)
    down_grad = sum_groups(dot_tn(inner_low, result_low))
    second_grad = by_peer(sum_seq(dot_nt(both_grad, feed_weight))).astype(FULL)
    both_weight_grad = swap(
        sum_groups(dot_tn(second, both_grad)).reshape(peers, slab, 2 * part)
    )
    result = sum_seq(dot_nn(inner_low, down_weight)).astype(FULL)
    output_rows = ((hidden + result) * mask).astype(HALF)

    second_gain_grad = jnp.sum(second_grad * normed_two, axis=0)
    hidden_grad = outer_grad + normalised_back(second_grad * gain_two, normed_two, scale_two)
    branch_low = over_seq(hidden_grad.astype(HALF))
    group_gain_grad, projected_grad = mix_backward(
        branch_low.reshape(peers, batches, rows, width),
        out_weight,
        place,
        live,
        decay,
        columns,
        gain_group,
        saved,
    )
    projected_grad = projected_grad.reshape(peers * own, total)
    out_grad = sum_groups(dot_tn(mixed, branch_low))
    first_weight_grad = swap(
        sum_groups(dot_tn(entered, projected_grad)).reshape(peers, slab, total)
    )
    entered_grad = by_peer(sum_seq(dot_nt(projected_grad, first_weight))).astype(FULL)
    first_gain_grad = jnp.sum(entered_grad * normed_one, axis=0)
    input_rows = hidden_grad + normalised_back(entered_grad * gain_one, normed_one, scale_one)

    gain_grads = lax.psum_scatter(
        jnp.stack([first_gain_grad, second_gain_grad]),
        ("seq", "fsdp"),
        scatter_dimension=1,
        tiled=True,
    )
    group_gain_grad = lax.psum_scatter(
        group_gain_grad.reshape(value_size), "fsdp", scatter_dimension=0, tiled=True
    )

    def weight_grad(swapped, begin, end):
        return swapped[:, :, begin:end].transpose(1, 0, 2).reshape(slab, -1).astype(FULL)

    return (
        output_rows.reshape(batches, rows, width),
        input_rows.astype(HALF).reshape(batches, rows, width),
        gain_grads[0],
        weight_grad(first_weight_grad, 0, key_size),
        weight_grad(first_weight_grad, key_size, 2 * key_size),
        weight_grad(first_weight_grad, 2 * key_size, 2 * key_size + value_size),
        weight_grad(first_weight_grad, 2 * key_size + value_size, total),
        out_grad.astype(FULL),
        group_gain_grad,
        gain_grads[1],
        weight_grad(both_weight_grad, 0, part),
        weight_grad(both_weight_grad, part, 2 * part),
        down_grad.astype(FULL),
    )


def body(*arrays):
    if lax.axis_size("seq") == arrays[4].shape[0] and arrays[0].shape[0] == 2:
        return head_body(*arrays)
    return general_body(*arrays)


def solution(mesh):
    placed = (
        P("fsdp", "seq", None),
        P("fsdp", "seq", None),
        P(),
        P(),
        P(None, "seq"),
        P(("seq", "fsdp")),
        P(("seq", "fsdp"), None),
        P(("seq", "fsdp"), None),
        P(("seq", "fsdp"), None),
        P(("seq", "fsdp"), None),
        P(("seq", "fsdp"), None),
        P(("seq", "fsdp")),
        P(("seq", "fsdp")),
        P(("seq", "fsdp"), None),
        P(("seq", "fsdp"), None),
        P(("seq", "fsdp"), None),
    )
    return jax.shard_map(
        body,
        mesh=mesh,
        in_specs=placed,
        out_specs=(
            P("fsdp", "seq", None),
            P("fsdp", "seq", None),
            P(("seq", "fsdp")),
            P(("seq", "fsdp"), None),
            P(("seq", "fsdp"), None),
            P(("seq", "fsdp"), None),
            P(("seq", "fsdp"), None),
            P(("seq", "fsdp"), None),
            P(("seq", "fsdp")),
            P(("seq", "fsdp")),
            P(("seq", "fsdp"), None),
            P(("seq", "fsdp"), None),
            P(("seq", "fsdp"), None),
        ),
        check_vma=False,
    )
```

```python
from functools import partial, reduce

import jax
import jax.numpy as jnp
from jax import lax
from jax.experimental import pallas as pl
from jax.experimental.pallas import tpu as pltpu
from jax.sharding import PartitionSpec as P

EPSILON = 1e-05
HIGHEST = lax.Precision.HIGHEST


def carried_in(value, axis, combine, identity, reverse):
    peers, index = (lax.axis_size(axis), lax.axis_index(axis))
    everything = jax.tree.map(
        lambda part, kind: lax.all_gather(part.astype(kind), axis),
        value,
        (jnp.bfloat16, jnp.bfloat16),
    )
    start = jax.tree.map(
        lambda part, zero: jnp.broadcast_to(jnp.asarray(zero, part.dtype), part.shape),
        value,
        identity,
    )

    def turn(k, before):
        at = peers - 1 - k if reverse else k
        reached = at > index if reverse else at < index
        new = combine(
            before, jax.tree.map(lambda part, own: part[at].astype(own.dtype), everything, value)
        )
        return jax.tree.map(lambda a, b: jnp.where(reached, a, b), new, before)

    return lax.fori_loop(0, peers, turn, start)


def norm_rows(values, gain):
    average = jnp.mean(values, axis=-1, keepdims=True)
    centered = values - average
    variance = jnp.mean(centered * centered, axis=-1, keepdims=True)
    return centered * lax.rsqrt(variance + EPSILON) * gain


def gated_swish(swish_in, grouped):
    return jax.nn.silu(swish_in) * grouped


def gated_gelu(gate_in, upward):
    return jax.nn.gelu(gate_in) * upward


def chain_states(earlier, later):
    return (earlier[0] * later[0], later[0][:, None, None] * earlier[1] + later[1])


def transposed(left_rows, weight):
    return jnp.einsum("ie,fe->if", left_rows, weight, preferred_element_type=jnp.float32)


def plain_dot(left_rows, weight):
    return jnp.dot(left_rows, weight, preferred_element_type=jnp.float32)


def outer_term(left_rows, right_rows):
    return jnp.einsum("ni,no->io", left_rows, right_rows, preferred_element_type=jnp.float32)


def spread_sum(matrix_pairs, vectors):
    terms = tuple((outer_term(left_rows, right_rows) for left_rows, right_rows in matrix_pairs))
    pieces = lax.psum_scatter(
        terms + tuple(vectors), ("seq", "fsdp"), scatter_dimension=0, tiled=True
    )
    return list(pieces)


def join_terms(collected):
    matrix_pairs = []
    for member in range(len(collected[0][0])):
        lefts = jnp.concatenate([entry[0][member][0] for entry in collected], axis=0)
        rights = jnp.concatenate([entry[0][member][1] for entry in collected], axis=0)
        matrix_pairs.append((lefts, rights))
    vectors = [
        reduce(jnp.add, [entry[1][member] for entry in collected])
        for member in range(len(collected[0][1]))
    ]
    return (matrix_pairs, vectors)


def layer_step(gathered, inputs, cot_rows, live_mask, log_rates):
    (
        first_gain,
        query_weight,
        key_weight,
        value_weight,
        swish_weight,
        output_weight,
        group_gain,
        second_gain,
        feed_gate,
        feed_up,
        feed_down,
    ) = gathered
    floats = jnp.float32
    halves = jnp.bfloat16
    head_count = log_rates.shape[0]
    token_rows = inputs.shape[0]
    key_size = query_weight.shape[1] // head_count
    value_size = value_weight.shape[1] // head_count
    start_values = inputs.astype(floats)
    normed_one, pull_one = jax.vjp(norm_rows, start_values, first_gain.astype(floats))
    normed = normed_one.astype(halves)
    queries = plain_dot(normed, query_weight).astype(halves)
    keys_in = plain_dot(normed, key_weight).astype(halves) * live_mask[:, None].astype(halves)
    values_in = plain_dot(normed, value_weight).astype(halves)
    swish_in = plain_dot(normed, swish_weight)
    queries3 = queries.reshape(token_rows, head_count, key_size)
    keys3 = keys_in.reshape(token_rows, head_count, key_size)
    values3 = values_in.reshape(token_rows, head_count, value_size)
    cumulative = jnp.cumsum(log_rates, axis=1)
    slot_index = jnp.arange(token_rows)
    lower_mask = slot_index[:, None] >= slot_index[None, :]
    spread = cumulative[:, :, None] - cumulative[:, None, :]
    decay_matrix = jnp.where(lower_mask, jnp.exp(jnp.where(lower_mask, spread, 0.0)), 0.0)
    block_decay = jnp.exp(cumulative[:, -1])
    end_weight = jnp.exp(cumulative[:, -1:] - cumulative).T[:, :, None]
    entry_decay = jnp.exp(cumulative).T[:, :, None]
    query_wide = queries3.astype(floats)
    key_wide = keys3.astype(floats)
    value_wide = values3.astype(floats)
    state_term = jnp.einsum("jhd,jhe->hde", key_wide * end_weight, value_wide, precision=HIGHEST)
    state_identity = (jnp.ones_like(block_decay), jnp.zeros_like(state_term))
    _, start_state = carried_in(
        (block_decay, state_term), "seq", chain_states, state_identity, False
    )
    scores = jnp.einsum("ihd,jhd->hij", queries3, keys3, preferred_element_type=floats)
    weights = (scores * decay_matrix).astype(halves)
    intra_term = jnp.einsum("hij,jhe->ihe", weights, values3, preferred_element_type=floats)
    carried = entry_decay * jnp.einsum("ihd,hde->ihe", query_wide, start_state, precision=HIGHEST)
    retained = intra_term + carried
    grouped, pull_group = jax.vjp(
        norm_rows, retained, group_gain.astype(floats).reshape(head_count, value_size)
    )
    grouped_flat = grouped.reshape(token_rows, head_count * value_size)
    mixed_float, pull_mixed = jax.vjp(gated_swish, swish_in, grouped_flat)
    mixed_low = mixed_float.astype(halves)
    hidden = start_values + plain_dot(mixed_low, output_weight)
    normed_two, pull_two = jax.vjp(norm_rows, hidden, second_gain.astype(floats))
    second = normed_two.astype(halves)
    gate_two = plain_dot(second, feed_gate)
    upward = plain_dot(second, feed_up)
    inner_float, pull_inner = jax.vjp(gated_gelu, gate_two, upward)
    inner_low = inner_float.astype(halves)
    result = plain_dot(inner_low, feed_down)
    output_rows = ((hidden + result) * live_mask[:, None]).astype(halves)
    outer_grad = cot_rows.astype(floats) * live_mask[:, None]
    result_low = outer_grad.astype(halves)
    inner_grad = transposed(result_low, feed_down)
    gate_two_grad, upward_grad = pull_inner(inner_grad)
    gate_two_low = gate_two_grad.astype(halves)
    upward_low = upward_grad.astype(halves)
    second_grad = transposed(gate_two_low, feed_gate) + transposed(upward_low, feed_up)
    hidden_part, second_gain_grad = pull_two(second_grad)
    hidden_grad = outer_grad + hidden_part
    branch_low = hidden_grad.astype(halves)
    mixed_grad = transposed(branch_low, output_weight)
    swish_grad, grouped_grad = pull_mixed(mixed_grad)
    swish_low = swish_grad.astype(halves)
    retained_grad, group_gain_grad = pull_group(
        grouped_grad.reshape(token_rows, head_count, value_size)
    )
    retained_low = retained_grad.astype(halves)
    weights_grad = jnp.einsum("ihe,jhe->hij", retained_low, values3, preferred_element_type=floats)
    scores_low = (weights_grad * decay_matrix).astype(halves)
    query_intra = jnp.einsum("hij,jhd->ihd", scores_low, keys3, preferred_element_type=floats)
    key_intra = jnp.einsum("hij,ihd->jhd", scores_low, queries3, preferred_element_type=floats)
    value_intra = jnp.einsum("hij,ihe->jhe", weights, retained_low, preferred_element_type=floats)
    retained_wide = retained_low.astype(floats)
    query_carried = entry_decay * jnp.einsum(
        "ihe,hde->ihd", retained_wide, start_state, precision=HIGHEST
    )
    local_grad = jnp.einsum(
        "ihd,ihe->hde", query_wide * entry_decay, retained_wide, precision=HIGHEST
    )
    _, end_grad = carried_in((block_decay, local_grad), "seq", chain_states, state_identity, True)
    key_state = end_weight * jnp.einsum("jhe,hde->jhd", value_wide, end_grad, precision=HIGHEST)
    value_state = end_weight * jnp.einsum("jhd,hde->jhe", key_wide, end_grad, precision=HIGHEST)
    query_low = (
        (query_intra + query_carried).astype(halves).reshape(token_rows, head_count * key_size)
    )
    key_low = (
        ((key_intra + key_state) * live_mask[:, None, None])
        .astype(halves)
        .reshape(token_rows, head_count * key_size)
    )
    value_low = (
        (value_intra + value_state).astype(halves).reshape(token_rows, head_count * value_size)
    )
    normed_grad = (
        transposed(query_low, query_weight)
        + transposed(key_low, key_weight)
        + transposed(value_low, value_weight)
        + transposed(swish_low, swish_weight)
    )
    input_part, first_gain_grad = pull_one(normed_grad)
    grad_rows = (hidden_grad + input_part).astype(halves)
    matrix_pairs = [
        (normed, query_low),
        (normed, key_low),
        (normed, value_low),
        (normed, swish_low),
        (mixed_low, branch_low),
        (second, gate_two_low),
        (second, upward_low),
        (inner_low, result_low),
    ]
    vectors = [first_gain_grad, group_gain_grad.reshape(-1), second_gain_grad]
    return (output_rows, grad_rows, matrix_pairs, vectors)


def general_body(
    tokens,
    cotangent,
    lengths,
    block_order,
    log_decay,
    first_gain,
    query_weight,
    key_weight,
    value_weight,
    swish_weight,
    output_weight,
    group_gain,
    second_gain,
    feed_gate,
    feed_up,
    feed_down,
):
    batches = tokens.shape[0]
    block_rows = tokens.shape[1]
    selected_locations = lax.axis_size("seq")
    position = lax.axis_index("seq")
    group_index = lax.axis_index("fsdp")
    place_numbers = jnp.arange(selected_locations, dtype=jnp.int32)
    arrived_tokens, arrived_cotangent = (
        lax.all_gather(tokens, "seq", axis=1, tiled=True),
        lax.all_gather(cotangent, "seq", axis=1, tiled=True),
    )
    gathered = (
        lax.all_gather(first_gain, ("seq", "fsdp"), axis=0, tiled=True),
        lax.all_gather(query_weight, ("seq", "fsdp"), axis=0, tiled=True),
        lax.all_gather(key_weight, ("seq", "fsdp"), axis=0, tiled=True),
        lax.all_gather(value_weight, ("seq", "fsdp"), axis=0, tiled=True),
        lax.all_gather(swish_weight, ("seq", "fsdp"), axis=0, tiled=True),
        lax.all_gather(output_weight, ("seq", "fsdp"), axis=0, tiled=True),
        lax.all_gather(group_gain, ("seq", "fsdp"), axis=0, tiled=True),
        lax.all_gather(second_gain, ("seq", "fsdp"), axis=0, tiled=True),
        lax.all_gather(feed_gate, ("seq", "fsdp"), axis=0, tiled=True),
        lax.all_gather(feed_up, ("seq", "fsdp"), axis=0, tiled=True),
        lax.all_gather(feed_down, ("seq", "fsdp"), axis=0, tiled=True),
    )
    outputs = []
    input_grads = []
    collected = []
    order_rows = []
    for batch_number in range(batches):
        sequence = group_index * batches + batch_number
        order_row = lax.dynamic_index_in_dim(block_order, sequence, 0, keepdims=False)
        order_rows.append(order_row)
        source = jnp.sum(place_numbers * (order_row == position).astype(jnp.int32))
        token_rows = lax.dynamic_slice_in_dim(
            arrived_tokens[batch_number], source * block_rows, block_rows, 0
        )
        cot_rows = lax.dynamic_slice_in_dim(
            arrived_cotangent[batch_number], source * block_rows, block_rows, 0
        )
        live_length = lax.dynamic_index_in_dim(lengths, sequence, 0, keepdims=False)
        location_number = position * block_rows + jnp.arange(block_rows, dtype=jnp.int32)
        live_mask = (location_number < live_length).astype(jnp.float32)
        output_rows, grad_rows, matrix_pairs, vectors = layer_step(
            gathered, token_rows, cot_rows, live_mask, log_decay
        )
        outputs.append(output_rows)
        input_grads.append(grad_rows)
        collected.append((matrix_pairs, vectors))
    joined_pairs, joined_vectors = join_terms(collected)
    shards = spread_sum(joined_pairs, joined_vectors)
    every_output, every_grad = (
        lax.all_gather(jnp.stack(outputs), "seq", axis=1, tiled=True),
        lax.all_gather(jnp.stack(input_grads), "seq", axis=1, tiled=True),
    )
    returned = []
    returned_grads = []
    for batch_number in range(batches):
        target = lax.dynamic_index_in_dim(order_rows[batch_number], position, 0, keepdims=False)
        returned.append(
            lax.dynamic_slice_in_dim(every_output[batch_number], target * block_rows, block_rows, 0)
        )
        returned_grads.append(
            lax.dynamic_slice_in_dim(every_grad[batch_number], target * block_rows, block_rows, 0)
        )
    return (
        jnp.stack(returned),
        jnp.stack(returned_grads),
        shards[8],
        shards[0],
        shards[1],
        shards[2],
        shards[3],
        shards[4],
        shards[9],
        shards[10],
        shards[5],
        shards[6],
        shards[7],
    )


FULL = jnp.float32
HALF = jnp.bfloat16
MESH = pl.DeviceIdType.MESH
VMEM_BYTES = 56 * 1024 * 1024
LANES = 128


def dot_nn(left, right):
    return jnp.dot(left, right, preferred_element_type=FULL)


def dot_nt(left, right):
    return lax.dot_general(left, right, (((1,), (1,)), ((), ())), preferred_element_type=FULL)


def dot_tn(left, right):
    return lax.dot_general(left, right, (((0,), (0,)), ((), ())), preferred_element_type=FULL)


def plane_peers():
    me = lax.axis_index("seq")
    core = lax.rem(me, 2)
    across = 2 - 4 * lax.rem(me // 2, 2)
    down = 4 - 8 * (me // 4)
    return me, me + 1 - 2 * core, me + across, me + down, me + across + down


def to_peer(source, target, send, receive, peer):
    return pltpu.make_async_remote_copy(
        src_ref=source,
        dst_ref=target,
        send_sem=send,
        recv_sem=receive,
        device_id={"seq": peer},
        device_id_type=MESH,
    )


def greet_neighbours():
    _, other, near, below, _ = plane_peers()
    barrier = pltpu.get_barrier_semaphore()
    for peer in (other, near, below):
        pl.semaphore_signal(barrier, inc=1, device_id={"seq": peer}, device_id_type=MESH)
    pl.semaphore_wait(barrier, 3)


GATHER_COPIES = 14


def gather_plan():
    me, other, near, below, far = plane_peers()
    flip = other - me
    return (
        (me, 0, near, near),
        (me, 1, below, below),
        (me, 0, other, other),
        (me, 1, other, other),
        (me, 1, near, near),
        (me, 0, below, below),
        (near, 0, below, far),
        (below, 1, near, far),
        (near, 0, other, near + flip),
        (below, 1, other, below + flip),
        (near, 1, other, near + flip),
        (below, 0, other, below + flip),
        (far, 0, other, far + flip),
        (far, 1, other, far + flip),
    )


class PlaneGather:
    def __init__(self, own, out, keep, sends, receives):
        self.own, self.out = own, out
        self.keep, self.sends, self.receives = keep, sends, receives
        self.half = own.shape[0] // 2

    def rows(self, which):
        return pl.ds(which * self.half, self.half)

    def kept(self):
        me = lax.axis_index("seq")
        return pltpu.make_async_copy(self.own, self.out.at[me], self.keep)

    def copy(self, number):
        block, which, peer, _ = gather_plan()[number]
        target = self.out.at[block, self.rows(which)]
        source = self.own.at[self.rows(which)] if number < 6 else target
        return to_peer(source, target, self.sends.at[number], self.receives.at[number], peer)

    def landed(self, number):
        _, which, peer, landing = gather_plan()[number]
        target = self.out.at[landing, self.rows(which)]
        to_peer(target, target, self.sends.at[number], self.receives.at[number], peer).wait_recv()

    def begin(self):
        self.kept().start()
        for number in range(6):
            self.copy(number).start()

    def relay(self):
        for arrived, onward in ((0, (6, 8)), (1, (7, 9)), (4, (10,)), (5, (11,))):
            self.landed(arrived)
            for number in onward:
                self.copy(number).start()

    def finish(self):
        for arrived, onward in ((6, 12), (7, 13)):
            self.landed(arrived)
            self.copy(onward).start()
        for number in (2, 3, 8, 9, 10, 11, 12, 13):
            self.landed(number)
        for number in range(GATHER_COPIES):
            self.copy(number).wait_send()
        self.kept().wait()


def gather_scratch():
    return [
        pltpu.SemaphoreType.DMA,
        pltpu.SemaphoreType.DMA((GATHER_COPIES,)),
        pltpu.SemaphoreType.DMA((GATHER_COPIES,)),
    ]


SCATTER_COPIES = 10
CHUNK = 32


def by_chunks(rows, work):
    def step(number, carry):
        work(pl.ds(pl.multiple_of(number * CHUNK, CHUNK), CHUNK))
        return carry

    lax.fori_loop(0, rows // CHUNK, step, 0)


class PlaneScatter:
    def __init__(self, term, terms, cores, nears, belows, sends, receives):
        self.term, self.terms, self.cores = term, terms, cores
        self.nears, self.belows = nears, belows
        self.sends, self.receives = sends, receives
        self.size = terms.shape[1]
        self.half = self.size // 2

    def copy(self, number):
        _, other, near, below, _ = plane_peers()
        upper, lower = pl.ds(0, self.half), pl.ds(self.half, self.half)
        if number < 4:
            source, target, peer = self.terms.at[4 + number], self.cores.at[number], other
        else:
            source, target, peer = (
                (self.terms.at[0, upper], self.nears.at[0], near),
                (self.terms.at[0, lower], self.belows.at[0], below),
                (self.terms.at[1, upper], self.nears.at[1], near),
                (self.terms.at[2, lower], self.belows.at[1], below),
                (self.terms.at[1, lower], self.nears.at[2], near),
                (self.terms.at[2, upper], self.belows.at[2], below),
            )[number - 4]
        return to_peer(source, target, self.sends.at[number], self.receives.at[number], peer)

    def fold(self, slot):
        def work(rows):
            self.terms[slot, rows] = (
                self.terms[slot, rows].astype(FULL) + self.cores[slot, rows].astype(FULL)
            ).astype(HALF)

        by_chunks(self.size, work)

    def fold_half(self, slot, start, landed):
        def work(rows):
            here = pl.ds(pl.multiple_of(start + rows.start, CHUNK), CHUNK)
            self.terms[slot, here] = (
                self.terms[slot, here].astype(FULL) + landed[rows].astype(FULL)
            ).astype(HALF)

        by_chunks(self.half, work)

    def run(self):
        me, other, near, below, far = plane_peers()
        blocks = (far, near, below, me)
        flip = other - me
        for slot in range(4):
            self.terms[4 + slot] = self.term(blocks[slot] + flip)
            self.copy(slot).start()
        for slot in range(4):
            self.terms[slot] = self.term(blocks[slot])
        self.copy(0).wait_recv()
        self.fold(0)
        self.copy(4).start()
        self.copy(5).start()
        self.copy(1).wait_recv()
        self.fold(1)
        self.copy(6).start()
        self.copy(2).wait_recv()
        self.fold(2)
        self.copy(7).start()
        self.copy(3).wait_recv()
        self.fold(3)
        self.copy(4).wait_recv()
        self.fold_half(2, 0, self.nears.at[0])
        self.copy(9).start()
        self.copy(5).wait_recv()
        self.fold_half(1, self.half, self.belows.at[0])
        self.copy(8).start()
        for number in (6, 7, 8, 9):
            self.copy(number).wait_recv()
        for number in range(SCATTER_COPIES):
            self.copy(number).wait_send()

    def total(self, start, size):
        upper = start < self.half
        at = start if upper else start - self.half
        near, below = (1, 2) if upper else (2, 1)
        rows = pl.ds(at, size)
        return (
            self.terms[3, pl.ds(start, size)].astype(FULL)
            + self.nears[near, rows].astype(FULL)
            + self.belows[below, rows].astype(FULL)
        )


def scatter_scratch(rows, width):
    return [
        pltpu.VMEM((8, rows, width), HALF),
        pltpu.VMEM((4, rows, width), HALF),
        pltpu.VMEM((3, rows // 2, width), HALF),
        pltpu.VMEM((3, rows // 2, width), HALF),
        pltpu.SemaphoreType.DMA((SCATTER_COPIES,)),
        pltpu.SemaphoreType.DMA((SCATTER_COPIES,)),
    ]


def regroup(values, outer, inner):
    rows = values.shape[0]
    low_half = lax.broadcasted_iota(jnp.int32, (rows, LANES), 1) < LANES // 2

    def piece(p, q):
        at = (p * inner + q) // 2
        return values[:, at * LANES : (at + 1) * LANES]

    def turned(value):
        return pltpu.roll(value, LANES // 2, 1)

    groups = []
    for q in range(inner):
        for p in range(0, outer, 2):
            first, second = piece(p, q), piece(p + 1, q)
            if q % 2 == 0:
                groups.append(jnp.where(low_half, first, turned(second)))
            else:
                groups.append(jnp.where(low_half, turned(first), second))
    return jnp.concatenate(groups, axis=1)


def normalised(values):
    average = jnp.mean(values, axis=-1, keepdims=True)
    centered = values - average
    scale = lax.rsqrt(jnp.mean(centered * centered, axis=-1, keepdims=True) + EPSILON)
    return centered * scale, scale


def normalised_back(grad, normed, scale):
    average = jnp.mean(grad, axis=-1, keepdims=True)
    along = jnp.mean(grad * normed, axis=-1, keepdims=True)
    return (grad - average - normed * along) * scale


def vmem():
    return pl.BlockSpec(memory_space=pltpu.VMEM)


def in_hbm():
    return pl.BlockSpec(memory_space=pl.ANY)


def cost(flops, link_bytes):
    return pl.CostEstimate(flops=int(flops), bytes_accessed=int(link_bytes) * 16, transcendentals=0)


def linked(collective):
    return pltpu.CompilerParams(
        collective_id=collective, has_side_effects=True, vmem_limit_bytes=VMEM_BYTES
    )


class PlaneSwap:
    def __init__(self, weights, targets, keeps, sends, receives):
        self.weights, self.targets = weights, targets
        self.keeps, self.sends, self.receives = keeps, sends, receives
        self.peers = lax.axis_size("seq")

    def part(self, number, peer):
        weight, (target, start) = self.weights[number], self.targets[number]
        size = weight.shape[1] // self.peers
        return weight.at[:, pl.ds(pl.multiple_of(peer * size, LANES), size)]

    def place(self, number, peer):
        weight, (target, start) = self.weights[number], self.targets[number]
        return target.at[peer, :, pl.ds(start, weight.shape[1] // self.peers)]

    def copy(self, number, turn):
        me = lax.axis_index("seq")
        peer = lax.rem(me + turn, self.peers)
        return to_peer(
            self.part(number, peer),
            self.place(number, me),
            self.sends.at[number, turn],
            self.receives.at[number, turn],
            peer,
        )

    def landed(self, number, turn):
        me = lax.axis_index("seq")
        peer = lax.rem(me + self.peers - turn, self.peers)
        target = self.place(number, peer)
        to_peer(
            target, target, self.sends.at[number, turn], self.receives.at[number, turn], peer
        ).wait_recv()

    def kept(self, number):
        me = lax.axis_index("seq")
        return pltpu.make_async_copy(
            self.part(number, me), self.place(number, me), self.keeps.at[number]
        )

    def begin(self):
        for number in range(len(self.weights)):
            for turn in range(1, self.peers):
                self.copy(number, turn).start()
            self.kept(number).start()

    def finish(self):
        for number in range(len(self.weights)):
            for turn in range(1, self.peers):
                self.landed(number, turn)
                self.copy(number, turn).wait_send()
            self.kept(number).wait()


def swap_scratch(count, peers):
    return [
        pltpu.SemaphoreType.DMA((count,)),
        pltpu.SemaphoreType.DMA((count, peers)),
        pltpu.SemaphoreType.DMA((count, peers)),
    ]


def greet_plane(with_groups):
    me, group = lax.axis_index("seq"), lax.axis_index("fsdp")
    peers, groups = lax.axis_size("seq"), lax.axis_size("fsdp")
    barrier = pltpu.get_barrier_semaphore()
    count = peers - 1
    for turn in range(1, peers):
        peer = lax.rem(me + turn, peers)
        pl.semaphore_signal(barrier, inc=1, device_id={"seq": peer}, device_id_type=MESH)
    if with_groups:
        count += groups - 1
        for turn in range(1, groups):
            peer = lax.rem(group + turn, groups)
            pl.semaphore_signal(barrier, inc=1, device_id={"fsdp": peer}, device_id_type=MESH)
    pl.semaphore_wait(barrier, count)


def all_to_each(source, out, axis, size, keep, sends, receives):
    me = lax.axis_index(axis)

    def copy(turn, slot):
        peer = lax.rem(me + turn, size)
        return pltpu.make_async_remote_copy(
            src_ref=source,
            dst_ref=out.at[slot],
            send_sem=sends.at[turn],
            recv_sem=receives.at[turn],
            device_id={axis: peer},
            device_id_type=MESH,
        )

    def begin():
        pltpu.make_async_copy(source, out.at[me], keep).start()
        for turn in range(1, size):
            copy(turn, me).start()

    def finish():
        for turn in range(1, size):
            copy(turn, lax.rem(me + size - turn, size)).wait_recv()
            copy(turn, me).wait_send()
        pltpu.make_async_copy(source, out.at[me], keep).wait()

    return begin, finish


def first_swap_kernel(
    query_ref, key_ref, value_ref, swish_ref, rates_ref, gains_ref,
    pair_ref, value_out, swish_out, rates_out, gains_out,
    column, keeps, sends, receives, rate_keep, rate_sends, rate_receives,
    group_keep, group_sends, group_receives, gain_keep, gain_sends, gain_receives,
):
    peers, groups = lax.axis_size("seq"), lax.axis_size("fsdp")
    size = query_ref.shape[1] // peers
    greet_plane(True)
    begin_groups, finish_groups = all_to_each(
        gains_ref, column, "fsdp", groups, group_keep, group_sends, group_receives
    )
    begin_rates, finish_rates = all_to_each(
        rates_ref, rates_out, "seq", peers, rate_keep, rate_sends, rate_receives
    )
    begin_gains, finish_gains = all_to_each(
        column, gains_out, "seq", peers, gain_keep, gain_sends, gain_receives
    )
    swap = PlaneSwap(
        (query_ref, key_ref, value_ref, swish_ref),
        ((pair_ref, 0), (pair_ref, size), (value_out, 0), (swish_out, 0)),
        keeps,
        sends,
        receives,
    )
    begin_groups()
    begin_rates()
    swap.begin()
    finish_groups()
    begin_gains()
    finish_rates()
    finish_gains()
    swap.finish()


def first_swap(query, key, value, swish, rates, gains):
    peers, groups = lax.axis_size("seq"), lax.axis_size("fsdp")
    slab = query.shape[0]
    pair, single, gate = (
        2 * query.shape[1] // peers,
        value.shape[1] // peers,
        swish.shape[1] // peers,
    )
    return pl.pallas_call(
        first_swap_kernel,
        in_specs=[in_hbm()] * 4 + [vmem()] * 2,
        out_specs=[in_hbm()] * 3 + [vmem()] * 2,
        out_shape=[
            jax.ShapeDtypeStruct((peers, slab, pair), HALF),
            jax.ShapeDtypeStruct((peers, slab, single), HALF),
            jax.ShapeDtypeStruct((peers, slab, gate), HALF),
            jax.ShapeDtypeStruct((peers,) + rates.shape, FULL),
            jax.ShapeDtypeStruct((peers, groups) + gains.shape, FULL),
        ],
        scratch_shapes=[pltpu.VMEM((groups,) + gains.shape, FULL)]
        + swap_scratch(4, peers)
        + [pltpu.SemaphoreType.DMA] + [pltpu.SemaphoreType.DMA((peers,))] * 2
        + [pltpu.SemaphoreType.DMA] + [pltpu.SemaphoreType.DMA((groups,))] * 2
        + [pltpu.SemaphoreType.DMA] + [pltpu.SemaphoreType.DMA((peers,))] * 2,
        compiler_params=linked(0),
        cost_estimate=cost(0, 2 * slab * peers * (pair + single + gate)),
    )(query, key, value, swish, rates, gains)


def inputs_kernel(
    tokens_ref, grad_ref, mask_ref, gain_ref, gate_ref, up_ref,
    entered_out, grads_out, feed_out,
    own_entered, own_grad, keep_one, sends_one, receives_one, keep_two, sends_two, receives_two,
    keeps, sends, receives,
):
    peers, groups = lax.axis_size("seq"), lax.axis_size("fsdp")
    greet_plane(False)
    size = gate_ref.shape[1] // peers
    gain = gain_ref[...]

    def work(rows):
        normed, _ = normalised(tokens_ref[rows].astype(FULL))
        own_entered[rows] = regroup(normed * gain, peers, groups).astype(HALF)
        own_grad[rows] = (grad_ref[rows].astype(FULL) * mask_ref[rows]).astype(HALF)

    by_chunks(tokens_ref.shape[0], work)
    one = PlaneGather(own_entered, entered_out, keep_one, sends_one, receives_one)
    two = PlaneGather(own_grad, grads_out, keep_two, sends_two, receives_two)
    swap = PlaneSwap((gate_ref, up_ref), ((feed_out, 0), (feed_out, size)), keeps, sends, receives)
    one.begin()
    one.relay()
    swap.begin()
    two.begin()
    one.finish()
    two.relay()
    swap.finish()
    two.finish()


def gather_inputs(tokens, grad, mask, gain, gate, up):
    peers = lax.axis_size("seq")
    own, width = tokens.shape
    slab, columns = gate.shape
    part = columns // peers
    return pl.pallas_call(
        inputs_kernel,
        in_specs=[vmem()] * 4 + [in_hbm()] * 2,
        out_specs=[in_hbm()] * 3,
        out_shape=[
            jax.ShapeDtypeStruct((peers, own, width), HALF),
            jax.ShapeDtypeStruct((peers, own, width), HALF),
            jax.ShapeDtypeStruct((peers, slab, 2 * part), HALF),
        ],
        scratch_shapes=[pltpu.VMEM((own, width), HALF)] * 2
        + gather_scratch()
        + gather_scratch()
        + swap_scratch(2, peers),
        compiler_params=linked(1),
        cost_estimate=cost(0, 2 * peers * (2 * own * width + slab * 2 * part)),
    )(tokens, grad, mask, gain, gate, up)


def retention_kernel(
    place_ref, live_ref, first_ref, second_ref, pair_ref, value_weight_ref, decay_ref, column_ref,
    qkv_ref, scale_ref, entry_ref, normed_hbm, state, normed_buffer, sems,
):
    step, steps = pl.program_id(0), pl.num_programs(0)
    rows = first_ref.shape[2]
    batches, key_size, _ = state.shape
    slot = lax.rem(step, 2)

    def sent(at, which, batch):
        return pltpu.make_async_copy(
            normed_buffer.at[which, batch],
            normed_hbm.at[place_ref[batch, at], batch],
            sems.at[which, batch],
        )

    @pl.when(step == 0)
    def _():
        state[...] = jnp.zeros_like(state)

    @pl.when(step >= 2)
    def _():
        for batch in range(batches):
            sent(step - 2, slot, batch).wait()

    rows_in = jnp.concatenate([first_ref[0, 0], second_ref[0, 0]], axis=0)
    pairs = dot_nn(rows_in, pair_ref[...])
    values = dot_nn(rows_in, value_weight_ref[...])
    decay = decay_ref[0]
    entry_decay = column_ref[0, :, 0:1]
    end_weight = column_ref[0, :, 1:2]
    block_decay = column_ref[0, rows - 1 : rows, 0:1]
    positions = step * rows + lax.broadcasted_iota(jnp.int32, (rows, 1), 0)
    for batch in range(batches):
        mine = slice(batch * rows, (batch + 1) * rows)
        live = (positions < live_ref[batch]).astype(FULL)
        query = pairs[mine, :key_size].astype(HALF)
        key = (pairs[mine, key_size:] * live).astype(HALF)
        value = values[mine].astype(HALF)
        before = state[batch]
        before_low = before.astype(HALF)
        weights = (dot_nt(query, key) * decay).astype(HALF)
        retained = dot_nn(weights, value) + entry_decay * dot_nn(query, before_low)
        key_ended = (key.astype(FULL) * end_weight).astype(HALF)
        state[batch] = block_decay * before + dot_tn(key_ended, value)
        normed, scale = normalised(retained)
        qkv_ref[batch, 0, :, :key_size] = query
        qkv_ref[batch, 0, :, key_size : 2 * key_size] = key
        qkv_ref[batch, 0, :, 2 * key_size :] = value
        scale_ref[batch, 0] = jnp.broadcast_to(scale, scale_ref.shape[2:])
        entry_ref[batch, 0] = before_low
        normed_buffer[slot, batch] = normed.astype(HALF)
        sent(step, slot, batch).start()

    @pl.when(step == steps - 1)
    def _():
        for batch in range(batches):
            sent(step, slot, batch).wait()
            sent(step - 1, 1 - slot, batch).wait()


def retention(rows_in, pair_weight, value_weight, place, live, decay, columns):
    blocks, batches, rows, width = rows_in.shape
    key_size, value_size = pair_weight.shape[1] // 2, value_weight.shape[1]
    total = 2 * key_size + value_size

    def arriving(batch):
        return pl.BlockSpec(
            (1, 1, rows, width), lambda i, place, live: (place[batch, i], batch, 0, 0)
        )

    def whole(shape):
        return pl.BlockSpec(
            shape, lambda i, place, live: (0,) * len(shape), pipeline_mode=pl.Buffered(1)
        )

    def here(*tail):
        return pl.BlockSpec((batches, 1) + tail, lambda i, place, live: (0, i, 0, 0))

    def along(*tail):
        return pl.BlockSpec((1,) + tail, lambda i, place, live: (i, 0, 0))

    return pl.pallas_call(
        retention_kernel,
        grid_spec=pltpu.PrefetchScalarGridSpec(
            num_scalar_prefetch=2,
            grid=(blocks,),
            in_specs=[
                arriving(0),
                arriving(1),
                whole((width, 2 * key_size)),
                whole((width, value_size)),
                along(rows, rows),
                along(rows, 2),
            ],
            out_specs=[
                here(rows, total),
                here(rows, LANES),
                here(key_size, value_size),
                in_hbm(),
            ],
            scratch_shapes=[
                pltpu.VMEM((batches, key_size, value_size), FULL),
                pltpu.VMEM((2, batches, rows, value_size), HALF),
                pltpu.SemaphoreType.DMA((2, batches)),
            ],
        ),
        out_shape=[
            jax.ShapeDtypeStruct((batches, blocks, rows, total), HALF),
            jax.ShapeDtypeStruct((batches, blocks, rows, LANES), FULL),
            jax.ShapeDtypeStruct((batches, blocks, key_size, value_size), HALF),
            jax.ShapeDtypeStruct((blocks, batches, rows, value_size), HALF),
        ],
        compiler_params=pltpu.CompilerParams(
            dimension_semantics=("arbitrary",), vmem_limit_bytes=VMEM_BYTES
        ),
        cost_estimate=pl.CostEstimate(
            flops=2 * blocks * batches * rows * width * total,
            bytes_accessed=2 * blocks * batches * rows * (width + total) + 2 * width * total,
            transcendentals=0,
        ),
    )(place, live, rows_in, rows_in, pair_weight, value_weight, decay, columns)


def retention_back_kernel(
    place_ref, live_ref, first_ref, second_ref, swish_one, swish_two, normed_one, normed_two,
    weight_ref, decay_ref, column_ref, gain_ref, qkv_ref, scale_ref, entry_ref,
    gain_grad_ref, grads_hbm, state, grads_buffer, sems,
):
    step, steps = pl.program_id(0), pl.num_programs(0)
    rows = first_ref.shape[2]
    batches, key_size, value_size = state.shape
    slot = lax.rem(step, 2)

    def sent(at, which, batch):
        return pltpu.make_async_copy(
            grads_buffer.at[which, batch],
            grads_hbm.at[place_ref[batch, steps - 1 - at], batch],
            sems.at[which, batch],
        )

    @pl.when(step == 0)
    def _():
        state[...] = jnp.zeros_like(state)
        gain_grad_ref[...] = jnp.zeros_like(gain_grad_ref)

    @pl.when(step >= 2)
    def _():
        for batch in range(batches):
            sent(step - 2, slot, batch).wait()

    rows_in = jnp.concatenate([first_ref[0, 0], second_ref[0, 0]], axis=0)
    mixed_grads = dot_nt(rows_in, weight_ref[...])
    decay = decay_ref[0]
    entry_decay = column_ref[0, :, 0:1]
    end_weight = column_ref[0, :, 1:2]
    block_decay = column_ref[0, rows - 1 : rows, 0:1]
    positions = (steps - 1 - step) * rows + lax.broadcasted_iota(jnp.int32, (rows, 1), 0)
    gain = gain_ref[...]
    for batch, (swish_ref, normed_ref) in enumerate(
        ((swish_one, normed_one), (swish_two, normed_two))
    ):
        live = (positions < live_ref[batch]).astype(FULL)
        mixed_grad = mixed_grads[batch * rows : (batch + 1) * rows]
        query = qkv_ref[batch, 0, :, :key_size]
        key = qkv_ref[batch, 0, :, key_size : 2 * key_size]
        value = qkv_ref[batch, 0, :, 2 * key_size :]
        swish = swish_ref[0, 0].astype(FULL)
        normed = normed_ref[0, 0].astype(FULL)
        scale = scale_ref[batch, 0, :, 0:1]
        entry = entry_ref[batch, 0]
        sigmoid = jax.nn.sigmoid(swish)
        silu = swish * sigmoid
        swish_grad = mixed_grad * (normed * gain) * (sigmoid * (1.0 + swish - silu))
        scaled_grad = mixed_grad * silu
        gain_grad_ref[...] += jnp.sum(scaled_grad * normed, axis=0, keepdims=True)
        retained_grad = normalised_back(scaled_grad * gain, normed, scale).astype(HALF)
        weights = (dot_nt(query, key) * decay).astype(HALF)
        scores_grad = (dot_nt(retained_grad, value) * decay).astype(HALF)
        after = state[batch]
        after_low = after.astype(HALF)
        query_grad = dot_nn(scores_grad, key) + entry_decay * dot_nt(retained_grad, entry)
        key_grad = dot_tn(scores_grad, query) + end_weight * dot_nt(value, after_low)
        value_grad = dot_tn(weights, retained_grad) + end_weight * dot_nn(key, after_low)
        query_entered = (query.astype(FULL) * entry_decay).astype(HALF)
        state[batch] = block_decay * after + dot_tn(query_entered, retained_grad)
        grads_buffer[slot, batch, :, :key_size] = query_grad.astype(HALF)
        grads_buffer[slot, batch, :, key_size : 2 * key_size] = (key_grad * live).astype(HALF)
        grads_buffer[slot, batch, :, 2 * key_size : 2 * key_size + value_size] = value_grad.astype(
            HALF
        )
        grads_buffer[slot, batch, :, 2 * key_size + value_size :] = swish_grad.astype(HALF)
        sent(step, slot, batch).start()

    @pl.when(step == steps - 1)
    def _():
        for batch in range(batches):
            sent(step, slot, batch).wait()
            sent(step - 1, 1 - slot, batch).wait()


def retention_back(rows_in, swish, normed, weight, place, live, decay, columns, gain, saved):
    blocks, batches, rows, width = rows_in.shape
    qkv, scale, entry = saved
    value_size = gain.shape[-1]
    key_size = entry.shape[2]
    total = 2 * key_size + 2 * value_size

    def arriving(batch, size):
        return pl.BlockSpec(
            (1, 1, rows, size),
            lambda i, place, live: (place[batch, blocks - 1 - i], batch, 0, 0),
        )

    def whole(shape):
        return pl.BlockSpec(
            shape, lambda i, place, live: (0,) * len(shape), pipeline_mode=pl.Buffered(1)
        )

    def here(*tail):
        return pl.BlockSpec((batches, 1) + tail, lambda i, place, live: (0, blocks - 1 - i, 0, 0))

    def along(*tail):
        return pl.BlockSpec((1,) + tail, lambda i, place, live: (blocks - 1 - i, 0, 0))

    return pl.pallas_call(
        retention_back_kernel,
        grid_spec=pltpu.PrefetchScalarGridSpec(
            num_scalar_prefetch=2,
            grid=(blocks,),
            in_specs=[
                arriving(0, width),
                arriving(1, width),
                arriving(0, value_size),
                arriving(1, value_size),
                arriving(0, value_size),
                arriving(1, value_size),
                whole((value_size, width)),
                along(rows, rows),
                along(rows, 2),
                whole((1, value_size)),
                here(rows, 2 * key_size + value_size),
                here(rows, LANES),
                here(key_size, value_size),
            ],
            out_specs=[
                pl.BlockSpec((1, value_size), lambda i, place, live: (0, 0)),
                in_hbm(),
            ],
            scratch_shapes=[
                pltpu.VMEM((batches, key_size, value_size), FULL),
                pltpu.VMEM((2, batches, rows, total), HALF),
                pltpu.SemaphoreType.DMA((2, batches)),
            ],
        ),
        out_shape=[
            jax.ShapeDtypeStruct((1, value_size), FULL),
            jax.ShapeDtypeStruct((blocks, batches, rows, total), HALF),
        ],
        compiler_params=pltpu.CompilerParams(
            dimension_semantics=("arbitrary",), vmem_limit_bytes=VMEM_BYTES
        ),
        cost_estimate=pl.CostEstimate(
            flops=6 * blocks * batches * rows * width * value_size,
            bytes_accessed=2 * blocks * batches * rows * (width + 2 * total)
            + 2 * width * value_size,
            transcendentals=0,
        ),
    )(
        place, live, rows_in, rows_in, swish, swish, normed, normed, weight, decay, columns, gain,
        qkv, scale, entry,
    )


def middle_kernel(
    mixed_ref, weight_ref, tokens_ref, gain_ref, hidden_ref, second_out,
    terms, cores, nears, belows, sends, receives, own, keep, gather_sends, gather_receives,
):
    peers, groups = lax.axis_size("seq"), lax.axis_size("fsdp")
    size = tokens_ref.shape[0]
    greet_neighbours()

    def term(block):
        return dot_nn(mixed_ref[block], weight_ref[...]).astype(HALF)

    scatter = PlaneScatter(term, terms, cores, nears, belows, sends, receives)
    scatter.run()
    gain = gain_ref[...]
    for start in range(0, size, CHUNK):
        rows = pl.ds(start, CHUNK)
        hidden = tokens_ref[rows].astype(FULL) + scatter.total(start, CHUNK)
        hidden_ref[rows] = hidden
        normed, _ = normalised(hidden)
        own[rows] = regroup(normed * gain, peers, groups).astype(HALF)
    gather = PlaneGather(own, second_out, keep, gather_sends, gather_receives)
    gather.begin()
    gather.relay()
    gather.finish()


def middle(mixed, weight, tokens, gain):
    peers, own, inner = mixed.shape
    width = weight.shape[1]
    return pl.pallas_call(
        middle_kernel,
        in_specs=[vmem()] * 4,
        out_specs=[vmem(), in_hbm()],
        out_shape=[
            jax.ShapeDtypeStruct((own, width), FULL),
            jax.ShapeDtypeStruct((peers, own, width), HALF),
        ],
        scratch_shapes=scatter_scratch(own, width)
        + [pltpu.VMEM((own, width), HALF)]
        + gather_scratch(),
        compiler_params=linked(2),
        cost_estimate=cost(2 * peers * own * inner * width, 4 * peers * own * width),
    )(mixed, weight, tokens, gain)


def middle_back_kernel(
    grads_ref, weight_ref, hidden_ref, outer_ref, mask_ref, gain_ref,
    hidden_grad_ref, gain_grad_ref, branch_out,
    terms, cores, nears, belows, sends, receives, own, keep, gather_sends, gather_receives,
):
    peers, groups = lax.axis_size("seq"), lax.axis_size("fsdp")
    size = hidden_ref.shape[0]
    greet_neighbours()

    def term(block):
        return dot_nt(grads_ref[block], weight_ref[...]).astype(HALF)

    scatter = PlaneScatter(term, terms, cores, nears, belows, sends, receives)
    scatter.run()
    gain = gain_ref[...]
    gain_grad_ref[...] = jnp.zeros_like(gain_grad_ref)
    for start in range(0, size, CHUNK):
        rows = pl.ds(start, CHUNK)
        grad = regroup(scatter.total(start, CHUNK), groups, peers)
        normed, scale = normalised(hidden_ref[rows])
        gain_grad_ref[...] += jnp.sum(grad * normed, axis=0, keepdims=True)
        outer = outer_ref[rows].astype(FULL) * mask_ref[rows]
        hidden_grad = outer + normalised_back(grad * gain, normed, scale)
        hidden_grad_ref[rows] = hidden_grad
        own[rows] = hidden_grad.astype(HALF)
    gather = PlaneGather(own, branch_out, keep, gather_sends, gather_receives)
    gather.begin()
    gather.relay()
    gather.finish()


def middle_back(grads, weight, hidden, outer, mask, gain):
    peers, own, inner = grads.shape
    width = weight.shape[0]
    return pl.pallas_call(
        middle_back_kernel,
        in_specs=[vmem()] * 6,
        out_specs=[vmem(), vmem(), in_hbm()],
        out_shape=[
            jax.ShapeDtypeStruct((own, width), FULL),
            jax.ShapeDtypeStruct((1, width), FULL),
            jax.ShapeDtypeStruct((peers, own, width), HALF),
        ],
        scratch_shapes=scatter_scratch(own, width)
        + [pltpu.VMEM((own, width), HALF)]
        + gather_scratch(),
        compiler_params=linked(3),
        cost_estimate=cost(2 * peers * own * inner * width, 4 * peers * own * width),
    )(grads, weight, hidden, outer, mask, gain)


def result_kernel(
    inner_ref, weight_ref, hidden_ref, mask_ref, output_ref,
    terms, cores, nears, belows, sends, receives,
):
    greet_neighbours()

    def term(block):
        return dot_nn(inner_ref[block], weight_ref[...]).astype(HALF)

    scatter = PlaneScatter(term, terms, cores, nears, belows, sends, receives)
    scatter.run()
    for start in range(0, hidden_ref.shape[0], CHUNK):
        rows = pl.ds(start, CHUNK)
        total = hidden_ref[rows] + scatter.total(start, CHUNK)
        output_ref[rows] = (total * mask_ref[rows]).astype(HALF)


def result_rows(inner, weight, hidden, mask):
    peers, own, size = inner.shape
    width = weight.shape[1]
    return pl.pallas_call(
        result_kernel,
        in_specs=[vmem()] * 4,
        out_specs=vmem(),
        out_shape=jax.ShapeDtypeStruct((own, width), HALF),
        scratch_shapes=scatter_scratch(own, width),
        compiler_params=linked(4),
        cost_estimate=cost(2 * peers * own * size * width, 2 * peers * own * width),
    )(inner, weight, hidden, mask)


def last_kernel(
    grads_ref, pair_ref, value_ref, swish_ref, tokens_ref, hidden_grad_ref, gain_ref,
    second_grad_ref, group_grad_ref,
    input_ref, gains_ref, group_ref,
    terms, cores, nears, belows, sends, receives,
    sums, parts, across, totals, keep, part_sends, part_receives, group_keep, group_sends,
    group_receives,
):
    peers, groups = lax.axis_size("seq"), lax.axis_size("fsdp")
    group = lax.axis_index("fsdp")
    greet_plane(True)
    pair, single = pair_ref.shape[1], value_ref.shape[1]

    def term(block):
        total = dot_nt(grads_ref[block, :, :pair], pair_ref[...])
        total += dot_nt(grads_ref[block, :, pair : pair + single], value_ref[...])
        total += dot_nt(grads_ref[block, :, pair + single :], swish_ref[...])
        return total.astype(HALF)

    scatter = PlaneScatter(term, terms, cores, nears, belows, sends, receives)
    scatter.run()
    gain = gain_ref[...]
    first_grad = jnp.zeros(gain.shape, FULL)
    for start in range(0, tokens_ref.shape[0], CHUNK):
        rows = pl.ds(start, CHUNK)
        grad = regroup(scatter.total(start, CHUNK), groups, peers)
        normed, scale = normalised(tokens_ref[rows].astype(FULL))
        first_grad += jnp.sum(grad * normed, axis=0, keepdims=True)
        input_ref[rows] = (
            hidden_grad_ref[rows] + normalised_back(grad * gain, normed, scale)
        ).astype(HALF)
    tile = LANES * 2
    for peer in range(peers):
        for row in range(tile // LANES):
            at = peer * tile + row * LANES
            sums[peer, row : row + 1] = first_grad[:, at : at + LANES]
            sums[peer, 2 + row : 3 + row] = second_grad_ref[:, at : at + LANES]
        sums[peer, 4:8] = jnp.zeros((4, LANES), FULL)
    me = lax.axis_index("seq")

    def copy(turn):
        peer = lax.rem(me + turn, peers)
        return to_peer(sums.at[peer], parts.at[turn], part_sends.at[turn], part_receives.at[turn], peer)

    def kept():
        return pltpu.make_async_copy(sums.at[me], parts.at[0], keep)

    kept().start()
    for turn in range(1, peers):
        copy(turn).start()
    kept().wait()
    for turn in range(1, peers):
        copy(turn).wait_recv()
        copy(turn).wait_send()
    total = parts[0]
    for turn in range(1, peers):
        total += parts[turn]
    across[0:8] = total
    for row in range(4):
        across[8 + row : 9 + row] = group_grad_ref[:, row * LANES : (row + 1) * LANES]
    across[12:16] = jnp.zeros((4, LANES), FULL)
    begin, finish = all_to_each(
        across, totals, "fsdp", groups, group_keep, group_sends, group_receives
    )
    begin()
    finish()
    summed = totals[0]
    for turn in range(1, groups):
        summed += totals[turn]
    gains_ref[...] = summed[0:8]
    group_ref[...] = summed[8:16]


def last_rows(grads, pair, value, swish, tokens, hidden_grad, gain, second_grad, group_grad):
    peers, own, inner = grads.shape
    groups = lax.axis_size("fsdp")
    width = pair.shape[0]
    return pl.pallas_call(
        last_kernel,
        in_specs=[vmem()] * 9,
        out_specs=[vmem()] * 3,
        out_shape=[
            jax.ShapeDtypeStruct((own, width), HALF),
            jax.ShapeDtypeStruct((8, LANES), FULL),
            jax.ShapeDtypeStruct((8, LANES), FULL),
        ],
        scratch_shapes=scatter_scratch(own, width)
        + [
            pltpu.VMEM((peers, 8, LANES), FULL),
            pltpu.VMEM((peers, 8, LANES), FULL),
            pltpu.VMEM((16, LANES), FULL),
            pltpu.VMEM((groups, 16, LANES), FULL),
            pltpu.SemaphoreType.DMA,
            pltpu.SemaphoreType.DMA((peers,)),
            pltpu.SemaphoreType.DMA((peers,)),
            pltpu.SemaphoreType.DMA,
            pltpu.SemaphoreType.DMA((groups,)),
            pltpu.SemaphoreType.DMA((groups,)),
        ],
        compiler_params=linked(5),
        cost_estimate=cost(2 * peers * own * inner * width, 2 * peers * own * width),
    )(grads, pair, value, swish, tokens, hidden_grad, gain, second_grad, group_grad)


def return_kernel(count, *refs):
    sources, targets = refs[:count], refs[count : 2 * count]
    keeps, sends, receives = refs[2 * count :]
    peers = lax.axis_size("seq")
    me = lax.axis_index("seq")
    greet_plane(False)

    def columns(number, peer):
        size = sources[number].shape[2]
        return pl.ds(pl.multiple_of(peer * size, LANES), size)

    def copy(number, turn):
        peer = lax.rem(me + turn, peers)
        return to_peer(
            sources[number].at[peer],
            targets[number].at[:, columns(number, me)],
            sends.at[number, turn],
            receives.at[number, turn],
            peer,
        )

    def landed(number, turn):
        peer = lax.rem(me + peers - turn, peers)
        target = targets[number].at[:, columns(number, peer)]
        return to_peer(
            target, target, sends.at[number, turn], receives.at[number, turn], peer
        )

    def kept(number):
        return pltpu.make_async_copy(
            sources[number].at[me], targets[number].at[:, columns(number, me)], keeps.at[number]
        )

    for number in range(count):
        for turn in range(1, peers):
            copy(number, turn).start()
        kept(number).start()
    for number in range(count):
        for turn in range(1, peers):
            landed(number, turn).wait_recv()
            copy(number, turn).wait_send()
        kept(number).wait()


def return_grads(collective, *parts):
    peers, slab, _ = parts[0].shape
    count = len(parts)
    return pl.pallas_call(
        partial(return_kernel, count),
        in_specs=[in_hbm()] * count,
        out_specs=[in_hbm()] * count,
        out_shape=[jax.ShapeDtypeStruct((slab, peers * part.shape[2]), HALF) for part in parts],
        scratch_shapes=swap_scratch(count, peers),
        compiler_params=linked(collective),
        cost_estimate=cost(0, sum(2 * part.size for part in parts)),
    )(*parts)


def head_body(
    tokens,
    cotangent,
    lengths,
    block_order,
    log_decay,
    first_gain,
    query_weight,
    key_weight,
    value_weight,
    swish_weight,
    output_weight,
    group_gain,
    second_gain,
    feed_gate,
    feed_up,
    feed_down,
):
    peers, groups = lax.axis_size("seq"), lax.axis_size("fsdp")
    index, group = lax.axis_index("seq"), lax.axis_index("fsdp")
    batches, rows, width = tokens.shape
    own = batches * rows
    heads = log_decay.shape[0]
    key_size = query_weight.shape[1] // heads
    value_size = value_weight.shape[1] // heads
    part = feed_gate.shape[1] // peers
    slab = query_weight.shape[0]
    total = 2 * key_size + 2 * value_size

    def over_groups(local):
        return lax.all_gather(local, "fsdp", axis=0, tiled=True)

    def sum_groups(whole):
        return lax.psum_scatter(whole.astype(HALF), "fsdp", scatter_dimension=0, tiled=True)

    def gathered(cut):
        return over_groups(cut[None]).reshape(width, cut.shape[2])

    gains = jnp.concatenate(
        [
            group_gain.astype(FULL)[None],
            jnp.concatenate([first_gain, second_gain]).astype(FULL)[None],
            jnp.zeros((6, LANES), FULL),
        ],
        axis=0,
    )
    pair_cut, value_cut, swish_cut, rates, gains = first_swap(
        query_weight, key_weight, value_weight, swish_weight, log_decay, gains
    )
    out_weight = over_groups(output_weight)
    pair_weight = gathered(pair_cut)
    value_part = gathered(value_cut)
    swish_part = gathered(swish_cut)
    gain_one = gains[:, :, 1, :slab].reshape(1, width)
    gain_two = gains[:, :, 1, slab:].reshape(1, width)
    gain_group = lax.dynamic_index_in_dim(gains, index, 0, keepdims=False)[:, 0].reshape(
        1, value_size
    )

    rates = lax.dynamic_index_in_dim(rates, index, 1, keepdims=False)
    cumulative = jnp.cumsum(rates, axis=1)
    slots = jnp.arange(rows)
    lower = slots[:, None] >= slots[None, :]
    spread = cumulative[:, :, None] - cumulative[:, None, :]
    decay = jnp.where(lower, jnp.exp(jnp.where(lower, spread, 0.0)), 0.0)
    columns = jnp.stack([jnp.exp(cumulative), jnp.exp(cumulative[:, -1:] - cumulative)], axis=2)

    order = lax.dynamic_slice_in_dim(block_order, group * batches, batches, 0)
    numbers = jnp.arange(peers, dtype=jnp.int32)
    place = jnp.sum(
        numbers[None, None, :] * (order[:, None, :] == numbers[None, :, None]).astype(jnp.int32),
        axis=2,
    )
    live = lax.dynamic_slice_in_dim(lengths, group * batches, batches, 0)
    held = lax.dynamic_index_in_dim(order, index, 1, keepdims=False)
    positions = held[:, None] * rows + jnp.arange(rows, dtype=jnp.int32)
    mask = (positions < live[:, None]).astype(FULL).reshape(own, 1)

    token_rows = tokens.reshape(own, width)
    outer_rows = cotangent.reshape(own, width)
    entered, result_low, feed_cut = gather_inputs(
        token_rows, outer_rows, mask, gain_one, feed_gate, feed_up
    )
    feed_weight = gathered(feed_cut)
    down_weight = over_groups(feed_down)

    qkv, scale, entry, normed = retention(
        entered.reshape(peers, batches, rows, width),
        pair_weight,
        value_part,
        place,
        live,
        decay,
        columns,
    )
    entered = entered.reshape(peers * own, width)
    swish = dot_nn(entered, swish_part)
    grouped = normed.reshape(peers * own, value_size).astype(FULL) * gain_group
    mixed = (jax.nn.silu(swish) * grouped).astype(HALF)
    swish = swish.astype(HALF)
    hidden, second = middle(mixed.reshape(peers, own, value_size), out_weight, token_rows, gain_two)
    second = second.reshape(peers * own, width)
    result_low = result_low.reshape(peers * own, width)
    both = dot_nn(second, feed_weight)
    inner, pull_inner = jax.vjp(gated_gelu, both[:, :part], both[:, part:])
    inner_low = inner.astype(HALF)
    down_grad = sum_groups(dot_tn(inner_low, result_low))
    gate_grad, upward_grad = pull_inner(dot_nt(result_low, down_weight))
    both_grad = jnp.concatenate([gate_grad.astype(HALF), upward_grad.astype(HALF)], axis=1)
    both_weight_grad = sum_groups(dot_tn(second, both_grad)).reshape(peers, slab, 2 * part)
    hidden_grad, second_gain_grad, branch_low = middle_back(
        both_grad.reshape(peers, own, 2 * part),
        feed_weight,
        hidden,
        outer_rows,
        mask,
        gain_two,
    )
    group_gain_grad, projected_grad = retention_back(
        branch_low.reshape(peers, batches, rows, width),
        swish.reshape(peers, batches, rows, value_size),
        normed,
        out_weight,
        place,
        live,
        decay,
        columns,
        gain_group,
        (qkv, scale, entry),
    )
    branch_low = branch_low.reshape(peers * own, width)
    flat_grad = projected_grad.reshape(peers * own, total)
    out_grad = sum_groups(dot_tn(mixed, branch_low))
    first_weight_grad = sum_groups(dot_tn(entered, flat_grad)).reshape(peers, slab, total)
    input_rows, gain_grads, group_grads = last_rows(
        projected_grad.reshape(peers, own, total),
        pair_weight,
        value_part,
        swish_part,
        token_rows,
        hidden_grad,
        gain_one,
        second_gain_grad,
        group_gain_grad,
    )
    output_rows = result_rows(
        inner_low.reshape(peers, own, part), down_weight, hidden, mask
    )
    gate_back, up_back = return_grads(
        6, both_weight_grad[:, :, :part], both_weight_grad[:, :, part:]
    )
    query_back, key_back, value_back, swish_back = return_grads(
        7,
        first_weight_grad[:, :, :key_size],
        first_weight_grad[:, :, key_size : 2 * key_size],
        first_weight_grad[:, :, 2 * key_size : 2 * key_size + value_size],
        first_weight_grad[:, :, 2 * key_size + value_size :],
    )

    def mine(summed, start):
        flat = summed[start : start + 2].reshape(groups, slab)
        return lax.dynamic_index_in_dim(flat, group, 0, keepdims=False)

    return (
        output_rows.reshape(batches, rows, width),
        input_rows.reshape(batches, rows, width),
        mine(gain_grads, 0),
        query_back.astype(FULL),
        key_back.astype(FULL),
        value_back.astype(FULL),
        swish_back.astype(FULL),
        out_grad.astype(FULL),
        lax.dynamic_index_in_dim(group_grads, group, 0, keepdims=False),
        mine(gain_grads, 2),
        gate_back.astype(FULL),
        up_back.astype(FULL),
        down_grad.astype(FULL),
    )


def body(*arrays):
    peers, groups = lax.axis_size("seq"), lax.axis_size("fsdp")
    fits = peers == 8 and groups == 4 and arrays[4].shape[0] == peers and arrays[0].shape[0] == 2
    if fits:
        return head_body(*arrays)
    return general_body(*arrays)


def solution(mesh):
    placed = (
        P("fsdp", "seq", None),
        P("fsdp", "seq", None),
        P(),
        P(),
        P(None, "seq"),
        P(("seq", "fsdp")),
        P(("seq", "fsdp"), None),
        P(("seq", "fsdp"), None),
        P(("seq", "fsdp"), None),
        P(("seq", "fsdp"), None),
        P(("seq", "fsdp"), None),
        P(("seq", "fsdp")),
        P(("seq", "fsdp")),
        P(("seq", "fsdp"), None),
        P(("seq", "fsdp"), None),
        P(("seq", "fsdp"), None),
    )
    return jax.shard_map(
        body,
        mesh=mesh,
        in_specs=placed,
        out_specs=(
            P("fsdp", "seq", None),
            P("fsdp", "seq", None),
            P(("seq", "fsdp")),
            P(("seq", "fsdp"), None),
            P(("seq", "fsdp"), None),
            P(("seq", "fsdp"), None),
            P(("seq", "fsdp"), None),
            P(("seq", "fsdp"), None),
            P(("seq", "fsdp")),
            P(("seq", "fsdp")),
            P(("seq", "fsdp"), None),
            P(("seq", "fsdp"), None),
            P(("seq", "fsdp"), None),
        ),
        check_vma=False,
    )
```

```python
from functools import partial, reduce

import jax
import jax.numpy as jnp
from jax import lax
from jax.experimental import pallas as pl
from jax.experimental.pallas import tpu as pltpu
from jax.sharding import PartitionSpec as P

EPSILON = 1e-05
HIGHEST = lax.Precision.HIGHEST


def carried_in(value, axis, combine, identity, reverse):
    peers, index = (lax.axis_size(axis), lax.axis_index(axis))
    everything = jax.tree.map(
        lambda part, kind: lax.all_gather(part.astype(kind), axis),
        value,
        (jnp.bfloat16, jnp.bfloat16),
    )
    start = jax.tree.map(
        lambda part, zero: jnp.broadcast_to(jnp.asarray(zero, part.dtype), part.shape),
        value,
        identity,
    )

    def turn(k, before):
        at = peers - 1 - k if reverse else k
        reached = at > index if reverse else at < index
        new = combine(
            before, jax.tree.map(lambda part, own: part[at].astype(own.dtype), everything, value)
        )
        return jax.tree.map(lambda a, b: jnp.where(reached, a, b), new, before)

    return lax.fori_loop(0, peers, turn, start)


def norm_rows(values, gain):
    average = jnp.mean(values, axis=-1, keepdims=True)
    centered = values - average
    variance = jnp.mean(centered * centered, axis=-1, keepdims=True)
    return centered * lax.rsqrt(variance + EPSILON) * gain


def gated_swish(swish_in, grouped):
    return jax.nn.silu(swish_in) * grouped


def gated_gelu(gate_in, upward):
    return jax.nn.gelu(gate_in) * upward


def chain_states(earlier, later):
    return (earlier[0] * later[0], later[0][:, None, None] * earlier[1] + later[1])


def transposed(left_rows, weight):
    return jnp.einsum("ie,fe->if", left_rows, weight, preferred_element_type=jnp.float32)


def plain_dot(left_rows, weight):
    return jnp.dot(left_rows, weight, preferred_element_type=jnp.float32)


def outer_term(left_rows, right_rows):
    return jnp.einsum("ni,no->io", left_rows, right_rows, preferred_element_type=jnp.float32)


def spread_sum(matrix_pairs, vectors):
    terms = tuple((outer_term(left_rows, right_rows) for left_rows, right_rows in matrix_pairs))
    pieces = lax.psum_scatter(
        terms + tuple(vectors), ("seq", "fsdp"), scatter_dimension=0, tiled=True
    )
    return list(pieces)


def join_terms(collected):
    matrix_pairs = []
    for member in range(len(collected[0][0])):
        lefts = jnp.concatenate([entry[0][member][0] for entry in collected], axis=0)
        rights = jnp.concatenate([entry[0][member][1] for entry in collected], axis=0)
        matrix_pairs.append((lefts, rights))
    vectors = [
        reduce(jnp.add, [entry[1][member] for entry in collected])
        for member in range(len(collected[0][1]))
    ]
    return (matrix_pairs, vectors)


def layer_step(gathered, inputs, cot_rows, live_mask, log_rates):
    (
        first_gain,
        query_weight,
        key_weight,
        value_weight,
        swish_weight,
        output_weight,
        group_gain,
        second_gain,
        feed_gate,
        feed_up,
        feed_down,
    ) = gathered
    floats = jnp.float32
    halves = jnp.bfloat16
    head_count = log_rates.shape[0]
    token_rows = inputs.shape[0]
    key_size = query_weight.shape[1] // head_count
    value_size = value_weight.shape[1] // head_count
    start_values = inputs.astype(floats)
    normed_one, pull_one = jax.vjp(norm_rows, start_values, first_gain.astype(floats))
    normed = normed_one.astype(halves)
    queries = plain_dot(normed, query_weight).astype(halves)
    keys_in = plain_dot(normed, key_weight).astype(halves) * live_mask[:, None].astype(halves)
    values_in = plain_dot(normed, value_weight).astype(halves)
    swish_in = plain_dot(normed, swish_weight)
    queries3 = queries.reshape(token_rows, head_count, key_size)
    keys3 = keys_in.reshape(token_rows, head_count, key_size)
    values3 = values_in.reshape(token_rows, head_count, value_size)
    cumulative = jnp.cumsum(log_rates, axis=1)
    slot_index = jnp.arange(token_rows)
    lower_mask = slot_index[:, None] >= slot_index[None, :]
    spread = cumulative[:, :, None] - cumulative[:, None, :]
    decay_matrix = jnp.where(lower_mask, jnp.exp(jnp.where(lower_mask, spread, 0.0)), 0.0)
    block_decay = jnp.exp(cumulative[:, -1])
    end_weight = jnp.exp(cumulative[:, -1:] - cumulative).T[:, :, None]
    entry_decay = jnp.exp(cumulative).T[:, :, None]
    query_wide = queries3.astype(floats)
    key_wide = keys3.astype(floats)
    value_wide = values3.astype(floats)
    state_term = jnp.einsum("jhd,jhe->hde", key_wide * end_weight, value_wide, precision=HIGHEST)
    state_identity = (jnp.ones_like(block_decay), jnp.zeros_like(state_term))
    _, start_state = carried_in(
        (block_decay, state_term), "seq", chain_states, state_identity, False
    )
    scores = jnp.einsum("ihd,jhd->hij", queries3, keys3, preferred_element_type=floats)
    weights = (scores * decay_matrix).astype(halves)
    intra_term = jnp.einsum("hij,jhe->ihe", weights, values3, preferred_element_type=floats)
    carried = entry_decay * jnp.einsum("ihd,hde->ihe", query_wide, start_state, precision=HIGHEST)
    retained = intra_term + carried
    grouped, pull_group = jax.vjp(
        norm_rows, retained, group_gain.astype(floats).reshape(head_count, value_size)
    )
    grouped_flat = grouped.reshape(token_rows, head_count * value_size)
    mixed_float, pull_mixed = jax.vjp(gated_swish, swish_in, grouped_flat)
    mixed_low = mixed_float.astype(halves)
    hidden = start_values + plain_dot(mixed_low, output_weight)
    normed_two, pull_two = jax.vjp(norm_rows, hidden, second_gain.astype(floats))
    second = normed_two.astype(halves)
    gate_two = plain_dot(second, feed_gate)
    upward = plain_dot(second, feed_up)
    inner_float, pull_inner = jax.vjp(gated_gelu, gate_two, upward)
    inner_low = inner_float.astype(halves)
    result = plain_dot(inner_low, feed_down)
    output_rows = ((hidden + result) * live_mask[:, None]).astype(halves)
    outer_grad = cot_rows.astype(floats) * live_mask[:, None]
    result_low = outer_grad.astype(halves)
    inner_grad = transposed(result_low, feed_down)
    gate_two_grad, upward_grad = pull_inner(inner_grad)
    gate_two_low = gate_two_grad.astype(halves)
    upward_low = upward_grad.astype(halves)
    second_grad = transposed(gate_two_low, feed_gate) + transposed(upward_low, feed_up)
    hidden_part, second_gain_grad = pull_two(second_grad)
    hidden_grad = outer_grad + hidden_part
    branch_low = hidden_grad.astype(halves)
    mixed_grad = transposed(branch_low, output_weight)
    swish_grad, grouped_grad = pull_mixed(mixed_grad)
    swish_low = swish_grad.astype(halves)
    retained_grad, group_gain_grad = pull_group(
        grouped_grad.reshape(token_rows, head_count, value_size)
    )
    retained_low = retained_grad.astype(halves)
    weights_grad = jnp.einsum("ihe,jhe->hij", retained_low, values3, preferred_element_type=floats)
    scores_low = (weights_grad * decay_matrix).astype(halves)
    query_intra = jnp.einsum("hij,jhd->ihd", scores_low, keys3, preferred_element_type=floats)
    key_intra = jnp.einsum("hij,ihd->jhd", scores_low, queries3, preferred_element_type=floats)
    value_intra = jnp.einsum("hij,ihe->jhe", weights, retained_low, preferred_element_type=floats)
    retained_wide = retained_low.astype(floats)
    query_carried = entry_decay * jnp.einsum(
        "ihe,hde->ihd", retained_wide, start_state, precision=HIGHEST
    )
    local_grad = jnp.einsum(
        "ihd,ihe->hde", query_wide * entry_decay, retained_wide, precision=HIGHEST
    )
    _, end_grad = carried_in((block_decay, local_grad), "seq", chain_states, state_identity, True)
    key_state = end_weight * jnp.einsum("jhe,hde->jhd", value_wide, end_grad, precision=HIGHEST)
    value_state = end_weight * jnp.einsum("jhd,hde->jhe", key_wide, end_grad, precision=HIGHEST)
    query_low = (
        (query_intra + query_carried).astype(halves).reshape(token_rows, head_count * key_size)
    )
    key_low = (
        ((key_intra + key_state) * live_mask[:, None, None])
        .astype(halves)
        .reshape(token_rows, head_count * key_size)
    )
    value_low = (
        (value_intra + value_state).astype(halves).reshape(token_rows, head_count * value_size)
    )
    normed_grad = (
        transposed(query_low, query_weight)
        + transposed(key_low, key_weight)
        + transposed(value_low, value_weight)
        + transposed(swish_low, swish_weight)
    )
    input_part, first_gain_grad = pull_one(normed_grad)
    grad_rows = (hidden_grad + input_part).astype(halves)
    matrix_pairs = [
        (normed, query_low),
        (normed, key_low),
        (normed, value_low),
        (normed, swish_low),
        (mixed_low, branch_low),
        (second, gate_two_low),
        (second, upward_low),
        (inner_low, result_low),
    ]
    vectors = [first_gain_grad, group_gain_grad.reshape(-1), second_gain_grad]
    return (output_rows, grad_rows, matrix_pairs, vectors)


def general_body(
    tokens,
    cotangent,
    lengths,
    block_order,
    log_decay,
    first_gain,
    query_weight,
    key_weight,
    value_weight,
    swish_weight,
    output_weight,
    group_gain,
    second_gain,
    feed_gate,
    feed_up,
    feed_down,
):
    batches = tokens.shape[0]
    block_rows = tokens.shape[1]
    selected_locations = lax.axis_size("seq")
    position = lax.axis_index("seq")
    group_index = lax.axis_index("fsdp")
    place_numbers = jnp.arange(selected_locations, dtype=jnp.int32)
    arrived_tokens, arrived_cotangent = (
        lax.all_gather(tokens, "seq", axis=1, tiled=True),
        lax.all_gather(cotangent, "seq", axis=1, tiled=True),
    )
    gathered = (
        lax.all_gather(first_gain, ("seq", "fsdp"), axis=0, tiled=True),
        lax.all_gather(query_weight, ("seq", "fsdp"), axis=0, tiled=True),
        lax.all_gather(key_weight, ("seq", "fsdp"), axis=0, tiled=True),
        lax.all_gather(value_weight, ("seq", "fsdp"), axis=0, tiled=True),
        lax.all_gather(swish_weight, ("seq", "fsdp"), axis=0, tiled=True),
        lax.all_gather(output_weight, ("seq", "fsdp"), axis=0, tiled=True),
        lax.all_gather(group_gain, ("seq", "fsdp"), axis=0, tiled=True),
        lax.all_gather(second_gain, ("seq", "fsdp"), axis=0, tiled=True),
        lax.all_gather(feed_gate, ("seq", "fsdp"), axis=0, tiled=True),
        lax.all_gather(feed_up, ("seq", "fsdp"), axis=0, tiled=True),
        lax.all_gather(feed_down, ("seq", "fsdp"), axis=0, tiled=True),
    )
    outputs = []
    input_grads = []
    collected = []
    order_rows = []
    for batch_number in range(batches):
        sequence = group_index * batches + batch_number
        order_row = lax.dynamic_index_in_dim(block_order, sequence, 0, keepdims=False)
        order_rows.append(order_row)
        source = jnp.sum(place_numbers * (order_row == position).astype(jnp.int32))
        token_rows = lax.dynamic_slice_in_dim(
            arrived_tokens[batch_number], source * block_rows, block_rows, 0
        )
        cot_rows = lax.dynamic_slice_in_dim(
            arrived_cotangent[batch_number], source * block_rows, block_rows, 0
        )
        live_length = lax.dynamic_index_in_dim(lengths, sequence, 0, keepdims=False)
        location_number = position * block_rows + jnp.arange(block_rows, dtype=jnp.int32)
        live_mask = (location_number < live_length).astype(jnp.float32)
        output_rows, grad_rows, matrix_pairs, vectors = layer_step(
            gathered, token_rows, cot_rows, live_mask, log_decay
        )
        outputs.append(output_rows)
        input_grads.append(grad_rows)
        collected.append((matrix_pairs, vectors))
    joined_pairs, joined_vectors = join_terms(collected)
    shards = spread_sum(joined_pairs, joined_vectors)
    every_output, every_grad = (
        lax.all_gather(jnp.stack(outputs), "seq", axis=1, tiled=True),
        lax.all_gather(jnp.stack(input_grads), "seq", axis=1, tiled=True),
    )
    returned = []
    returned_grads = []
    for batch_number in range(batches):
        target = lax.dynamic_index_in_dim(order_rows[batch_number], position, 0, keepdims=False)
        returned.append(
            lax.dynamic_slice_in_dim(every_output[batch_number], target * block_rows, block_rows, 0)
        )
        returned_grads.append(
            lax.dynamic_slice_in_dim(every_grad[batch_number], target * block_rows, block_rows, 0)
        )
    return (
        jnp.stack(returned),
        jnp.stack(returned_grads),
        shards[8],
        shards[0],
        shards[1],
        shards[2],
        shards[3],
        shards[4],
        shards[9],
        shards[10],
        shards[5],
        shards[6],
        shards[7],
    )


FULL = jnp.float32
HALF = jnp.bfloat16
MESH = pl.DeviceIdType.MESH
VMEM_BYTES = 56 * 1024 * 1024
LANES = 128


def dot_nn(left, right):
    return jnp.dot(left, right, preferred_element_type=FULL)


def dot_nt(left, right):
    return lax.dot_general(left, right, (((1,), (1,)), ((), ())), preferred_element_type=FULL)


def dot_tn(left, right):
    return lax.dot_general(left, right, (((0,), (0,)), ((), ())), preferred_element_type=FULL)


def plane_peers():
    me = lax.axis_index("seq")
    core = lax.rem(me, 2)
    across = 2 - 4 * lax.rem(me // 2, 2)
    down = 4 - 8 * (me // 4)
    return me, me + 1 - 2 * core, me + across, me + down, me + across + down


def to_peer(source, target, send, receive, peer):
    return pltpu.make_async_remote_copy(
        src_ref=source,
        dst_ref=target,
        send_sem=send,
        recv_sem=receive,
        device_id={"seq": peer},
        device_id_type=MESH,
    )


def greet_neighbours():
    _, other, near, below, _ = plane_peers()
    barrier = pltpu.get_barrier_semaphore()
    for peer in (other, near, below):
        pl.semaphore_signal(barrier, inc=1, device_id={"seq": peer}, device_id_type=MESH)
    pl.semaphore_wait(barrier, 3)


GATHER_COPIES = 14


def gather_plan():
    me, other, near, below, far = plane_peers()
    flip = other - me
    return (
        (me, 0, near, near),
        (me, 1, below, below),
        (me, 0, other, other),
        (me, 1, other, other),
        (me, 1, near, near),
        (me, 0, below, below),
        (near, 0, below, far),
        (below, 1, near, far),
        (near, 0, other, near + flip),
        (below, 1, other, below + flip),
        (near, 1, other, near + flip),
        (below, 0, other, below + flip),
        (far, 0, other, far + flip),
        (far, 1, other, far + flip),
    )


class PlaneGather:
    def __init__(self, own, out, keep, sends, receives):
        self.own, self.out = own, out
        self.keep, self.sends, self.receives = keep, sends, receives
        self.half = own.shape[0] // 2

    def rows(self, which):
        return pl.ds(which * self.half, self.half)

    def kept(self):
        me = lax.axis_index("seq")
        return pltpu.make_async_copy(self.own, self.out.at[me], self.keep)

    def copy(self, number):
        block, which, peer, _ = gather_plan()[number]
        target = self.out.at[block, self.rows(which)]
        source = self.own.at[self.rows(which)] if number < 6 else target
        return to_peer(source, target, self.sends.at[number], self.receives.at[number], peer)

    def landed(self, number):
        _, which, peer, landing = gather_plan()[number]
        target = self.out.at[landing, self.rows(which)]
        to_peer(target, target, self.sends.at[number], self.receives.at[number], peer).wait_recv()

    def begin(self):
        self.kept().start()
        for number in range(6):
            self.copy(number).start()

    def relay(self):
        for arrived, onward in ((0, (6, 8)), (1, (7, 9)), (4, (10,)), (5, (11,))):
            self.landed(arrived)
            for number in onward:
                self.copy(number).start()

    def finish(self):
        for arrived, onward in ((6, 12), (7, 13)):
            self.landed(arrived)
            self.copy(onward).start()
        for number in (2, 3, 8, 9, 10, 11, 12, 13):
            self.landed(number)
        for number in range(GATHER_COPIES):
            self.copy(number).wait_send()
        self.kept().wait()


def gather_scratch():
    return [
        pltpu.SemaphoreType.DMA,
        pltpu.SemaphoreType.DMA((GATHER_COPIES,)),
        pltpu.SemaphoreType.DMA((GATHER_COPIES,)),
    ]


SCATTER_COPIES = 10
CHUNK = 32


def by_chunks(rows, work):
    def step(number, carry):
        work(pl.ds(pl.multiple_of(number * CHUNK, CHUNK), CHUNK))
        return carry

    lax.fori_loop(0, rows // CHUNK, step, 0)


class PlaneScatter:
    def __init__(self, term, terms, cores, nears, belows, sends, receives):
        self.term, self.terms, self.cores = term, terms, cores
        self.nears, self.belows = nears, belows
        self.sends, self.receives = sends, receives
        self.size = terms.shape[1]
        self.half = self.size // 2

    def copy(self, number):
        _, other, near, below, _ = plane_peers()
        upper, lower = pl.ds(0, self.half), pl.ds(self.half, self.half)
        if number < 4:
            source, target, peer = self.terms.at[4 + number], self.cores.at[number], other
        else:
            source, target, peer = (
                (self.terms.at[0, upper], self.nears.at[0], near),
                (self.terms.at[0, lower], self.belows.at[0], below),
                (self.terms.at[1, upper], self.nears.at[1], near),
                (self.terms.at[2, lower], self.belows.at[1], below),
                (self.terms.at[1, lower], self.nears.at[2], near),
                (self.terms.at[2, upper], self.belows.at[2], below),
            )[number - 4]
        return to_peer(source, target, self.sends.at[number], self.receives.at[number], peer)

    def fold(self, slot):
        def work(rows):
            self.terms[slot, rows] = (
                self.terms[slot, rows].astype(FULL) + self.cores[slot, rows].astype(FULL)
            ).astype(HALF)

        by_chunks(self.size, work)

    def fold_half(self, slot, start, landed):
        def work(rows):
            here = pl.ds(pl.multiple_of(start + rows.start, CHUNK), CHUNK)
            self.terms[slot, here] = (
                self.terms[slot, here].astype(FULL) + landed[rows].astype(FULL)
            ).astype(HALF)

        by_chunks(self.half, work)

    def run(self):
        me, other, near, below, far = plane_peers()
        blocks = (far, near, below, me)
        flip = other - me
        onward = ((4, 5), (6,), (7,), ())

        def fill(slot):
            self.terms[4 + slot] = self.term(blocks[slot] + flip)
            self.copy(slot).start()
            self.terms[slot] = self.term(blocks[slot])

        fill(0)
        for slot in range(4):
            if slot < 3:
                fill(slot + 1)
            self.copy(slot).wait_recv()
            self.fold(slot)
            for number in onward[slot]:
                self.copy(number).start()
        self.copy(4).wait_recv()
        self.fold_half(2, 0, self.nears.at[0])
        self.copy(9).start()
        self.copy(5).wait_recv()
        self.fold_half(1, self.half, self.belows.at[0])
        self.copy(8).start()
        for number in (6, 7, 8, 9):
            self.copy(number).wait_recv()
        for number in range(SCATTER_COPIES):
            self.copy(number).wait_send()

    def total(self, start, size):
        upper = start < self.half
        at = start if upper else start - self.half
        near, below = (1, 2) if upper else (2, 1)
        rows = pl.ds(at, size)
        return (
            self.terms[3, pl.ds(start, size)].astype(FULL)
            + self.nears[near, rows].astype(FULL)
            + self.belows[below, rows].astype(FULL)
        )


def scatter_scratch(rows, width):
    return [
        pltpu.VMEM((8, rows, width), HALF),
        pltpu.VMEM((4, rows, width), HALF),
        pltpu.VMEM((3, rows // 2, width), HALF),
        pltpu.VMEM((3, rows // 2, width), HALF),
        pltpu.SemaphoreType.DMA((SCATTER_COPIES,)),
        pltpu.SemaphoreType.DMA((SCATTER_COPIES,)),
    ]


def regroup(values, outer, inner):
    rows = values.shape[0]
    low_half = lax.broadcasted_iota(jnp.int32, (rows, LANES), 1) < LANES // 2

    def piece(p, q):
        at = (p * inner + q) // 2
        return values[:, at * LANES : (at + 1) * LANES]

    def turned(value):
        return pltpu.roll(value, LANES // 2, 1)

    groups = []
    for q in range(inner):
        for p in range(0, outer, 2):
            first, second = piece(p, q), piece(p + 1, q)
            if q % 2 == 0:
                groups.append(jnp.where(low_half, first, turned(second)))
            else:
                groups.append(jnp.where(low_half, turned(first), second))
    return jnp.concatenate(groups, axis=1)


def normalised(values):
    average = jnp.mean(values, axis=-1, keepdims=True)
    centered = values - average
    scale = lax.rsqrt(jnp.mean(centered * centered, axis=-1, keepdims=True) + EPSILON)
    return centered * scale, scale


def normalised_back(grad, normed, scale):
    average = jnp.mean(grad, axis=-1, keepdims=True)
    along = jnp.mean(grad * normed, axis=-1, keepdims=True)
    return (grad - average - normed * along) * scale


def vmem():
    return pl.BlockSpec(memory_space=pltpu.VMEM)


def in_hbm():
    return pl.BlockSpec(memory_space=pl.ANY)


def cost(flops, link_bytes):
    return pl.CostEstimate(flops=int(flops), bytes_accessed=int(link_bytes) * 16, transcendentals=0)


def linked(collective):
    return pltpu.CompilerParams(
        collective_id=collective, has_side_effects=True, vmem_limit_bytes=VMEM_BYTES
    )


class PlaneSwap:
    def __init__(self, weights, targets, keeps, sends, receives):
        self.weights, self.targets = weights, targets
        self.keeps, self.sends, self.receives = keeps, sends, receives
        self.peers = lax.axis_size("seq")

    def part(self, number, peer):
        weight, (target, start) = self.weights[number], self.targets[number]
        size = weight.shape[1] // self.peers
        return weight.at[:, pl.ds(pl.multiple_of(peer * size, LANES), size)]

    def place(self, number, peer):
        weight, (target, start) = self.weights[number], self.targets[number]
        return target.at[peer, :, pl.ds(start, weight.shape[1] // self.peers)]

    def copy(self, number, turn):
        me = lax.axis_index("seq")
        peer = lax.rem(me + turn, self.peers)
        return to_peer(
            self.part(number, peer),
            self.place(number, me),
            self.sends.at[number, turn],
            self.receives.at[number, turn],
            peer,
        )

    def landed(self, number, turn):
        me = lax.axis_index("seq")
        peer = lax.rem(me + self.peers - turn, self.peers)
        target = self.place(number, peer)
        to_peer(
            target, target, self.sends.at[number, turn], self.receives.at[number, turn], peer
        ).wait_recv()

    def kept(self, number):
        me = lax.axis_index("seq")
        return pltpu.make_async_copy(
            self.part(number, me), self.place(number, me), self.keeps.at[number]
        )

    def begin(self):
        for number in range(len(self.weights)):
            for turn in range(1, self.peers):
                self.copy(number, turn).start()
            self.kept(number).start()

    def finish(self):
        for number in range(len(self.weights)):
            for turn in range(1, self.peers):
                self.landed(number, turn)
                self.copy(number, turn).wait_send()
            self.kept(number).wait()


def swap_scratch(count, peers):
    return [
        pltpu.SemaphoreType.DMA((count,)),
        pltpu.SemaphoreType.DMA((count, peers)),
        pltpu.SemaphoreType.DMA((count, peers)),
    ]


def greet_plane(with_groups):
    me, group = lax.axis_index("seq"), lax.axis_index("fsdp")
    peers, groups = lax.axis_size("seq"), lax.axis_size("fsdp")
    barrier = pltpu.get_barrier_semaphore()
    count = peers - 1
    for turn in range(1, peers):
        peer = lax.rem(me + turn, peers)
        pl.semaphore_signal(barrier, inc=1, device_id={"seq": peer}, device_id_type=MESH)
    if with_groups:
        count += groups - 1
        for turn in range(1, groups):
            peer = lax.rem(group + turn, groups)
            pl.semaphore_signal(barrier, inc=1, device_id={"fsdp": peer}, device_id_type=MESH)
    pl.semaphore_wait(barrier, count)


def all_to_each(source, out, axis, size, keep, sends, receives):
    me = lax.axis_index(axis)

    def copy(turn, slot):
        peer = lax.rem(me + turn, size)
        return pltpu.make_async_remote_copy(
            src_ref=source,
            dst_ref=out.at[slot],
            send_sem=sends.at[turn],
            recv_sem=receives.at[turn],
            device_id={axis: peer},
            device_id_type=MESH,
        )

    def begin():
        pltpu.make_async_copy(source, out.at[me], keep).start()
        for turn in range(1, size):
            copy(turn, me).start()

    def finish():
        for turn in range(1, size):
            copy(turn, lax.rem(me + size - turn, size)).wait_recv()
            copy(turn, me).wait_send()
        pltpu.make_async_copy(source, out.at[me], keep).wait()

    return begin, finish


def first_swap_kernel(
    query_ref, key_ref, value_ref, swish_ref, rates_ref, gains_ref,
    cut_out, rates_out, gains_out,
    column, keeps, sends, receives, rate_keep, rate_sends, rate_receives,
    group_keep, group_sends, group_receives, gain_keep, gain_sends, gain_receives,
):
    peers, groups = lax.axis_size("seq"), lax.axis_size("fsdp")
    size, wide = query_ref.shape[1] // peers, value_ref.shape[1] // peers
    greet_plane(True)
    begin_groups, finish_groups = all_to_each(
        gains_ref, column, "fsdp", groups, group_keep, group_sends, group_receives
    )
    begin_rates, finish_rates = all_to_each(
        rates_ref, rates_out, "seq", peers, rate_keep, rate_sends, rate_receives
    )
    begin_gains, finish_gains = all_to_each(
        column, gains_out, "seq", peers, gain_keep, gain_sends, gain_receives
    )
    swap = PlaneSwap(
        (query_ref, key_ref, value_ref, swish_ref),
        ((cut_out, 0), (cut_out, size), (cut_out, 2 * size), (cut_out, 2 * size + wide)),
        keeps,
        sends,
        receives,
    )
    begin_groups()
    begin_rates()
    finish_groups()
    begin_gains()
    swap.begin()
    finish_rates()
    finish_gains()
    swap.finish()


def first_swap(query, key, value, swish, rates, gains):
    peers, groups = lax.axis_size("seq"), lax.axis_size("fsdp")
    slab = query.shape[0]
    total = sum(weight.shape[1] for weight in (query, key, value, swish)) // peers
    return pl.pallas_call(
        first_swap_kernel,
        in_specs=[in_hbm()] * 4 + [vmem()] * 2,
        out_specs=[in_hbm()] + [vmem()] * 2,
        out_shape=[
            jax.ShapeDtypeStruct((peers, slab, total), HALF),
            jax.ShapeDtypeStruct((peers,) + rates.shape, FULL),
            jax.ShapeDtypeStruct((peers, groups) + gains.shape, FULL),
        ],
        scratch_shapes=[pltpu.VMEM((groups,) + gains.shape, FULL)]
        + swap_scratch(4, peers)
        + [pltpu.SemaphoreType.DMA] + [pltpu.SemaphoreType.DMA((peers,))] * 2
        + [pltpu.SemaphoreType.DMA] + [pltpu.SemaphoreType.DMA((groups,))] * 2
        + [pltpu.SemaphoreType.DMA] + [pltpu.SemaphoreType.DMA((peers,))] * 2,
        compiler_params=linked(0),
        cost_estimate=cost(0, 2 * slab * peers * total),
    )(query, key, value, swish, rates, gains)


def inputs_kernel(
    tokens_ref, grad_ref, mask_ref, gain_ref, gate_ref, up_ref,
    entered_out, grads_out, feed_out,
    own_entered, own_grad, keep_one, sends_one, receives_one, keep_two, sends_two, receives_two,
    keeps, sends, receives,
):
    peers, groups = lax.axis_size("seq"), lax.axis_size("fsdp")
    greet_plane(False)
    size = gate_ref.shape[1] // peers
    gain = gain_ref[...]

    def work(rows):
        normed, _ = normalised(tokens_ref[rows].astype(FULL))
        own_entered[rows] = regroup(normed * gain, peers, groups).astype(HALF)
        own_grad[rows] = (grad_ref[rows].astype(FULL) * mask_ref[rows]).astype(HALF)

    by_chunks(tokens_ref.shape[0], work)
    one = PlaneGather(own_entered, entered_out, keep_one, sends_one, receives_one)
    two = PlaneGather(own_grad, grads_out, keep_two, sends_two, receives_two)
    swap = PlaneSwap((gate_ref, up_ref), ((feed_out, 0), (feed_out, size)), keeps, sends, receives)
    one.begin()
    one.relay()
    swap.begin()
    two.begin()
    one.finish()
    two.relay()
    swap.finish()
    two.finish()


def gather_inputs(tokens, grad, mask, gain, gate, up):
    peers = lax.axis_size("seq")
    own, width = tokens.shape
    slab, columns = gate.shape
    part = columns // peers
    return pl.pallas_call(
        inputs_kernel,
        in_specs=[vmem()] * 4 + [in_hbm()] * 2,
        out_specs=[in_hbm()] * 3,
        out_shape=[
            jax.ShapeDtypeStruct((peers, own, width), HALF),
            jax.ShapeDtypeStruct((peers, own, width), HALF),
            jax.ShapeDtypeStruct((peers, slab, 2 * part), HALF),
        ],
        scratch_shapes=[pltpu.VMEM((own, width), HALF)] * 2
        + gather_scratch()
        + gather_scratch()
        + swap_scratch(2, peers),
        compiler_params=linked(1),
        cost_estimate=cost(0, 2 * peers * (2 * own * width + slab * 2 * part)),
    )(tokens, grad, mask, gain, gate, up)


def retention_kernel(
    place_ref, live_ref, first_ref, second_ref, weight_ref, decay_ref, column_ref,
    qkv_ref, scale_ref, entry_ref, normed_hbm, state, normed_buffer, sems,
):
    step, steps = pl.program_id(0), pl.num_programs(0)
    rows = first_ref.shape[2]
    batches, key_size, _ = state.shape
    slot = lax.rem(step, 2)

    def sent(at, which, batch):
        return pltpu.make_async_copy(
            normed_buffer.at[which, batch],
            normed_hbm.at[place_ref[batch, at], batch],
            sems.at[which, batch],
        )

    @pl.when(step == 0)
    def _():
        state[...] = jnp.zeros_like(state)

    @pl.when(step >= 2)
    def _():
        for batch in range(batches):
            sent(step - 2, slot, batch).wait()

    rows_in = jnp.concatenate([first_ref[0, 0], second_ref[0, 0]], axis=0)
    projected = dot_nn(rows_in, weight_ref[...])
    decay = decay_ref[0]
    entry_decay = column_ref[0, :, 0:1]
    end_weight = column_ref[0, :, 1:2]
    block_decay = column_ref[0, rows - 1 : rows, 0:1]
    positions = step * rows + lax.broadcasted_iota(jnp.int32, (rows, 1), 0)
    for batch in range(batches):
        mine = slice(batch * rows, (batch + 1) * rows)
        live = (positions < live_ref[batch]).astype(FULL)
        query = projected[mine, :key_size].astype(HALF)
        key = (projected[mine, key_size : 2 * key_size] * live).astype(HALF)
        value = projected[mine, 2 * key_size :].astype(HALF)
        before = state[batch]
        before_low = before.astype(HALF)
        weights = (dot_nt(query, key) * decay).astype(HALF)
        retained = dot_nn(weights, value) + entry_decay * dot_nn(query, before_low)
        key_ended = (key.astype(FULL) * end_weight).astype(HALF)
        state[batch] = block_decay * before + dot_tn(key_ended, value)
        normed, scale = normalised(retained)
        qkv_ref[batch, 0, :, :key_size] = query
        qkv_ref[batch, 0, :, key_size : 2 * key_size] = key
        qkv_ref[batch, 0, :, 2 * key_size :] = value
        scale_ref[batch, 0] = jnp.broadcast_to(scale, scale_ref.shape[2:])
        entry_ref[batch, 0] = before_low
        normed_buffer[slot, batch] = normed.astype(HALF)
        sent(step, slot, batch).start()

    @pl.when(step == steps - 1)
    def _():
        for batch in range(batches):
            sent(step, slot, batch).wait()
            sent(step - 1, 1 - slot, batch).wait()


def retention(rows_in, weight, place, live, decay, columns, key_size, value_size):
    blocks, batches, rows, width = rows_in.shape
    total = 2 * key_size + value_size

    def arriving(batch):
        return pl.BlockSpec(
            (1, 1, rows, width), lambda i, place, live: (place[batch, i], batch, 0, 0)
        )

    def whole(shape):
        return pl.BlockSpec(
            shape, lambda i, place, live: (0,) * len(shape), pipeline_mode=pl.Buffered(1)
        )

    def here(*tail):
        return pl.BlockSpec((batches, 1) + tail, lambda i, place, live: (0, i, 0, 0))

    def along(*tail):
        return pl.BlockSpec((1,) + tail, lambda i, place, live: (i, 0, 0))

    return pl.pallas_call(
        retention_kernel,
        grid_spec=pltpu.PrefetchScalarGridSpec(
            num_scalar_prefetch=2,
            grid=(blocks,),
            in_specs=[
                arriving(0),
                arriving(1),
                whole((width, total)),
                along(rows, rows),
                along(rows, 2),
            ],
            out_specs=[
                here(rows, total),
                here(rows, LANES),
                here(key_size, value_size),
                in_hbm(),
            ],
            scratch_shapes=[
                pltpu.VMEM((batches, key_size, value_size), FULL),
                pltpu.VMEM((2, batches, rows, value_size), HALF),
                pltpu.SemaphoreType.DMA((2, batches)),
            ],
        ),
        out_shape=[
            jax.ShapeDtypeStruct((batches, blocks, rows, total), HALF),
            jax.ShapeDtypeStruct((batches, blocks, rows, LANES), FULL),
            jax.ShapeDtypeStruct((batches, blocks, key_size, value_size), HALF),
            jax.ShapeDtypeStruct((blocks, batches, rows, value_size), HALF),
        ],
        compiler_params=pltpu.CompilerParams(
            dimension_semantics=("arbitrary",), vmem_limit_bytes=VMEM_BYTES
        ),
        cost_estimate=pl.CostEstimate(
            flops=2 * blocks * batches * rows * width * total,
            bytes_accessed=2 * blocks * batches * rows * (width + total) + 2 * width * total,
            transcendentals=0,
        ),
    )(place, live, rows_in, rows_in, weight, decay, columns)


def retention_back_kernel(
    place_ref, live_ref, first_ref, second_ref, swish_one, swish_two, normed_one, normed_two,
    weight_ref, decay_ref, column_ref, gain_ref, qkv_ref, scale_ref, entry_ref,
    gain_grad_ref, grads_hbm, state, grads_buffer, sems,
):
    step, steps = pl.program_id(0), pl.num_programs(0)
    rows = first_ref.shape[2]
    batches, key_size, value_size = state.shape
    slot = lax.rem(step, 2)

    def sent(at, which, batch):
        return pltpu.make_async_copy(
            grads_buffer.at[which, batch],
            grads_hbm.at[place_ref[batch, steps - 1 - at], batch],
            sems.at[which, batch],
        )

    @pl.when(step == 0)
    def _():
        state[...] = jnp.zeros_like(state)
        gain_grad_ref[...] = jnp.zeros_like(gain_grad_ref)

    @pl.when(step >= 2)
    def _():
        for batch in range(batches):
            sent(step - 2, slot, batch).wait()

    rows_in = jnp.concatenate([first_ref[0, 0], second_ref[0, 0]], axis=0)
    mixed_grads = dot_nt(rows_in, weight_ref[...])
    decay = decay_ref[0]
    entry_decay = column_ref[0, :, 0:1]
    end_weight = column_ref[0, :, 1:2]
    block_decay = column_ref[0, rows - 1 : rows, 0:1]
    positions = (steps - 1 - step) * rows + lax.broadcasted_iota(jnp.int32, (rows, 1), 0)
    gain = gain_ref[...]
    for batch, (swish_ref, normed_ref) in enumerate(
        ((swish_one, normed_one), (swish_two, normed_two))
    ):
        live = (positions < live_ref[batch]).astype(FULL)
        mixed_grad = mixed_grads[batch * rows : (batch + 1) * rows]
        query = qkv_ref[batch, 0, :, :key_size]
        key = qkv_ref[batch, 0, :, key_size : 2 * key_size]
        value = qkv_ref[batch, 0, :, 2 * key_size :]
        swish = swish_ref[0, 0].astype(FULL)
        normed = normed_ref[0, 0].astype(FULL)
        scale = scale_ref[batch, 0, :, 0:1]
        entry = entry_ref[batch, 0]
        sigmoid = jax.nn.sigmoid(swish)
        silu = swish * sigmoid
        swish_grad = mixed_grad * (normed * gain) * (sigmoid * (1.0 + swish - silu))
        scaled_grad = mixed_grad * silu
        gain_grad_ref[...] += jnp.sum(scaled_grad * normed, axis=0, keepdims=True)
        retained_grad = normalised_back(scaled_grad * gain, normed, scale).astype(HALF)
        weights = (dot_nt(query, key) * decay).astype(HALF)
        scores_grad = (dot_nt(retained_grad, value) * decay).astype(HALF)
        after = state[batch]
        after_low = after.astype(HALF)
        query_grad = dot_nn(scores_grad, key) + entry_decay * dot_nt(retained_grad, entry)
        key_grad = dot_tn(scores_grad, query) + end_weight * dot_nt(value, after_low)
        value_grad = dot_tn(weights, retained_grad) + end_weight * dot_nn(key, after_low)
        query_entered = (query.astype(FULL) * entry_decay).astype(HALF)
        state[batch] = block_decay * after + dot_tn(query_entered, retained_grad)
        grads_buffer[slot, batch, :, :key_size] = query_grad.astype(HALF)
        grads_buffer[slot, batch, :, key_size : 2 * key_size] = (key_grad * live).astype(HALF)
        grads_buffer[slot, batch, :, 2 * key_size : 2 * key_size + value_size] = value_grad.astype(
            HALF
        )
        grads_buffer[slot, batch, :, 2 * key_size + value_size :] = swish_grad.astype(HALF)
        sent(step, slot, batch).start()

    @pl.when(step == steps - 1)
    def _():
        for batch in range(batches):
            sent(step, slot, batch).wait()
            sent(step - 1, 1 - slot, batch).wait()


def retention_back(rows_in, swish, normed, weight, place, live, decay, columns, gain, saved):
    blocks, batches, rows, width = rows_in.shape
    qkv, scale, entry = saved
    value_size = gain.shape[-1]
    key_size = entry.shape[2]
    total = 2 * key_size + 2 * value_size

    def arriving(batch, size):
        return pl.BlockSpec(
            (1, 1, rows, size),
            lambda i, place, live: (place[batch, blocks - 1 - i], batch, 0, 0),
        )

    def whole(shape):
        return pl.BlockSpec(
            shape, lambda i, place, live: (0,) * len(shape), pipeline_mode=pl.Buffered(1)
        )

    def here(*tail):
        return pl.BlockSpec((batches, 1) + tail, lambda i, place, live: (0, blocks - 1 - i, 0, 0))

    def along(*tail):
        return pl.BlockSpec((1,) + tail, lambda i, place, live: (blocks - 1 - i, 0, 0))

    return pl.pallas_call(
        retention_back_kernel,
        grid_spec=pltpu.PrefetchScalarGridSpec(
            num_scalar_prefetch=2,
            grid=(blocks,),
            in_specs=[
                arriving(0, width),
                arriving(1, width),
                arriving(0, value_size),
                arriving(1, value_size),
                arriving(0, value_size),
                arriving(1, value_size),
                whole((value_size, width)),
                along(rows, rows),
                along(rows, 2),
                whole((1, value_size)),
                here(rows, 2 * key_size + value_size),
                here(rows, LANES),
                here(key_size, value_size),
            ],
            out_specs=[
                pl.BlockSpec((1, value_size), lambda i, place, live: (0, 0)),
                in_hbm(),
            ],
            scratch_shapes=[
                pltpu.VMEM((batches, key_size, value_size), FULL),
                pltpu.VMEM((2, batches, rows, total), HALF),
                pltpu.SemaphoreType.DMA((2, batches)),
            ],
        ),
        out_shape=[
            jax.ShapeDtypeStruct((1, value_size), FULL),
            jax.ShapeDtypeStruct((blocks, batches, rows, total), HALF),
        ],
        compiler_params=pltpu.CompilerParams(
            dimension_semantics=("arbitrary",), vmem_limit_bytes=VMEM_BYTES
        ),
        cost_estimate=pl.CostEstimate(
            flops=6 * blocks * batches * rows * width * value_size,
            bytes_accessed=2 * blocks * batches * rows * (width + 2 * total)
            + 2 * width * value_size,
            transcendentals=0,
        ),
    )(
        place, live, rows_in, rows_in, swish, swish, normed, normed, weight, decay, columns, gain,
        qkv, scale, entry,
    )


def middle_kernel(
    mixed_ref, weight_ref, tokens_ref, gain_ref, hidden_ref, second_out,
    terms, cores, nears, belows, sends, receives, own, keep, gather_sends, gather_receives,
):
    peers, groups = lax.axis_size("seq"), lax.axis_size("fsdp")
    size = tokens_ref.shape[0]
    greet_neighbours()

    def term(block):
        return dot_nn(mixed_ref[block], weight_ref[...]).astype(HALF)

    scatter = PlaneScatter(term, terms, cores, nears, belows, sends, receives)
    scatter.run()
    gain = gain_ref[...]
    for start in range(0, size, CHUNK):
        rows = pl.ds(start, CHUNK)
        hidden = tokens_ref[rows].astype(FULL) + scatter.total(start, CHUNK)
        hidden_ref[rows] = hidden
        normed, _ = normalised(hidden)
        own[rows] = regroup(normed * gain, peers, groups).astype(HALF)
    gather = PlaneGather(own, second_out, keep, gather_sends, gather_receives)
    gather.begin()
    gather.relay()
    gather.finish()


def middle(mixed, weight, tokens, gain):
    peers, own, inner = mixed.shape
    width = weight.shape[1]
    return pl.pallas_call(
        middle_kernel,
        in_specs=[vmem()] * 4,
        out_specs=[vmem(), in_hbm()],
        out_shape=[
            jax.ShapeDtypeStruct((own, width), FULL),
            jax.ShapeDtypeStruct((peers, own, width), HALF),
        ],
        scratch_shapes=scatter_scratch(own, width)
        + [pltpu.VMEM((own, width), HALF)]
        + gather_scratch(),
        compiler_params=linked(2),
        cost_estimate=cost(2 * peers * own * inner * width, 4 * peers * own * width),
    )(mixed, weight, tokens, gain)


def middle_back_kernel(
    grads_ref, weight_ref, hidden_ref, outer_ref, mask_ref, gain_ref,
    hidden_grad_ref, gain_grad_ref, branch_out,
    terms, cores, nears, belows, sends, receives, own, keep, gather_sends, gather_receives,
):
    peers, groups = lax.axis_size("seq"), lax.axis_size("fsdp")
    size = hidden_ref.shape[0]
    greet_neighbours()

    def term(block):
        return dot_nt(grads_ref[block], weight_ref[...]).astype(HALF)

    scatter = PlaneScatter(term, terms, cores, nears, belows, sends, receives)
    scatter.run()
    gain = gain_ref[...]
    gain_grad_ref[...] = jnp.zeros_like(gain_grad_ref)
    for start in range(0, size, CHUNK):
        rows = pl.ds(start, CHUNK)
        grad = regroup(scatter.total(start, CHUNK), groups, peers)
        normed, scale = normalised(hidden_ref[rows])
        gain_grad_ref[...] += jnp.sum(grad * normed, axis=0, keepdims=True)
        outer = outer_ref[rows].astype(FULL) * mask_ref[rows]
        hidden_grad = outer + normalised_back(grad * gain, normed, scale)
        hidden_grad_ref[rows] = hidden_grad
        own[rows] = hidden_grad.astype(HALF)
    gather = PlaneGather(own, branch_out, keep, gather_sends, gather_receives)
    gather.begin()
    gather.relay()
    gather.finish()


def middle_back(grads, weight, hidden, outer, mask, gain):
    peers, own, inner = grads.shape
    width = weight.shape[0]
    return pl.pallas_call(
        middle_back_kernel,
        in_specs=[vmem()] * 6,
        out_specs=[vmem(), vmem(), in_hbm()],
        out_shape=[
            jax.ShapeDtypeStruct((own, width), FULL),
            jax.ShapeDtypeStruct((1, width), FULL),
            jax.ShapeDtypeStruct((peers, own, width), HALF),
        ],
        scratch_shapes=scatter_scratch(own, width)
        + [pltpu.VMEM((own, width), HALF)]
        + gather_scratch(),
        compiler_params=linked(3),
        cost_estimate=cost(2 * peers * own * inner * width, 4 * peers * own * width),
    )(grads, weight, hidden, outer, mask, gain)


def result_kernel(
    inner_ref, weight_ref, hidden_ref, mask_ref, output_ref,
    terms, cores, nears, belows, sends, receives,
):
    greet_neighbours()

    def term(block):
        return dot_nn(inner_ref[block], weight_ref[...]).astype(HALF)

    scatter = PlaneScatter(term, terms, cores, nears, belows, sends, receives)
    scatter.run()
    for start in range(0, hidden_ref.shape[0], CHUNK):
        rows = pl.ds(start, CHUNK)
        total = hidden_ref[rows] + scatter.total(start, CHUNK)
        output_ref[rows] = (total * mask_ref[rows]).astype(HALF)


def result_rows(inner, weight, hidden, mask):
    peers, own, size = inner.shape
    width = weight.shape[1]
    return pl.pallas_call(
        result_kernel,
        in_specs=[vmem()] * 4,
        out_specs=vmem(),
        out_shape=jax.ShapeDtypeStruct((own, width), HALF),
        scratch_shapes=scatter_scratch(own, width),
        compiler_params=linked(4),
        cost_estimate=cost(2 * peers * own * size * width, 2 * peers * own * width),
    )(inner, weight, hidden, mask)


def last_kernel(
    grads_ref, weight_ref, tokens_ref, hidden_grad_ref, gain_ref,
    second_grad_ref, group_grad_ref,
    input_ref, gains_ref, group_ref,
    terms, cores, nears, belows, sends, receives,
    sums, parts, across, totals, keep, part_sends, part_receives, group_keep, group_sends,
    group_receives,
):
    peers, groups = lax.axis_size("seq"), lax.axis_size("fsdp")
    group = lax.axis_index("fsdp")
    greet_plane(True)

    def term(block):
        return dot_nt(grads_ref[block], weight_ref[...]).astype(HALF)

    scatter = PlaneScatter(term, terms, cores, nears, belows, sends, receives)
    scatter.run()
    gain = gain_ref[...]
    first_grad = jnp.zeros(gain.shape, FULL)
    for start in range(0, tokens_ref.shape[0], CHUNK):
        rows = pl.ds(start, CHUNK)
        grad = regroup(scatter.total(start, CHUNK), groups, peers)
        normed, scale = normalised(tokens_ref[rows].astype(FULL))
        first_grad += jnp.sum(grad * normed, axis=0, keepdims=True)
        input_ref[rows] = (
            hidden_grad_ref[rows] + normalised_back(grad * gain, normed, scale)
        ).astype(HALF)
    tile = LANES * 2
    for peer in range(peers):
        for row in range(tile // LANES):
            at = peer * tile + row * LANES
            sums[peer, row : row + 1] = first_grad[:, at : at + LANES]
            sums[peer, 2 + row : 3 + row] = second_grad_ref[:, at : at + LANES]
        sums[peer, 4:8] = jnp.zeros((4, LANES), FULL)
    me = lax.axis_index("seq")

    def copy(turn):
        peer = lax.rem(me + turn, peers)
        return to_peer(sums.at[peer], parts.at[turn], part_sends.at[turn], part_receives.at[turn], peer)

    def kept():
        return pltpu.make_async_copy(sums.at[me], parts.at[0], keep)

    kept().start()
    for turn in range(1, peers):
        copy(turn).start()
    kept().wait()
    for turn in range(1, peers):
        copy(turn).wait_recv()
        copy(turn).wait_send()
    total = parts[0]
    for turn in range(1, peers):
        total += parts[turn]
    across[0:8] = total
    for row in range(4):
        across[8 + row : 9 + row] = group_grad_ref[:, row * LANES : (row + 1) * LANES]
    across[12:16] = jnp.zeros((4, LANES), FULL)
    begin, finish = all_to_each(
        across, totals, "fsdp", groups, group_keep, group_sends, group_receives
    )
    begin()
    finish()
    summed = totals[0]
    for turn in range(1, groups):
        summed += totals[turn]
    gains_ref[...] = summed[0:8]
    group_ref[...] = summed[8:16]


def last_rows(grads, weight, tokens, hidden_grad, gain, second_grad, group_grad):
    peers, own, inner = grads.shape
    groups = lax.axis_size("fsdp")
    width = weight.shape[0]
    return pl.pallas_call(
        last_kernel,
        in_specs=[vmem()] * 7,
        out_specs=[vmem()] * 3,
        out_shape=[
            jax.ShapeDtypeStruct((own, width), HALF),
            jax.ShapeDtypeStruct((8, LANES), FULL),
            jax.ShapeDtypeStruct((8, LANES), FULL),
        ],
        scratch_shapes=scatter_scratch(own, width)
        + [
            pltpu.VMEM((peers, 8, LANES), FULL),
            pltpu.VMEM((peers, 8, LANES), FULL),
            pltpu.VMEM((16, LANES), FULL),
            pltpu.VMEM((groups, 16, LANES), FULL),
            pltpu.SemaphoreType.DMA,
            pltpu.SemaphoreType.DMA((peers,)),
            pltpu.SemaphoreType.DMA((peers,)),
            pltpu.SemaphoreType.DMA,
            pltpu.SemaphoreType.DMA((groups,)),
            pltpu.SemaphoreType.DMA((groups,)),
        ],
        compiler_params=linked(5),
        cost_estimate=cost(2 * peers * own * inner * width, 2 * peers * own * width),
    )(grads, weight, tokens, hidden_grad, gain, second_grad, group_grad)


def return_kernel(cuts, source, *refs):
    count = len(cuts)
    targets = refs[:count]
    keeps, sends, receives = refs[count:]
    peers = lax.axis_size("seq")
    me = lax.axis_index("seq")
    greet_plane(False)

    def part(number, peer):
        start, size = cuts[number]
        return source.at[peer, :, pl.ds(start, size)]

    def place(number, peer):
        size = cuts[number][1]
        return targets[number].at[:, pl.ds(pl.multiple_of(peer * size, LANES), size)]

    def copy(number, turn):
        peer = lax.rem(me + turn, peers)
        return to_peer(
            part(number, peer),
            place(number, me),
            sends.at[number, turn],
            receives.at[number, turn],
            peer,
        )

    def landed(number, turn):
        peer = lax.rem(me + peers - turn, peers)
        target = place(number, peer)
        return to_peer(target, target, sends.at[number, turn], receives.at[number, turn], peer)

    def kept(number):
        return pltpu.make_async_copy(part(number, me), place(number, me), keeps.at[number])

    for number in range(count):
        for turn in range(1, peers):
            copy(number, turn).start()
        kept(number).start()
    for number in range(count):
        for turn in range(1, peers):
            landed(number, turn).wait_recv()
            copy(number, turn).wait_send()
        kept(number).wait()


def return_grads(collective, summed, *sizes):
    peers, slab, _ = summed.shape
    starts = [sum(sizes[:number]) for number in range(len(sizes))]
    return pl.pallas_call(
        partial(return_kernel, tuple(zip(starts, sizes))),
        in_specs=[in_hbm()],
        out_specs=[in_hbm()] * len(sizes),
        out_shape=[jax.ShapeDtypeStruct((slab, peers * size), HALF) for size in sizes],
        scratch_shapes=swap_scratch(len(sizes), peers),
        compiler_params=linked(collective),
        cost_estimate=cost(0, 2 * summed.size),
    )(summed)


def widen_kernel(*refs):
    count = len(refs) // 2
    for source, target in zip(refs[:count], refs[count:]):
        target[...] = source[...].astype(target.dtype)


def widen(*arrays):
    return pl.pallas_call(
        widen_kernel,
        in_specs=[vmem()] * len(arrays),
        out_specs=[vmem()] * len(arrays),
        out_shape=[jax.ShapeDtypeStruct(array.shape, FULL) for array in arrays],
        compiler_params=pltpu.CompilerParams(vmem_limit_bytes=VMEM_BYTES),
    )(*arrays)


def head_body(
    tokens,
    cotangent,
    lengths,
    block_order,
    log_decay,
    first_gain,
    query_weight,
    key_weight,
    value_weight,
    swish_weight,
    output_weight,
    group_gain,
    second_gain,
    feed_gate,
    feed_up,
    feed_down,
):
    peers, groups = lax.axis_size("seq"), lax.axis_size("fsdp")
    index, group = lax.axis_index("seq"), lax.axis_index("fsdp")
    batches, rows, width = tokens.shape
    own = batches * rows
    heads = log_decay.shape[0]
    key_size = query_weight.shape[1] // heads
    value_size = value_weight.shape[1] // heads
    part = feed_gate.shape[1] // peers
    slab = query_weight.shape[0]
    total = 2 * key_size + 2 * value_size

    def over_groups(local):
        return lax.all_gather(local, "fsdp", axis=0, tiled=True)

    def sum_groups(whole):
        return lax.psum_scatter(whole.astype(HALF), "fsdp", scatter_dimension=0, tiled=True)

    def gathered(cut):
        return over_groups(cut[None]).reshape(width, cut.shape[2])

    gains = jnp.concatenate(
        [
            group_gain.astype(FULL)[None],
            jnp.concatenate([first_gain, second_gain]).astype(FULL)[None],
            jnp.zeros((6, LANES), FULL),
        ],
        axis=0,
    )
    first_cut, rates, gains = first_swap(
        query_weight, key_weight, value_weight, swish_weight, log_decay, gains
    )
    out_weight = over_groups(output_weight)
    first_weight = gathered(first_cut)
    gain_one = gains[:, :, 1, :slab].reshape(1, width)
    gain_two = gains[:, :, 1, slab:].reshape(1, width)
    gain_group = lax.dynamic_index_in_dim(gains, index, 0, keepdims=False)[:, 0].reshape(
        1, value_size
    )

    rates = lax.dynamic_index_in_dim(rates, index, 1, keepdims=False)
    cumulative = jnp.cumsum(rates, axis=1)
    slots = jnp.arange(rows)
    lower = slots[:, None] >= slots[None, :]
    spread = cumulative[:, :, None] - cumulative[:, None, :]
    decay = jnp.where(lower, jnp.exp(jnp.where(lower, spread, 0.0)), 0.0)
    columns = jnp.stack([jnp.exp(cumulative), jnp.exp(cumulative[:, -1:] - cumulative)], axis=2)

    order = lax.dynamic_slice_in_dim(block_order, group * batches, batches, 0)
    numbers = jnp.arange(peers, dtype=jnp.int32)
    place = jnp.sum(
        numbers[None, None, :] * (order[:, None, :] == numbers[None, :, None]).astype(jnp.int32),
        axis=2,
    )
    live = lax.dynamic_slice_in_dim(lengths, group * batches, batches, 0)
    held = lax.dynamic_index_in_dim(order, index, 1, keepdims=False)
    positions = held[:, None] * rows + jnp.arange(rows, dtype=jnp.int32)
    mask = (positions < live[:, None]).astype(FULL).reshape(own, 1)

    out_weight, tokens = lax.optimization_barrier((out_weight, tokens))
    token_rows = tokens.reshape(own, width)
    outer_rows = cotangent.reshape(own, width)
    entered, result_low, feed_cut = gather_inputs(
        token_rows, outer_rows, mask, gain_one, feed_gate, feed_up
    )
    feed_weight = gathered(feed_cut)
    down_weight = over_groups(feed_down)

    qkv, scale, entry, normed = retention(
        entered.reshape(peers, batches, rows, width),
        first_weight,
        place,
        live,
        decay,
        columns,
        key_size,
        value_size,
    )
    entered = entered.reshape(peers * own, width)
    swish = dot_nn(entered, first_weight[:, 2 * key_size + value_size :])
    grouped = normed.reshape(peers * own, value_size).astype(FULL) * gain_group
    mixed = (jax.nn.silu(swish) * grouped).astype(HALF)
    swish = swish.astype(HALF)
    hidden, second = middle(mixed.reshape(peers, own, value_size), out_weight, token_rows, gain_two)
    second = second.reshape(peers * own, width)
    result_low = result_low.reshape(peers * own, width)
    both = dot_nn(second, feed_weight)
    inner, pull_inner = jax.vjp(gated_gelu, both[:, :part], both[:, part:])
    inner_low = inner.astype(HALF)
    down_term, late_low = lax.optimization_barrier(
        (dot_tn(inner_low, result_low).astype(HALF), result_low)
    )
    down_grad = sum_groups(down_term)
    gate_grad, upward_grad = pull_inner(dot_nt(late_low, down_weight))
    both_grad = jnp.concatenate([gate_grad.astype(HALF), upward_grad.astype(HALF)], axis=1)
    both_term, both_grad = lax.optimization_barrier(
        (dot_tn(second, both_grad).astype(HALF), both_grad)
    )
    both_weight_grad = sum_groups(both_term).reshape(peers, slab, 2 * part)
    hidden_grad, second_gain_grad, branch_low = middle_back(
        both_grad.reshape(peers, own, 2 * part),
        feed_weight,
        hidden,
        outer_rows,
        mask,
        gain_two,
    )
    out_term, branch_low, down_grad = lax.optimization_barrier(
        (dot_tn(mixed, branch_low.reshape(peers * own, width)).astype(HALF), branch_low, down_grad)
    )
    group_gain_grad, projected_grad = retention_back(
        branch_low.reshape(peers, batches, rows, width),
        swish.reshape(peers, batches, rows, value_size),
        normed,
        out_weight,
        place,
        live,
        decay,
        columns,
        gain_group,
        (qkv, scale, entry),
    )
    flat_grad = projected_grad.reshape(peers * own, total)
    out_grad = sum_groups(out_term)
    first_term, projected_grad = lax.optimization_barrier(
        (dot_tn(entered, flat_grad).astype(HALF), projected_grad)
    )
    first_weight_grad = sum_groups(first_term).reshape(peers, slab, total)
    projected_grad, both_weight_grad = lax.optimization_barrier((projected_grad, both_weight_grad))
    input_rows, gain_grads, group_grads = last_rows(
        projected_grad.reshape(peers, own, total),
        first_weight,
        token_rows,
        hidden_grad,
        gain_one,
        second_gain_grad,
        group_gain_grad,
    )
    inner_low, out_grad = lax.optimization_barrier((inner_low, out_grad))
    output_rows = result_rows(
        inner_low.reshape(peers, own, part), down_weight, hidden, mask
    )
    both_back = return_grads(6, both_weight_grad, part, part)
    first_back = return_grads(
        7, first_weight_grad, key_size, key_size, value_size, value_size
    )
    gate_back, up_back, out_back, down_back = widen(*both_back, out_grad, down_grad)
    query_back, key_back, value_back, swish_back = widen(*first_back)

    def mine(summed, start):
        flat = summed[start : start + 2].reshape(groups, slab)
        return lax.dynamic_index_in_dim(flat, group, 0, keepdims=False)

    return (
        output_rows.reshape(batches, rows, width),
        input_rows.reshape(batches, rows, width),
        mine(gain_grads, 0),
        query_back,
        key_back,
        value_back,
        swish_back,
        out_back,
        lax.dynamic_index_in_dim(group_grads, group, 0, keepdims=False),
        mine(gain_grads, 2),
        gate_back,
        up_back,
        down_back,
    )


def body(*arrays):
    peers, groups = lax.axis_size("seq"), lax.axis_size("fsdp")
    fits = peers == 8 and groups == 4 and arrays[4].shape[0] == peers and arrays[0].shape[0] == 2
    if fits:
        return head_body(*arrays)
    return general_body(*arrays)


def solution(mesh):
    placed = (
        P("fsdp", "seq", None),
        P("fsdp", "seq", None),
        P(),
        P(),
        P(None, "seq"),
        P(("seq", "fsdp")),
        P(("seq", "fsdp"), None),
        P(("seq", "fsdp"), None),
        P(("seq", "fsdp"), None),
        P(("seq", "fsdp"), None),
        P(("seq", "fsdp"), None),
        P(("seq", "fsdp")),
        P(("seq", "fsdp")),
        P(("seq", "fsdp"), None),
        P(("seq", "fsdp"), None),
        P(("seq", "fsdp"), None),
    )
    return jax.shard_map(
        body,
        mesh=mesh,
        in_specs=placed,
        out_specs=(
            P("fsdp", "seq", None),
            P("fsdp", "seq", None),
            P(("seq", "fsdp")),
            P(("seq", "fsdp"), None),
            P(("seq", "fsdp"), None),
            P(("seq", "fsdp"), None),
            P(("seq", "fsdp"), None),
            P(("seq", "fsdp"), None),
            P(("seq", "fsdp")),
            P(("seq", "fsdp")),
            P(("seq", "fsdp"), None),
            P(("seq", "fsdp"), None),
            P(("seq", "fsdp"), None),
        ),
        check_vma=False,
    )
```

```python
from functools import partial, reduce

import jax
import jax.numpy as jnp
from jax import lax
from jax.experimental import pallas as pl
from jax.experimental.pallas import tpu as pltpu
from jax.sharding import PartitionSpec as P

EPSILON = 1e-05
HIGHEST = lax.Precision.HIGHEST


def carried_in(value, axis, combine, identity, reverse):
    peers, index = (lax.axis_size(axis), lax.axis_index(axis))
    everything = jax.tree.map(
        lambda part, kind: lax.all_gather(part.astype(kind), axis),
        value,
        (jnp.bfloat16, jnp.bfloat16),
    )
    start = jax.tree.map(
        lambda part, zero: jnp.broadcast_to(jnp.asarray(zero, part.dtype), part.shape),
        value,
        identity,
    )

    def turn(k, before):
        at = peers - 1 - k if reverse else k
        reached = at > index if reverse else at < index
        new = combine(
            before, jax.tree.map(lambda part, own: part[at].astype(own.dtype), everything, value)
        )
        return jax.tree.map(lambda a, b: jnp.where(reached, a, b), new, before)

    return lax.fori_loop(0, peers, turn, start)


def norm_rows(values, gain):
    average = jnp.mean(values, axis=-1, keepdims=True)
    centered = values - average
    variance = jnp.mean(centered * centered, axis=-1, keepdims=True)
    return centered * lax.rsqrt(variance + EPSILON) * gain


def gated_swish(swish_in, grouped):
    return jax.nn.silu(swish_in) * grouped


def gated_gelu(gate_in, upward):
    return jax.nn.gelu(gate_in) * upward


def chain_states(earlier, later):
    return (earlier[0] * later[0], later[0][:, None, None] * earlier[1] + later[1])


def transposed(left_rows, weight):
    return jnp.einsum("ie,fe->if", left_rows, weight, preferred_element_type=jnp.float32)


def plain_dot(left_rows, weight):
    return jnp.dot(left_rows, weight, preferred_element_type=jnp.float32)


def outer_term(left_rows, right_rows):
    return jnp.einsum("ni,no->io", left_rows, right_rows, preferred_element_type=jnp.float32)


def spread_sum(matrix_pairs, vectors):
    terms = tuple((outer_term(left_rows, right_rows) for left_rows, right_rows in matrix_pairs))
    pieces = lax.psum_scatter(
        terms + tuple(vectors), ("seq", "fsdp"), scatter_dimension=0, tiled=True
    )
    return list(pieces)


def join_terms(collected):
    matrix_pairs = []
    for member in range(len(collected[0][0])):
        lefts = jnp.concatenate([entry[0][member][0] for entry in collected], axis=0)
        rights = jnp.concatenate([entry[0][member][1] for entry in collected], axis=0)
        matrix_pairs.append((lefts, rights))
    vectors = [
        reduce(jnp.add, [entry[1][member] for entry in collected])
        for member in range(len(collected[0][1]))
    ]
    return (matrix_pairs, vectors)


def layer_step(gathered, inputs, cot_rows, live_mask, log_rates):
    (
        first_gain,
        query_weight,
        key_weight,
        value_weight,
        swish_weight,
        output_weight,
        group_gain,
        second_gain,
        feed_gate,
        feed_up,
        feed_down,
    ) = gathered
    floats = jnp.float32
    halves = jnp.bfloat16
    head_count = log_rates.shape[0]
    token_rows = inputs.shape[0]
    key_size = query_weight.shape[1] // head_count
    value_size = value_weight.shape[1] // head_count
    start_values = inputs.astype(floats)
    normed_one, pull_one = jax.vjp(norm_rows, start_values, first_gain.astype(floats))
    normed = normed_one.astype(halves)
    queries = plain_dot(normed, query_weight).astype(halves)
    keys_in = plain_dot(normed, key_weight).astype(halves) * live_mask[:, None].astype(halves)
    values_in = plain_dot(normed, value_weight).astype(halves)
    swish_in = plain_dot(normed, swish_weight)
    queries3 = queries.reshape(token_rows, head_count, key_size)
    keys3 = keys_in.reshape(token_rows, head_count, key_size)
    values3 = values_in.reshape(token_rows, head_count, value_size)
    cumulative = jnp.cumsum(log_rates, axis=1)
    slot_index = jnp.arange(token_rows)
    lower_mask = slot_index[:, None] >= slot_index[None, :]
    spread = cumulative[:, :, None] - cumulative[:, None, :]
    decay_matrix = jnp.where(lower_mask, jnp.exp(jnp.where(lower_mask, spread, 0.0)), 0.0)
    block_decay = jnp.exp(cumulative[:, -1])
    end_weight = jnp.exp(cumulative[:, -1:] - cumulative).T[:, :, None]
    entry_decay = jnp.exp(cumulative).T[:, :, None]
    query_wide = queries3.astype(floats)
    key_wide = keys3.astype(floats)
    value_wide = values3.astype(floats)
    state_term = jnp.einsum("jhd,jhe->hde", key_wide * end_weight, value_wide, precision=HIGHEST)
    state_identity = (jnp.ones_like(block_decay), jnp.zeros_like(state_term))
    _, start_state = carried_in(
        (block_decay, state_term), "seq", chain_states, state_identity, False
    )
    scores = jnp.einsum("ihd,jhd->hij", queries3, keys3, preferred_element_type=floats)
    weights = (scores * decay_matrix).astype(halves)
    intra_term = jnp.einsum("hij,jhe->ihe", weights, values3, preferred_element_type=floats)
    carried = entry_decay * jnp.einsum("ihd,hde->ihe", query_wide, start_state, precision=HIGHEST)
    retained = intra_term + carried
    grouped, pull_group = jax.vjp(
        norm_rows, retained, group_gain.astype(floats).reshape(head_count, value_size)
    )
    grouped_flat = grouped.reshape(token_rows, head_count * value_size)
    mixed_float, pull_mixed = jax.vjp(gated_swish, swish_in, grouped_flat)
    mixed_low = mixed_float.astype(halves)
    hidden = start_values + plain_dot(mixed_low, output_weight)
    normed_two, pull_two = jax.vjp(norm_rows, hidden, second_gain.astype(floats))
    second = normed_two.astype(halves)
    gate_two = plain_dot(second, feed_gate)
    upward = plain_dot(second, feed_up)
    inner_float, pull_inner = jax.vjp(gated_gelu, gate_two, upward)
    inner_low = inner_float.astype(halves)
    result = plain_dot(inner_low, feed_down)
    output_rows = ((hidden + result) * live_mask[:, None]).astype(halves)
    outer_grad = cot_rows.astype(floats) * live_mask[:, None]
    result_low = outer_grad.astype(halves)
    inner_grad = transposed(result_low, feed_down)
    gate_two_grad, upward_grad = pull_inner(inner_grad)
    gate_two_low = gate_two_grad.astype(halves)
    upward_low = upward_grad.astype(halves)
    second_grad = transposed(gate_two_low, feed_gate) + transposed(upward_low, feed_up)
    hidden_part, second_gain_grad = pull_two(second_grad)
    hidden_grad = outer_grad + hidden_part
    branch_low = hidden_grad.astype(halves)
    mixed_grad = transposed(branch_low, output_weight)
    swish_grad, grouped_grad = pull_mixed(mixed_grad)
    swish_low = swish_grad.astype(halves)
    retained_grad, group_gain_grad = pull_group(
        grouped_grad.reshape(token_rows, head_count, value_size)
    )
    retained_low = retained_grad.astype(halves)
    weights_grad = jnp.einsum("ihe,jhe->hij", retained_low, values3, preferred_element_type=floats)
    scores_low = (weights_grad * decay_matrix).astype(halves)
    query_intra = jnp.einsum("hij,jhd->ihd", scores_low, keys3, preferred_element_type=floats)
    key_intra = jnp.einsum("hij,ihd->jhd", scores_low, queries3, preferred_element_type=floats)
    value_intra = jnp.einsum("hij,ihe->jhe", weights, retained_low, preferred_element_type=floats)
    retained_wide = retained_low.astype(floats)
    query_carried = entry_decay * jnp.einsum(
        "ihe,hde->ihd", retained_wide, start_state, precision=HIGHEST
    )
    local_grad = jnp.einsum(
        "ihd,ihe->hde", query_wide * entry_decay, retained_wide, precision=HIGHEST
    )
    _, end_grad = carried_in((block_decay, local_grad), "seq", chain_states, state_identity, True)
    key_state = end_weight * jnp.einsum("jhe,hde->jhd", value_wide, end_grad, precision=HIGHEST)
    value_state = end_weight * jnp.einsum("jhd,hde->jhe", key_wide, end_grad, precision=HIGHEST)
    query_low = (
        (query_intra + query_carried).astype(halves).reshape(token_rows, head_count * key_size)
    )
    key_low = (
        ((key_intra + key_state) * live_mask[:, None, None])
        .astype(halves)
        .reshape(token_rows, head_count * key_size)
    )
    value_low = (
        (value_intra + value_state).astype(halves).reshape(token_rows, head_count * value_size)
    )
    normed_grad = (
        transposed(query_low, query_weight)
        + transposed(key_low, key_weight)
        + transposed(value_low, value_weight)
        + transposed(swish_low, swish_weight)
    )
    input_part, first_gain_grad = pull_one(normed_grad)
    grad_rows = (hidden_grad + input_part).astype(halves)
    matrix_pairs = [
        (normed, query_low),
        (normed, key_low),
        (normed, value_low),
        (normed, swish_low),
        (mixed_low, branch_low),
        (second, gate_two_low),
        (second, upward_low),
        (inner_low, result_low),
    ]
    vectors = [first_gain_grad, group_gain_grad.reshape(-1), second_gain_grad]
    return (output_rows, grad_rows, matrix_pairs, vectors)


def general_body(
    tokens,
    cotangent,
    lengths,
    block_order,
    log_decay,
    first_gain,
    query_weight,
    key_weight,
    value_weight,
    swish_weight,
    output_weight,
    group_gain,
    second_gain,
    feed_gate,
    feed_up,
    feed_down,
):
    batches = tokens.shape[0]
    block_rows = tokens.shape[1]
    selected_locations = lax.axis_size("seq")
    position = lax.axis_index("seq")
    group_index = lax.axis_index("fsdp")
    place_numbers = jnp.arange(selected_locations, dtype=jnp.int32)
    arrived_tokens, arrived_cotangent = (
        lax.all_gather(tokens, "seq", axis=1, tiled=True),
        lax.all_gather(cotangent, "seq", axis=1, tiled=True),
    )
    gathered = (
        lax.all_gather(first_gain, ("seq", "fsdp"), axis=0, tiled=True),
        lax.all_gather(query_weight, ("seq", "fsdp"), axis=0, tiled=True),
        lax.all_gather(key_weight, ("seq", "fsdp"), axis=0, tiled=True),
        lax.all_gather(value_weight, ("seq", "fsdp"), axis=0, tiled=True),
        lax.all_gather(swish_weight, ("seq", "fsdp"), axis=0, tiled=True),
        lax.all_gather(output_weight, ("seq", "fsdp"), axis=0, tiled=True),
        lax.all_gather(group_gain, ("seq", "fsdp"), axis=0, tiled=True),
        lax.all_gather(second_gain, ("seq", "fsdp"), axis=0, tiled=True),
        lax.all_gather(feed_gate, ("seq", "fsdp"), axis=0, tiled=True),
        lax.all_gather(feed_up, ("seq", "fsdp"), axis=0, tiled=True),
        lax.all_gather(feed_down, ("seq", "fsdp"), axis=0, tiled=True),
    )
    outputs = []
    input_grads = []
    collected = []
    order_rows = []
    for batch_number in range(batches):
        sequence = group_index * batches + batch_number
        order_row = lax.dynamic_index_in_dim(block_order, sequence, 0, keepdims=False)
        order_rows.append(order_row)
        source = jnp.sum(place_numbers * (order_row == position).astype(jnp.int32))
        token_rows = lax.dynamic_slice_in_dim(
            arrived_tokens[batch_number], source * block_rows, block_rows, 0
        )
        cot_rows = lax.dynamic_slice_in_dim(
            arrived_cotangent[batch_number], source * block_rows, block_rows, 0
        )
        live_length = lax.dynamic_index_in_dim(lengths, sequence, 0, keepdims=False)
        location_number = position * block_rows + jnp.arange(block_rows, dtype=jnp.int32)
        live_mask = (location_number < live_length).astype(jnp.float32)
        output_rows, grad_rows, matrix_pairs, vectors = layer_step(
            gathered, token_rows, cot_rows, live_mask, log_decay
        )
        outputs.append(output_rows)
        input_grads.append(grad_rows)
        collected.append((matrix_pairs, vectors))
    joined_pairs, joined_vectors = join_terms(collected)
    shards = spread_sum(joined_pairs, joined_vectors)
    every_output, every_grad = (
        lax.all_gather(jnp.stack(outputs), "seq", axis=1, tiled=True),
        lax.all_gather(jnp.stack(input_grads), "seq", axis=1, tiled=True),
    )
    returned = []
    returned_grads = []
    for batch_number in range(batches):
        target = lax.dynamic_index_in_dim(order_rows[batch_number], position, 0, keepdims=False)
        returned.append(
            lax.dynamic_slice_in_dim(every_output[batch_number], target * block_rows, block_rows, 0)
        )
        returned_grads.append(
            lax.dynamic_slice_in_dim(every_grad[batch_number], target * block_rows, block_rows, 0)
        )
    return (
        jnp.stack(returned),
        jnp.stack(returned_grads),
        shards[8],
        shards[0],
        shards[1],
        shards[2],
        shards[3],
        shards[4],
        shards[9],
        shards[10],
        shards[5],
        shards[6],
        shards[7],
    )


FULL = jnp.float32
HALF = jnp.bfloat16
MESH = pl.DeviceIdType.MESH
VMEM_BYTES = 56 * 1024 * 1024
LARGE_BYTES = 63 * 1024 * 1024
LANES = 128


def dot_nn(left, right):
    return jnp.dot(left, right, preferred_element_type=FULL)


def dot_nt(left, right):
    return lax.dot_general(left, right, (((1,), (1,)), ((), ())), preferred_element_type=FULL)


def dot_tn(left, right):
    return lax.dot_general(left, right, (((0,), (0,)), ((), ())), preferred_element_type=FULL)


def plane_peers():
    me = lax.axis_index("seq")
    core = lax.rem(me, 2)
    across = 2 - 4 * lax.rem(me // 2, 2)
    down = 4 - 8 * (me // 4)
    return me, me + 1 - 2 * core, me + across, me + down, me + across + down


def to_peer(source, target, send, receive, peer):
    return pltpu.make_async_remote_copy(
        src_ref=source,
        dst_ref=target,
        send_sem=send,
        recv_sem=receive,
        device_id={"seq": peer},
        device_id_type=MESH,
    )


def greet_neighbours():
    _, other, near, below, _ = plane_peers()
    barrier = pltpu.get_barrier_semaphore()
    for peer in (other, near, below):
        pl.semaphore_signal(barrier, inc=1, device_id={"seq": peer}, device_id_type=MESH)
    pl.semaphore_wait(barrier, 3)


GATHER_COPIES = 14


def gather_plan():
    me, other, near, below, far = plane_peers()
    flip = other - me
    return (
        (me, 0, near, near),
        (me, 1, below, below),
        (me, 0, other, other),
        (me, 1, other, other),
        (me, 1, near, near),
        (me, 0, below, below),
        (near, 0, below, far),
        (below, 1, near, far),
        (near, 0, other, near + flip),
        (below, 1, other, below + flip),
        (near, 1, other, near + flip),
        (below, 0, other, below + flip),
        (far, 0, other, far + flip),
        (far, 1, other, far + flip),
    )


class PlaneGather:
    def __init__(self, own, out, keeps, sends, receives, window=0, windows=1):
        self.own, self.out = own, out
        self.keep, self.sends, self.receives = keeps.at[window], sends, receives
        self.size = own.shape[0] // windows
        self.window, self.start = window, window * self.size
        self.half = self.size // 2

    def rows(self, which):
        return pl.ds(self.start + which * self.half, self.half)

    def kept(self):
        me = lax.axis_index("seq")
        rows = pl.ds(self.start, self.size)
        return pltpu.make_async_copy(self.own.at[rows], self.out.at[me, rows], self.keep)

    def sent(self, source, target, number, peer):
        at = (self.window, number)
        return to_peer(source, target, self.sends.at[at], self.receives.at[at], peer)

    def copy(self, number):
        block, which, peer, _ = gather_plan()[number]
        target = self.out.at[block, self.rows(which)]
        source = self.own.at[self.rows(which)] if number < 6 else target
        return self.sent(source, target, number, peer)

    def landed(self, number):
        _, which, peer, landing = gather_plan()[number]
        target = self.out.at[landing, self.rows(which)]
        self.sent(target, target, number, peer).wait_recv()

    def begin(self):
        self.kept().start()
        for number in range(6):
            self.copy(number).start()

    def relay(self):
        for arrived, onward in ((0, (6, 8)), (1, (7, 9)), (4, (10,)), (5, (11,))):
            self.landed(arrived)
            for number in onward:
                self.copy(number).start()

    def finish(self):
        for arrived, onward in ((6, 12), (7, 13)):
            self.landed(arrived)
            self.copy(onward).start()
        for number in (2, 3, 8, 9, 10, 11, 12, 13):
            self.landed(number)
        for number in range(GATHER_COPIES):
            self.copy(number).wait_send()
        self.kept().wait()


def gather_scratch(windows=1):
    return [
        pltpu.SemaphoreType.DMA((windows,)),
        pltpu.SemaphoreType.DMA((windows, GATHER_COPIES)),
        pltpu.SemaphoreType.DMA((windows, GATHER_COPIES)),
    ]


SCATTER_COPIES = 10
WINDOWS = 2
CHUNK = 32


def by_chunks(rows, work):
    def step(number, carry):
        work(pl.ds(pl.multiple_of(number * CHUNK, CHUNK), CHUNK))
        return carry

    lax.fori_loop(0, rows // CHUNK, step, 0)


class PlaneScatter:
    def __init__(self, window, others, terms, cores, nears, belows, sends, receives):
        self.window = window
        self.others, self.terms, self.cores = others, terms, cores
        self.nears, self.belows = nears, belows
        self.sends, self.receives = sends, receives
        self.size = terms.shape[1] // WINDOWS
        self.half = self.size // 2
        self.start = window * self.size

    def copy(self, number):
        _, other, near, below, _ = plane_peers()
        whole = pl.ds(self.start, self.size)
        upper, lower = (pl.ds(self.start + at * self.half, self.half) for at in (0, 1))
        if number < 4:
            source, target, peer = (
                self.others.at[number, whole],
                self.cores.at[number, whole],
                other,
            )
        else:
            slot, rows, landing, place, peer = (
                (0, upper, self.nears, 0, near),
                (0, lower, self.belows, 0, below),
                (1, upper, self.nears, 1, near),
                (2, lower, self.belows, 1, below),
                (1, lower, self.nears, 2, near),
                (2, upper, self.belows, 2, below),
            )[number - 4]
            source, target = self.terms.at[slot, rows], landing.at[self.window, place]
        at = (self.window, number)
        return to_peer(source, target, self.sends.at[at], self.receives.at[at], peer)

    def fold(self, slot):
        def work(rows):
            here = pl.ds(pl.multiple_of(self.start + rows.start, CHUNK), CHUNK)
            self.terms[slot, here] = (
                self.terms[slot, here].astype(FULL) + self.cores[slot, here].astype(FULL)
            ).astype(HALF)

        by_chunks(self.size, work)

    def fold_half(self, slot, which, landed):
        def work(rows):
            at = self.start + which * self.half
            here = pl.ds(pl.multiple_of(at + rows.start, CHUNK), CHUNK)
            self.terms[slot, here] = (
                self.terms[slot, here].astype(FULL) + landed[self.window, 0, rows].astype(FULL)
            ).astype(HALF)

        by_chunks(self.half, work)

    def advance(self, slot):
        self.copy(slot).wait_recv()
        self.fold(slot)
        for number in ((4, 5), (6,), (7,), ())[slot]:
            self.copy(number).start()

    def relay(self):
        self.copy(4).wait_recv()
        self.fold_half(2, 0, self.nears)
        self.copy(9).start()
        self.copy(5).wait_recv()
        self.fold_half(1, 1, self.belows)
        self.copy(8).start()

    def finish(self):
        for number in (6, 7, 8, 9):
            self.copy(number).wait_recv()

    def drain(self, first=0):
        for number in range(first, SCATTER_COPIES):
            self.copy(number).wait_send()

    def total(self, at):
        upper = at < self.half
        rows = pl.ds(at if upper else at - self.half, CHUNK)
        near, below = (1, 2) if upper else (2, 1)
        return (
            self.terms[3, pl.ds(self.start + at, CHUNK)].astype(FULL)
            + self.nears[self.window, near, rows].astype(FULL)
            + self.belows[self.window, below, rows].astype(FULL)
        )


def block_order_of_plane():
    me, other, near, below, far = plane_peers()
    return [block + at for block in (far, near, below, me) for at in (other - me, 0)]


def scatter_head(term, refs, earlier=(), relay_later=False):
    windows = [PlaneScatter(window, *refs) for window in range(WINDOWS)]
    others, terms = refs[:2]
    blocks = block_order_of_plane()

    def fill(slot):
        for window in earlier:
            window.copy(slot).wait_send()
        others[slot] = term(blocks[2 * slot])
        for window in windows:
            window.copy(slot).start()
        terms[slot] = term(blocks[2 * slot + 1])

    fill(0)
    for slot in range(4):
        if slot < 3:
            fill(slot + 1)
        windows[0].advance(slot)
    if not relay_later:
        windows[0].relay()
    for window in windows[1:]:
        for slot in range(4):
            window.advance(slot)
        if not relay_later:
            window.relay()
    return windows


def scatter_tail(windows, use, after=lambda window: None):
    for number, window in enumerate(windows):
        window.finish()
        for at in range(0, window.size, CHUNK):
            use(window.start + at, window.total(at))
        after(number)


def scatter_scratch(rows, width):
    half = rows // WINDOWS // 2
    return [
        pltpu.VMEM((4, rows, width), HALF),
        pltpu.VMEM((4, rows, width), HALF),
        pltpu.VMEM((4, rows, width), HALF),
        pltpu.VMEM((WINDOWS, 3, half, width), HALF),
        pltpu.VMEM((WINDOWS, 3, half, width), HALF),
        pltpu.SemaphoreType.DMA((WINDOWS, SCATTER_COPIES)),
        pltpu.SemaphoreType.DMA((WINDOWS, SCATTER_COPIES)),
    ]


def regroup(values, outer, inner):
    rows = values.shape[0]
    low_half = lax.broadcasted_iota(jnp.int32, (rows, LANES), 1) < LANES // 2

    def piece(p, q):
        at = (p * inner + q) // 2
        return values[:, at * LANES : (at + 1) * LANES]

    def turned(value):
        return pltpu.roll(value, LANES // 2, 1)

    groups = []
    for q in range(inner):
        for p in range(0, outer, 2):
            first, second = piece(p, q), piece(p + 1, q)
            if q % 2 == 0:
                groups.append(jnp.where(low_half, first, turned(second)))
            else:
                groups.append(jnp.where(low_half, turned(first), second))
    return jnp.concatenate(groups, axis=1)


def normalised(values):
    average = jnp.mean(values, axis=-1, keepdims=True)
    centered = values - average
    scale = lax.rsqrt(jnp.mean(centered * centered, axis=-1, keepdims=True) + EPSILON)
    return centered * scale, scale


def normalised_back(grad, normed, scale):
    average = jnp.mean(grad, axis=-1, keepdims=True)
    along = jnp.mean(grad * normed, axis=-1, keepdims=True)
    return (grad - average - normed * along) * scale


def vmem():
    return pl.BlockSpec(memory_space=pltpu.VMEM)


def in_hbm():
    return pl.BlockSpec(memory_space=pl.ANY)


def cost(flops, link_bytes):
    return pl.CostEstimate(flops=int(flops), bytes_accessed=int(link_bytes) * 16, transcendentals=0)


def linked(collective):
    return pltpu.CompilerParams(
        collective_id=collective, has_side_effects=True, vmem_limit_bytes=VMEM_BYTES
    )


class PlaneSwap:
    def __init__(self, weights, targets, keeps, sends, receives):
        self.weights, self.targets = weights, targets
        self.keeps, self.sends, self.receives = keeps, sends, receives
        self.peers = lax.axis_size("seq")

    def part(self, number, peer):
        weight, (target, start) = self.weights[number], self.targets[number]
        size = weight.shape[1] // self.peers
        return weight.at[:, pl.ds(pl.multiple_of(peer * size, LANES), size)]

    def place(self, number, peer):
        weight, (target, start) = self.weights[number], self.targets[number]
        return target.at[peer, :, pl.ds(start, weight.shape[1] // self.peers)]

    def copy(self, number, turn):
        me = lax.axis_index("seq")
        peer = lax.rem(me + turn, self.peers)
        return to_peer(
            self.part(number, peer),
            self.place(number, me),
            self.sends.at[number, turn],
            self.receives.at[number, turn],
            peer,
        )

    def landed(self, number, turn):
        me = lax.axis_index("seq")
        peer = lax.rem(me + self.peers - turn, self.peers)
        target = self.place(number, peer)
        to_peer(
            target, target, self.sends.at[number, turn], self.receives.at[number, turn], peer
        ).wait_recv()

    def kept(self, number):
        me = lax.axis_index("seq")
        return pltpu.make_async_copy(
            self.part(number, me), self.place(number, me), self.keeps.at[number]
        )

    def begin(self):
        for number in range(len(self.weights)):
            for turn in range(1, self.peers):
                self.copy(number, turn).start()
            self.kept(number).start()

    def finish(self):
        for number in range(len(self.weights)):
            for turn in range(1, self.peers):
                self.landed(number, turn)
                self.copy(number, turn).wait_send()
            self.kept(number).wait()


def swap_scratch(count, peers):
    return [
        pltpu.SemaphoreType.DMA((count,)),
        pltpu.SemaphoreType.DMA((count, peers)),
        pltpu.SemaphoreType.DMA((count, peers)),
    ]


def greet_plane(with_groups):
    me, group = lax.axis_index("seq"), lax.axis_index("fsdp")
    peers, groups = lax.axis_size("seq"), lax.axis_size("fsdp")
    barrier = pltpu.get_barrier_semaphore()
    count = peers - 1
    for turn in range(1, peers):
        peer = lax.rem(me + turn, peers)
        pl.semaphore_signal(barrier, inc=1, device_id={"seq": peer}, device_id_type=MESH)
    if with_groups:
        count += groups - 1
        for turn in range(1, groups):
            peer = lax.rem(group + turn, groups)
            pl.semaphore_signal(barrier, inc=1, device_id={"fsdp": peer}, device_id_type=MESH)
    pl.semaphore_wait(barrier, count)


def all_to_each(source, out, axis, size, keep, sends, receives):
    me = lax.axis_index(axis)

    def copy(turn, slot):
        peer = lax.rem(me + turn, size)
        return pltpu.make_async_remote_copy(
            src_ref=source,
            dst_ref=out.at[slot],
            send_sem=sends.at[turn],
            recv_sem=receives.at[turn],
            device_id={axis: peer},
            device_id_type=MESH,
        )

    def begin():
        pltpu.make_async_copy(source, out.at[me], keep).start()
        for turn in range(1, size):
            copy(turn, me).start()

    def finish():
        for turn in range(1, size):
            copy(turn, lax.rem(me + size - turn, size)).wait_recv()
            copy(turn, me).wait_send()
        pltpu.make_async_copy(source, out.at[me], keep).wait()

    return begin, finish


def first_swap_kernel(
    query_ref, key_ref, value_ref, swish_ref, rates_ref, gains_ref,
    cut_out, rates_out, gains_out,
    column, keeps, sends, receives, rate_keep, rate_sends, rate_receives,
    group_keep, group_sends, group_receives, gain_keep, gain_sends, gain_receives,
):
    peers, groups = lax.axis_size("seq"), lax.axis_size("fsdp")
    size, wide = query_ref.shape[1] // peers, value_ref.shape[1] // peers
    greet_plane(True)
    begin_groups, finish_groups = all_to_each(
        gains_ref, column, "fsdp", groups, group_keep, group_sends, group_receives
    )
    begin_rates, finish_rates = all_to_each(
        rates_ref, rates_out, "seq", peers, rate_keep, rate_sends, rate_receives
    )
    begin_gains, finish_gains = all_to_each(
        column, gains_out, "seq", peers, gain_keep, gain_sends, gain_receives
    )
    swap = PlaneSwap(
        (query_ref, key_ref, value_ref, swish_ref),
        ((cut_out, 0), (cut_out, size), (cut_out, 2 * size), (cut_out, 2 * size + wide)),
        keeps,
        sends,
        receives,
    )
    begin_groups()
    begin_rates()
    finish_groups()
    begin_gains()
    swap.begin()
    finish_rates()
    finish_gains()
    swap.finish()


def first_swap(query, key, value, swish, rates, gains):
    peers, groups = lax.axis_size("seq"), lax.axis_size("fsdp")
    slab = query.shape[0]
    total = sum(weight.shape[1] for weight in (query, key, value, swish)) // peers
    return pl.pallas_call(
        first_swap_kernel,
        in_specs=[in_hbm()] * 4 + [vmem()] * 2,
        out_specs=[in_hbm()] + [vmem()] * 2,
        out_shape=[
            jax.ShapeDtypeStruct((peers, slab, total), HALF),
            jax.ShapeDtypeStruct((peers,) + rates.shape, FULL),
            jax.ShapeDtypeStruct((peers, groups) + gains.shape, FULL),
        ],
        scratch_shapes=[pltpu.VMEM((groups,) + gains.shape, FULL)]
        + swap_scratch(4, peers)
        + [pltpu.SemaphoreType.DMA] + [pltpu.SemaphoreType.DMA((peers,))] * 2
        + [pltpu.SemaphoreType.DMA] + [pltpu.SemaphoreType.DMA((groups,))] * 2
        + [pltpu.SemaphoreType.DMA] + [pltpu.SemaphoreType.DMA((peers,))] * 2,
        compiler_params=linked(0),
        cost_estimate=cost(0, 2 * slab * peers * total),
    )(query, key, value, swish, rates, gains)


def inputs_kernel(
    tokens_ref, grad_ref, mask_ref, gain_ref, gate_ref, up_ref,
    entered_out, grads_out, feed_out,
    own_entered, own_grad, keep_one, sends_one, receives_one, keep_two, sends_two, receives_two,
    keeps, sends, receives,
):
    peers, groups = lax.axis_size("seq"), lax.axis_size("fsdp")
    greet_plane(False)
    size = gate_ref.shape[1] // peers
    gain = gain_ref[...]

    def work(rows):
        normed, _ = normalised(tokens_ref[rows].astype(FULL))
        own_entered[rows] = regroup(normed * gain, peers, groups).astype(HALF)
        own_grad[rows] = (grad_ref[rows].astype(FULL) * mask_ref[rows]).astype(HALF)

    by_chunks(tokens_ref.shape[0], work)
    one = PlaneGather(own_entered, entered_out, keep_one, sends_one, receives_one)
    two = PlaneGather(own_grad, grads_out, keep_two, sends_two, receives_two)
    swap = PlaneSwap((gate_ref, up_ref), ((feed_out, 0), (feed_out, size)), keeps, sends, receives)
    one.begin()
    one.relay()
    swap.begin()
    two.begin()
    one.finish()
    two.relay()
    swap.finish()
    two.finish()


def gather_inputs(tokens, grad, mask, gain, gate, up):
    peers = lax.axis_size("seq")
    own, width = tokens.shape
    slab, columns = gate.shape
    part = columns // peers
    return pl.pallas_call(
        inputs_kernel,
        in_specs=[vmem()] * 4 + [in_hbm()] * 2,
        out_specs=[in_hbm()] * 3,
        out_shape=[
            jax.ShapeDtypeStruct((peers, own, width), HALF),
            jax.ShapeDtypeStruct((peers, own, width), HALF),
            jax.ShapeDtypeStruct((peers, slab, 2 * part), HALF),
        ],
        scratch_shapes=[pltpu.VMEM((own, width), HALF)] * 2
        + gather_scratch()
        + gather_scratch()
        + swap_scratch(2, peers),
        compiler_params=linked(1),
        cost_estimate=cost(0, 2 * peers * (2 * own * width + slab * 2 * part)),
    )(tokens, grad, mask, gain, gate, up)


def feed_kernel(rows_ref, weight_ref, inner_ref, up_slope_ref, gate_slope_ref):
    both = dot_nn(rows_ref[...], weight_ref[...])
    part = both.shape[1] // 2
    gate, upward = both[:, :part], both[:, part:]
    inside = 0.7978845608028654 * (gate + 0.044715 * (gate * gate * gate))
    bend = jnp.tanh(inside)
    share = 0.5 * (1.0 + bend)
    value = gate * share
    steep = 0.7978845608028654 * (1.0 + 3.0 * 0.044715 * (gate * gate))
    slope = share + 0.5 * gate * (1.0 - bend * bend) * steep
    inner_ref[...] = (value * upward).astype(HALF)
    up_slope_ref[...] = value.astype(HALF)
    gate_slope_ref[...] = (upward * slope).astype(HALF)


def feed(rows, weight):
    count, width = rows.shape
    columns = weight.shape[1]
    tile = 256
    out = pl.BlockSpec((tile, columns // 2), lambda i: (i, 0))
    return pl.pallas_call(
        feed_kernel,
        grid=(count // tile,),
        in_specs=[
            pl.BlockSpec((tile, width), lambda i: (i, 0)),
            pl.BlockSpec((width, columns), lambda i: (0, 0), pipeline_mode=pl.Buffered(1)),
        ],
        out_specs=[out] * 3,
        out_shape=[jax.ShapeDtypeStruct((count, columns // 2), HALF)] * 3,
        compiler_params=pltpu.CompilerParams(
            dimension_semantics=("arbitrary",), vmem_limit_bytes=VMEM_BYTES
        ),
        cost_estimate=pl.CostEstimate(
            flops=2 * count * width * columns,
            bytes_accessed=2 * (count * width + width * columns + 2 * count * columns),
            transcendentals=0,
        ),
    )(rows, weight)


def feed_back_kernel(rows_ref, weight_ref, up_slope_ref, gate_slope_ref, grad_ref):
    inner_grad = dot_nt(rows_ref[...], weight_ref[...])
    part = inner_grad.shape[1]
    grad_ref[:, :part] = (inner_grad * gate_slope_ref[...].astype(FULL)).astype(HALF)
    grad_ref[:, part:] = (inner_grad * up_slope_ref[...].astype(FULL)).astype(HALF)


def feed_back(rows, weight, up_slope, gate_slope):
    count, width = rows.shape
    part = weight.shape[0]
    tile = 512
    slope = pl.BlockSpec((tile, part), lambda i: (i, 0))
    return pl.pallas_call(
        feed_back_kernel,
        grid=(count // tile,),
        in_specs=[
            pl.BlockSpec((tile, width), lambda i: (i, 0)),
            pl.BlockSpec((part, width), lambda i: (0, 0), pipeline_mode=pl.Buffered(1)),
            slope,
            slope,
        ],
        out_specs=pl.BlockSpec((tile, 2 * part), lambda i: (i, 0)),
        out_shape=jax.ShapeDtypeStruct((count, 2 * part), HALF),
        compiler_params=pltpu.CompilerParams(
            dimension_semantics=("arbitrary",), vmem_limit_bytes=VMEM_BYTES
        ),
        cost_estimate=pl.CostEstimate(
            flops=2 * count * width * part,
            bytes_accessed=2 * (count * width + width * part + 4 * count * part),
            transcendentals=0,
        ),
    )(rows, weight, up_slope, gate_slope)


def retention_kernel(
    place_ref, live_ref, first_ref, second_ref, weight_ref, decay_ref, column_ref, gain_ref,
    qkv_ref, swish_ref, normed_ref, scale_ref, entry_ref, mixed_hbm, state, mixed_buffer, sems,
):
    step, steps = pl.program_id(0), pl.num_programs(0)
    rows = first_ref.shape[2]
    batches, key_size, value_size = state.shape
    total = 2 * key_size + value_size
    slot = lax.rem(step, 2)

    def sent(at, which, batch):
        return pltpu.make_async_copy(
            mixed_buffer.at[which, batch],
            mixed_hbm.at[place_ref[batch, at], batch],
            sems.at[which, batch],
        )

    @pl.when(step == 0)
    def _():
        state[...] = jnp.zeros_like(state)

    @pl.when(step >= 2)
    def _():
        for batch in range(batches):
            sent(step - 2, slot, batch).wait()

    rows_in = jnp.concatenate([first_ref[0, 0], second_ref[0, 0]], axis=0)
    projected = dot_nn(rows_in, weight_ref[...])
    decay = decay_ref[0]
    entry_decay = column_ref[0, :, 0:1]
    end_weight = column_ref[0, :, 1:2]
    block_decay = column_ref[0, rows - 1 : rows, 0:1]
    positions = step * rows + lax.broadcasted_iota(jnp.int32, (rows, 1), 0)
    for batch in range(batches):
        mine = slice(batch * rows, (batch + 1) * rows)
        live = (positions < live_ref[batch]).astype(FULL)
        query = projected[mine, :key_size].astype(HALF)
        key = (projected[mine, key_size : 2 * key_size] * live).astype(HALF)
        value = projected[mine, 2 * key_size : total].astype(HALF)
        swish = projected[mine, total:]
        before = state[batch]
        before_low = before.astype(HALF)
        weights = (dot_nt(query, key) * decay).astype(HALF)
        retained = dot_nn(weights, value) + entry_decay * dot_nn(query, before_low)
        key_ended = (key.astype(FULL) * end_weight).astype(HALF)
        state[batch] = block_decay * before + dot_tn(key_ended, value)
        normed, scale = normalised(retained)
        qkv_ref[batch, 0, :, :key_size] = query
        qkv_ref[batch, 0, :, key_size : 2 * key_size] = key
        qkv_ref[batch, 0, :, 2 * key_size :] = value
        scale_ref[batch, 0] = jnp.broadcast_to(scale, scale_ref.shape[2:])
        entry_ref[batch, 0] = before_low
        swish_ref[batch, 0] = swish.astype(HALF)
        normed_ref[batch, 0] = normed.astype(HALF)
        mixed = swish * jax.nn.sigmoid(swish) * (normed * gain_ref[...])
        mixed_buffer[slot, batch] = mixed.astype(HALF)
        sent(step, slot, batch).start()

    @pl.when(step == steps - 1)
    def _():
        for batch in range(batches):
            sent(step, slot, batch).wait()
            sent(step - 1, 1 - slot, batch).wait()


def retention(rows_in, weight, place, live, decay, columns, gain, key_size):
    blocks, batches, rows, width = rows_in.shape
    value_size = gain.shape[-1]
    total = 2 * key_size + value_size

    def arriving(batch):
        return pl.BlockSpec(
            (1, 1, rows, width), lambda i, place, live: (place[batch, i], batch, 0, 0)
        )

    def whole(shape):
        return pl.BlockSpec(
            shape, lambda i, place, live: (0,) * len(shape), pipeline_mode=pl.Buffered(1)
        )

    def here(*tail):
        return pl.BlockSpec((batches, 1) + tail, lambda i, place, live: (0, i, 0, 0))

    def along(*tail):
        return pl.BlockSpec((1,) + tail, lambda i, place, live: (i, 0, 0))

    return pl.pallas_call(
        retention_kernel,
        grid_spec=pltpu.PrefetchScalarGridSpec(
            num_scalar_prefetch=2,
            grid=(blocks,),
            in_specs=[
                arriving(0),
                arriving(1),
                whole((width, total + value_size)),
                along(rows, rows),
                along(rows, 2),
                whole((1, value_size)),
            ],
            out_specs=[
                here(rows, total),
                here(rows, value_size),
                here(rows, value_size),
                here(rows, LANES),
                here(key_size, value_size),
                in_hbm(),
            ],
            scratch_shapes=[
                pltpu.VMEM((batches, key_size, value_size), FULL),
                pltpu.VMEM((2, batches, rows, value_size), HALF),
                pltpu.SemaphoreType.DMA((2, batches)),
            ],
        ),
        out_shape=[
            jax.ShapeDtypeStruct((batches, blocks, rows, total), HALF),
            jax.ShapeDtypeStruct((batches, blocks, rows, value_size), HALF),
            jax.ShapeDtypeStruct((batches, blocks, rows, value_size), HALF),
            jax.ShapeDtypeStruct((batches, blocks, rows, LANES), FULL),
            jax.ShapeDtypeStruct((batches, blocks, key_size, value_size), HALF),
            jax.ShapeDtypeStruct((blocks, batches, rows, value_size), HALF),
        ],
        compiler_params=pltpu.CompilerParams(
            dimension_semantics=("arbitrary",), vmem_limit_bytes=VMEM_BYTES
        ),
        cost_estimate=pl.CostEstimate(
            flops=3 * blocks * batches * rows * width * total,
            bytes_accessed=2 * blocks * batches * rows * (width + 2 * total) + 4 * width * total,
            transcendentals=0,
        ),
    )(place, live, rows_in, rows_in, weight, decay, columns, gain)


def retention_back_kernel(
    place_ref, live_ref, first_ref, second_ref,
    weight_ref, decay_ref, column_ref, gain_ref, qkv_ref, swish_ref, normed_ref, scale_ref, entry_ref,
    gain_grad_ref, grads_hbm, state, grads_buffer, sems,
):
    step, steps = pl.program_id(0), pl.num_programs(0)
    rows = first_ref.shape[2]
    batches, key_size, value_size = state.shape
    slot = lax.rem(step, 2)

    def sent(at, which, batch):
        return pltpu.make_async_copy(
            grads_buffer.at[which, batch],
            grads_hbm.at[place_ref[batch, steps - 1 - at], batch],
            sems.at[which, batch],
        )

    @pl.when(step == 0)
    def _():
        state[...] = jnp.zeros_like(state)
        gain_grad_ref[...] = jnp.zeros_like(gain_grad_ref)

    @pl.when(step >= 2)
    def _():
        for batch in range(batches):
            sent(step - 2, slot, batch).wait()

    rows_in = jnp.concatenate([first_ref[0, 0], second_ref[0, 0]], axis=0)
    mixed_grads = dot_nt(rows_in, weight_ref[...])
    decay = decay_ref[0]
    entry_decay = column_ref[0, :, 0:1]
    end_weight = column_ref[0, :, 1:2]
    block_decay = column_ref[0, rows - 1 : rows, 0:1]
    positions = (steps - 1 - step) * rows + lax.broadcasted_iota(jnp.int32, (rows, 1), 0)
    gain = gain_ref[...]
    for batch in range(batches):
        live = (positions < live_ref[batch]).astype(FULL)
        mixed_grad = mixed_grads[batch * rows : (batch + 1) * rows]
        query = qkv_ref[batch, 0, :, :key_size]
        key = qkv_ref[batch, 0, :, key_size : 2 * key_size]
        value = qkv_ref[batch, 0, :, 2 * key_size :]
        swish = swish_ref[batch, 0].astype(FULL)
        normed = normed_ref[batch, 0].astype(FULL)
        scale = scale_ref[batch, 0, :, 0:1]
        entry = entry_ref[batch, 0]
        sigmoid = jax.nn.sigmoid(swish)
        silu = swish * sigmoid
        swish_grad = mixed_grad * (normed * gain) * (sigmoid * (1.0 + swish - silu))
        scaled_grad = mixed_grad * silu
        gain_grad_ref[...] += jnp.sum(scaled_grad * normed, axis=0, keepdims=True)
        retained_grad = normalised_back(scaled_grad * gain, normed, scale).astype(HALF)
        weights = (dot_nt(query, key) * decay).astype(HALF)
        scores_grad = (dot_nt(retained_grad, value) * decay).astype(HALF)
        after = state[batch]
        after_low = after.astype(HALF)
        query_grad = dot_nn(scores_grad, key) + entry_decay * dot_nt(retained_grad, entry)
        key_grad = dot_tn(scores_grad, query) + end_weight * dot_nt(value, after_low)
        value_grad = dot_tn(weights, retained_grad) + end_weight * dot_nn(key, after_low)
        query_entered = (query.astype(FULL) * entry_decay).astype(HALF)
        state[batch] = block_decay * after + dot_tn(query_entered, retained_grad)
        grads_buffer[slot, batch, :, :key_size] = query_grad.astype(HALF)
        grads_buffer[slot, batch, :, key_size : 2 * key_size] = (key_grad * live).astype(HALF)
        grads_buffer[slot, batch, :, 2 * key_size : 2 * key_size + value_size] = value_grad.astype(
            HALF
        )
        grads_buffer[slot, batch, :, 2 * key_size + value_size :] = swish_grad.astype(HALF)
        sent(step, slot, batch).start()

    @pl.when(step == steps - 1)
    def _():
        for batch in range(batches):
            sent(step, slot, batch).wait()
            sent(step - 1, 1 - slot, batch).wait()


def retention_back(rows_in, weight, place, live, decay, columns, gain, saved):
    blocks, batches, rows, width = rows_in.shape
    value_size = gain.shape[-1]
    key_size = saved[-1].shape[2]
    total = 2 * key_size + 2 * value_size

    def arriving(batch, size):
        return pl.BlockSpec(
            (1, 1, rows, size),
            lambda i, place, live: (place[batch, blocks - 1 - i], batch, 0, 0),
        )

    def whole(shape):
        return pl.BlockSpec(
            shape, lambda i, place, live: (0,) * len(shape), pipeline_mode=pl.Buffered(1)
        )

    def here(*tail):
        return pl.BlockSpec((batches, 1) + tail, lambda i, place, live: (0, blocks - 1 - i, 0, 0))

    def along(*tail):
        return pl.BlockSpec((1,) + tail, lambda i, place, live: (blocks - 1 - i, 0, 0))

    return pl.pallas_call(
        retention_back_kernel,
        grid_spec=pltpu.PrefetchScalarGridSpec(
            num_scalar_prefetch=2,
            grid=(blocks,),
            in_specs=[
                arriving(0, width),
                arriving(1, width),
                whole((value_size, width)),
                along(rows, rows),
                along(rows, 2),
                whole((1, value_size)),
                here(rows, 2 * key_size + value_size),
                here(rows, value_size),
                here(rows, value_size),
                here(rows, LANES),
                here(key_size, value_size),
            ],
            out_specs=[
                pl.BlockSpec((1, value_size), lambda i, place, live: (0, 0)),
                in_hbm(),
            ],
            scratch_shapes=[
                pltpu.VMEM((batches, key_size, value_size), FULL),
                pltpu.VMEM((2, batches, rows, total), HALF),
                pltpu.SemaphoreType.DMA((2, batches)),
            ],
        ),
        out_shape=[
            jax.ShapeDtypeStruct((1, value_size), FULL),
            jax.ShapeDtypeStruct((blocks, batches, rows, total), HALF),
        ],
        compiler_params=pltpu.CompilerParams(
            dimension_semantics=("arbitrary",), vmem_limit_bytes=VMEM_BYTES
        ),
        cost_estimate=pl.CostEstimate(
            flops=6 * blocks * batches * rows * width * value_size,
            bytes_accessed=2 * blocks * batches * rows * (width + 2 * total)
            + 2 * width * value_size,
            transcendentals=0,
        ),
    )(place, live, rows_in, rows_in, weight, decay, columns, gain, *saved)


def middle_kernel(
    mixed_ref, weight_ref, tokens_ref, gain_ref, hidden_ref, second_out,
    *scratch,
):
    scatter = scratch[:7]
    own, keeps, gather_sends, gather_receives = scratch[7:]
    peers, groups = lax.axis_size("seq"), lax.axis_size("fsdp")
    greet_neighbours()

    def term(block):
        return dot_nn(mixed_ref[block], weight_ref[...]).astype(HALF)

    gain = gain_ref[...]

    def use(start, total):
        rows = pl.ds(start, CHUNK)
        hidden = tokens_ref[rows].astype(FULL) + total
        hidden_ref[rows] = hidden
        normed, _ = normalised(hidden)
        own[rows] = regroup(normed * gain, peers, groups).astype(HALF)

    gathers = [
        PlaneGather(own, second_out, keeps, gather_sends, gather_receives, window, WINDOWS)
        for window in range(WINDOWS)
    ]
    windows = scatter_head(term, scatter)
    scatter_tail(windows, use, lambda window: gathers[window].begin())
    for gather in gathers:
        gather.relay()
    for gather in gathers:
        gather.finish()
    for window in windows:
        window.drain()


def middle(mixed, weight, tokens, gain):
    peers, own, inner = mixed.shape
    width = weight.shape[1]
    return pl.pallas_call(
        middle_kernel,
        in_specs=[vmem()] * 4,
        out_specs=[vmem(), in_hbm()],
        out_shape=[
            jax.ShapeDtypeStruct((own, width), FULL),
            jax.ShapeDtypeStruct((peers, own, width), HALF),
        ],
        scratch_shapes=scatter_scratch(own, width)
        + [pltpu.VMEM((own, width), HALF)]
        + gather_scratch(WINDOWS),
        compiler_params=linked(2),
        cost_estimate=cost(2 * peers * own * inner * width, 4 * peers * own * width),
    )(mixed, weight, tokens, gain)


def middle_back_kernel(
    grads_ref, weight_ref, hidden_ref, outer_ref, mask_ref, gain_ref,
    hidden_grad_ref, gain_grad_ref, branch_out,
    *scratch,
):
    scatter = scratch[:7]
    own, keeps, gather_sends, gather_receives = scratch[7:]
    peers, groups = lax.axis_size("seq"), lax.axis_size("fsdp")
    greet_neighbours()

    def term(block):
        return dot_nt(grads_ref[block], weight_ref[...]).astype(HALF)

    gain = gain_ref[...]
    gain_grad_ref[...] = jnp.zeros_like(gain_grad_ref)

    def use(start, total):
        rows = pl.ds(start, CHUNK)
        grad = regroup(total, groups, peers)
        normed, scale = normalised(hidden_ref[rows])
        gain_grad_ref[...] += jnp.sum(grad * normed, axis=0, keepdims=True)
        outer = outer_ref[rows].astype(FULL) * mask_ref[rows]
        hidden_grad = outer + normalised_back(grad * gain, normed, scale)
        hidden_grad_ref[rows] = hidden_grad
        own[rows] = hidden_grad.astype(HALF)

    gathers = [
        PlaneGather(own, branch_out, keeps, gather_sends, gather_receives, window, WINDOWS)
        for window in range(WINDOWS)
    ]
    windows = scatter_head(term, scatter)
    scatter_tail(windows, use, lambda window: gathers[window].begin())
    for gather in gathers:
        gather.relay()
    for gather in gathers:
        gather.finish()
    for window in windows:
        window.drain()


def middle_back(grads, weight, hidden, outer, mask, gain):
    peers, own, inner = grads.shape
    width = weight.shape[0]
    return pl.pallas_call(
        middle_back_kernel,
        in_specs=[vmem()] * 6,
        out_specs=[vmem(), vmem(), in_hbm()],
        out_shape=[
            jax.ShapeDtypeStruct((own, width), FULL),
            jax.ShapeDtypeStruct((1, width), FULL),
            jax.ShapeDtypeStruct((peers, own, width), HALF),
        ],
        scratch_shapes=scatter_scratch(own, width)
        + [pltpu.VMEM((own, width), HALF)]
        + gather_scratch(WINDOWS),
        compiler_params=linked(3),
        cost_estimate=cost(2 * peers * own * inner * width, 4 * peers * own * width),
    )(grads, weight, hidden, outer, mask, gain)


class PlaneReturn:
    def __init__(self, cuts, source, targets, keeps, sends, receives):
        self.cuts, self.source, self.targets = cuts, source, targets
        self.keeps, self.sends, self.receives = keeps, sends, receives
        self.peers, self.me = lax.axis_size("seq"), lax.axis_index("seq")

    def part(self, number, peer):
        start, size = self.cuts[number]
        return self.source.at[peer, :, pl.ds(start, size)]

    def place(self, number, peer):
        size = self.cuts[number][1]
        return self.targets[number].at[:, pl.ds(pl.multiple_of(peer * size, LANES), size)]

    def sent(self, source, target, number, turn, peer):
        at = (number, turn)
        return to_peer(source, target, self.sends.at[at], self.receives.at[at], peer)

    def copy(self, number, turn):
        peer = lax.rem(self.me + turn, self.peers)
        return self.sent(
            self.part(number, peer), self.place(number, self.me), number, turn, peer
        )

    def landed(self, number, turn):
        peer = lax.rem(self.me + self.peers - turn, self.peers)
        target = self.place(number, peer)
        return self.sent(target, target, number, turn, peer)

    def kept(self, number):
        return pltpu.make_async_copy(
            self.part(number, self.me), self.place(number, self.me), self.keeps.at[number]
        )

    def begin(self, turn):
        for number in range(len(self.cuts)):
            if turn > 0:
                self.copy(number, turn).start()
            else:
                self.kept(number).start()

    def finish(self):
        for number in range(len(self.cuts)):
            for turn in range(1, self.peers):
                self.landed(number, turn).wait_recv()
                self.copy(number, turn).wait_send()
            self.kept(number).wait()


class LineSum:
    def __init__(self, terms, landed, own, final, loads, sends, receives):
        self.terms, self.landed, self.own, self.final = terms, landed, own, final
        self.loads, self.sends, self.receives = loads, sends, receives
        self.me, self.last = lax.axis_index("fsdp"), lax.axis_size("fsdp") - 1
        self.peers, self.place = lax.axis_size("seq"), lax.axis_index("seq")

    def piece(self, turn):
        return lax.rem(self.place + turn, self.peers)

    def depth(self, way):
        return self.me if way == 0 else self.last - self.me

    def block(self, way, order):
        return self.last - order if way == 0 else order

    def slot(self, way, order):
        return order if way == 0 else 2 * self.last - 2 - order

    def sent(self, source, way, order, turn):
        at = (way, order, turn)
        return pltpu.make_async_remote_copy(
            src_ref=source,
            dst_ref=self.landed.at[self.slot(way, order), self.piece(turn)],
            send_sem=self.sends.at[at],
            recv_sem=self.receives.at[at],
            device_id={"fsdp": self.me + 1 if way == 0 else self.me - 1},
            device_id_type=MESH,
        )

    def first(self, way, order, turn):
        source = self.terms.at[self.block(way, order), self.piece(turn)]
        return self.sent(source, way, order, turn)

    def onward(self, way, order, turn):
        source = self.landed.at[self.slot(way, order), self.piece(turn)]
        return self.sent(source, way, order, turn)

    def load(self, way, order):
        return pltpu.make_async_copy(
            self.terms.at[self.block(way, order)], self.own.at[way], self.loads.at[way]
        )

    def load_final(self):
        return pltpu.make_async_copy(self.terms.at[self.me], self.final, self.loads.at[2])

    def begin(self):
        for way in (0, 1):

            @pl.when(self.depth(way) == 0)
            def _():
                for order in range(self.last):
                    for turn in range(self.peers):
                        self.first(way, order, turn).start()

            self.load(way, 0).start()
        self.load_final().start()

    def loaded(self, order):
        for way in (0, 1):
            self.load(way, order).wait()

    def load_next(self, order):
        for way in (0, 1):
            self.load(way, order).start()

    def hand_on(self, order, depth, turns):
        for turn in turns:
            for way in (0, 1):

                @pl.when(self.depth(way) == depth)
                def _():
                    at, piece = self.slot(way, order), self.piece(turn)
                    self.onward(way, order, turn).wait_recv()
                    self.landed[at, piece] = (
                        self.landed[at, piece].astype(FULL) + self.own[way, piece].astype(FULL)
                    ).astype(HALF)
                    self.onward(way, order, turn).start()

    def finish(self, use):
        self.load_final().wait()
        for turn in range(self.peers):
            piece = self.piece(turn)
            for way in (0, 1):

                @pl.when(self.depth(way) > 0)
                def _():
                    order = self.last - self.depth(way)
                    self.onward(way, order, turn).wait_recv()
                    self.final[piece] = (
                        self.final[piece].astype(FULL)
                        + self.landed[self.slot(way, order), piece].astype(FULL)
                    ).astype(HALF)

            use(turn)

    def drain(self):
        for way in (0, 1):
            for order in range(self.last):
                for turn in range(self.peers):

                    @pl.when(self.depth(way) == 0)
                    def _():
                        self.first(way, order, turn).wait_send()

                    @pl.when((self.depth(way) > 0) & (self.depth(way) < self.last - order))
                    def _():
                        self.onward(way, order, turn).wait_send()


def line_scratch(groups, peers, slab, columns):
    block = (peers, slab, columns)
    return [
        pltpu.VMEM((2 * groups - 3,) + block, HALF),
        pltpu.VMEM((2,) + block, HALF),
        pltpu.VMEM(block, HALF),
        pltpu.SemaphoreType.DMA((3,)),
        pltpu.SemaphoreType.DMA((2, groups - 1, peers)),
        pltpu.SemaphoreType.DMA((2, groups - 1, peers)),
    ]


def last_kernel(
    cuts, line_cuts, grads_hbm, weight_ref, tokens_ref, hidden_grad_ref, gain_ref, second_grad_ref,
    group_grad_ref, inner_ref, down_ref, hidden_ref, mask_ref, summed_ref, terms_ref,
    *refs,
):
    count, line_count = len(cuts), len(line_cuts)
    input_ref, output_ref, gains_ref, group_ref = refs[:4]
    returned, refs = refs[4 : 4 + count], refs[4 + count :]
    line_returned, scratch = refs[:line_count], refs[line_count:]
    scatter, result = scratch[:7], scratch[:1] + scratch[7:13]
    (
        sums, parts, across, totals, first_grad, keep, part_sends, part_receives,
        group_keep, group_sends, group_receives,
    ) = scratch[13:24]
    peers, groups = lax.axis_size("seq"), lax.axis_size("fsdp")
    me = lax.axis_index("seq")
    greet_plane(True)
    back = PlaneReturn(cuts, summed_ref, returned, *scratch[24:27])
    line_back = PlaneReturn(line_cuts, scratch[32], line_returned, *scratch[27:30])
    line = LineSum(terms_ref, *scratch[30:36])
    grads, grad_loads = scratch[36:]
    blocks = block_order_of_plane()

    def load(number):
        return pltpu.make_async_copy(
            grads_hbm.at[blocks[number]], grads.at[number % 2], grad_loads.at[number % 2]
        )

    taken = []

    def term(block):
        number = len(taken)
        taken.append(block)
        load(number).wait()
        if number + 1 < len(blocks):
            load(number + 1).start()
        return dot_nt(grads[number % 2], weight_ref[...]).astype(HALF)

    def result_term(block):
        return dot_nn(inner_ref[block], down_ref[...]).astype(HALF)

    gain = gain_ref[...]
    first_grad[...] = jnp.zeros_like(first_grad)

    def use(start, total):
        rows = pl.ds(start, CHUNK)
        grad = regroup(total, groups, peers)
        normed, scale = normalised(tokens_ref[rows].astype(FULL))
        first_grad[...] += jnp.sum(grad * normed, axis=0, keepdims=True)
        input_ref[rows] = (
            hidden_grad_ref[rows] + normalised_back(grad * gain, normed, scale)
        ).astype(HALF)

    def use_result(start, total):
        rows = pl.ds(start, CHUNK)
        output_ref[rows] = ((hidden_ref[rows] + total) * mask_ref[rows]).astype(HALF)

    load(0).start()
    line.begin()
    every, early, late = range(peers), range(peers // 2), range(peers // 2, peers)
    windows = scatter_head(term, scatter, (), True)
    windows[0].relay()
    line.loaded(0)
    line.hand_on(0, 1, every)
    windows[1].relay()
    result_windows = scatter_head(result_term, result, windows, True)
    for turn in every:
        back.begin(turn)
    result_windows[0].relay()
    line.hand_on(0, 2, every)
    line.load_next(1)
    scatter_tail(windows, use)
    line.loaded(1)
    line.hand_on(1, 1, early)
    result_windows[1].relay()
    tile = LANES * 2
    for peer in range(peers):
        for row in range(tile // LANES):
            at = peer * tile + row * LANES
            sums[peer, row : row + 1] = first_grad[:, at : at + LANES]
            sums[peer, 2 + row : 3 + row] = second_grad_ref[:, at : at + LANES]
        sums[peer, 4:8] = jnp.zeros((4, LANES), FULL)

    def copy(turn):
        peer = lax.rem(me + turn, peers)
        return to_peer(
            sums.at[peer], parts.at[turn], part_sends.at[turn], part_receives.at[turn], peer
        )

    kept = pltpu.make_async_copy(sums.at[me], parts.at[0], keep)
    kept.start()
    for turn in range(1, peers):
        copy(turn).start()
    line.hand_on(1, 1, late)
    scatter_tail(result_windows, use_result)
    kept.wait()
    for turn in range(1, peers):
        copy(turn).wait_recv()
        copy(turn).wait_send()
    total = parts[0]
    for turn in range(1, peers):
        total += parts[turn]
    across[0:8] = total
    for row in range(4):
        across[8 + row : 9 + row] = group_grad_ref[:, row * LANES : (row + 1) * LANES]
    across[12:16] = jnp.zeros((4, LANES), FULL)
    begin, finish = all_to_each(
        across, totals, "fsdp", groups, group_keep, group_sends, group_receives
    )
    begin()
    line.finish(line_back.begin)
    back.finish()
    line_back.finish()
    line.drain()
    for window in windows:
        window.drain(4)
    for window in result_windows:
        window.drain()
    finish()
    summed = totals[0]
    for turn in range(1, groups):
        summed += totals[turn]
    gains_ref[...] = summed[0:8]
    group_ref[...] = summed[8:16]


def last_rows(
    grads, weight, tokens, hidden_grad, gain, second_grad, group_grad, inner, down, hidden, mask,
    summed, sizes, terms, line_sizes,
):
    peers, own, size = grads.shape
    groups = lax.axis_size("fsdp")
    width = weight.shape[0]
    slab = summed.shape[1]

    def cuts_of(sizes):
        return tuple((sum(sizes[:number]), sizes[number]) for number in range(len(sizes)))

    return pl.pallas_call(
        partial(last_kernel, cuts_of(sizes), cuts_of(line_sizes)),
        in_specs=[in_hbm()] + [vmem()] * 10 + [in_hbm()] * 2,
        out_specs=[vmem()] * 4 + [in_hbm()] * len(sizes + line_sizes),
        out_shape=[
            jax.ShapeDtypeStruct((own, width), HALF),
            jax.ShapeDtypeStruct((own, width), HALF),
            jax.ShapeDtypeStruct((8, LANES), FULL),
            jax.ShapeDtypeStruct((8, LANES), FULL),
        ]
        + [jax.ShapeDtypeStruct((slab, peers * part), HALF) for part in sizes + line_sizes],
        scratch_shapes=scatter_scratch(own, width)
        + scatter_scratch(own, width)[1:]
        + [
            pltpu.VMEM((peers, 8, LANES), FULL),
            pltpu.VMEM((peers, 8, LANES), FULL),
            pltpu.VMEM((16, LANES), FULL),
            pltpu.VMEM((groups, 16, LANES), FULL),
            pltpu.VMEM((1, width), FULL),
            pltpu.SemaphoreType.DMA,
            pltpu.SemaphoreType.DMA((peers,)),
            pltpu.SemaphoreType.DMA((peers,)),
            pltpu.SemaphoreType.DMA,
            pltpu.SemaphoreType.DMA((groups,)),
            pltpu.SemaphoreType.DMA((groups,)),
        ]
        + swap_scratch(len(sizes), peers)
        + swap_scratch(len(line_sizes), peers)
        + line_scratch(groups, peers, slab, terms.shape[3])
        + [pltpu.VMEM((2, own, size), HALF), pltpu.SemaphoreType.DMA((2,))],
        compiler_params=pltpu.CompilerParams(
            collective_id=5, has_side_effects=True, vmem_limit_bytes=LARGE_BYTES
        ),
        cost_estimate=cost(
            2 * peers * own * (size + inner.shape[2]) * width, 5 * peers * own * width
        ),
    )(
        grads, weight, tokens, hidden_grad, gain, second_grad, group_grad, inner, down, hidden, mask,
        summed, terms,
    )


def widen_kernel(*refs):
    count = len(refs) // 2
    for source, target in zip(refs[:count], refs[count:]):
        target[...] = source[...].astype(target.dtype)


def widen(*arrays):
    return pl.pallas_call(
        widen_kernel,
        in_specs=[vmem()] * len(arrays),
        out_specs=[vmem()] * len(arrays),
        out_shape=[jax.ShapeDtypeStruct(array.shape, FULL) for array in arrays],
        compiler_params=pltpu.CompilerParams(vmem_limit_bytes=VMEM_BYTES),
    )(*arrays)


def head_body(
    tokens,
    cotangent,
    lengths,
    block_order,
    log_decay,
    first_gain,
    query_weight,
    key_weight,
    value_weight,
    swish_weight,
    output_weight,
    group_gain,
    second_gain,
    feed_gate,
    feed_up,
    feed_down,
):
    peers, groups = lax.axis_size("seq"), lax.axis_size("fsdp")
    index, group = lax.axis_index("seq"), lax.axis_index("fsdp")
    batches, rows, width = tokens.shape
    own = batches * rows
    heads = log_decay.shape[0]
    key_size = query_weight.shape[1] // heads
    value_size = value_weight.shape[1] // heads
    part = feed_gate.shape[1] // peers
    slab = query_weight.shape[0]
    total = 2 * key_size + 2 * value_size

    def over_groups(local):
        return lax.all_gather(local, "fsdp", axis=0, tiled=True)

    def sum_groups(whole):
        return lax.psum_scatter(whole.astype(HALF), "fsdp", scatter_dimension=0, tiled=True)

    def gathered(cut):
        return over_groups(cut[None]).reshape(width, cut.shape[2])

    gains = jnp.concatenate(
        [
            group_gain.astype(FULL)[None],
            jnp.concatenate([first_gain, second_gain]).astype(FULL)[None],
            jnp.zeros((6, LANES), FULL),
        ],
        axis=0,
    )
    first_cut, rates, gains = first_swap(
        query_weight, key_weight, value_weight, swish_weight, log_decay, gains
    )
    out_weight = over_groups(output_weight)
    first_weight = gathered(first_cut)
    gain_one = gains[:, :, 1, :slab].reshape(1, width)
    gain_two = gains[:, :, 1, slab:].reshape(1, width)
    gain_group = lax.dynamic_index_in_dim(gains, index, 0, keepdims=False)[:, 0].reshape(
        1, value_size
    )

    rates = lax.dynamic_index_in_dim(rates, index, 1, keepdims=False)
    cumulative = jnp.cumsum(rates, axis=1)
    slots = jnp.arange(rows)
    lower = slots[:, None] >= slots[None, :]
    spread = cumulative[:, :, None] - cumulative[:, None, :]
    decay = jnp.where(lower, jnp.exp(jnp.where(lower, spread, 0.0)), 0.0)
    columns = jnp.stack([jnp.exp(cumulative), jnp.exp(cumulative[:, -1:] - cumulative)], axis=2)

    order = lax.dynamic_slice_in_dim(block_order, group * batches, batches, 0)
    numbers = jnp.arange(peers, dtype=jnp.int32)
    place = jnp.sum(
        numbers[None, None, :] * (order[:, None, :] == numbers[None, :, None]).astype(jnp.int32),
        axis=2,
    )
    live = lax.dynamic_slice_in_dim(lengths, group * batches, batches, 0)
    held = lax.dynamic_index_in_dim(order, index, 1, keepdims=False)
    positions = held[:, None] * rows + jnp.arange(rows, dtype=jnp.int32)
    mask = (positions < live[:, None]).astype(FULL).reshape(own, 1)

    out_weight, tokens = lax.optimization_barrier((out_weight, tokens))
    token_rows = tokens.reshape(own, width)
    outer_rows = cotangent.reshape(own, width)
    entered, result_low, feed_cut = gather_inputs(
        token_rows, outer_rows, mask, gain_one, feed_gate, feed_up
    )
    feed_weight = gathered(feed_cut)
    down_weight = over_groups(feed_down)

    *saved, mixed = retention(
        entered.reshape(peers, batches, rows, width),
        first_weight,
        place,
        live,
        decay,
        columns,
        gain_group,
        key_size,
    )
    entered = entered.reshape(peers * own, width)
    mixed = mixed.reshape(peers * own, value_size)
    hidden, second = middle(mixed.reshape(peers, own, value_size), out_weight, token_rows, gain_two)
    second = second.reshape(peers * own, width)
    result_low = result_low.reshape(peers * own, width)
    inner_low, up_slope, gate_slope = feed(second, feed_weight)
    down_term, late_low = lax.optimization_barrier(
        (dot_tn(inner_low, result_low).astype(HALF), result_low)
    )
    down_grad = sum_groups(down_term)
    both_grad = feed_back(late_low, down_weight, up_slope, gate_slope)
    both_term, both_grad = lax.optimization_barrier(
        (dot_tn(second, both_grad).astype(HALF), both_grad)
    )
    both_weight_grad = sum_groups(both_term).reshape(peers, slab, 2 * part)
    hidden_grad, second_gain_grad, branch_low = middle_back(
        both_grad.reshape(peers, own, 2 * part),
        feed_weight,
        hidden,
        outer_rows,
        mask,
        gain_two,
    )
    out_term, branch_low, down_grad = lax.optimization_barrier(
        (dot_tn(mixed, branch_low.reshape(peers * own, width)).astype(HALF), branch_low, down_grad)
    )
    out_grad = sum_groups(out_term)
    branch_low, both_weight_grad = lax.optimization_barrier((branch_low, both_weight_grad))
    group_gain_grad, projected_grad = retention_back(
        branch_low.reshape(peers, batches, rows, width),
        out_weight,
        place,
        live,
        decay,
        columns,
        gain_group,
        saved,
    )
    flat_grad = projected_grad.reshape(peers * own, total)
    first_term = dot_tn(entered, flat_grad).astype(HALF)
    (
        input_rows, output_rows, gain_grads, group_grads,
        gate_back, up_back, query_back, key_back, value_back, swish_back,
    ) = last_rows(
        projected_grad.reshape(peers, own, total),
        first_weight,
        token_rows,
        hidden_grad,
        gain_one,
        second_gain_grad,
        group_gain_grad,
        inner_low.reshape(peers, own, part),
        down_weight,
        hidden,
        mask,
        both_weight_grad,
        (part, part),
        first_term.reshape(groups, peers, slab, total),
        (key_size, key_size, value_size, value_size),
    )
    out_grad, output_rows = lax.optimization_barrier((out_grad, output_rows))
    query_back, key_back, value_back, swish_back, gate_back, up_back, down_back, out_back = widen(
        query_back, key_back, value_back, swish_back, gate_back, up_back, down_grad, out_grad
    )

    def mine(summed, start):
        flat = summed[start : start + 2].reshape(groups, slab)
        return lax.dynamic_index_in_dim(flat, group, 0, keepdims=False)

    return (
        output_rows.reshape(batches, rows, width),
        input_rows.reshape(batches, rows, width),
        mine(gain_grads, 0),
        query_back,
        key_back,
        value_back,
        swish_back,
        out_back,
        lax.dynamic_index_in_dim(group_grads, group, 0, keepdims=False),
        mine(gain_grads, 2),
        gate_back,
        up_back,
        down_back,
    )


def body(*arrays):
    peers, groups = lax.axis_size("seq"), lax.axis_size("fsdp")
    fits = peers == 8 and groups == 4 and arrays[4].shape[0] == peers and arrays[0].shape[0] == 2
    if fits:
        return head_body(*arrays)
    return general_body(*arrays)


def solution(mesh):
    placed = (
        P("fsdp", "seq", None),
        P("fsdp", "seq", None),
        P(),
        P(),
        P(None, "seq"),
        P(("seq", "fsdp")),
        P(("seq", "fsdp"), None),
        P(("seq", "fsdp"), None),
        P(("seq", "fsdp"), None),
        P(("seq", "fsdp"), None),
        P(("seq", "fsdp"), None),
        P(("seq", "fsdp")),
        P(("seq", "fsdp")),
        P(("seq", "fsdp"), None),
        P(("seq", "fsdp"), None),
        P(("seq", "fsdp"), None),
    )
    return jax.shard_map(
        body,
        mesh=mesh,
        in_specs=placed,
        out_specs=(
            P("fsdp", "seq", None),
            P("fsdp", "seq", None),
            P(("seq", "fsdp")),
            P(("seq", "fsdp"), None),
            P(("seq", "fsdp"), None),
            P(("seq", "fsdp"), None),
            P(("seq", "fsdp"), None),
            P(("seq", "fsdp"), None),
            P(("seq", "fsdp")),
            P(("seq", "fsdp")),
            P(("seq", "fsdp"), None),
            P(("seq", "fsdp"), None),
            P(("seq", "fsdp"), None),
        ),
        check_vma=False,
    )
```

```python
from functools import partial, reduce

import jax
import jax.numpy as jnp
from jax import lax
from jax.experimental import pallas as pl
from jax.experimental.pallas import tpu as pltpu
from jax.sharding import PartitionSpec as P

EPSILON = 1e-05
HIGHEST = lax.Precision.HIGHEST


def carried_in(value, axis, combine, identity, reverse):
    peers, index = (lax.axis_size(axis), lax.axis_index(axis))
    everything = jax.tree.map(
        lambda part, kind: lax.all_gather(part.astype(kind), axis),
        value,
        (jnp.bfloat16, jnp.bfloat16),
    )
    start = jax.tree.map(
        lambda part, zero: jnp.broadcast_to(jnp.asarray(zero, part.dtype), part.shape),
        value,
        identity,
    )

    def turn(k, before):
        at = peers - 1 - k if reverse else k
        reached = at > index if reverse else at < index
        new = combine(
            before, jax.tree.map(lambda part, own: part[at].astype(own.dtype), everything, value)
        )
        return jax.tree.map(lambda a, b: jnp.where(reached, a, b), new, before)

    return lax.fori_loop(0, peers, turn, start)


def norm_rows(values, gain):
    average = jnp.mean(values, axis=-1, keepdims=True)
    centered = values - average
    variance = jnp.mean(centered * centered, axis=-1, keepdims=True)
    return centered * lax.rsqrt(variance + EPSILON) * gain


def gated_swish(swish_in, grouped):
    return jax.nn.silu(swish_in) * grouped


def gated_gelu(gate_in, upward):
    return jax.nn.gelu(gate_in) * upward


def chain_states(earlier, later):
    return (earlier[0] * later[0], later[0][:, None, None] * earlier[1] + later[1])


def transposed(left_rows, weight):
    return jnp.einsum("ie,fe->if", left_rows, weight, preferred_element_type=jnp.float32)


def plain_dot(left_rows, weight):
    return jnp.dot(left_rows, weight, preferred_element_type=jnp.float32)


def outer_term(left_rows, right_rows):
    return jnp.einsum("ni,no->io", left_rows, right_rows, preferred_element_type=jnp.float32)


def spread_sum(matrix_pairs, vectors):
    terms = tuple((outer_term(left_rows, right_rows) for left_rows, right_rows in matrix_pairs))
    pieces = lax.psum_scatter(
        terms + tuple(vectors), ("seq", "fsdp"), scatter_dimension=0, tiled=True
    )
    return list(pieces)


def join_terms(collected):
    matrix_pairs = []
    for member in range(len(collected[0][0])):
        lefts = jnp.concatenate([entry[0][member][0] for entry in collected], axis=0)
        rights = jnp.concatenate([entry[0][member][1] for entry in collected], axis=0)
        matrix_pairs.append((lefts, rights))
    vectors = [
        reduce(jnp.add, [entry[1][member] for entry in collected])
        for member in range(len(collected[0][1]))
    ]
    return (matrix_pairs, vectors)


def layer_step(gathered, inputs, cot_rows, live_mask, log_rates):
    (
        first_gain,
        query_weight,
        key_weight,
        value_weight,
        swish_weight,
        output_weight,
        group_gain,
        second_gain,
        feed_gate,
        feed_up,
        feed_down,
    ) = gathered
    floats = jnp.float32
    halves = jnp.bfloat16
    head_count = log_rates.shape[0]
    token_rows = inputs.shape[0]
    key_size = query_weight.shape[1] // head_count
    value_size = value_weight.shape[1] // head_count
    start_values = inputs.astype(floats)
    normed_one, pull_one = jax.vjp(norm_rows, start_values, first_gain.astype(floats))
    normed = normed_one.astype(halves)
    queries = plain_dot(normed, query_weight).astype(halves)
    keys_in = plain_dot(normed, key_weight).astype(halves) * live_mask[:, None].astype(halves)
    values_in = plain_dot(normed, value_weight).astype(halves)
    swish_in = plain_dot(normed, swish_weight)
    queries3 = queries.reshape(token_rows, head_count, key_size)
    keys3 = keys_in.reshape(token_rows, head_count, key_size)
    values3 = values_in.reshape(token_rows, head_count, value_size)
    cumulative = jnp.cumsum(log_rates, axis=1)
    slot_index = jnp.arange(token_rows)
    lower_mask = slot_index[:, None] >= slot_index[None, :]
    spread = cumulative[:, :, None] - cumulative[:, None, :]
    decay_matrix = jnp.where(lower_mask, jnp.exp(jnp.where(lower_mask, spread, 0.0)), 0.0)
    block_decay = jnp.exp(cumulative[:, -1])
    end_weight = jnp.exp(cumulative[:, -1:] - cumulative).T[:, :, None]
    entry_decay = jnp.exp(cumulative).T[:, :, None]
    query_wide = queries3.astype(floats)
    key_wide = keys3.astype(floats)
    value_wide = values3.astype(floats)
    state_term = jnp.einsum("jhd,jhe->hde", key_wide * end_weight, value_wide, precision=HIGHEST)
    state_identity = (jnp.ones_like(block_decay), jnp.zeros_like(state_term))
    _, start_state = carried_in(
        (block_decay, state_term), "seq", chain_states, state_identity, False
    )
    scores = jnp.einsum("ihd,jhd->hij", queries3, keys3, preferred_element_type=floats)
    weights = (scores * decay_matrix).astype(halves)
    intra_term = jnp.einsum("hij,jhe->ihe", weights, values3, preferred_element_type=floats)
    carried = entry_decay * jnp.einsum("ihd,hde->ihe", query_wide, start_state, precision=HIGHEST)
    retained = intra_term + carried
    grouped, pull_group = jax.vjp(
        norm_rows, retained, group_gain.astype(floats).reshape(head_count, value_size)
    )
    grouped_flat = grouped.reshape(token_rows, head_count * value_size)
    mixed_float, pull_mixed = jax.vjp(gated_swish, swish_in, grouped_flat)
    mixed_low = mixed_float.astype(halves)
    hidden = start_values + plain_dot(mixed_low, output_weight)
    normed_two, pull_two = jax.vjp(norm_rows, hidden, second_gain.astype(floats))
    second = normed_two.astype(halves)
    gate_two = plain_dot(second, feed_gate)
    upward = plain_dot(second, feed_up)
    inner_float, pull_inner = jax.vjp(gated_gelu, gate_two, upward)
    inner_low = inner_float.astype(halves)
    result = plain_dot(inner_low, feed_down)
    output_rows = ((hidden + result) * live_mask[:, None]).astype(halves)
    outer_grad = cot_rows.astype(floats) * live_mask[:, None]
    result_low = outer_grad.astype(halves)
    inner_grad = transposed(result_low, feed_down)
    gate_two_grad, upward_grad = pull_inner(inner_grad)
    gate_two_low = gate_two_grad.astype(halves)
    upward_low = upward_grad.astype(halves)
    second_grad = transposed(gate_two_low, feed_gate) + transposed(upward_low, feed_up)
    hidden_part, second_gain_grad = pull_two(second_grad)
    hidden_grad = outer_grad + hidden_part
    branch_low = hidden_grad.astype(halves)
    mixed_grad = transposed(branch_low, output_weight)
    swish_grad, grouped_grad = pull_mixed(mixed_grad)
    swish_low = swish_grad.astype(halves)
    retained_grad, group_gain_grad = pull_group(
        grouped_grad.reshape(token_rows, head_count, value_size)
    )
    retained_low = retained_grad.astype(halves)
    weights_grad = jnp.einsum("ihe,jhe->hij", retained_low, values3, preferred_element_type=floats)
    scores_low = (weights_grad * decay_matrix).astype(halves)
    query_intra = jnp.einsum("hij,jhd->ihd", scores_low, keys3, preferred_element_type=floats)
    key_intra = jnp.einsum("hij,ihd->jhd", scores_low, queries3, preferred_element_type=floats)
    value_intra = jnp.einsum("hij,ihe->jhe", weights, retained_low, preferred_element_type=floats)
    retained_wide = retained_low.astype(floats)
    query_carried = entry_decay * jnp.einsum(
        "ihe,hde->ihd", retained_wide, start_state, precision=HIGHEST
    )
    local_grad = jnp.einsum(
        "ihd,ihe->hde", query_wide * entry_decay, retained_wide, precision=HIGHEST
    )
    _, end_grad = carried_in((block_decay, local_grad), "seq", chain_states, state_identity, True)
    key_state = end_weight * jnp.einsum("jhe,hde->jhd", value_wide, end_grad, precision=HIGHEST)
    value_state = end_weight * jnp.einsum("jhd,hde->jhe", key_wide, end_grad, precision=HIGHEST)
    query_low = (
        (query_intra + query_carried).astype(halves).reshape(token_rows, head_count * key_size)
    )
    key_low = (
        ((key_intra + key_state) * live_mask[:, None, None])
        .astype(halves)
        .reshape(token_rows, head_count * key_size)
    )
    value_low = (
        (value_intra + value_state).astype(halves).reshape(token_rows, head_count * value_size)
    )
    normed_grad = (
        transposed(query_low, query_weight)
        + transposed(key_low, key_weight)
        + transposed(value_low, value_weight)
        + transposed(swish_low, swish_weight)
    )
    input_part, first_gain_grad = pull_one(normed_grad)
    grad_rows = (hidden_grad + input_part).astype(halves)
    matrix_pairs = [
        (normed, query_low),
        (normed, key_low),
        (normed, value_low),
        (normed, swish_low),
        (mixed_low, branch_low),
        (second, gate_two_low),
        (second, upward_low),
        (inner_low, result_low),
    ]
    vectors = [first_gain_grad, group_gain_grad.reshape(-1), second_gain_grad]
    return (output_rows, grad_rows, matrix_pairs, vectors)


def general_body(
    tokens,
    cotangent,
    lengths,
    block_order,
    log_decay,
    first_gain,
    query_weight,
    key_weight,
    value_weight,
    swish_weight,
    output_weight,
    group_gain,
    second_gain,
    feed_gate,
    feed_up,
    feed_down,
):
    batches = tokens.shape[0]
    block_rows = tokens.shape[1]
    selected_locations = lax.axis_size("seq")
    position = lax.axis_index("seq")
    group_index = lax.axis_index("fsdp")
    place_numbers = jnp.arange(selected_locations, dtype=jnp.int32)
    arrived_tokens, arrived_cotangent = (
        lax.all_gather(tokens, "seq", axis=1, tiled=True),
        lax.all_gather(cotangent, "seq", axis=1, tiled=True),
    )
    gathered = (
        lax.all_gather(first_gain, ("seq", "fsdp"), axis=0, tiled=True),
        lax.all_gather(query_weight, ("seq", "fsdp"), axis=0, tiled=True),
        lax.all_gather(key_weight, ("seq", "fsdp"), axis=0, tiled=True),
        lax.all_gather(value_weight, ("seq", "fsdp"), axis=0, tiled=True),
        lax.all_gather(swish_weight, ("seq", "fsdp"), axis=0, tiled=True),
        lax.all_gather(output_weight, ("seq", "fsdp"), axis=0, tiled=True),
        lax.all_gather(group_gain, ("seq", "fsdp"), axis=0, tiled=True),
        lax.all_gather(second_gain, ("seq", "fsdp"), axis=0, tiled=True),
        lax.all_gather(feed_gate, ("seq", "fsdp"), axis=0, tiled=True),
        lax.all_gather(feed_up, ("seq", "fsdp"), axis=0, tiled=True),
        lax.all_gather(feed_down, ("seq", "fsdp"), axis=0, tiled=True),
    )
    outputs = []
    input_grads = []
    collected = []
    order_rows = []
    for batch_number in range(batches):
        sequence = group_index * batches + batch_number
        order_row = lax.dynamic_index_in_dim(block_order, sequence, 0, keepdims=False)
        order_rows.append(order_row)
        source = jnp.sum(place_numbers * (order_row == position).astype(jnp.int32))
        token_rows = lax.dynamic_slice_in_dim(
            arrived_tokens[batch_number], source * block_rows, block_rows, 0
        )
        cot_rows = lax.dynamic_slice_in_dim(
            arrived_cotangent[batch_number], source * block_rows, block_rows, 0
        )
        live_length = lax.dynamic_index_in_dim(lengths, sequence, 0, keepdims=False)
        location_number = position * block_rows + jnp.arange(block_rows, dtype=jnp.int32)
        live_mask = (location_number < live_length).astype(jnp.float32)
        output_rows, grad_rows, matrix_pairs, vectors = layer_step(
            gathered, token_rows, cot_rows, live_mask, log_decay
        )
        outputs.append(output_rows)
        input_grads.append(grad_rows)
        collected.append((matrix_pairs, vectors))
    joined_pairs, joined_vectors = join_terms(collected)
    shards = spread_sum(joined_pairs, joined_vectors)
    every_output, every_grad = (
        lax.all_gather(jnp.stack(outputs), "seq", axis=1, tiled=True),
        lax.all_gather(jnp.stack(input_grads), "seq", axis=1, tiled=True),
    )
    returned = []
    returned_grads = []
    for batch_number in range(batches):
        target = lax.dynamic_index_in_dim(order_rows[batch_number], position, 0, keepdims=False)
        returned.append(
            lax.dynamic_slice_in_dim(every_output[batch_number], target * block_rows, block_rows, 0)
        )
        returned_grads.append(
            lax.dynamic_slice_in_dim(every_grad[batch_number], target * block_rows, block_rows, 0)
        )
    return (
        jnp.stack(returned),
        jnp.stack(returned_grads),
        shards[8],
        shards[0],
        shards[1],
        shards[2],
        shards[3],
        shards[4],
        shards[9],
        shards[10],
        shards[5],
        shards[6],
        shards[7],
    )


FULL = jnp.float32
HALF = jnp.bfloat16
MESH = pl.DeviceIdType.MESH
VMEM_BYTES = 56 * 1024 * 1024
LARGE_BYTES = 63 * 1024 * 1024
LANES = 128


def dot_nn(left, right):
    return jnp.dot(left, right, preferred_element_type=FULL)


def dot_nt(left, right):
    return lax.dot_general(left, right, (((1,), (1,)), ((), ())), preferred_element_type=FULL)


def dot_tn(left, right):
    return lax.dot_general(left, right, (((0,), (0,)), ((), ())), preferred_element_type=FULL)


def plane_peers():
    me = lax.axis_index("seq")
    core = lax.rem(me, 2)
    across = 2 - 4 * lax.rem(me // 2, 2)
    down = 4 - 8 * (me // 4)
    return me, me + 1 - 2 * core, me + across, me + down, me + across + down


def to_peer(source, target, send, receive, peer):
    return pltpu.make_async_remote_copy(
        src_ref=source,
        dst_ref=target,
        send_sem=send,
        recv_sem=receive,
        device_id={"seq": peer},
        device_id_type=MESH,
    )


def greet_neighbours():
    _, other, near, below, _ = plane_peers()
    barrier = pltpu.get_barrier_semaphore()
    for peer in (other, near, below):
        pl.semaphore_signal(barrier, inc=1, device_id={"seq": peer}, device_id_type=MESH)
    pl.semaphore_wait(barrier, 3)


GATHER_COPIES = 14


def gather_plan():
    me, other, near, below, far = plane_peers()
    flip = other - me
    return (
        (me, 0, near, near),
        (me, 1, below, below),
        (me, 0, other, other),
        (me, 1, other, other),
        (me, 1, near, near),
        (me, 0, below, below),
        (near, 0, below, far),
        (below, 1, near, far),
        (near, 0, other, near + flip),
        (below, 1, other, below + flip),
        (near, 1, other, near + flip),
        (below, 0, other, below + flip),
        (far, 0, other, far + flip),
        (far, 1, other, far + flip),
    )


class PlaneGather:
    def __init__(self, own, out, keeps, sends, receives, window=0, windows=1):
        self.own, self.out = own, out
        self.keep, self.sends, self.receives = keeps.at[window], sends, receives
        self.size = own.shape[0] // windows
        self.window, self.start = window, window * self.size
        self.half = self.size // 2

    def rows(self, which):
        return pl.ds(self.start + which * self.half, self.half)

    def kept(self):
        me = lax.axis_index("seq")
        rows = pl.ds(self.start, self.size)
        return pltpu.make_async_copy(self.own.at[rows], self.out.at[me, rows], self.keep)

    def sent(self, source, target, number, peer):
        at = (self.window, number)
        return to_peer(source, target, self.sends.at[at], self.receives.at[at], peer)

    def copy(self, number):
        block, which, peer, _ = gather_plan()[number]
        target = self.out.at[block, self.rows(which)]
        source = self.own.at[self.rows(which)] if number < 6 else target
        return self.sent(source, target, number, peer)

    def landed(self, number):
        _, which, peer, landing = gather_plan()[number]
        target = self.out.at[landing, self.rows(which)]
        self.sent(target, target, number, peer).wait_recv()

    def begin(self):
        self.kept().start()
        for number in range(6):
            self.copy(number).start()

    def relay(self):
        for arrived, onward in ((0, (6, 8)), (1, (7, 9)), (4, (10,)), (5, (11,))):
            self.landed(arrived)
            for number in onward:
                self.copy(number).start()

    def finish(self):
        for arrived, onward in ((6, 12), (7, 13)):
            self.landed(arrived)
            self.copy(onward).start()
        for number in (2, 3, 8, 9, 10, 11, 12, 13):
            self.landed(number)
        for number in range(GATHER_COPIES):
            self.copy(number).wait_send()
        self.kept().wait()


def gather_scratch(windows=1):
    return [
        pltpu.SemaphoreType.DMA((windows,)),
        pltpu.SemaphoreType.DMA((windows, GATHER_COPIES)),
        pltpu.SemaphoreType.DMA((windows, GATHER_COPIES)),
    ]


SCATTER_COPIES = 10
WINDOWS = 2
CHUNK = 32


def by_chunks(rows, work):
    def step(number, carry):
        work(pl.ds(pl.multiple_of(number * CHUNK, CHUNK), CHUNK))
        return carry

    lax.fori_loop(0, rows // CHUNK, step, 0)


class PlaneScatter:
    def __init__(self, window, others, terms, cores, nears, belows, sends, receives):
        self.window = window
        self.others, self.terms, self.cores = others, terms, cores
        self.nears, self.belows = nears, belows
        self.sends, self.receives = sends, receives
        self.size = terms.shape[1] // WINDOWS
        self.half = self.size // 2
        self.start = window * self.size

    def copy(self, number):
        _, other, near, below, _ = plane_peers()
        whole = pl.ds(self.start, self.size)
        upper, lower = (pl.ds(self.start + at * self.half, self.half) for at in (0, 1))
        if number < 4:
            source, target, peer = (
                self.others.at[number, whole],
                self.cores.at[number, whole],
                other,
            )
        else:
            slot, rows, landing, place, peer = (
                (0, upper, self.nears, 0, near),
                (0, lower, self.belows, 0, below),
                (1, upper, self.nears, 1, near),
                (2, lower, self.belows, 1, below),
                (1, lower, self.nears, 2, near),
                (2, upper, self.belows, 2, below),
            )[number - 4]
            source, target = self.terms.at[slot, rows], landing.at[self.window, place]
        at = (self.window, number)
        return to_peer(source, target, self.sends.at[at], self.receives.at[at], peer)

    def fold(self, slot):
        def work(rows):
            here = pl.ds(pl.multiple_of(self.start + rows.start, CHUNK), CHUNK)
            self.terms[slot, here] = (
                self.terms[slot, here].astype(FULL) + self.cores[slot, here].astype(FULL)
            ).astype(HALF)

        by_chunks(self.size, work)

    def fold_half(self, slot, which, landed):
        def work(rows):
            at = self.start + which * self.half
            here = pl.ds(pl.multiple_of(at + rows.start, CHUNK), CHUNK)
            self.terms[slot, here] = (
                self.terms[slot, here].astype(FULL) + landed[self.window, 0, rows].astype(FULL)
            ).astype(HALF)

        by_chunks(self.half, work)

    def advance(self, slot):
        self.copy(slot).wait_recv()
        self.fold(slot)
        for number in ((4, 5), (6,), (7,), ())[slot]:
            self.copy(number).start()

    def relay(self):
        self.copy(4).wait_recv()
        self.fold_half(2, 0, self.nears)
        self.copy(9).start()
        self.copy(5).wait_recv()
        self.fold_half(1, 1, self.belows)
        self.copy(8).start()

    def finish(self):
        for number in (6, 7, 8, 9):
            self.copy(number).wait_recv()

    def drain(self, first=0):
        for number in range(first, SCATTER_COPIES):
            self.copy(number).wait_send()

    def total(self, at):
        upper = at < self.half
        rows = pl.ds(at if upper else at - self.half, CHUNK)
        near, below = (1, 2) if upper else (2, 1)
        return (
            self.terms[3, pl.ds(self.start + at, CHUNK)].astype(FULL)
            + self.nears[self.window, near, rows].astype(FULL)
            + self.belows[self.window, below, rows].astype(FULL)
        )


def block_order_of_plane():
    me, other, near, below, far = plane_peers()
    return [block + at for block in (far, near, below, me) for at in (other - me, 0)]


class Blocks:
    def __init__(self, source, target, sems):
        self.source, self.target, self.sems = source, target, sems
        self.blocks, self.taken = block_order_of_plane(), 0

    def load(self, number):
        slot = number % self.target.shape[0]
        return pltpu.make_async_copy(
            self.source.at[self.blocks[number]], self.target.at[slot], self.sems.at[slot]
        )

    def begin(self):
        for number in range(min(len(self.blocks), self.target.shape[0])):
            self.load(number).start()

    def take(self, work):
        number, slots = self.taken, self.target.shape[0]
        self.taken += 1
        self.load(number).wait()
        out = work(self.target[number % slots])
        if number + slots < len(self.blocks):
            self.load(number + slots).start()
        return out


def staged(sources, targets, sems):
    copies = [
        pltpu.make_async_copy(source, target, sems.at[number])
        for number, (source, target) in enumerate(zip(sources, targets))
    ]
    for copy in copies:
        copy.start()
    return copies


def stage_scratch(*arrays):
    return [pltpu.VMEM(array.shape, array.dtype) for array in arrays] + [
        pltpu.SemaphoreType.DMA((len(arrays),))
    ]


def block_scratch(count, array):
    return [
        pltpu.VMEM((count,) + array.shape[1:], array.dtype),
        pltpu.SemaphoreType.DMA((count,)),
    ]


def scatter_head(term, refs, earlier=(), relay_later=False):
    windows = [PlaneScatter(window, *refs) for window in range(WINDOWS)]
    others, terms = refs[:2]
    blocks = block_order_of_plane()

    def fill(slot):
        for window in earlier:
            window.copy(slot).wait_send()
        others[slot] = term(blocks[2 * slot])
        for window in windows:
            window.copy(slot).start()
        terms[slot] = term(blocks[2 * slot + 1])

    fill(0)
    for slot in range(4):
        if slot < 3:
            fill(slot + 1)
        windows[0].advance(slot)
    if not relay_later:
        windows[0].relay()
    for window in windows[1:]:
        for slot in range(4):
            window.advance(slot)
        if not relay_later:
            window.relay()
    return windows


def scatter_tail(windows, use, after=lambda window: None):
    for number, window in enumerate(windows):
        window.finish()
        for at in range(0, window.size, CHUNK):
            use(window.start + at, window.total(at))
        after(number)


def scatter_scratch(rows, width):
    half = rows // WINDOWS // 2
    return [
        pltpu.VMEM((4, rows, width), HALF),
        pltpu.VMEM((4, rows, width), HALF),
        pltpu.VMEM((4, rows, width), HALF),
        pltpu.VMEM((WINDOWS, 3, half, width), HALF),
        pltpu.VMEM((WINDOWS, 3, half, width), HALF),
        pltpu.SemaphoreType.DMA((WINDOWS, SCATTER_COPIES)),
        pltpu.SemaphoreType.DMA((WINDOWS, SCATTER_COPIES)),
    ]


def regroup(values, outer, inner):
    rows = values.shape[0]
    low_half = lax.broadcasted_iota(jnp.int32, (rows, LANES), 1) < LANES // 2

    def piece(p, q):
        at = (p * inner + q) // 2
        return values[:, at * LANES : (at + 1) * LANES]

    def turned(value):
        return pltpu.roll(value, LANES // 2, 1)

    groups = []
    for q in range(inner):
        for p in range(0, outer, 2):
            first, second = piece(p, q), piece(p + 1, q)
            if q % 2 == 0:
                groups.append(jnp.where(low_half, first, turned(second)))
            else:
                groups.append(jnp.where(low_half, turned(first), second))
    return jnp.concatenate(groups, axis=1)


def normalised(values):
    average = jnp.mean(values, axis=-1, keepdims=True)
    centered = values - average
    scale = lax.rsqrt(jnp.mean(centered * centered, axis=-1, keepdims=True) + EPSILON)
    return centered * scale, scale


def normalised_back(grad, normed, scale):
    average = jnp.mean(grad, axis=-1, keepdims=True)
    along = jnp.mean(grad * normed, axis=-1, keepdims=True)
    return (grad - average - normed * along) * scale


def vmem():
    return pl.BlockSpec(memory_space=pltpu.VMEM)


def in_hbm():
    return pl.BlockSpec(memory_space=pl.ANY)


def cost(flops, link_bytes):
    return pl.CostEstimate(flops=int(flops), bytes_accessed=int(link_bytes) * 16, transcendentals=0)


def linked(collective):
    return pltpu.CompilerParams(
        collective_id=collective, has_side_effects=True, vmem_limit_bytes=VMEM_BYTES
    )


class PlaneSwap:
    def __init__(self, weights, targets, keeps, sends, receives):
        self.weights, self.targets = weights, targets
        self.keeps, self.sends, self.receives = keeps, sends, receives
        self.peers = lax.axis_size("seq")

    def part(self, number, peer):
        weight, (target, start) = self.weights[number], self.targets[number]
        size = weight.shape[1] // self.peers
        return weight.at[:, pl.ds(pl.multiple_of(peer * size, LANES), size)]

    def place(self, number, peer):
        weight, (target, start) = self.weights[number], self.targets[number]
        return target.at[peer, :, pl.ds(start, weight.shape[1] // self.peers)]

    def copy(self, number, turn):
        me = lax.axis_index("seq")
        peer = lax.rem(me + turn, self.peers)
        return to_peer(
            self.part(number, peer),
            self.place(number, me),
            self.sends.at[number, turn],
            self.receives.at[number, turn],
            peer,
        )

    def landed(self, number, turn):
        me = lax.axis_index("seq")
        peer = lax.rem(me + self.peers - turn, self.peers)
        target = self.place(number, peer)
        to_peer(
            target, target, self.sends.at[number, turn], self.receives.at[number, turn], peer
        ).wait_recv()

    def kept(self, number):
        me = lax.axis_index("seq")
        return pltpu.make_async_copy(
            self.part(number, me), self.place(number, me), self.keeps.at[number]
        )

    def begin(self):
        for number in range(len(self.weights)):
            for turn in range(1, self.peers):
                self.copy(number, turn).start()
            self.kept(number).start()

    def finish(self):
        for number in range(len(self.weights)):
            for turn in range(1, self.peers):
                self.landed(number, turn)
                self.copy(number, turn).wait_send()
            self.kept(number).wait()


def swap_scratch(count, peers):
    return [
        pltpu.SemaphoreType.DMA((count,)),
        pltpu.SemaphoreType.DMA((count, peers)),
        pltpu.SemaphoreType.DMA((count, peers)),
    ]


def greet_plane(with_groups):
    me, group = lax.axis_index("seq"), lax.axis_index("fsdp")
    peers, groups = lax.axis_size("seq"), lax.axis_size("fsdp")
    barrier = pltpu.get_barrier_semaphore()
    count = peers - 1
    for turn in range(1, peers):
        peer = lax.rem(me + turn, peers)
        pl.semaphore_signal(barrier, inc=1, device_id={"seq": peer}, device_id_type=MESH)
    if with_groups:
        count += groups - 1
        for turn in range(1, groups):
            peer = lax.rem(group + turn, groups)
            pl.semaphore_signal(barrier, inc=1, device_id={"fsdp": peer}, device_id_type=MESH)
    pl.semaphore_wait(barrier, count)


def all_to_each(source, out, axis, size, keep, sends, receives):
    me = lax.axis_index(axis)

    def copy(turn, slot):
        peer = lax.rem(me + turn, size)
        return pltpu.make_async_remote_copy(
            src_ref=source,
            dst_ref=out.at[slot],
            send_sem=sends.at[turn],
            recv_sem=receives.at[turn],
            device_id={axis: peer},
            device_id_type=MESH,
        )

    def begin():
        pltpu.make_async_copy(source, out.at[me], keep).start()
        for turn in range(1, size):
            copy(turn, me).start()

    def finish():
        for turn in range(1, size):
            copy(turn, lax.rem(me + size - turn, size)).wait_recv()
            copy(turn, me).wait_send()
        pltpu.make_async_copy(source, out.at[me], keep).wait()

    return begin, finish


def first_swap_kernel(
    query_ref, key_ref, value_ref, swish_ref, rates_ref, gains_ref,
    cut_out, rates_out, gains_out,
    column, keeps, sends, receives, rate_keep, rate_sends, rate_receives,
    group_keep, group_sends, group_receives, gain_keep, gain_sends, gain_receives,
):
    peers, groups = lax.axis_size("seq"), lax.axis_size("fsdp")
    size, wide = query_ref.shape[1] // peers, value_ref.shape[1] // peers
    greet_plane(True)
    begin_groups, finish_groups = all_to_each(
        gains_ref, column, "fsdp", groups, group_keep, group_sends, group_receives
    )
    begin_rates, finish_rates = all_to_each(
        rates_ref, rates_out, "seq", peers, rate_keep, rate_sends, rate_receives
    )
    begin_gains, finish_gains = all_to_each(
        column, gains_out, "seq", peers, gain_keep, gain_sends, gain_receives
    )
    swap = PlaneSwap(
        (query_ref, key_ref, value_ref, swish_ref),
        ((cut_out, 0), (cut_out, size), (cut_out, 2 * size), (cut_out, 2 * size + wide)),
        keeps,
        sends,
        receives,
    )
    begin_groups()
    begin_rates()
    finish_groups()
    begin_gains()
    swap.begin()
    finish_rates()
    finish_gains()
    swap.finish()


def first_swap(query, key, value, swish, rates, gains):
    peers, groups = lax.axis_size("seq"), lax.axis_size("fsdp")
    slab = query.shape[0]
    total = sum(weight.shape[1] for weight in (query, key, value, swish)) // peers
    return pl.pallas_call(
        first_swap_kernel,
        in_specs=[in_hbm()] * 4 + [vmem()] * 2,
        out_specs=[in_hbm()] + [vmem()] * 2,
        out_shape=[
            jax.ShapeDtypeStruct((peers, slab, total), HALF),
            jax.ShapeDtypeStruct((peers,) + rates.shape, FULL),
            jax.ShapeDtypeStruct((peers, groups) + gains.shape, FULL),
        ],
        scratch_shapes=[pltpu.VMEM((groups,) + gains.shape, FULL)]
        + swap_scratch(4, peers)
        + [pltpu.SemaphoreType.DMA] + [pltpu.SemaphoreType.DMA((peers,))] * 2
        + [pltpu.SemaphoreType.DMA] + [pltpu.SemaphoreType.DMA((groups,))] * 2
        + [pltpu.SemaphoreType.DMA] + [pltpu.SemaphoreType.DMA((peers,))] * 2,
        compiler_params=linked(0),
        cost_estimate=cost(0, 2 * slab * peers * total),
    )(query, key, value, swish, rates, gains)


class LineGather:
    def __init__(self, own, out, keep, sends, receives):
        self.own, self.out = own, out
        self.keep, self.sends, self.receives = keep, sends, receives
        self.me, self.last = lax.axis_index("fsdp"), lax.axis_size("fsdp") - 1
        self.pieces = own.shape[0]

    def block(self, way, depth):
        return self.me - depth if way == 0 else self.me + depth

    def holds(self, way, depth):
        return self.me >= depth if way == 0 else self.me + depth <= self.last

    def passes(self, way):
        return self.me < self.last if way == 0 else self.me > 0

    def sent(self, source, way, depth, piece, block):
        at = (way, depth, piece)
        return pltpu.make_async_remote_copy(
            src_ref=source,
            dst_ref=self.out.at[block, piece],
            send_sem=self.sends.at[at],
            recv_sem=self.receives.at[at],
            device_id={"fsdp": self.me + 1 if way == 0 else self.me - 1},
            device_id_type=MESH,
        )

    def copy(self, way, depth, piece):
        block = self.block(way, depth)
        source = self.own.at[piece] if depth == 0 else self.out.at[block, piece]
        return self.sent(source, way, depth, piece, block)

    def landed(self, way, depth, piece):
        block = self.block(way, depth)
        self.sent(self.out.at[block, piece], way, depth - 1, piece, block).wait_recv()

    def kept(self):
        return pltpu.make_async_copy(self.own, self.out.at[self.me], self.keep)

    def begin(self):
        for piece in range(self.pieces):
            for way in (0, 1):

                @pl.when(self.passes(way))
                def _():
                    self.copy(way, 0, piece).start()

        self.kept().start()

    def hand_on(self, depth):
        for piece in range(self.pieces):
            for way in (0, 1):

                @pl.when(self.holds(way, depth) & self.passes(way))
                def _():
                    self.landed(way, depth, piece)
                    self.copy(way, depth, piece).start()

    def finish(self):
        for depth in range(1, self.last + 1):
            for piece in range(self.pieces):
                for way in (0, 1):

                    @pl.when(self.holds(way, depth) & jnp.logical_not(self.passes(way)))
                    def _():
                        self.landed(way, depth, piece)

        for depth in range(self.last):
            for piece in range(self.pieces):
                for way in (0, 1):

                    @pl.when(self.holds(way, depth) & self.passes(way))
                    def _():
                        self.copy(way, depth, piece).wait_send()

        self.kept().wait()


def unpack_gains(gains_ref, one_ref, two_ref, group_ref):
    peers, groups = gains_ref.shape[:2]
    low_half = lax.broadcasted_iota(jnp.int32, (1, LANES), 1) < LANES // 2
    for peer in range(peers):
        for at in range(0, groups, 2):
            left, right = gains_ref[peer, at, 1:2], gains_ref[peer, at + 1, 1:2]
            lanes = pl.ds((peer * groups + at) * LANES // 2, LANES)
            one_ref[:, lanes] = jnp.where(low_half, left, pltpu.roll(right, LANES // 2, 1))
            two_ref[:, lanes] = jnp.where(low_half, pltpu.roll(left, LANES // 2, 1), right)
    me = lax.axis_index("seq")
    for at in range(groups):
        group_ref[:, at * LANES : (at + 1) * LANES] = gains_ref[me, at, 0:1]


def unpack_rates(rates_ref, decay_ref, column_ref):
    blocks, _, rows = rates_ref.shape
    me = lax.axis_index("seq")
    total = jnp.concatenate([rates_ref[block, pl.ds(me, 1)] for block in range(blocks)], axis=0)
    lane = lax.broadcasted_iota(jnp.int32, total.shape, 1)
    shift = 1
    while shift < rows:
        total += jnp.where(lane >= shift, pltpu.roll(total, shift, 1), 0.0)
        shift *= 2
    square = (rows, rows)
    lower = lax.broadcasted_iota(jnp.int32, square, 0) >= lax.broadcasted_iota(jnp.int32, square, 1)
    for block in range(blocks):
        along = jnp.broadcast_to(total[block : block + 1], square)
        down = along.T
        spread = jnp.where(lower, down - along, 0.0)
        decay_ref[block] = jnp.where(lower, jnp.exp(spread), 0.0)
        first = down[:, 0:1]
        column_ref[block, :, 0:1] = jnp.exp(first)
        column_ref[block, :, 1:2] = jnp.exp(first[rows - 1 : rows] - first)


def inputs_kernel(
    lengths_ref, order_ref, tokens_ref, grad_ref, gains_ref, rates_ref, gate_ref, up_ref, cut_ref,
    entered_out, grads_out, feed_out, weight_out,
    mask_ref, gain_ref, second_ref, group_ref, decay_ref, column_ref,
    own_entered, own_grad, keep_one, sends_one, receives_one, keep_two, sends_two, receives_two,
    keeps, sends, receives, line_keep, line_sends, line_receives,
):
    peers, groups = lax.axis_size("seq"), lax.axis_size("fsdp")
    greet_plane(True)
    line = LineGather(cut_ref, weight_out, line_keep, line_sends, line_receives)
    line.begin()
    size = gate_ref.shape[1] // peers
    me, group = lax.axis_index("seq"), lax.axis_index("fsdp")
    batches = lengths_ref.shape[0] // groups
    block = tokens_ref.shape[0] // batches
    for batch in range(batches):
        sequence = group * batches + batch
        numbers = order_ref[sequence, me] * block + lax.broadcasted_iota(jnp.int32, (block, 1), 0)
        live = (numbers < lengths_ref[sequence]).astype(FULL)
        mask_ref[batch * block : (batch + 1) * block] = live
    unpack_gains(gains_ref, gain_ref, second_ref, group_ref)
    gain = gain_ref[...]

    def work(rows):
        normed, _ = normalised(tokens_ref[rows].astype(FULL))
        own_entered[rows] = regroup(normed * gain, peers, groups).astype(HALF)
        own_grad[rows] = (grad_ref[rows].astype(FULL) * mask_ref[rows]).astype(HALF)

    by_chunks(tokens_ref.shape[0], work)
    one = PlaneGather(own_entered, entered_out, keep_one, sends_one, receives_one)
    two = PlaneGather(own_grad, grads_out, keep_two, sends_two, receives_two)
    swap = PlaneSwap((gate_ref, up_ref), ((feed_out, 0), (feed_out, size)), keeps, sends, receives)
    one.begin()
    one.relay()
    swap.begin()
    two.begin()
    unpack_rates(rates_ref, decay_ref, column_ref)
    line.hand_on(1)
    one.finish()
    two.relay()
    line.hand_on(2)
    swap.finish()
    two.finish()
    line.finish()


def gather_inputs(lengths, order, tokens, grad, gains, rates, gate, up, cut, value_size):
    peers, groups = lax.axis_size("seq"), lax.axis_size("fsdp")
    own, width = tokens.shape
    slab, columns = gate.shape
    part = columns // peers
    blocks, _, rows = rates.shape
    return pl.pallas_call(
        inputs_kernel,
        in_specs=[pl.BlockSpec(memory_space=pltpu.SMEM)] * 2 + [vmem()] * 4 + [in_hbm()] * 3,
        out_specs=[in_hbm()] * 4 + [vmem()] * 6,
        out_shape=[
            jax.ShapeDtypeStruct((peers, own, width), HALF),
            jax.ShapeDtypeStruct((peers, own, width), HALF),
            jax.ShapeDtypeStruct((peers, slab, 2 * part), HALF),
            jax.ShapeDtypeStruct((groups,) + cut.shape, HALF),
            jax.ShapeDtypeStruct((own, 1), FULL),
            jax.ShapeDtypeStruct((1, width), FULL),
            jax.ShapeDtypeStruct((1, width), FULL),
            jax.ShapeDtypeStruct((1, value_size), FULL),
            jax.ShapeDtypeStruct((blocks, rows, rows), FULL),
            jax.ShapeDtypeStruct((blocks, rows, 2), FULL),
        ],
        scratch_shapes=[pltpu.VMEM((own, width), HALF)] * 2
        + gather_scratch()
        + gather_scratch()
        + swap_scratch(2, peers)
        + [
            pltpu.SemaphoreType.DMA,
            pltpu.SemaphoreType.DMA((2, groups - 1, peers)),
            pltpu.SemaphoreType.DMA((2, groups - 1, peers)),
        ],
        compiler_params=linked(1),
        cost_estimate=cost(0, 2 * peers * (2 * own * width + slab * 2 * part)),
    )(lengths, order, tokens, grad, gains, rates, gate, up, cut)


def feed_kernel(rows_ref, weight_ref, inner_ref, up_slope_ref, gate_slope_ref):
    both = dot_nn(rows_ref[...], weight_ref[...])
    part = both.shape[1] // 2
    gate, upward = both[:, :part], both[:, part:]
    inside = 0.7978845608028654 * (gate + 0.044715 * (gate * gate * gate))
    bend = jnp.tanh(inside)
    share = 0.5 * (1.0 + bend)
    value = gate * share
    steep = 0.7978845608028654 * (1.0 + 3.0 * 0.044715 * (gate * gate))
    slope = share + 0.5 * gate * (1.0 - bend * bend) * steep
    inner_ref[...] = (value * upward).astype(HALF)
    up_slope_ref[...] = value.astype(HALF)
    gate_slope_ref[...] = (upward * slope).astype(HALF)


def feed(rows, weight):
    count, width = rows.shape
    columns = weight.shape[1]
    tile = 256
    out = pl.BlockSpec((tile, columns // 2), lambda i: (i, 0))
    return pl.pallas_call(
        feed_kernel,
        grid=(count // tile,),
        in_specs=[
            pl.BlockSpec((tile, width), lambda i: (i, 0)),
            pl.BlockSpec((width, columns), lambda i: (0, 0), pipeline_mode=pl.Buffered(1)),
        ],
        out_specs=[out] * 3,
        out_shape=[jax.ShapeDtypeStruct((count, columns // 2), HALF)] * 3,
        compiler_params=pltpu.CompilerParams(
            dimension_semantics=("arbitrary",), vmem_limit_bytes=VMEM_BYTES
        ),
        cost_estimate=pl.CostEstimate(
            flops=2 * count * width * columns,
            bytes_accessed=2 * (count * width + width * columns + 2 * count * columns),
            transcendentals=0,
        ),
    )(rows, weight)


def feed_back_kernel(rows_ref, weight_ref, up_slope_ref, gate_slope_ref, grad_ref):
    inner_grad = dot_nt(rows_ref[...], weight_ref[...])
    part = inner_grad.shape[1]
    grad_ref[:, :part] = (inner_grad * gate_slope_ref[...].astype(FULL)).astype(HALF)
    grad_ref[:, part:] = (inner_grad * up_slope_ref[...].astype(FULL)).astype(HALF)


def feed_back(rows, weight, up_slope, gate_slope):
    count, width = rows.shape
    part = weight.shape[0]
    tile = 512
    slope = pl.BlockSpec((tile, part), lambda i: (i, 0))
    return pl.pallas_call(
        feed_back_kernel,
        grid=(count // tile,),
        in_specs=[
            pl.BlockSpec((tile, width), lambda i: (i, 0)),
            pl.BlockSpec((part, width), lambda i: (0, 0), pipeline_mode=pl.Buffered(1)),
            slope,
            slope,
        ],
        out_specs=pl.BlockSpec((tile, 2 * part), lambda i: (i, 0)),
        out_shape=jax.ShapeDtypeStruct((count, 2 * part), HALF),
        compiler_params=pltpu.CompilerParams(
            dimension_semantics=("arbitrary",), vmem_limit_bytes=VMEM_BYTES
        ),
        cost_estimate=pl.CostEstimate(
            flops=2 * count * width * part,
            bytes_accessed=2 * (count * width + width * part + 4 * count * part),
            transcendentals=0,
        ),
    )(rows, weight, up_slope, gate_slope)


def retention_kernel(
    place_ref, live_ref, first_ref, second_ref, weight_ref, decay_ref, column_ref, gain_ref,
    qkv_ref, swish_ref, normed_ref, scale_ref, entry_ref, mixed_hbm, state, mixed_buffer, sems,
):
    step, steps = pl.program_id(0), pl.num_programs(0)
    rows = first_ref.shape[2]
    batches, key_size, value_size = state.shape
    total = 2 * key_size + value_size
    slot = lax.rem(step, 2)

    def sent(at, which, batch):
        return pltpu.make_async_copy(
            mixed_buffer.at[which, batch],
            mixed_hbm.at[place_ref[batch, at], batch],
            sems.at[which, batch],
        )

    @pl.when(step == 0)
    def _():
        state[...] = jnp.zeros_like(state)

    @pl.when(step >= 2)
    def _():
        for batch in range(batches):
            sent(step - 2, slot, batch).wait()

    rows_in = jnp.concatenate([first_ref[0, 0], second_ref[0, 0]], axis=0)
    projected = dot_nn(rows_in, weight_ref[...])
    decay = decay_ref[0]
    entry_decay = column_ref[0, :, 0:1]
    end_weight = column_ref[0, :, 1:2]
    block_decay = column_ref[0, rows - 1 : rows, 0:1]
    positions = step * rows + lax.broadcasted_iota(jnp.int32, (rows, 1), 0)
    for batch in range(batches):
        mine = slice(batch * rows, (batch + 1) * rows)
        live = (positions < live_ref[batch]).astype(FULL)
        query = projected[mine, :key_size].astype(HALF)
        key = (projected[mine, key_size : 2 * key_size] * live).astype(HALF)
        value = projected[mine, 2 * key_size : total].astype(HALF)
        swish = projected[mine, total:]
        before = state[batch]
        before_low = before.astype(HALF)
        weights = (dot_nt(query, key) * decay).astype(HALF)
        retained = dot_nn(weights, value) + entry_decay * dot_nn(query, before_low)
        key_ended = (key.astype(FULL) * end_weight).astype(HALF)
        state[batch] = block_decay * before + dot_tn(key_ended, value)
        normed, scale = normalised(retained)
        qkv_ref[batch, 0, :, :key_size] = query
        qkv_ref[batch, 0, :, key_size : 2 * key_size] = key
        qkv_ref[batch, 0, :, 2 * key_size :] = value
        scale_ref[batch, 0] = jnp.broadcast_to(scale, scale_ref.shape[2:])
        entry_ref[batch, 0] = before_low
        swish_ref[batch, 0] = swish.astype(HALF)
        normed_ref[batch, 0] = normed.astype(HALF)
        mixed = swish * jax.nn.sigmoid(swish) * (normed * gain_ref[...])
        mixed_buffer[slot, batch] = mixed.astype(HALF)
        sent(step, slot, batch).start()

    @pl.when(step == steps - 1)
    def _():
        for batch in range(batches):
            sent(step, slot, batch).wait()
            sent(step - 1, 1 - slot, batch).wait()


def retention(rows_in, weight, place, live, decay, columns, gain, key_size):
    blocks, batches, rows, width = rows_in.shape
    value_size = gain.shape[-1]
    total = 2 * key_size + value_size

    def arriving(batch):
        return pl.BlockSpec(
            (1, 1, rows, width), lambda i, place, live: (place[batch, i], batch, 0, 0)
        )

    def whole(shape):
        return pl.BlockSpec(
            shape, lambda i, place, live: (0,) * len(shape), pipeline_mode=pl.Buffered(1)
        )

    def here(*tail):
        return pl.BlockSpec((batches, 1) + tail, lambda i, place, live: (0, i, 0, 0))

    def along(*tail):
        return pl.BlockSpec((1,) + tail, lambda i, place, live: (i, 0, 0))

    return pl.pallas_call(
        retention_kernel,
        grid_spec=pltpu.PrefetchScalarGridSpec(
            num_scalar_prefetch=2,
            grid=(blocks,),
            in_specs=[
                arriving(0),
                arriving(1),
                whole((width, total + value_size)),
                along(rows, rows),
                along(rows, 2),
                whole((1, value_size)),
            ],
            out_specs=[
                here(rows, total),
                here(rows, value_size),
                here(rows, value_size),
                here(rows, LANES),
                here(key_size, value_size),
                in_hbm(),
            ],
            scratch_shapes=[
                pltpu.VMEM((batches, key_size, value_size), FULL),
                pltpu.VMEM((2, batches, rows, value_size), HALF),
                pltpu.SemaphoreType.DMA((2, batches)),
            ],
        ),
        out_shape=[
            jax.ShapeDtypeStruct((batches, blocks, rows, total), HALF),
            jax.ShapeDtypeStruct((batches, blocks, rows, value_size), HALF),
            jax.ShapeDtypeStruct((batches, blocks, rows, value_size), HALF),
            jax.ShapeDtypeStruct((batches, blocks, rows, LANES), FULL),
            jax.ShapeDtypeStruct((batches, blocks, key_size, value_size), HALF),
            jax.ShapeDtypeStruct((blocks, batches, rows, value_size), HALF),
        ],
        compiler_params=pltpu.CompilerParams(
            dimension_semantics=("arbitrary",), vmem_limit_bytes=VMEM_BYTES
        ),
        cost_estimate=pl.CostEstimate(
            flops=3 * blocks * batches * rows * width * total,
            bytes_accessed=2 * blocks * batches * rows * (width + 2 * total) + 4 * width * total,
            transcendentals=0,
        ),
    )(place, live, rows_in, rows_in, weight, decay, columns, gain)


def retention_back_kernel(
    place_ref, live_ref, first_ref, second_ref,
    weight_ref, decay_ref, column_ref, gain_ref, qkv_ref, swish_ref, normed_ref, scale_ref, entry_ref,
    gain_grad_ref, grads_hbm, state, grads_buffer, sems,
):
    step, steps = pl.program_id(0), pl.num_programs(0)
    rows = first_ref.shape[2]
    batches, key_size, value_size = state.shape
    slot = lax.rem(step, 2)

    def sent(at, which, batch):
        return pltpu.make_async_copy(
            grads_buffer.at[which, batch],
            grads_hbm.at[place_ref[batch, steps - 1 - at], batch],
            sems.at[which, batch],
        )

    @pl.when(step == 0)
    def _():
        state[...] = jnp.zeros_like(state)
        gain_grad_ref[...] = jnp.zeros_like(gain_grad_ref)

    @pl.when(step >= 2)
    def _():
        for batch in range(batches):
            sent(step - 2, slot, batch).wait()

    rows_in = jnp.concatenate([first_ref[0, 0], second_ref[0, 0]], axis=0)
    mixed_grads = dot_nt(rows_in, weight_ref[...])
    decay = decay_ref[0]
    entry_decay = column_ref[0, :, 0:1]
    end_weight = column_ref[0, :, 1:2]
    block_decay = column_ref[0, rows - 1 : rows, 0:1]
    positions = (steps - 1 - step) * rows + lax.broadcasted_iota(jnp.int32, (rows, 1), 0)
    gain = gain_ref[...]
    for batch in range(batches):
        live = (positions < live_ref[batch]).astype(FULL)
        mixed_grad = mixed_grads[batch * rows : (batch + 1) * rows]
        query = qkv_ref[batch, 0, :, :key_size]
        key = qkv_ref[batch, 0, :, key_size : 2 * key_size]
        value = qkv_ref[batch, 0, :, 2 * key_size :]
        swish = swish_ref[batch, 0].astype(FULL)
        normed = normed_ref[batch, 0].astype(FULL)
        scale = scale_ref[batch, 0, :, 0:1]
        entry = entry_ref[batch, 0]
        sigmoid = jax.nn.sigmoid(swish)
        silu = swish * sigmoid
        swish_grad = mixed_grad * (normed * gain) * (sigmoid * (1.0 + swish - silu))
        scaled_grad = mixed_grad * silu
        gain_grad_ref[...] += jnp.sum(scaled_grad * normed, axis=0, keepdims=True)
        retained_grad = normalised_back(scaled_grad * gain, normed, scale).astype(HALF)
        weights = (dot_nt(query, key) * decay).astype(HALF)
        scores_grad = (dot_nt(retained_grad, value) * decay).astype(HALF)
        after = state[batch]
        after_low = after.astype(HALF)
        query_grad = dot_nn(scores_grad, key) + entry_decay * dot_nt(retained_grad, entry)
        key_grad = dot_tn(scores_grad, query) + end_weight * dot_nt(value, after_low)
        value_grad = dot_tn(weights, retained_grad) + end_weight * dot_nn(key, after_low)
        query_entered = (query.astype(FULL) * entry_decay).astype(HALF)
        state[batch] = block_decay * after + dot_tn(query_entered, retained_grad)
        grads_buffer[slot, batch, :, :key_size] = query_grad.astype(HALF)
        grads_buffer[slot, batch, :, key_size : 2 * key_size] = (key_grad * live).astype(HALF)
        grads_buffer[slot, batch, :, 2 * key_size : 2 * key_size + value_size] = value_grad.astype(
            HALF
        )
        grads_buffer[slot, batch, :, 2 * key_size + value_size :] = swish_grad.astype(HALF)
        sent(step, slot, batch).start()

    @pl.when(step == steps - 1)
    def _():
        for batch in range(batches):
            sent(step, slot, batch).wait()
            sent(step - 1, 1 - slot, batch).wait()


def retention_back(rows_in, weight, place, live, decay, columns, gain, saved):
    blocks, batches, rows, width = rows_in.shape
    value_size = gain.shape[-1]
    key_size = saved[-1].shape[2]
    total = 2 * key_size + 2 * value_size

    def arriving(batch, size):
        return pl.BlockSpec(
            (1, 1, rows, size),
            lambda i, place, live: (place[batch, blocks - 1 - i], batch, 0, 0),
        )

    def whole(shape):
        return pl.BlockSpec(
            shape, lambda i, place, live: (0,) * len(shape), pipeline_mode=pl.Buffered(1)
        )

    def here(*tail):
        return pl.BlockSpec((batches, 1) + tail, lambda i, place, live: (0, blocks - 1 - i, 0, 0))

    def along(*tail):
        return pl.BlockSpec((1,) + tail, lambda i, place, live: (blocks - 1 - i, 0, 0))

    return pl.pallas_call(
        retention_back_kernel,
        grid_spec=pltpu.PrefetchScalarGridSpec(
            num_scalar_prefetch=2,
            grid=(blocks,),
            in_specs=[
                arriving(0, width),
                arriving(1, width),
                whole((value_size, width)),
                along(rows, rows),
                along(rows, 2),
                whole((1, value_size)),
                here(rows, 2 * key_size + value_size),
                here(rows, value_size),
                here(rows, value_size),
                here(rows, LANES),
                here(key_size, value_size),
            ],
            out_specs=[
                pl.BlockSpec((1, value_size), lambda i, place, live: (0, 0)),
                in_hbm(),
            ],
            scratch_shapes=[
                pltpu.VMEM((batches, key_size, value_size), FULL),
                pltpu.VMEM((2, batches, rows, total), HALF),
                pltpu.SemaphoreType.DMA((2, batches)),
            ],
        ),
        out_shape=[
            jax.ShapeDtypeStruct((1, value_size), FULL),
            jax.ShapeDtypeStruct((blocks, batches, rows, total), HALF),
        ],
        compiler_params=pltpu.CompilerParams(
            dimension_semantics=("arbitrary",), vmem_limit_bytes=VMEM_BYTES
        ),
        cost_estimate=pl.CostEstimate(
            flops=6 * blocks * batches * rows * width * value_size,
            bytes_accessed=2 * blocks * batches * rows * (width + 2 * total)
            + 2 * width * value_size,
            transcendentals=0,
        ),
    )(place, live, rows_in, rows_in, weight, decay, columns, gain, *saved)


def middle_kernel(
    mixed_hbm, weight_hbm, tokens_hbm, gain_ref, hidden_ref, second_out,
    *scratch,
):
    scatter = scratch[:7]
    own, keeps, gather_sends, gather_receives = scratch[7:11]
    weight_ref, tokens_ref, stage_sems, mixed, mixed_sems = scratch[11:]
    peers, groups = lax.axis_size("seq"), lax.axis_size("fsdp")
    sources, targets = (weight_hbm, tokens_hbm), (weight_ref, tokens_ref)
    weight_copy, tokens_copy = staged(sources, targets, stage_sems)
    blocks = Blocks(mixed_hbm, mixed, mixed_sems)
    blocks.begin()
    greet_neighbours()
    weight_copy.wait()

    def term(block):
        return blocks.take(lambda value: dot_nn(value, weight_ref[...]).astype(HALF))

    gain = gain_ref[...]

    def use(start, total):
        rows = pl.ds(start, CHUNK)
        hidden = tokens_ref[rows].astype(FULL) + total
        hidden_ref[rows] = hidden
        normed, _ = normalised(hidden)
        own[rows] = regroup(normed * gain, peers, groups).astype(HALF)

    gathers = [
        PlaneGather(own, second_out, keeps, gather_sends, gather_receives, window, WINDOWS)
        for window in range(WINDOWS)
    ]
    windows = scatter_head(term, scatter)
    tokens_copy.wait()
    scatter_tail(windows, use, lambda window: gathers[window].begin())
    for gather in gathers:
        gather.relay()
    for gather in gathers:
        gather.finish()
    for window in windows:
        window.drain()


def middle(mixed, weight, tokens, gain):
    peers, own, inner = mixed.shape
    width = weight.shape[1]
    return pl.pallas_call(
        middle_kernel,
        in_specs=[in_hbm()] * 3 + [vmem()],
        out_specs=[vmem(), in_hbm()],
        out_shape=[
            jax.ShapeDtypeStruct((own, width), FULL),
            jax.ShapeDtypeStruct((peers, own, width), HALF),
        ],
        scratch_shapes=scatter_scratch(own, width)
        + [pltpu.VMEM((own, width), HALF)]
        + gather_scratch(WINDOWS)
        + stage_scratch(weight, tokens)
        + block_scratch(peers, mixed),
        compiler_params=linked(2),
        cost_estimate=cost(2 * peers * own * inner * width, 4 * peers * own * width),
    )(mixed, weight, tokens, gain)


def middle_back_kernel(
    grads_hbm, weight_hbm, hidden_hbm, outer_hbm, mask_ref, gain_ref,
    hidden_grad_ref, gain_grad_ref, branch_out,
    *scratch,
):
    scatter = scratch[:7]
    own, keeps, gather_sends, gather_receives = scratch[7:11]
    weight_ref, hidden_ref, outer_ref, stage_sems, grads, grad_sems = scratch[11:]
    peers, groups = lax.axis_size("seq"), lax.axis_size("fsdp")
    blocks = Blocks(grads_hbm, grads, grad_sems)
    sources, targets = (weight_hbm, hidden_hbm, outer_hbm), (weight_ref, hidden_ref, outer_ref)
    weight_copy, *later = staged(sources, targets, stage_sems)
    blocks.begin()
    greet_neighbours()
    weight_copy.wait()

    def term(block):
        return blocks.take(lambda value: dot_nt(value, weight_ref[...]).astype(HALF))

    gain = gain_ref[...]
    gain_grad_ref[...] = jnp.zeros_like(gain_grad_ref)

    def use(start, total):
        rows = pl.ds(start, CHUNK)
        grad = regroup(total, groups, peers)
        normed, scale = normalised(hidden_ref[rows])
        gain_grad_ref[...] += jnp.sum(grad * normed, axis=0, keepdims=True)
        outer = outer_ref[rows].astype(FULL) * mask_ref[rows]
        hidden_grad = outer + normalised_back(grad * gain, normed, scale)
        hidden_grad_ref[rows] = hidden_grad
        own[rows] = hidden_grad.astype(HALF)

    gathers = [
        PlaneGather(own, branch_out, keeps, gather_sends, gather_receives, window, WINDOWS)
        for window in range(WINDOWS)
    ]
    windows = scatter_head(term, scatter)
    for copy in later:
        copy.wait()
    scatter_tail(windows, use, lambda window: gathers[window].begin())
    for gather in gathers:
        gather.relay()
    for gather in gathers:
        gather.finish()
    for window in windows:
        window.drain()


def middle_back(grads, weight, hidden, outer, mask, gain):
    peers, own, inner = grads.shape
    width = weight.shape[0]
    return pl.pallas_call(
        middle_back_kernel,
        in_specs=[in_hbm()] * 4 + [vmem()] * 2,
        out_specs=[vmem(), vmem(), in_hbm()],
        out_shape=[
            jax.ShapeDtypeStruct((own, width), FULL),
            jax.ShapeDtypeStruct((1, width), FULL),
            jax.ShapeDtypeStruct((peers, own, width), HALF),
        ],
        scratch_shapes=scatter_scratch(own, width)
        + [pltpu.VMEM((own, width), HALF)]
        + gather_scratch(WINDOWS)
        + stage_scratch(weight, hidden, outer)
        + block_scratch(peers, grads),
        compiler_params=linked(3),
        cost_estimate=cost(2 * peers * own * inner * width, 4 * peers * own * width),
    )(grads, weight, hidden, outer, mask, gain)


class PlaneReturn:
    def __init__(self, cuts, source, targets, keeps, sends, receives):
        self.cuts, self.source, self.targets = cuts, source, targets
        self.keeps, self.sends, self.receives = keeps, sends, receives
        self.peers, self.me = lax.axis_size("seq"), lax.axis_index("seq")

    def part(self, number, peer):
        start, size = self.cuts[number]
        return self.source.at[peer, :, pl.ds(start, size)]

    def place(self, number, peer):
        size = self.cuts[number][1]
        return self.targets[number].at[:, pl.ds(pl.multiple_of(peer * size, LANES), size)]

    def sent(self, source, target, number, turn, peer):
        at = (number, turn)
        return to_peer(source, target, self.sends.at[at], self.receives.at[at], peer)

    def copy(self, number, turn):
        peer = lax.rem(self.me + turn, self.peers)
        return self.sent(
            self.part(number, peer), self.place(number, self.me), number, turn, peer
        )

    def landed(self, number, turn):
        peer = lax.rem(self.me + self.peers - turn, self.peers)
        target = self.place(number, peer)
        return self.sent(target, target, number, turn, peer)

    def kept(self, number):
        return pltpu.make_async_copy(
            self.part(number, self.me), self.place(number, self.me), self.keeps.at[number]
        )

    def begin(self, turn):
        for number in range(len(self.cuts)):
            if turn > 0:
                self.copy(number, turn).start()
            else:
                self.kept(number).start()

    def finish(self):
        for number in range(len(self.cuts)):
            for turn in range(1, self.peers):
                self.landed(number, turn).wait_recv()
                self.copy(number, turn).wait_send()
            self.kept(number).wait()


class LineSum:
    def __init__(self, terms, landed, own, final, loads, sends, receives):
        self.terms, self.landed, self.own, self.final = terms, landed, own, final
        self.loads, self.sends, self.receives = loads, sends, receives
        self.me, self.last = lax.axis_index("fsdp"), lax.axis_size("fsdp") - 1
        self.peers, self.place = lax.axis_size("seq"), lax.axis_index("seq")

    def piece(self, turn):
        return lax.rem(self.place + turn, self.peers)

    def depth(self, way):
        return self.me if way == 0 else self.last - self.me

    def block(self, way, order):
        return self.last - order if way == 0 else order

    def slot(self, way, order):
        return order if way == 0 else 2 * self.last - 2 - order

    def sent(self, source, way, order, turn):
        at = (way, order, turn)
        return pltpu.make_async_remote_copy(
            src_ref=source,
            dst_ref=self.landed.at[self.slot(way, order), self.piece(turn)],
            send_sem=self.sends.at[at],
            recv_sem=self.receives.at[at],
            device_id={"fsdp": self.me + 1 if way == 0 else self.me - 1},
            device_id_type=MESH,
        )

    def first(self, way, order, turn):
        source = self.terms.at[self.block(way, order), self.piece(turn)]
        return self.sent(source, way, order, turn)

    def onward(self, way, order, turn):
        source = self.landed.at[self.slot(way, order), self.piece(turn)]
        return self.sent(source, way, order, turn)

    def load(self, way, order):
        return pltpu.make_async_copy(
            self.terms.at[self.block(way, order)], self.own.at[way], self.loads.at[way]
        )

    def load_final(self):
        return pltpu.make_async_copy(self.terms.at[self.me], self.final, self.loads.at[2])

    def begin(self):
        for way in (0, 1):

            @pl.when(self.depth(way) == 0)
            def _():
                for order in range(self.last):
                    for turn in range(self.peers):
                        self.first(way, order, turn).start()

            self.load(way, 0).start()
        self.load_final().start()

    def loaded(self, order):
        for way in (0, 1):
            self.load(way, order).wait()

    def load_next(self, order):
        for way in (0, 1):
            self.load(way, order).start()

    def hand_on(self, order, depth, turns):
        for turn in turns:
            for way in (0, 1):

                @pl.when(self.depth(way) == depth)
                def _():
                    at, piece = self.slot(way, order), self.piece(turn)
                    self.onward(way, order, turn).wait_recv()
                    self.landed[at, piece] = (
                        self.landed[at, piece].astype(FULL) + self.own[way, piece].astype(FULL)
                    ).astype(HALF)
                    self.onward(way, order, turn).start()

    def finish(self, use):
        self.load_final().wait()
        for turn in range(self.peers):
            piece = self.piece(turn)
            for way in (0, 1):

                @pl.when(self.depth(way) > 0)
                def _():
                    order = self.last - self.depth(way)
                    self.onward(way, order, turn).wait_recv()
                    self.final[piece] = (
                        self.final[piece].astype(FULL)
                        + self.landed[self.slot(way, order), piece].astype(FULL)
                    ).astype(HALF)

            use(turn)

    def drain(self):
        for way in (0, 1):
            for order in range(self.last):
                for turn in range(self.peers):

                    @pl.when(self.depth(way) == 0)
                    def _():
                        self.first(way, order, turn).wait_send()

                    @pl.when((self.depth(way) > 0) & (self.depth(way) < self.last - order))
                    def _():
                        self.onward(way, order, turn).wait_send()


def line_scratch(groups, peers, slab, columns):
    block = (peers, slab, columns)
    return [
        pltpu.VMEM((2 * groups - 3,) + block, HALF),
        pltpu.VMEM((2,) + block, HALF),
        pltpu.VMEM(block, HALF),
        pltpu.SemaphoreType.DMA((3,)),
        pltpu.SemaphoreType.DMA((2, groups - 1, peers)),
        pltpu.SemaphoreType.DMA((2, groups - 1, peers)),
    ]


def last_kernel(
    cuts, line_cuts, grads_hbm, weight_hbm, tokens_hbm, hidden_grad_hbm, gain_ref, second_grad_ref,
    group_grad_ref, inner_hbm, down_hbm, hidden_hbm, mask_ref, summed_ref, terms_ref,
    *refs,
):
    count, line_count = len(cuts), len(line_cuts)
    input_ref, output_ref, gains_ref, group_ref = refs[:4]
    returned, refs = refs[4 : 4 + count], refs[4 + count :]
    line_returned, scratch = refs[:line_count], refs[line_count:]
    scatter, result = scratch[:7], scratch[:1] + scratch[7:13]
    (
        sums, parts, across, totals, first_grad, keep, part_sends, part_receives,
        group_keep, group_sends, group_receives,
    ) = scratch[13:24]
    peers, groups = lax.axis_size("seq"), lax.axis_size("fsdp")
    me = lax.axis_index("seq")
    grads, grad_sems = scratch[36:38]
    inner_ref = scratch[38]
    weight_ref, down_ref, hidden_ref, tokens_ref, hidden_grad_ref, stage_sems = scratch[39:]
    blocks = Blocks(grads_hbm, grads, grad_sems)
    weight_copy, inner_copy, down_copy, *later = staged(
        (weight_hbm, inner_hbm, down_hbm, hidden_hbm, tokens_hbm, hidden_grad_hbm),
        (weight_ref, inner_ref, down_ref, hidden_ref, tokens_ref, hidden_grad_ref),
        stage_sems,
    )
    blocks.begin()
    greet_plane(True)
    back = PlaneReturn(cuts, summed_ref, returned, *scratch[24:27])
    line_back = PlaneReturn(line_cuts, scratch[32], line_returned, *scratch[27:30])
    line = LineSum(terms_ref, *scratch[30:36])

    def term(block):
        return blocks.take(lambda value: dot_nt(value, weight_ref[...]).astype(HALF))

    def result_term(block):
        return dot_nn(inner_ref[block], down_ref[...]).astype(HALF)

    gain = gain_ref[...]
    first_grad[...] = jnp.zeros_like(first_grad)

    def use(start, total):
        rows = pl.ds(start, CHUNK)
        grad = regroup(total, groups, peers)
        normed, scale = normalised(tokens_ref[rows].astype(FULL))
        first_grad[...] += jnp.sum(grad * normed, axis=0, keepdims=True)
        input_ref[rows] = (
            hidden_grad_ref[rows] + normalised_back(grad * gain, normed, scale)
        ).astype(HALF)

    def use_result(start, total):
        rows = pl.ds(start, CHUNK)
        output_ref[rows] = ((hidden_ref[rows] + total) * mask_ref[rows]).astype(HALF)

    line.begin()
    weight_copy.wait()
    every, early, late = range(peers), range(peers // 2), range(peers // 2, peers)
    windows = scatter_head(term, scatter, (), True)
    windows[0].relay()
    line.loaded(0)
    line.hand_on(0, 1, every)
    windows[1].relay()
    inner_copy.wait()
    down_copy.wait()
    result_windows = scatter_head(result_term, result, windows, True)
    for turn in every:
        back.begin(turn)
    result_windows[0].relay()
    line.hand_on(0, 2, every)
    line.load_next(1)
    for copy in later:
        copy.wait()
    scatter_tail(windows, use)
    line.loaded(1)
    line.hand_on(1, 1, early)
    result_windows[1].relay()
    tile = LANES * 2
    for peer in range(peers):
        for row in range(tile // LANES):
            at = peer * tile + row * LANES
            sums[peer, row : row + 1] = first_grad[:, at : at + LANES]
            sums[peer, 2 + row : 3 + row] = second_grad_ref[:, at : at + LANES]
        sums[peer, 4:8] = jnp.zeros((4, LANES), FULL)

    def copy(turn):
        peer = lax.rem(me + turn, peers)
        return to_peer(
            sums.at[peer], parts.at[turn], part_sends.at[turn], part_receives.at[turn], peer
        )

    kept = pltpu.make_async_copy(sums.at[me], parts.at[0], keep)
    kept.start()
    for turn in range(1, peers):
        copy(turn).start()
    line.hand_on(1, 1, late)
    scatter_tail(result_windows, use_result)
    kept.wait()
    for turn in range(1, peers):
        copy(turn).wait_recv()
        copy(turn).wait_send()
    total = parts[0]
    for turn in range(1, peers):
        total += parts[turn]
    across[0:8] = total
    for row in range(4):
        across[8 + row : 9 + row] = group_grad_ref[:, row * LANES : (row + 1) * LANES]
    across[12:16] = jnp.zeros((4, LANES), FULL)
    begin, finish = all_to_each(
        across, totals, "fsdp", groups, group_keep, group_sends, group_receives
    )
    begin()
    line.finish(line_back.begin)
    back.finish()
    line_back.finish()
    line.drain()
    for window in windows:
        window.drain(4)
    for window in result_windows:
        window.drain()
    finish()
    summed = totals[0]
    for turn in range(1, groups):
        summed += totals[turn]
    gains_ref[...] = summed[0:8]
    group_ref[...] = summed[8:16]


def last_rows(
    grads, weight, tokens, hidden_grad, gain, second_grad, group_grad, inner, down, hidden, mask,
    summed, sizes, terms, line_sizes,
):
    peers, own, size = grads.shape
    groups = lax.axis_size("fsdp")
    width = weight.shape[0]
    slab = summed.shape[1]

    def cuts_of(sizes):
        return tuple((sum(sizes[:number]), sizes[number]) for number in range(len(sizes)))

    return pl.pallas_call(
        partial(last_kernel, cuts_of(sizes), cuts_of(line_sizes)),
        in_specs=[in_hbm()] * 4 + [vmem()] * 3 + [in_hbm()] * 3 + [vmem()] + [in_hbm()] * 2,
        out_specs=[vmem()] * 4 + [in_hbm()] * len(sizes + line_sizes),
        out_shape=[
            jax.ShapeDtypeStruct((own, width), HALF),
            jax.ShapeDtypeStruct((own, width), HALF),
            jax.ShapeDtypeStruct((8, LANES), FULL),
            jax.ShapeDtypeStruct((8, LANES), FULL),
        ]
        + [jax.ShapeDtypeStruct((slab, peers * part), HALF) for part in sizes + line_sizes],
        scratch_shapes=scatter_scratch(own, width)
        + scatter_scratch(own, width)[1:]
        + [
            pltpu.VMEM((peers, 8, LANES), FULL),
            pltpu.VMEM((peers, 8, LANES), FULL),
            pltpu.VMEM((16, LANES), FULL),
            pltpu.VMEM((groups, 16, LANES), FULL),
            pltpu.VMEM((1, width), FULL),
            pltpu.SemaphoreType.DMA,
            pltpu.SemaphoreType.DMA((peers,)),
            pltpu.SemaphoreType.DMA((peers,)),
            pltpu.SemaphoreType.DMA,
            pltpu.SemaphoreType.DMA((groups,)),
            pltpu.SemaphoreType.DMA((groups,)),
        ]
        + swap_scratch(len(sizes), peers)
        + swap_scratch(len(line_sizes), peers)
        + line_scratch(groups, peers, slab, terms.shape[3])
        + block_scratch(2, grads)
        + [pltpu.VMEM(inner.shape, HALF)]
        + stage_scratch(weight, down, hidden, tokens, hidden_grad, inner)[:5]
        + [pltpu.SemaphoreType.DMA((6,))],
        compiler_params=pltpu.CompilerParams(
            collective_id=5, has_side_effects=True, vmem_limit_bytes=LARGE_BYTES
        ),
        cost_estimate=cost(
            2 * peers * own * (size + inner.shape[2]) * width, 5 * peers * own * width
        ),
    )(
        grads, weight, tokens, hidden_grad, gain, second_grad, group_grad, inner, down, hidden, mask,
        summed, terms,
    )


def widen_kernel(*refs):
    count = len(refs) // 2
    for source, target in zip(refs[:count], refs[count:]):
        target[...] = source[...].astype(target.dtype)


def widen(*arrays):
    return pl.pallas_call(
        widen_kernel,
        in_specs=[vmem()] * len(arrays),
        out_specs=[vmem()] * len(arrays),
        out_shape=[jax.ShapeDtypeStruct(array.shape, FULL) for array in arrays],
        compiler_params=pltpu.CompilerParams(vmem_limit_bytes=VMEM_BYTES),
    )(*arrays)


def head_body(
    tokens,
    cotangent,
    lengths,
    block_order,
    log_decay,
    first_gain,
    query_weight,
    key_weight,
    value_weight,
    swish_weight,
    output_weight,
    group_gain,
    second_gain,
    feed_gate,
    feed_up,
    feed_down,
):
    peers, groups = lax.axis_size("seq"), lax.axis_size("fsdp")
    group = lax.axis_index("fsdp")
    batches, rows, width = tokens.shape
    own = batches * rows
    heads = log_decay.shape[0]
    key_size = query_weight.shape[1] // heads
    value_size = value_weight.shape[1] // heads
    part = feed_gate.shape[1] // peers
    slab = query_weight.shape[0]
    total = 2 * key_size + 2 * value_size

    def over_groups(local):
        return lax.all_gather(local, "fsdp", axis=0, tiled=True)

    def sum_groups(whole):
        return lax.psum_scatter(whole.astype(HALF), "fsdp", scatter_dimension=0, tiled=True)

    def gathered(cut):
        return over_groups(cut[None]).reshape(width, cut.shape[2])

    gains = jnp.concatenate(
        [
            group_gain.astype(FULL)[None],
            jnp.concatenate([first_gain, second_gain]).astype(FULL)[None],
            jnp.zeros((6, LANES), FULL),
        ],
        axis=0,
    )
    first_cut, rates, gains = first_swap(
        query_weight, key_weight, value_weight, swish_weight, log_decay, gains
    )
    out_weight = over_groups(output_weight)
    order = lax.dynamic_slice_in_dim(block_order, group * batches, batches, 0)
    numbers = jnp.arange(peers, dtype=jnp.int32)
    place = jnp.sum(
        numbers[None, None, :] * (order[:, None, :] == numbers[None, :, None]).astype(jnp.int32),
        axis=2,
    )
    live = lax.dynamic_slice_in_dim(lengths, group * batches, batches, 0)

    token_rows = tokens.reshape(own, width)
    outer_rows = cotangent.reshape(own, width)
    (
        entered, result_low, feed_cut, first_weight,
        mask, gain_one, gain_two, gain_group, decay, columns,
    ) = gather_inputs(
        lengths, block_order, token_rows, outer_rows, gains, rates, feed_gate, feed_up, first_cut,
        value_size,
    )
    first_weight = first_weight.reshape(width, total)
    entered, out_weight = lax.optimization_barrier((entered, out_weight))
    feed_weight = gathered(feed_cut)

    *saved, mixed = retention(
        entered.reshape(peers, batches, rows, width),
        first_weight,
        place,
        live,
        decay,
        columns,
        gain_group,
        key_size,
    )
    entered = entered.reshape(peers * own, width)
    mixed, feed_down = lax.optimization_barrier((mixed, feed_down))
    down_weight = over_groups(feed_down)
    mixed = mixed.reshape(peers * own, value_size)
    hidden, second = middle(mixed.reshape(peers, own, value_size), out_weight, token_rows, gain_two)
    second = second.reshape(peers * own, width)
    result_low = result_low.reshape(peers * own, width)
    inner_low, up_slope, gate_slope = feed(second, feed_weight)
    down_term, late_low = lax.optimization_barrier(
        (dot_tn(inner_low, result_low).astype(HALF), result_low)
    )
    down_grad = sum_groups(down_term)
    both_grad = feed_back(late_low, down_weight, up_slope, gate_slope)
    both_term, both_grad = lax.optimization_barrier(
        (dot_tn(second, both_grad).astype(HALF), both_grad)
    )
    both_weight_grad = sum_groups(both_term).reshape(peers, slab, 2 * part)
    hidden_grad, second_gain_grad, branch_low = middle_back(
        both_grad.reshape(peers, own, 2 * part),
        feed_weight,
        hidden,
        outer_rows,
        mask,
        gain_two,
    )
    out_term, branch_low, down_grad = lax.optimization_barrier(
        (dot_tn(mixed, branch_low.reshape(peers * own, width)).astype(HALF), branch_low, down_grad)
    )
    out_grad = sum_groups(out_term)
    group_gain_grad, projected_grad = retention_back(
        branch_low.reshape(peers, batches, rows, width),
        out_weight,
        place,
        live,
        decay,
        columns,
        gain_group,
        saved,
    )
    flat_grad = projected_grad.reshape(peers * own, total)
    first_term = dot_tn(entered, flat_grad).astype(HALF)
    (
        input_rows, output_rows, gain_grads, group_grads,
        gate_back, up_back, query_back, key_back, value_back, swish_back,
    ) = last_rows(
        projected_grad.reshape(peers, own, total),
        first_weight,
        token_rows,
        hidden_grad,
        gain_one,
        second_gain_grad,
        group_gain_grad,
        inner_low.reshape(peers, own, part),
        down_weight,
        hidden,
        mask,
        both_weight_grad,
        (part, part),
        first_term.reshape(groups, peers, slab, total),
        (key_size, key_size, value_size, value_size),
    )
    out_grad, output_rows = lax.optimization_barrier((out_grad, output_rows))
    query_back, key_back, value_back, swish_back, gate_back, up_back, down_back, out_back = widen(
        query_back, key_back, value_back, swish_back, gate_back, up_back, down_grad, out_grad
    )

    def mine(summed, start):
        flat = summed[start : start + 2].reshape(groups, slab)
        return lax.dynamic_index_in_dim(flat, group, 0, keepdims=False)

    return (
        output_rows.reshape(batches, rows, width),
        input_rows.reshape(batches, rows, width),
        mine(gain_grads, 0),
        query_back,
        key_back,
        value_back,
        swish_back,
        out_back,
        lax.dynamic_index_in_dim(group_grads, group, 0, keepdims=False),
        mine(gain_grads, 2),
        gate_back,
        up_back,
        down_back,
    )


def body(*arrays):
    peers, groups = lax.axis_size("seq"), lax.axis_size("fsdp")
    fits = peers == 8 and groups == 4 and arrays[4].shape[0] == peers and arrays[0].shape[0] == 2
    if fits:
        return head_body(*arrays)
    return general_body(*arrays)


def solution(mesh):
    placed = (
        P("fsdp", "seq", None),
        P("fsdp", "seq", None),
        P(),
        P(),
        P(None, "seq"),
        P(("seq", "fsdp")),
        P(("seq", "fsdp"), None),
        P(("seq", "fsdp"), None),
        P(("seq", "fsdp"), None),
        P(("seq", "fsdp"), None),
        P(("seq", "fsdp"), None),
        P(("seq", "fsdp")),
        P(("seq", "fsdp")),
        P(("seq", "fsdp"), None),
        P(("seq", "fsdp"), None),
        P(("seq", "fsdp"), None),
    )
    return jax.shard_map(
        body,
        mesh=mesh,
        in_specs=placed,
        out_specs=(
            P("fsdp", "seq", None),
            P("fsdp", "seq", None),
            P(("seq", "fsdp")),
            P(("seq", "fsdp"), None),
            P(("seq", "fsdp"), None),
            P(("seq", "fsdp"), None),
            P(("seq", "fsdp"), None),
            P(("seq", "fsdp"), None),
            P(("seq", "fsdp")),
            P(("seq", "fsdp")),
            P(("seq", "fsdp"), None),
            P(("seq", "fsdp"), None),
            P(("seq", "fsdp"), None),
        ),
        check_vma=False,
    )
```

```python
from functools import partial, reduce

import jax
import jax.numpy as jnp
from jax import lax
from jax.experimental import pallas as pl
from jax.experimental.pallas import tpu as pltpu
from jax.sharding import PartitionSpec as P

EPSILON = 1e-05
HIGHEST = lax.Precision.HIGHEST


def carried_in(value, axis, combine, identity, reverse):
    peers, index = (lax.axis_size(axis), lax.axis_index(axis))
    everything = jax.tree.map(
        lambda part, kind: lax.all_gather(part.astype(kind), axis),
        value,
        (jnp.bfloat16, jnp.bfloat16),
    )
    start = jax.tree.map(
        lambda part, zero: jnp.broadcast_to(jnp.asarray(zero, part.dtype), part.shape),
        value,
        identity,
    )

    def turn(k, before):
        at = peers - 1 - k if reverse else k
        reached = at > index if reverse else at < index
        new = combine(
            before, jax.tree.map(lambda part, own: part[at].astype(own.dtype), everything, value)
        )
        return jax.tree.map(lambda a, b: jnp.where(reached, a, b), new, before)

    return lax.fori_loop(0, peers, turn, start)


def norm_rows(values, gain):
    average = jnp.mean(values, axis=-1, keepdims=True)
    centered = values - average
    variance = jnp.mean(centered * centered, axis=-1, keepdims=True)
    return centered * lax.rsqrt(variance + EPSILON) * gain


def gated_swish(swish_in, grouped):
    return jax.nn.silu(swish_in) * grouped


def gated_gelu(gate_in, upward):
    return jax.nn.gelu(gate_in) * upward


def chain_states(earlier, later):
    return (earlier[0] * later[0], later[0][:, None, None] * earlier[1] + later[1])


def transposed(left_rows, weight):
    return jnp.einsum("ie,fe->if", left_rows, weight, preferred_element_type=jnp.float32)


def plain_dot(left_rows, weight):
    return jnp.dot(left_rows, weight, preferred_element_type=jnp.float32)


def outer_term(left_rows, right_rows):
    return jnp.einsum("ni,no->io", left_rows, right_rows, preferred_element_type=jnp.float32)


def spread_sum(matrix_pairs, vectors):
    terms = tuple((outer_term(left_rows, right_rows) for left_rows, right_rows in matrix_pairs))
    pieces = lax.psum_scatter(
        terms + tuple(vectors), ("seq", "fsdp"), scatter_dimension=0, tiled=True
    )
    return list(pieces)


def join_terms(collected):
    matrix_pairs = []
    for member in range(len(collected[0][0])):
        lefts = jnp.concatenate([entry[0][member][0] for entry in collected], axis=0)
        rights = jnp.concatenate([entry[0][member][1] for entry in collected], axis=0)
        matrix_pairs.append((lefts, rights))
    vectors = [
        reduce(jnp.add, [entry[1][member] for entry in collected])
        for member in range(len(collected[0][1]))
    ]
    return (matrix_pairs, vectors)


def layer_step(gathered, inputs, cot_rows, live_mask, log_rates):
    (
        first_gain,
        query_weight,
        key_weight,
        value_weight,
        swish_weight,
        output_weight,
        group_gain,
        second_gain,
        feed_gate,
        feed_up,
        feed_down,
    ) = gathered
    floats = jnp.float32
    halves = jnp.bfloat16
    head_count = log_rates.shape[0]
    token_rows = inputs.shape[0]
    key_size = query_weight.shape[1] // head_count
    value_size = value_weight.shape[1] // head_count
    start_values = inputs.astype(floats)
    normed_one, pull_one = jax.vjp(norm_rows, start_values, first_gain.astype(floats))
    normed = normed_one.astype(halves)
    queries = plain_dot(normed, query_weight).astype(halves)
    keys_in = plain_dot(normed, key_weight).astype(halves) * live_mask[:, None].astype(halves)
    values_in = plain_dot(normed, value_weight).astype(halves)
    swish_in = plain_dot(normed, swish_weight)
    queries3 = queries.reshape(token_rows, head_count, key_size)
    keys3 = keys_in.reshape(token_rows, head_count, key_size)
    values3 = values_in.reshape(token_rows, head_count, value_size)
    cumulative = jnp.cumsum(log_rates, axis=1)
    slot_index = jnp.arange(token_rows)
    lower_mask = slot_index[:, None] >= slot_index[None, :]
    spread = cumulative[:, :, None] - cumulative[:, None, :]
    decay_matrix = jnp.where(lower_mask, jnp.exp(jnp.where(lower_mask, spread, 0.0)), 0.0)
    block_decay = jnp.exp(cumulative[:, -1])
    end_weight = jnp.exp(cumulative[:, -1:] - cumulative).T[:, :, None]
    entry_decay = jnp.exp(cumulative).T[:, :, None]
    query_wide = queries3.astype(floats)
    key_wide = keys3.astype(floats)
    value_wide = values3.astype(floats)
    state_term = jnp.einsum("jhd,jhe->hde", key_wide * end_weight, value_wide, precision=HIGHEST)
    state_identity = (jnp.ones_like(block_decay), jnp.zeros_like(state_term))
    _, start_state = carried_in(
        (block_decay, state_term), "seq", chain_states, state_identity, False
    )
    scores = jnp.einsum("ihd,jhd->hij", queries3, keys3, preferred_element_type=floats)
    weights = (scores * decay_matrix).astype(halves)
    intra_term = jnp.einsum("hij,jhe->ihe", weights, values3, preferred_element_type=floats)
    carried = entry_decay * jnp.einsum("ihd,hde->ihe", query_wide, start_state, precision=HIGHEST)
    retained = intra_term + carried
    grouped, pull_group = jax.vjp(
        norm_rows, retained, group_gain.astype(floats).reshape(head_count, value_size)
    )
    grouped_flat = grouped.reshape(token_rows, head_count * value_size)
    mixed_float, pull_mixed = jax.vjp(gated_swish, swish_in, grouped_flat)
    mixed_low = mixed_float.astype(halves)
    hidden = start_values + plain_dot(mixed_low, output_weight)
    normed_two, pull_two = jax.vjp(norm_rows, hidden, second_gain.astype(floats))
    second = normed_two.astype(halves)
    gate_two = plain_dot(second, feed_gate)
    upward = plain_dot(second, feed_up)
    inner_float, pull_inner = jax.vjp(gated_gelu, gate_two, upward)
    inner_low = inner_float.astype(halves)
    result = plain_dot(inner_low, feed_down)
    output_rows = ((hidden + result) * live_mask[:, None]).astype(halves)
    outer_grad = cot_rows.astype(floats) * live_mask[:, None]
    result_low = outer_grad.astype(halves)
    inner_grad = transposed(result_low, feed_down)
    gate_two_grad, upward_grad = pull_inner(inner_grad)
    gate_two_low = gate_two_grad.astype(halves)
    upward_low = upward_grad.astype(halves)
    second_grad = transposed(gate_two_low, feed_gate) + transposed(upward_low, feed_up)
    hidden_part, second_gain_grad = pull_two(second_grad)
    hidden_grad = outer_grad + hidden_part
    branch_low = hidden_grad.astype(halves)
    mixed_grad = transposed(branch_low, output_weight)
    swish_grad, grouped_grad = pull_mixed(mixed_grad)
    swish_low = swish_grad.astype(halves)
    retained_grad, group_gain_grad = pull_group(
        grouped_grad.reshape(token_rows, head_count, value_size)
    )
    retained_low = retained_grad.astype(halves)
    weights_grad = jnp.einsum("ihe,jhe->hij", retained_low, values3, preferred_element_type=floats)
    scores_low = (weights_grad * decay_matrix).astype(halves)
    query_intra = jnp.einsum("hij,jhd->ihd", scores_low, keys3, preferred_element_type=floats)
    key_intra = jnp.einsum("hij,ihd->jhd", scores_low, queries3, preferred_element_type=floats)
    value_intra = jnp.einsum("hij,ihe->jhe", weights, retained_low, preferred_element_type=floats)
    retained_wide = retained_low.astype(floats)
    query_carried = entry_decay * jnp.einsum(
        "ihe,hde->ihd", retained_wide, start_state, precision=HIGHEST
    )
    local_grad = jnp.einsum(
        "ihd,ihe->hde", query_wide * entry_decay, retained_wide, precision=HIGHEST
    )
    _, end_grad = carried_in((block_decay, local_grad), "seq", chain_states, state_identity, True)
    key_state = end_weight * jnp.einsum("jhe,hde->jhd", value_wide, end_grad, precision=HIGHEST)
    value_state = end_weight * jnp.einsum("jhd,hde->jhe", key_wide, end_grad, precision=HIGHEST)
    query_low = (
        (query_intra + query_carried).astype(halves).reshape(token_rows, head_count * key_size)
    )
    key_low = (
        ((key_intra + key_state) * live_mask[:, None, None])
        .astype(halves)
        .reshape(token_rows, head_count * key_size)
    )
    value_low = (
        (value_intra + value_state).astype(halves).reshape(token_rows, head_count * value_size)
    )
    normed_grad = (
        transposed(query_low, query_weight)
        + transposed(key_low, key_weight)
        + transposed(value_low, value_weight)
        + transposed(swish_low, swish_weight)
    )
    input_part, first_gain_grad = pull_one(normed_grad)
    grad_rows = (hidden_grad + input_part).astype(halves)
    matrix_pairs = [
        (normed, query_low),
        (normed, key_low),
        (normed, value_low),
        (normed, swish_low),
        (mixed_low, branch_low),
        (second, gate_two_low),
        (second, upward_low),
        (inner_low, result_low),
    ]
    vectors = [first_gain_grad, group_gain_grad.reshape(-1), second_gain_grad]
    return (output_rows, grad_rows, matrix_pairs, vectors)


def general_body(
    tokens,
    cotangent,
    lengths,
    block_order,
    log_decay,
    first_gain,
    query_weight,
    key_weight,
    value_weight,
    swish_weight,
    output_weight,
    group_gain,
    second_gain,
    feed_gate,
    feed_up,
    feed_down,
):
    batches = tokens.shape[0]
    block_rows = tokens.shape[1]
    selected_locations = lax.axis_size("seq")
    position = lax.axis_index("seq")
    group_index = lax.axis_index("fsdp")
    place_numbers = jnp.arange(selected_locations, dtype=jnp.int32)
    arrived_tokens, arrived_cotangent = (
        lax.all_gather(tokens, "seq", axis=1, tiled=True),
        lax.all_gather(cotangent, "seq", axis=1, tiled=True),
    )
    gathered = (
        lax.all_gather(first_gain, ("seq", "fsdp"), axis=0, tiled=True),
        lax.all_gather(query_weight, ("seq", "fsdp"), axis=0, tiled=True),
        lax.all_gather(key_weight, ("seq", "fsdp"), axis=0, tiled=True),
        lax.all_gather(value_weight, ("seq", "fsdp"), axis=0, tiled=True),
        lax.all_gather(swish_weight, ("seq", "fsdp"), axis=0, tiled=True),
        lax.all_gather(output_weight, ("seq", "fsdp"), axis=0, tiled=True),
        lax.all_gather(group_gain, ("seq", "fsdp"), axis=0, tiled=True),
        lax.all_gather(second_gain, ("seq", "fsdp"), axis=0, tiled=True),
        lax.all_gather(feed_gate, ("seq", "fsdp"), axis=0, tiled=True),
        lax.all_gather(feed_up, ("seq", "fsdp"), axis=0, tiled=True),
        lax.all_gather(feed_down, ("seq", "fsdp"), axis=0, tiled=True),
    )
    outputs = []
    input_grads = []
    collected = []
    order_rows = []
    for batch_number in range(batches):
        sequence = group_index * batches + batch_number
        order_row = lax.dynamic_index_in_dim(block_order, sequence, 0, keepdims=False)
        order_rows.append(order_row)
        source = jnp.sum(place_numbers * (order_row == position).astype(jnp.int32))
        token_rows = lax.dynamic_slice_in_dim(
            arrived_tokens[batch_number], source * block_rows, block_rows, 0
        )
        cot_rows = lax.dynamic_slice_in_dim(
            arrived_cotangent[batch_number], source * block_rows, block_rows, 0
        )
        live_length = lax.dynamic_index_in_dim(lengths, sequence, 0, keepdims=False)
        location_number = position * block_rows + jnp.arange(block_rows, dtype=jnp.int32)
        live_mask = (location_number < live_length).astype(jnp.float32)
        output_rows, grad_rows, matrix_pairs, vectors = layer_step(
            gathered, token_rows, cot_rows, live_mask, log_decay
        )
        outputs.append(output_rows)
        input_grads.append(grad_rows)
        collected.append((matrix_pairs, vectors))
    joined_pairs, joined_vectors = join_terms(collected)
    shards = spread_sum(joined_pairs, joined_vectors)
    every_output, every_grad = (
        lax.all_gather(jnp.stack(outputs), "seq", axis=1, tiled=True),
        lax.all_gather(jnp.stack(input_grads), "seq", axis=1, tiled=True),
    )
    returned = []
    returned_grads = []
    for batch_number in range(batches):
        target = lax.dynamic_index_in_dim(order_rows[batch_number], position, 0, keepdims=False)
        returned.append(
            lax.dynamic_slice_in_dim(every_output[batch_number], target * block_rows, block_rows, 0)
        )
        returned_grads.append(
            lax.dynamic_slice_in_dim(every_grad[batch_number], target * block_rows, block_rows, 0)
        )
    return (
        jnp.stack(returned),
        jnp.stack(returned_grads),
        shards[8],
        shards[0],
        shards[1],
        shards[2],
        shards[3],
        shards[4],
        shards[9],
        shards[10],
        shards[5],
        shards[6],
        shards[7],
    )


FULL = jnp.float32
HALF = jnp.bfloat16
MESH = pl.DeviceIdType.MESH
VMEM_BYTES = 56 * 1024 * 1024
LARGE_BYTES = 63 * 1024 * 1024
LANES = 128


def dot_nn(left, right):
    return jnp.dot(left, right, preferred_element_type=FULL)


def dot_nt(left, right):
    return lax.dot_general(left, right, (((1,), (1,)), ((), ())), preferred_element_type=FULL)


def dot_tn(left, right):
    return lax.dot_general(left, right, (((0,), (0,)), ((), ())), preferred_element_type=FULL)


def plane_peers():
    me = lax.axis_index("seq")
    core = lax.rem(me, 2)
    across = 2 - 4 * lax.rem(me // 2, 2)
    down = 4 - 8 * (me // 4)
    return me, me + 1 - 2 * core, me + across, me + down, me + across + down


def to_peer(source, target, send, receive, peer):
    return pltpu.make_async_remote_copy(
        src_ref=source,
        dst_ref=target,
        send_sem=send,
        recv_sem=receive,
        device_id={"seq": peer},
        device_id_type=MESH,
    )


def greet_neighbours():
    _, other, near, below, _ = plane_peers()
    barrier = pltpu.get_barrier_semaphore()
    for peer in (other, near, below):
        pl.semaphore_signal(barrier, inc=1, device_id={"seq": peer}, device_id_type=MESH)
    pl.semaphore_wait(barrier, 3)


GATHER_COPIES = 14


def gather_plan():
    me, other, near, below, far = plane_peers()
    flip = other - me
    return (
        (me, 0, near, near),
        (me, 1, below, below),
        (me, 0, other, other),
        (me, 1, other, other),
        (me, 1, near, near),
        (me, 0, below, below),
        (near, 0, below, far),
        (below, 1, near, far),
        (near, 0, other, near + flip),
        (below, 1, other, below + flip),
        (near, 1, other, near + flip),
        (below, 0, other, below + flip),
        (far, 0, other, far + flip),
        (far, 1, other, far + flip),
    )


class PlaneGather:
    def __init__(self, own, out, keeps, sends, receives, window=0, windows=1):
        self.own, self.out = own, out
        self.keep, self.sends, self.receives = keeps.at[window], sends, receives
        self.size = own.shape[0] // windows
        self.window, self.start = window, window * self.size
        self.half = self.size // 2

    def rows(self, which):
        return pl.ds(self.start + which * self.half, self.half)

    def kept(self):
        me = lax.axis_index("seq")
        rows = pl.ds(self.start, self.size)
        return pltpu.make_async_copy(self.own.at[rows], self.out.at[me, rows], self.keep)

    def sent(self, source, target, number, peer):
        at = (self.window, number)
        return to_peer(source, target, self.sends.at[at], self.receives.at[at], peer)

    def copy(self, number):
        block, which, peer, _ = gather_plan()[number]
        target = self.out.at[block, self.rows(which)]
        source = self.own.at[self.rows(which)] if number < 6 else target
        return self.sent(source, target, number, peer)

    def landed(self, number):
        _, which, peer, landing = gather_plan()[number]
        target = self.out.at[landing, self.rows(which)]
        self.sent(target, target, number, peer).wait_recv()

    def begin(self):
        self.kept().start()
        for number in range(6):
            self.copy(number).start()

    def relay(self):
        for arrived, onward in ((0, (6, 8)), (1, (7, 9)), (4, (10,)), (5, (11,))):
            self.landed(arrived)
            for number in onward:
                self.copy(number).start()

    def finish(self):
        for arrived, onward in ((6, 12), (7, 13)):
            self.landed(arrived)
            self.copy(onward).start()
        for number in (2, 3, 8, 9, 10, 11, 12, 13):
            self.landed(number)
        for number in range(GATHER_COPIES):
            self.copy(number).wait_send()
        self.kept().wait()


def gather_scratch(windows=1):
    return [
        pltpu.SemaphoreType.DMA((windows,)),
        pltpu.SemaphoreType.DMA((windows, GATHER_COPIES)),
        pltpu.SemaphoreType.DMA((windows, GATHER_COPIES)),
    ]


SCATTER_COPIES = 10
WINDOWS = 2
CHUNK = 32


def by_chunks(rows, work):
    def step(number, carry):
        work(pl.ds(pl.multiple_of(number * CHUNK, CHUNK), CHUNK))
        return carry

    lax.fori_loop(0, rows // CHUNK, step, 0)


class PlaneScatter:
    def __init__(self, window, others, terms, cores, nears, belows, sends, receives):
        self.window = window
        self.others, self.terms, self.cores = others, terms, cores
        self.nears, self.belows = nears, belows
        self.sends, self.receives = sends, receives
        self.size = terms.shape[1] // WINDOWS
        self.half = self.size // 2
        self.start = window * self.size

    def copy(self, number):
        _, other, near, below, _ = plane_peers()
        whole = pl.ds(self.start, self.size)
        upper, lower = (pl.ds(self.start + at * self.half, self.half) for at in (0, 1))
        if number < 4:
            source, target, peer = (
                self.others.at[number, whole],
                self.cores.at[number, whole],
                other,
            )
        else:
            slot, rows, landing, place, peer = (
                (0, upper, self.nears, 0, near),
                (0, lower, self.belows, 0, below),
                (1, upper, self.nears, 1, near),
                (2, lower, self.belows, 1, below),
                (1, lower, self.nears, 2, near),
                (2, upper, self.belows, 2, below),
            )[number - 4]
            source, target = self.terms.at[slot, rows], landing.at[self.window, place]
        at = (self.window, number)
        return to_peer(source, target, self.sends.at[at], self.receives.at[at], peer)

    def fold(self, slot):
        def work(rows):
            here = pl.ds(pl.multiple_of(self.start + rows.start, CHUNK), CHUNK)
            self.terms[slot, here] = (
                self.terms[slot, here].astype(FULL) + self.cores[slot, here].astype(FULL)
            ).astype(HALF)

        by_chunks(self.size, work)

    def fold_half(self, slot, which, landed):
        def work(rows):
            at = self.start + which * self.half
            here = pl.ds(pl.multiple_of(at + rows.start, CHUNK), CHUNK)
            self.terms[slot, here] = (
                self.terms[slot, here].astype(FULL) + landed[self.window, 0, rows].astype(FULL)
            ).astype(HALF)

        by_chunks(self.half, work)

    def advance(self, slot):
        self.copy(slot).wait_recv()
        self.fold(slot)
        for number in ((4, 5), (6,), (7,), ())[slot]:
            self.copy(number).start()

    def relay(self):
        self.copy(4).wait_recv()
        self.fold_half(2, 0, self.nears)
        self.copy(9).start()
        self.copy(5).wait_recv()
        self.fold_half(1, 1, self.belows)
        self.copy(8).start()

    def finish(self):
        for number in (6, 7, 8, 9):
            self.copy(number).wait_recv()

    def drain(self, first=0):
        for number in range(first, SCATTER_COPIES):
            self.copy(number).wait_send()

    def total(self, at):
        upper = at < self.half
        rows = pl.ds(at if upper else at - self.half, CHUNK)
        near, below = (1, 2) if upper else (2, 1)
        return (
            self.terms[3, pl.ds(self.start + at, CHUNK)].astype(FULL)
            + self.nears[self.window, near, rows].astype(FULL)
            + self.belows[self.window, below, rows].astype(FULL)
        )


def block_order_of_plane():
    me, other, near, below, far = plane_peers()
    return [block + at for block in (far, near, below, me) for at in (other - me, 0)]


class Blocks:
    def __init__(self, source, target, sems):
        self.source, self.target, self.sems = source, target, sems
        self.blocks, self.taken = block_order_of_plane(), 0

    def load(self, number):
        slot = number % self.target.shape[0]
        return pltpu.make_async_copy(
            self.source.at[self.blocks[number]], self.target.at[slot], self.sems.at[slot]
        )

    def begin(self):
        for number in range(min(len(self.blocks), self.target.shape[0])):
            self.load(number).start()

    def take(self, work):
        number, slots = self.taken, self.target.shape[0]
        self.taken += 1
        self.load(number).wait()
        out = work(self.target[number % slots])
        if number + slots < len(self.blocks):
            self.load(number + slots).start()
        return out


def staged(sources, targets, sems):
    copies = [
        pltpu.make_async_copy(source, target, sems.at[number])
        for number, (source, target) in enumerate(zip(sources, targets))
    ]
    for copy in copies:
        copy.start()
    return copies


def stage_scratch(*arrays):
    return [pltpu.VMEM(array.shape, array.dtype) for array in arrays] + [
        pltpu.SemaphoreType.DMA((len(arrays),))
    ]


def block_scratch(count, array):
    return [
        pltpu.VMEM((count,) + array.shape[1:], array.dtype),
        pltpu.SemaphoreType.DMA((count,)),
    ]


def scatter_head(term, refs, earlier=(), relay_later=False):
    windows = [PlaneScatter(window, *refs) for window in range(WINDOWS)]
    others, terms = refs[:2]
    blocks = block_order_of_plane()

    def fill(slot):
        for window in earlier:
            window.copy(slot).wait_send()
        others[slot] = term(blocks[2 * slot])
        for window in windows:
            window.copy(slot).start()
        terms[slot] = term(blocks[2 * slot + 1])

    fill(0)
    for slot in range(4):
        if slot < 3:
            fill(slot + 1)
        windows[0].advance(slot)
    if not relay_later:
        windows[0].relay()
    for window in windows[1:]:
        for slot in range(4):
            window.advance(slot)
        if not relay_later:
            window.relay()
    return windows


def scatter_tail(windows, use, after=lambda window: None):
    for number, window in enumerate(windows):
        window.finish()
        for at in range(0, window.size, CHUNK):
            use(window.start + at, window.total(at))
        after(number)


def scatter_scratch(rows, width):
    half = rows // WINDOWS // 2
    return [
        pltpu.VMEM((4, rows, width), HALF),
        pltpu.VMEM((4, rows, width), HALF),
        pltpu.VMEM((4, rows, width), HALF),
        pltpu.VMEM((WINDOWS, 3, half, width), HALF),
        pltpu.VMEM((WINDOWS, 3, half, width), HALF),
        pltpu.SemaphoreType.DMA((WINDOWS, SCATTER_COPIES)),
        pltpu.SemaphoreType.DMA((WINDOWS, SCATTER_COPIES)),
    ]


def regroup(values, outer, inner):
    rows = values.shape[0]
    low_half = lax.broadcasted_iota(jnp.int32, (rows, LANES), 1) < LANES // 2

    def piece(p, q):
        at = (p * inner + q) // 2
        return values[:, at * LANES : (at + 1) * LANES]

    def turned(value):
        return pltpu.roll(value, LANES // 2, 1)

    groups = []
    for q in range(inner):
        for p in range(0, outer, 2):
            first, second = piece(p, q), piece(p + 1, q)
            if q % 2 == 0:
                groups.append(jnp.where(low_half, first, turned(second)))
            else:
                groups.append(jnp.where(low_half, turned(first), second))
    return jnp.concatenate(groups, axis=1)


def normalised(values):
    average = jnp.mean(values, axis=-1, keepdims=True)
    centered = values - average
    scale = lax.rsqrt(jnp.mean(centered * centered, axis=-1, keepdims=True) + EPSILON)
    return centered * scale, scale


def normalised_back(grad, normed, scale):
    average = jnp.mean(grad, axis=-1, keepdims=True)
    along = jnp.mean(grad * normed, axis=-1, keepdims=True)
    return (grad - average - normed * along) * scale


def vmem():
    return pl.BlockSpec(memory_space=pltpu.VMEM)


def in_hbm():
    return pl.BlockSpec(memory_space=pl.ANY)


def cost(flops, link_bytes):
    return pl.CostEstimate(flops=int(flops), bytes_accessed=int(link_bytes) * 16, transcendentals=0)


def linked(collective):
    return pltpu.CompilerParams(
        collective_id=collective, has_side_effects=True, vmem_limit_bytes=VMEM_BYTES
    )


class PlaneSwap:
    def __init__(self, weights, targets, keeps, sends, receives):
        self.weights, self.targets = weights, targets
        self.keeps, self.sends, self.receives = keeps, sends, receives
        self.peers = lax.axis_size("seq")

    def part(self, number, peer):
        weight, (target, start) = self.weights[number], self.targets[number]
        size = weight.shape[1] // self.peers
        return weight.at[:, pl.ds(pl.multiple_of(peer * size, LANES), size)]

    def place(self, number, peer):
        weight, (target, start) = self.weights[number], self.targets[number]
        return target.at[peer, :, pl.ds(start, weight.shape[1] // self.peers)]

    def copy(self, number, turn):
        me = lax.axis_index("seq")
        peer = lax.rem(me + turn, self.peers)
        return to_peer(
            self.part(number, peer),
            self.place(number, me),
            self.sends.at[number, turn],
            self.receives.at[number, turn],
            peer,
        )

    def landed(self, number, turn):
        me = lax.axis_index("seq")
        peer = lax.rem(me + self.peers - turn, self.peers)
        target = self.place(number, peer)
        to_peer(
            target, target, self.sends.at[number, turn], self.receives.at[number, turn], peer
        ).wait_recv()

    def kept(self, number):
        me = lax.axis_index("seq")
        return pltpu.make_async_copy(
            self.part(number, me), self.place(number, me), self.keeps.at[number]
        )

    def begin(self):
        for number in range(len(self.weights)):
            for turn in range(1, self.peers):
                self.copy(number, turn).start()
            self.kept(number).start()

    def finish(self):
        for number in range(len(self.weights)):
            for turn in range(1, self.peers):
                self.landed(number, turn)
                self.copy(number, turn).wait_send()
            self.kept(number).wait()


def swap_scratch(count, peers):
    return [
        pltpu.SemaphoreType.DMA((count,)),
        pltpu.SemaphoreType.DMA((count, peers)),
        pltpu.SemaphoreType.DMA((count, peers)),
    ]


def greet_plane(with_groups):
    me, group = lax.axis_index("seq"), lax.axis_index("fsdp")
    peers, groups = lax.axis_size("seq"), lax.axis_size("fsdp")
    barrier = pltpu.get_barrier_semaphore()
    count = peers - 1
    for turn in range(1, peers):
        peer = lax.rem(me + turn, peers)
        pl.semaphore_signal(barrier, inc=1, device_id={"seq": peer}, device_id_type=MESH)
    if with_groups:
        count += groups - 1
        for turn in range(1, groups):
            peer = lax.rem(group + turn, groups)
            pl.semaphore_signal(barrier, inc=1, device_id={"fsdp": peer}, device_id_type=MESH)
    pl.semaphore_wait(barrier, count)


def all_to_each(source, out, axis, size, keep, sends, receives):
    me = lax.axis_index(axis)

    def copy(turn, slot):
        peer = lax.rem(me + turn, size)
        return pltpu.make_async_remote_copy(
            src_ref=source,
            dst_ref=out.at[slot],
            send_sem=sends.at[turn],
            recv_sem=receives.at[turn],
            device_id={axis: peer},
            device_id_type=MESH,
        )

    def begin():
        pltpu.make_async_copy(source, out.at[me], keep).start()
        for turn in range(1, size):
            copy(turn, me).start()

    def finish():
        for turn in range(1, size):
            copy(turn, lax.rem(me + size - turn, size)).wait_recv()
            copy(turn, me).wait_send()
        pltpu.make_async_copy(source, out.at[me], keep).wait()

    return begin, finish


def first_swap_kernel(
    query_ref, key_ref, value_ref, swish_ref, rates_ref, gains_ref,
    cut_out, rates_out, gains_out,
    column, keeps, sends, receives, rate_keep, rate_sends, rate_receives,
    group_keep, group_sends, group_receives, gain_keep, gain_sends, gain_receives,
):
    peers, groups = lax.axis_size("seq"), lax.axis_size("fsdp")
    size, wide = query_ref.shape[1] // peers, value_ref.shape[1] // peers
    greet_plane(True)
    begin_groups, finish_groups = all_to_each(
        gains_ref, column, "fsdp", groups, group_keep, group_sends, group_receives
    )
    begin_rates, finish_rates = all_to_each(
        rates_ref, rates_out, "seq", peers, rate_keep, rate_sends, rate_receives
    )
    begin_gains, finish_gains = all_to_each(
        column, gains_out, "seq", peers, gain_keep, gain_sends, gain_receives
    )
    swap = PlaneSwap(
        (query_ref, key_ref, value_ref, swish_ref),
        ((cut_out, 0), (cut_out, size), (cut_out, 2 * size), (cut_out, 2 * size + wide)),
        keeps,
        sends,
        receives,
    )
    begin_groups()
    begin_rates()
    finish_groups()
    begin_gains()
    swap.begin()
    finish_rates()
    finish_gains()
    swap.finish()


def first_swap(query, key, value, swish, rates, gains):
    peers, groups = lax.axis_size("seq"), lax.axis_size("fsdp")
    slab = query.shape[0]
    total = sum(weight.shape[1] for weight in (query, key, value, swish)) // peers
    return pl.pallas_call(
        first_swap_kernel,
        in_specs=[in_hbm()] * 4 + [vmem()] * 2,
        out_specs=[in_hbm()] + [vmem()] * 2,
        out_shape=[
            jax.ShapeDtypeStruct((peers, slab, total), HALF),
            jax.ShapeDtypeStruct((peers,) + rates.shape, FULL),
            jax.ShapeDtypeStruct((peers, groups) + gains.shape, FULL),
        ],
        scratch_shapes=[pltpu.VMEM((groups,) + gains.shape, FULL)]
        + swap_scratch(4, peers)
        + [pltpu.SemaphoreType.DMA] + [pltpu.SemaphoreType.DMA((peers,))] * 2
        + [pltpu.SemaphoreType.DMA] + [pltpu.SemaphoreType.DMA((groups,))] * 2
        + [pltpu.SemaphoreType.DMA] + [pltpu.SemaphoreType.DMA((peers,))] * 2,
        compiler_params=linked(0),
        cost_estimate=cost(0, 2 * slab * peers * total),
    )(query, key, value, swish, rates, gains)


class LineGather:
    def __init__(self, own, out, keep, sends, receives):
        self.own, self.out = own, out
        self.keep, self.sends, self.receives = keep, sends, receives
        self.me, self.last = lax.axis_index("fsdp"), lax.axis_size("fsdp") - 1
        self.pieces = own.shape[0]

    def block(self, way, depth):
        return self.me - depth if way == 0 else self.me + depth

    def holds(self, way, depth):
        return self.me >= depth if way == 0 else self.me + depth <= self.last

    def passes(self, way):
        return self.me < self.last if way == 0 else self.me > 0

    def sent(self, source, way, depth, piece, block):
        at = (way, depth, piece)
        return pltpu.make_async_remote_copy(
            src_ref=source,
            dst_ref=self.out.at[block, piece],
            send_sem=self.sends.at[at],
            recv_sem=self.receives.at[at],
            device_id={"fsdp": self.me + 1 if way == 0 else self.me - 1},
            device_id_type=MESH,
        )

    def copy(self, way, depth, piece):
        block = self.block(way, depth)
        source = self.own.at[piece] if depth == 0 else self.out.at[block, piece]
        return self.sent(source, way, depth, piece, block)

    def landed(self, way, depth, piece):
        block = self.block(way, depth)
        self.sent(self.out.at[block, piece], way, depth - 1, piece, block).wait_recv()

    def kept(self):
        return pltpu.make_async_copy(self.own, self.out.at[self.me], self.keep)

    def begin(self):
        for piece in range(self.pieces):
            for way in (0, 1):

                @pl.when(self.passes(way))
                def _():
                    self.copy(way, 0, piece).start()

        self.kept().start()

    def hand_on(self, depth):
        for piece in range(self.pieces):
            for way in (0, 1):

                @pl.when(self.holds(way, depth) & self.passes(way))
                def _():
                    self.landed(way, depth, piece)
                    self.copy(way, depth, piece).start()

    def finish(self):
        for depth in range(1, self.last + 1):
            for piece in range(self.pieces):
                for way in (0, 1):

                    @pl.when(self.holds(way, depth) & jnp.logical_not(self.passes(way)))
                    def _():
                        self.landed(way, depth, piece)

        for depth in range(self.last):
            for piece in range(self.pieces):
                for way in (0, 1):

                    @pl.when(self.holds(way, depth) & self.passes(way))
                    def _():
                        self.copy(way, depth, piece).wait_send()

        self.kept().wait()


def unpack_gains(gains_ref, one_ref, two_ref, group_ref):
    peers, groups = gains_ref.shape[:2]
    low_half = lax.broadcasted_iota(jnp.int32, (1, LANES), 1) < LANES // 2
    for peer in range(peers):
        for at in range(0, groups, 2):
            left, right = gains_ref[peer, at, 1:2], gains_ref[peer, at + 1, 1:2]
            lanes = pl.ds((peer * groups + at) * LANES // 2, LANES)
            one_ref[:, lanes] = jnp.where(low_half, left, pltpu.roll(right, LANES // 2, 1))
            two_ref[:, lanes] = jnp.where(low_half, pltpu.roll(left, LANES // 2, 1), right)
    me = lax.axis_index("seq")
    for at in range(groups):
        group_ref[:, at * LANES : (at + 1) * LANES] = gains_ref[me, at, 0:1]


def unpack_rates(rates_ref, decay_ref, column_ref):
    blocks, _, rows = rates_ref.shape
    me = lax.axis_index("seq")
    total = jnp.concatenate([rates_ref[block, pl.ds(me, 1)] for block in range(blocks)], axis=0)
    lane = lax.broadcasted_iota(jnp.int32, total.shape, 1)
    shift = 1
    while shift < rows:
        total += jnp.where(lane >= shift, pltpu.roll(total, shift, 1), 0.0)
        shift *= 2
    square = (rows, rows)
    lower = lax.broadcasted_iota(jnp.int32, square, 0) >= lax.broadcasted_iota(jnp.int32, square, 1)
    for block in range(blocks):
        along = jnp.broadcast_to(total[block : block + 1], square)
        down = along.T
        spread = jnp.where(lower, down - along, 0.0)
        decay_ref[block] = jnp.where(lower, jnp.exp(spread), 0.0)
        first = down[:, 0:1]
        column_ref[block, :, 0:1] = jnp.exp(first)
        column_ref[block, :, 1:2] = jnp.exp(first[rows - 1 : rows] - first)


def inputs_kernel(
    lengths_ref, order_ref, tokens_ref, grad_ref, gains_ref, rates_ref, gate_ref, up_ref, cut_ref,
    entered_out, grads_out, feed_out, weight_out,
    mask_ref, gain_ref, second_ref, group_ref, decay_ref, column_ref,
    own_entered, own_grad, keep_one, sends_one, receives_one, keep_two, sends_two, receives_two,
    keeps, sends, receives, line_keep, line_sends, line_receives,
):
    peers, groups = lax.axis_size("seq"), lax.axis_size("fsdp")
    greet_plane(True)
    line = LineGather(cut_ref, weight_out, line_keep, line_sends, line_receives)
    line.begin()
    size = gate_ref.shape[1] // peers
    me, group = lax.axis_index("seq"), lax.axis_index("fsdp")
    batches = lengths_ref.shape[0] // groups
    block = tokens_ref.shape[0] // batches
    for batch in range(batches):
        sequence = group * batches + batch
        numbers = order_ref[sequence, me] * block + lax.broadcasted_iota(jnp.int32, (block, 1), 0)
        live = (numbers < lengths_ref[sequence]).astype(FULL)
        mask_ref[batch * block : (batch + 1) * block] = live
    unpack_gains(gains_ref, gain_ref, second_ref, group_ref)
    gain = gain_ref[...]

    def work(rows):
        normed, _ = normalised(tokens_ref[rows].astype(FULL))
        own_entered[rows] = regroup(normed * gain, peers, groups).astype(HALF)
        own_grad[rows] = (grad_ref[rows].astype(FULL) * mask_ref[rows]).astype(HALF)

    by_chunks(tokens_ref.shape[0], work)
    one = PlaneGather(own_entered, entered_out, keep_one, sends_one, receives_one)
    two = PlaneGather(own_grad, grads_out, keep_two, sends_two, receives_two)
    swap = PlaneSwap((gate_ref, up_ref), ((feed_out, 0), (feed_out, size)), keeps, sends, receives)
    one.begin()
    one.relay()
    swap.begin()
    two.begin()
    unpack_rates(rates_ref, decay_ref, column_ref)
    line.hand_on(1)
    one.finish()
    two.relay()
    line.hand_on(2)
    swap.finish()
    two.finish()
    line.finish()


def gather_inputs(lengths, order, tokens, grad, gains, rates, gate, up, cut, value_size):
    peers, groups = lax.axis_size("seq"), lax.axis_size("fsdp")
    own, width = tokens.shape
    slab, columns = gate.shape
    part = columns // peers
    blocks, _, rows = rates.shape
    return pl.pallas_call(
        inputs_kernel,
        in_specs=[pl.BlockSpec(memory_space=pltpu.SMEM)] * 2 + [vmem()] * 4 + [in_hbm()] * 3,
        out_specs=[in_hbm()] * 4 + [vmem()] * 6,
        out_shape=[
            jax.ShapeDtypeStruct((peers, own, width), HALF),
            jax.ShapeDtypeStruct((peers, own, width), HALF),
            jax.ShapeDtypeStruct((peers, slab, 2 * part), HALF),
            jax.ShapeDtypeStruct((groups,) + cut.shape, HALF),
            jax.ShapeDtypeStruct((own, 1), FULL),
            jax.ShapeDtypeStruct((1, width), FULL),
            jax.ShapeDtypeStruct((1, width), FULL),
            jax.ShapeDtypeStruct((1, value_size), FULL),
            jax.ShapeDtypeStruct((blocks, rows, rows), FULL),
            jax.ShapeDtypeStruct((blocks, rows, 2), FULL),
        ],
        scratch_shapes=[pltpu.VMEM((own, width), HALF)] * 2
        + gather_scratch()
        + gather_scratch()
        + swap_scratch(2, peers)
        + [
            pltpu.SemaphoreType.DMA,
            pltpu.SemaphoreType.DMA((2, groups - 1, peers)),
            pltpu.SemaphoreType.DMA((2, groups - 1, peers)),
        ],
        compiler_params=linked(1),
        cost_estimate=cost(0, 2 * peers * (2 * own * width + slab * 2 * part)),
    )(lengths, order, tokens, grad, gains, rates, gate, up, cut)


def feed_kernel(
    rows_ref, weight_ref, grads_ref, inner_ref, up_slope_ref, gate_slope_ref, down_ref, total
):
    step = pl.program_id(0)
    both = dot_nn(rows_ref[...], weight_ref[...])
    part = both.shape[1] // 2
    gate, upward = both[:, :part], both[:, part:]
    inside = 0.7978845608028654 * (gate + 0.044715 * (gate * gate * gate))
    bend = jnp.tanh(inside)
    share = 0.5 * (1.0 + bend)
    value = gate * share
    steep = 0.7978845608028654 * (1.0 + 3.0 * 0.044715 * (gate * gate))
    slope = share + 0.5 * gate * (1.0 - bend * bend) * steep
    inner_ref[...] = (value * upward).astype(HALF)
    up_slope_ref[...] = value.astype(HALF)
    gate_slope_ref[...] = (upward * slope).astype(HALF)
    term = dot_tn(inner_ref[...], grads_ref[...])

    @pl.when(step == 0)
    def _():
        total[...] = term

    @pl.when(step > 0)
    def _():
        total[...] += term

    @pl.when(step == pl.num_programs(0) - 1)
    def _():
        down_ref[...] = total[...].astype(HALF)


def feed(rows, weight, grads):
    count, width = rows.shape
    columns = weight.shape[1]
    part = columns // 2
    tile = 512
    tokens = pl.BlockSpec((tile, width), lambda i: (i, 0))
    out = pl.BlockSpec((tile, part), lambda i: (i, 0))
    return pl.pallas_call(
        feed_kernel,
        grid=(count // tile,),
        in_specs=[
            tokens,
            pl.BlockSpec((width, columns), lambda i: (0, 0), pipeline_mode=pl.Buffered(1)),
            tokens,
        ],
        out_specs=[out] * 3 + [pl.BlockSpec((part, width), lambda i: (0, 0))],
        out_shape=[jax.ShapeDtypeStruct((count, part), HALF)] * 3
        + [jax.ShapeDtypeStruct((part, width), HALF)],
        scratch_shapes=[pltpu.VMEM((part, width), FULL)],
        compiler_params=pltpu.CompilerParams(
            dimension_semantics=("arbitrary",), vmem_limit_bytes=VMEM_BYTES
        ),
        cost_estimate=pl.CostEstimate(
            flops=3 * count * width * columns,
            bytes_accessed=2 * (2 * count * width + width * columns + 2 * count * columns),
            transcendentals=0,
        ),
    )(rows, weight, grads)


def feed_back_kernel(rows_ref, weight_ref, up_slope_ref, gate_slope_ref, grad_ref):
    inner_grad = dot_nt(rows_ref[...], weight_ref[...])
    part = inner_grad.shape[1]
    grad_ref[:, :part] = (inner_grad * gate_slope_ref[...].astype(FULL)).astype(HALF)
    grad_ref[:, part:] = (inner_grad * up_slope_ref[...].astype(FULL)).astype(HALF)


def feed_back(rows, weight, up_slope, gate_slope):
    count, width = rows.shape
    part = weight.shape[0]
    tile = 512
    slope = pl.BlockSpec((tile, part), lambda i: (i, 0))
    return pl.pallas_call(
        feed_back_kernel,
        grid=(count // tile,),
        in_specs=[
            pl.BlockSpec((tile, width), lambda i: (i, 0)),
            pl.BlockSpec((part, width), lambda i: (0, 0), pipeline_mode=pl.Buffered(1)),
            slope,
            slope,
        ],
        out_specs=pl.BlockSpec((tile, 2 * part), lambda i: (i, 0)),
        out_shape=jax.ShapeDtypeStruct((count, 2 * part), HALF),
        compiler_params=pltpu.CompilerParams(
            dimension_semantics=("arbitrary",), vmem_limit_bytes=VMEM_BYTES
        ),
        cost_estimate=pl.CostEstimate(
            flops=2 * count * width * part,
            bytes_accessed=2 * (count * width + width * part + 4 * count * part),
            transcendentals=0,
        ),
    )(rows, weight, up_slope, gate_slope)


def retention_kernel(
    place_ref, live_ref, first_ref, second_ref, weight_ref, decay_ref, column_ref, gain_ref,
    qkv_ref, swish_ref, normed_ref, scale_ref, entry_ref, mixed_hbm, state, mixed_buffer, sems,
):
    step, steps = pl.program_id(0), pl.num_programs(0)
    rows = first_ref.shape[2]
    batches, key_size, value_size = state.shape
    total = 2 * key_size + value_size
    slot = lax.rem(step, 2)

    def sent(at, which, batch):
        return pltpu.make_async_copy(
            mixed_buffer.at[which, batch],
            mixed_hbm.at[place_ref[batch, at], batch],
            sems.at[which, batch],
        )

    @pl.when(step == 0)
    def _():
        state[...] = jnp.zeros_like(state)

    @pl.when(step >= 2)
    def _():
        for batch in range(batches):
            sent(step - 2, slot, batch).wait()

    rows_in = jnp.concatenate([first_ref[0, 0], second_ref[0, 0]], axis=0)
    projected = dot_nn(rows_in, weight_ref[...])
    decay = decay_ref[0]
    entry_decay = column_ref[0, :, 0:1]
    end_weight = column_ref[0, :, 1:2]
    block_decay = column_ref[0, rows - 1 : rows, 0:1]
    positions = step * rows + lax.broadcasted_iota(jnp.int32, (rows, 1), 0)
    for batch in range(batches):
        mine = slice(batch * rows, (batch + 1) * rows)
        live = (positions < live_ref[batch]).astype(FULL)
        query = projected[mine, :key_size].astype(HALF)
        key = (projected[mine, key_size : 2 * key_size] * live).astype(HALF)
        value = projected[mine, 2 * key_size : total].astype(HALF)
        swish = projected[mine, total:]
        before = state[batch]
        before_low = before.astype(HALF)
        weights = (dot_nt(query, key) * decay).astype(HALF)
        retained = dot_nn(weights, value) + entry_decay * dot_nn(query, before_low)
        key_ended = (key.astype(FULL) * end_weight).astype(HALF)
        state[batch] = block_decay * before + dot_tn(key_ended, value)
        normed, scale = normalised(retained)
        qkv_ref[batch, 0, :, :key_size] = query
        qkv_ref[batch, 0, :, key_size : 2 * key_size] = key
        qkv_ref[batch, 0, :, 2 * key_size :] = value
        scale_ref[batch, 0] = jnp.broadcast_to(scale, scale_ref.shape[2:])
        entry_ref[batch, 0] = before_low
        swish_ref[batch, 0] = swish.astype(HALF)
        normed_ref[batch, 0] = normed.astype(HALF)
        mixed = swish * jax.nn.sigmoid(swish) * (normed * gain_ref[...])
        mixed_buffer[slot, batch] = mixed.astype(HALF)
        sent(step, slot, batch).start()

    @pl.when(step == steps - 1)
    def _():
        for batch in range(batches):
            sent(step, slot, batch).wait()
            sent(step - 1, 1 - slot, batch).wait()


def retention(rows_in, weight, place, live, decay, columns, gain, key_size):
    blocks, batches, rows, width = rows_in.shape
    value_size = gain.shape[-1]
    total = 2 * key_size + value_size

    def arriving(batch):
        return pl.BlockSpec(
            (1, 1, rows, width), lambda i, place, live: (place[batch, i], batch, 0, 0)
        )

    def whole(shape):
        return pl.BlockSpec(
            shape, lambda i, place, live: (0,) * len(shape), pipeline_mode=pl.Buffered(1)
        )

    def here(*tail):
        return pl.BlockSpec((batches, 1) + tail, lambda i, place, live: (0, i, 0, 0))

    def along(*tail):
        return pl.BlockSpec((1,) + tail, lambda i, place, live: (i, 0, 0))

    return pl.pallas_call(
        retention_kernel,
        grid_spec=pltpu.PrefetchScalarGridSpec(
            num_scalar_prefetch=2,
            grid=(blocks,),
            in_specs=[
                arriving(0),
                arriving(1),
                whole((width, total + value_size)),
                along(rows, rows),
                along(rows, 2),
                whole((1, value_size)),
            ],
            out_specs=[
                here(rows, total),
                here(rows, value_size),
                here(rows, value_size),
                here(rows, LANES),
                here(key_size, value_size),
                in_hbm(),
            ],
            scratch_shapes=[
                pltpu.VMEM((batches, key_size, value_size), FULL),
                pltpu.VMEM((2, batches, rows, value_size), HALF),
                pltpu.SemaphoreType.DMA((2, batches)),
            ],
        ),
        out_shape=[
            jax.ShapeDtypeStruct((batches, blocks, rows, total), HALF),
            jax.ShapeDtypeStruct((batches, blocks, rows, value_size), HALF),
            jax.ShapeDtypeStruct((batches, blocks, rows, value_size), HALF),
            jax.ShapeDtypeStruct((batches, blocks, rows, LANES), FULL),
            jax.ShapeDtypeStruct((batches, blocks, key_size, value_size), HALF),
            jax.ShapeDtypeStruct((blocks, batches, rows, value_size), HALF),
        ],
        compiler_params=pltpu.CompilerParams(
            dimension_semantics=("arbitrary",), vmem_limit_bytes=VMEM_BYTES
        ),
        cost_estimate=pl.CostEstimate(
            flops=3 * blocks * batches * rows * width * total,
            bytes_accessed=2 * blocks * batches * rows * (width + 2 * total) + 4 * width * total,
            transcendentals=0,
        ),
    )(place, live, rows_in, rows_in, weight, decay, columns, gain)


def retention_back_kernel(
    place_ref, live_ref, first_ref, second_ref,
    weight_ref, decay_ref, column_ref, gain_ref, qkv_ref, swish_ref, normed_ref, scale_ref, entry_ref,
    gain_grad_ref, grads_hbm, state, grads_buffer, sems,
):
    step, steps = pl.program_id(0), pl.num_programs(0)
    rows = first_ref.shape[2]
    batches, key_size, value_size = state.shape
    slot = lax.rem(step, 2)

    def sent(at, which, batch):
        return pltpu.make_async_copy(
            grads_buffer.at[which, batch],
            grads_hbm.at[place_ref[batch, steps - 1 - at], batch],
            sems.at[which, batch],
        )

    @pl.when(step == 0)
    def _():
        state[...] = jnp.zeros_like(state)
        gain_grad_ref[...] = jnp.zeros_like(gain_grad_ref)

    @pl.when(step >= 2)
    def _():
        for batch in range(batches):
            sent(step - 2, slot, batch).wait()

    rows_in = jnp.concatenate([first_ref[0, 0], second_ref[0, 0]], axis=0)
    mixed_grads = dot_nt(rows_in, weight_ref[...])
    decay = decay_ref[0]
    entry_decay = column_ref[0, :, 0:1]
    end_weight = column_ref[0, :, 1:2]
    block_decay = column_ref[0, rows - 1 : rows, 0:1]
    positions = (steps - 1 - step) * rows + lax.broadcasted_iota(jnp.int32, (rows, 1), 0)
    gain = gain_ref[...]
    for batch in range(batches):
        live = (positions < live_ref[batch]).astype(FULL)
        mixed_grad = mixed_grads[batch * rows : (batch + 1) * rows]
        query = qkv_ref[batch, 0, :, :key_size]
        key = qkv_ref[batch, 0, :, key_size : 2 * key_size]
        value = qkv_ref[batch, 0, :, 2 * key_size :]
        swish = swish_ref[batch, 0].astype(FULL)
        normed = normed_ref[batch, 0].astype(FULL)
        scale = scale_ref[batch, 0, :, 0:1]
        entry = entry_ref[batch, 0]
        sigmoid = jax.nn.sigmoid(swish)
        silu = swish * sigmoid
        swish_grad = mixed_grad * (normed * gain) * (sigmoid * (1.0 + swish - silu))
        scaled_grad = mixed_grad * silu
        gain_grad_ref[...] += jnp.sum(scaled_grad * normed, axis=0, keepdims=True)
        retained_grad = normalised_back(scaled_grad * gain, normed, scale).astype(HALF)
        weights = (dot_nt(query, key) * decay).astype(HALF)
        scores_grad = (dot_nt(retained_grad, value) * decay).astype(HALF)
        after = state[batch]
        after_low = after.astype(HALF)
        query_grad = dot_nn(scores_grad, key) + entry_decay * dot_nt(retained_grad, entry)
        key_grad = dot_tn(scores_grad, query) + end_weight * dot_nt(value, after_low)
        value_grad = dot_tn(weights, retained_grad) + end_weight * dot_nn(key, after_low)
        query_entered = (query.astype(FULL) * entry_decay).astype(HALF)
        state[batch] = block_decay * after + dot_tn(query_entered, retained_grad)
        grads_buffer[slot, batch, :, :key_size] = query_grad.astype(HALF)
        grads_buffer[slot, batch, :, key_size : 2 * key_size] = (key_grad * live).astype(HALF)
        grads_buffer[slot, batch, :, 2 * key_size : 2 * key_size + value_size] = value_grad.astype(
            HALF
        )
        grads_buffer[slot, batch, :, 2 * key_size + value_size :] = swish_grad.astype(HALF)
        sent(step, slot, batch).start()

    @pl.when(step == steps - 1)
    def _():
        for batch in range(batches):
            sent(step, slot, batch).wait()
            sent(step - 1, 1 - slot, batch).wait()


def retention_back(rows_in, weight, place, live, decay, columns, gain, saved):
    blocks, batches, rows, width = rows_in.shape
    value_size = gain.shape[-1]
    key_size = saved[-1].shape[2]
    total = 2 * key_size + 2 * value_size

    def arriving(batch, size):
        return pl.BlockSpec(
            (1, 1, rows, size),
            lambda i, place, live: (place[batch, blocks - 1 - i], batch, 0, 0),
        )

    def whole(shape):
        return pl.BlockSpec(
            shape, lambda i, place, live: (0,) * len(shape), pipeline_mode=pl.Buffered(1)
        )

    def here(*tail):
        return pl.BlockSpec((batches, 1) + tail, lambda i, place, live: (0, blocks - 1 - i, 0, 0))

    def along(*tail):
        return pl.BlockSpec((1,) + tail, lambda i, place, live: (blocks - 1 - i, 0, 0))

    return pl.pallas_call(
        retention_back_kernel,
        grid_spec=pltpu.PrefetchScalarGridSpec(
            num_scalar_prefetch=2,
            grid=(blocks,),
            in_specs=[
                arriving(0, width),
                arriving(1, width),
                whole((value_size, width)),
                along(rows, rows),
                along(rows, 2),
                whole((1, value_size)),
                here(rows, 2 * key_size + value_size),
                here(rows, value_size),
                here(rows, value_size),
                here(rows, LANES),
                here(key_size, value_size),
            ],
            out_specs=[
                pl.BlockSpec((1, value_size), lambda i, place, live: (0, 0)),
                in_hbm(),
            ],
            scratch_shapes=[
                pltpu.VMEM((batches, key_size, value_size), FULL),
                pltpu.VMEM((2, batches, rows, total), HALF),
                pltpu.SemaphoreType.DMA((2, batches)),
            ],
        ),
        out_shape=[
            jax.ShapeDtypeStruct((1, value_size), FULL),
            jax.ShapeDtypeStruct((blocks, batches, rows, total), HALF),
        ],
        compiler_params=pltpu.CompilerParams(
            dimension_semantics=("arbitrary",), vmem_limit_bytes=VMEM_BYTES
        ),
        cost_estimate=pl.CostEstimate(
            flops=6 * blocks * batches * rows * width * value_size,
            bytes_accessed=2 * blocks * batches * rows * (width + 2 * total)
            + 2 * width * value_size,
            transcendentals=0,
        ),
    )(place, live, rows_in, rows_in, weight, decay, columns, gain, *saved)


def middle_kernel(
    mixed_hbm, weight_hbm, tokens_hbm, gain_ref, hidden_ref, second_out,
    *scratch,
):
    scatter = scratch[:7]
    own, keeps, gather_sends, gather_receives = scratch[7:11]
    weight_ref, tokens_ref, stage_sems, mixed, mixed_sems = scratch[11:]
    peers, groups = lax.axis_size("seq"), lax.axis_size("fsdp")
    sources, targets = (weight_hbm, tokens_hbm), (weight_ref, tokens_ref)
    weight_copy, tokens_copy = staged(sources, targets, stage_sems)
    blocks = Blocks(mixed_hbm, mixed, mixed_sems)
    blocks.begin()
    greet_neighbours()
    weight_copy.wait()

    def term(block):
        return blocks.take(lambda value: dot_nn(value, weight_ref[...]).astype(HALF))

    gain = gain_ref[...]

    def use(start, total):
        rows = pl.ds(start, CHUNK)
        hidden = tokens_ref[rows].astype(FULL) + total
        hidden_ref[rows] = hidden
        normed, _ = normalised(hidden)
        own[rows] = regroup(normed * gain, peers, groups).astype(HALF)

    gathers = [
        PlaneGather(own, second_out, keeps, gather_sends, gather_receives, window, WINDOWS)
        for window in range(WINDOWS)
    ]
    windows = scatter_head(term, scatter)
    tokens_copy.wait()
    scatter_tail(windows, use, lambda window: gathers[window].begin())
    for gather in gathers:
        gather.relay()
    for gather in gathers:
        gather.finish()
    for window in windows:
        window.drain()


def middle(mixed, weight, tokens, gain):
    peers, own, inner = mixed.shape
    width = weight.shape[1]
    return pl.pallas_call(
        middle_kernel,
        in_specs=[in_hbm()] * 3 + [vmem()],
        out_specs=[vmem(), in_hbm()],
        out_shape=[
            jax.ShapeDtypeStruct((own, width), FULL),
            jax.ShapeDtypeStruct((peers, own, width), HALF),
        ],
        scratch_shapes=scatter_scratch(own, width)
        + [pltpu.VMEM((own, width), HALF)]
        + gather_scratch(WINDOWS)
        + stage_scratch(weight, tokens)
        + block_scratch(peers, mixed),
        compiler_params=linked(2),
        cost_estimate=cost(2 * peers * own * inner * width, 4 * peers * own * width),
    )(mixed, weight, tokens, gain)


def middle_back_kernel(
    grads_hbm, weight_hbm, hidden_hbm, outer_hbm, mask_ref, gain_ref,
    hidden_grad_ref, gain_grad_ref, branch_out,
    *scratch,
):
    scatter = scratch[:7]
    own, keeps, gather_sends, gather_receives = scratch[7:11]
    weight_ref, hidden_ref, outer_ref, stage_sems, grads, grad_sems = scratch[11:]
    peers, groups = lax.axis_size("seq"), lax.axis_size("fsdp")
    blocks = Blocks(grads_hbm, grads, grad_sems)
    sources, targets = (weight_hbm, hidden_hbm, outer_hbm), (weight_ref, hidden_ref, outer_ref)
    weight_copy, *later = staged(sources, targets, stage_sems)
    blocks.begin()
    greet_neighbours()
    weight_copy.wait()

    def term(block):
        return blocks.take(lambda value: dot_nt(value, weight_ref[...]).astype(HALF))

    gain = gain_ref[...]
    gain_grad_ref[...] = jnp.zeros_like(gain_grad_ref)

    def use(start, total):
        rows = pl.ds(start, CHUNK)
        grad = regroup(total, groups, peers)
        normed, scale = normalised(hidden_ref[rows])
        gain_grad_ref[...] += jnp.sum(grad * normed, axis=0, keepdims=True)
        outer = outer_ref[rows].astype(FULL) * mask_ref[rows]
        hidden_grad = outer + normalised_back(grad * gain, normed, scale)
        hidden_grad_ref[rows] = hidden_grad
        own[rows] = hidden_grad.astype(HALF)

    gathers = [
        PlaneGather(own, branch_out, keeps, gather_sends, gather_receives, window, WINDOWS)
        for window in range(WINDOWS)
    ]
    windows = scatter_head(term, scatter)
    for copy in later:
        copy.wait()
    scatter_tail(windows, use, lambda window: gathers[window].begin())
    for gather in gathers:
        gather.relay()
    for gather in gathers:
        gather.finish()
    for window in windows:
        window.drain()


def middle_back(grads, weight, hidden, outer, mask, gain):
    peers, own, inner = grads.shape
    width = weight.shape[0]
    return pl.pallas_call(
        middle_back_kernel,
        in_specs=[in_hbm()] * 4 + [vmem()] * 2,
        out_specs=[vmem(), vmem(), in_hbm()],
        out_shape=[
            jax.ShapeDtypeStruct((own, width), FULL),
            jax.ShapeDtypeStruct((1, width), FULL),
            jax.ShapeDtypeStruct((peers, own, width), HALF),
        ],
        scratch_shapes=scatter_scratch(own, width)
        + [pltpu.VMEM((own, width), HALF)]
        + gather_scratch(WINDOWS)
        + stage_scratch(weight, hidden, outer)
        + block_scratch(peers, grads),
        compiler_params=linked(3),
        cost_estimate=cost(2 * peers * own * inner * width, 4 * peers * own * width),
    )(grads, weight, hidden, outer, mask, gain)


class PlaneReturn:
    def __init__(self, cuts, source, targets, keeps, sends, receives):
        self.cuts, self.source, self.targets = cuts, source, targets
        self.keeps, self.sends, self.receives = keeps, sends, receives
        self.peers, self.me = lax.axis_size("seq"), lax.axis_index("seq")

    def part(self, number, peer):
        start, size = self.cuts[number]
        return self.source.at[peer, :, pl.ds(start, size)]

    def place(self, number, peer):
        size = self.cuts[number][1]
        return self.targets[number].at[:, pl.ds(pl.multiple_of(peer * size, LANES), size)]

    def sent(self, source, target, number, turn, peer):
        at = (number, turn)
        return to_peer(source, target, self.sends.at[at], self.receives.at[at], peer)

    def copy(self, number, turn):
        peer = lax.rem(self.me + turn, self.peers)
        return self.sent(
            self.part(number, peer), self.place(number, self.me), number, turn, peer
        )

    def landed(self, number, turn):
        peer = lax.rem(self.me + self.peers - turn, self.peers)
        target = self.place(number, peer)
        return self.sent(target, target, number, turn, peer)

    def kept(self, number):
        return pltpu.make_async_copy(
            self.part(number, self.me), self.place(number, self.me), self.keeps.at[number]
        )

    def begin(self, turn):
        for number in range(len(self.cuts)):
            if turn > 0:
                self.copy(number, turn).start()
            else:
                self.kept(number).start()

    def finish(self):
        for number in range(len(self.cuts)):
            for turn in range(1, self.peers):
                self.landed(number, turn).wait_recv()
                self.copy(number, turn).wait_send()
            self.kept(number).wait()


class LineSum:
    def __init__(self, terms, landed, own, final, loads, sends, receives):
        self.terms, self.landed, self.own, self.final = terms, landed, own, final
        self.loads, self.sends, self.receives = loads, sends, receives
        self.me, self.last = lax.axis_index("fsdp"), lax.axis_size("fsdp") - 1
        self.peers, self.place = lax.axis_size("seq"), lax.axis_index("seq")

    def piece(self, turn):
        return lax.rem(self.place + turn, self.peers)

    def depth(self, way):
        return self.me if way == 0 else self.last - self.me

    def block(self, way, order):
        return self.last - order if way == 0 else order

    def slot(self, way, order):
        return order if way == 0 else 2 * self.last - 2 - order

    def sent(self, source, way, order, turn):
        at = (way, order, turn)
        return pltpu.make_async_remote_copy(
            src_ref=source,
            dst_ref=self.landed.at[self.slot(way, order), self.piece(turn)],
            send_sem=self.sends.at[at],
            recv_sem=self.receives.at[at],
            device_id={"fsdp": self.me + 1 if way == 0 else self.me - 1},
            device_id_type=MESH,
        )

    def first(self, way, order, turn):
        source = self.terms.at[self.block(way, order), self.piece(turn)]
        return self.sent(source, way, order, turn)

    def onward(self, way, order, turn):
        source = self.landed.at[self.slot(way, order), self.piece(turn)]
        return self.sent(source, way, order, turn)

    def load(self, way, order):
        return pltpu.make_async_copy(
            self.terms.at[self.block(way, order)], self.own.at[way], self.loads.at[way]
        )

    def load_final(self):
        return pltpu.make_async_copy(self.terms.at[self.me], self.final, self.loads.at[2])

    def begin(self):
        for way in (0, 1):

            @pl.when(self.depth(way) == 0)
            def _():
                for order in range(self.last):
                    for turn in range(self.peers):
                        self.first(way, order, turn).start()

            self.load(way, 0).start()
        self.load_final().start()

    def loaded(self, order):
        for way in (0, 1):
            self.load(way, order).wait()

    def load_next(self, order):
        for way in (0, 1):
            self.load(way, order).start()

    def hand_on(self, order, depth, turns):
        for turn in turns:
            for way in (0, 1):

                @pl.when(self.depth(way) == depth)
                def _():
                    at, piece = self.slot(way, order), self.piece(turn)
                    self.onward(way, order, turn).wait_recv()
                    self.landed[at, piece] = (
                        self.landed[at, piece].astype(FULL) + self.own[way, piece].astype(FULL)
                    ).astype(HALF)
                    self.onward(way, order, turn).start()

    def finish(self, use):
        self.load_final().wait()
        for turn in range(self.peers):
            piece = self.piece(turn)
            for way in (0, 1):

                @pl.when(self.depth(way) > 0)
                def _():
                    order = self.last - self.depth(way)
                    self.onward(way, order, turn).wait_recv()
                    self.final[piece] = (
                        self.final[piece].astype(FULL)
                        + self.landed[self.slot(way, order), piece].astype(FULL)
                    ).astype(HALF)

            use(turn)

    def drain(self):
        for way in (0, 1):
            for order in range(self.last):
                for turn in range(self.peers):

                    @pl.when(self.depth(way) == 0)
                    def _():
                        self.first(way, order, turn).wait_send()

                    @pl.when((self.depth(way) > 0) & (self.depth(way) < self.last - order))
                    def _():
                        self.onward(way, order, turn).wait_send()


def line_scratch(groups, peers, slab, columns):
    block = (peers, slab, columns)
    return [
        pltpu.VMEM((2 * groups - 3,) + block, HALF),
        pltpu.VMEM((2,) + block, HALF),
        pltpu.VMEM(block, HALF),
        pltpu.SemaphoreType.DMA((3,)),
        pltpu.SemaphoreType.DMA((2, groups - 1, peers)),
        pltpu.SemaphoreType.DMA((2, groups - 1, peers)),
    ]


def last_kernel(
    cuts, line_cuts, grads_hbm, weight_hbm, tokens_hbm, hidden_grad_hbm, gain_ref, second_grad_ref,
    group_grad_ref, inner_hbm, down_hbm, hidden_hbm, mask_ref, summed_ref, terms_ref,
    *refs,
):
    count, line_count = len(cuts), len(line_cuts)
    input_ref, output_ref, gains_ref = refs[:3]
    returned, refs = refs[3 : 3 + count], refs[3 + count :]
    line_returned, scratch = refs[:line_count], refs[line_count:]
    scatter, result = scratch[:7], scratch[:1] + scratch[7:13]
    (
        sums, parts, across, totals, first_grad, keep, part_sends, part_receives,
        group_keep, group_sends, group_receives,
    ) = scratch[13:24]
    peers, groups = lax.axis_size("seq"), lax.axis_size("fsdp")
    me = lax.axis_index("seq")
    grads, grad_sems = scratch[36:38]
    inner_ref = scratch[38]
    weight_ref, down_ref, hidden_ref, tokens_ref, hidden_grad_ref, stage_sems = scratch[39:]
    blocks = Blocks(grads_hbm, grads, grad_sems)
    weight_copy, inner_copy, down_copy, *later = staged(
        (weight_hbm, inner_hbm, down_hbm, hidden_hbm, tokens_hbm, hidden_grad_hbm),
        (weight_ref, inner_ref, down_ref, hidden_ref, tokens_ref, hidden_grad_ref),
        stage_sems,
    )
    blocks.begin()
    greet_plane(True)
    back = PlaneReturn(cuts, summed_ref, returned, *scratch[24:27])
    line_back = PlaneReturn(line_cuts, scratch[32], line_returned, *scratch[27:30])
    line = LineSum(terms_ref, *scratch[30:36])

    def term(block):
        return blocks.take(lambda value: dot_nt(value, weight_ref[...]).astype(HALF))

    def result_term(block):
        return dot_nn(inner_ref[block], down_ref[...]).astype(HALF)

    gain = gain_ref[...]
    first_grad[...] = jnp.zeros_like(first_grad)

    def use(start, total):
        rows = pl.ds(start, CHUNK)
        grad = regroup(total, groups, peers)
        normed, scale = normalised(tokens_ref[rows].astype(FULL))
        first_grad[...] += jnp.sum(grad * normed, axis=0, keepdims=True)
        input_ref[rows] = (
            hidden_grad_ref[rows] + normalised_back(grad * gain, normed, scale)
        ).astype(HALF)

    def use_result(start, total):
        rows = pl.ds(start, CHUNK)
        output_ref[rows] = ((hidden_ref[rows] + total) * mask_ref[rows]).astype(HALF)

    line.begin()
    weight_copy.wait()
    every, early, late = range(peers), range(peers // 2), range(peers // 2, peers)
    windows = scatter_head(term, scatter, (), True)
    windows[0].relay()
    line.loaded(0)
    line.hand_on(0, 1, every)
    windows[1].relay()
    inner_copy.wait()
    down_copy.wait()
    result_windows = scatter_head(result_term, result, windows, True)
    for turn in every:
        back.begin(turn)
    result_windows[0].relay()
    line.hand_on(0, 2, every)
    line.load_next(1)
    for copy in later:
        copy.wait()
    scatter_tail(windows, use)
    line.loaded(1)
    line.hand_on(1, 1, early)
    result_windows[1].relay()
    tile = LANES * 2
    for peer in range(peers):
        for row in range(tile // LANES):
            at = peer * tile + row * LANES
            sums[peer, row : row + 1] = first_grad[:, at : at + LANES]
            sums[peer, 2 + row : 3 + row] = second_grad_ref[:, at : at + LANES]
        sums[peer, 4:8] = jnp.zeros((4, LANES), FULL)

    def copy(turn):
        peer = lax.rem(me + turn, peers)
        return to_peer(
            sums.at[peer], parts.at[turn], part_sends.at[turn], part_receives.at[turn], peer
        )

    kept = pltpu.make_async_copy(sums.at[me], parts.at[0], keep)
    kept.start()
    for turn in range(1, peers):
        copy(turn).start()
    line.hand_on(1, 1, late)
    scatter_tail(result_windows, use_result)
    kept.wait()
    for turn in range(1, peers):
        copy(turn).wait_recv()
        copy(turn).wait_send()
    total = parts[0]
    for turn in range(1, peers):
        total += parts[turn]
    across[0:8] = total
    for row in range(4):
        across[8 + row : 9 + row] = group_grad_ref[:, row * LANES : (row + 1) * LANES]
    across[12:16] = jnp.zeros((4, LANES), FULL)
    begin, finish = all_to_each(
        across, totals, "fsdp", groups, group_keep, group_sends, group_receives
    )
    begin()
    line.finish(line_back.begin)
    back.finish()
    line_back.finish()
    line.drain()
    for window in windows:
        window.drain(4)
    for window in result_windows:
        window.drain()
    finish()
    summed = totals[0]
    for turn in range(1, groups):
        summed += totals[turn]
    gains_ref[...] = summed


def last_rows(
    grads, weight, tokens, hidden_grad, gain, second_grad, group_grad, inner, down, hidden, mask,
    summed, sizes, terms, line_sizes,
):
    peers, own, size = grads.shape
    groups = lax.axis_size("fsdp")
    width = weight.shape[0]
    slab = summed.shape[1]

    def cuts_of(sizes):
        return tuple((sum(sizes[:number]), sizes[number]) for number in range(len(sizes)))

    return pl.pallas_call(
        partial(last_kernel, cuts_of(sizes), cuts_of(line_sizes)),
        in_specs=[in_hbm()] * 4 + [vmem()] * 3 + [in_hbm()] * 3 + [vmem()] + [in_hbm()] * 2,
        out_specs=[vmem()] * 3 + [in_hbm()] * len(sizes + line_sizes),
        out_shape=[
            jax.ShapeDtypeStruct((own, width), HALF),
            jax.ShapeDtypeStruct((own, width), HALF),
            jax.ShapeDtypeStruct((16, LANES), FULL),
        ]
        + [jax.ShapeDtypeStruct((slab, peers * part), HALF) for part in sizes + line_sizes],
        scratch_shapes=scatter_scratch(own, width)
        + scatter_scratch(own, width)[1:]
        + [
            pltpu.VMEM((peers, 8, LANES), FULL),
            pltpu.VMEM((peers, 8, LANES), FULL),
            pltpu.VMEM((16, LANES), FULL),
            pltpu.VMEM((groups, 16, LANES), FULL),
            pltpu.VMEM((1, width), FULL),
            pltpu.SemaphoreType.DMA,
            pltpu.SemaphoreType.DMA((peers,)),
            pltpu.SemaphoreType.DMA((peers,)),
            pltpu.SemaphoreType.DMA,
            pltpu.SemaphoreType.DMA((groups,)),
            pltpu.SemaphoreType.DMA((groups,)),
        ]
        + swap_scratch(len(sizes), peers)
        + swap_scratch(len(line_sizes), peers)
        + line_scratch(groups, peers, slab, terms.shape[3])
        + block_scratch(2, grads)
        + [pltpu.VMEM(inner.shape, HALF)]
        + stage_scratch(weight, down, hidden, tokens, hidden_grad, inner)[:5]
        + [pltpu.SemaphoreType.DMA((6,))],
        compiler_params=pltpu.CompilerParams(
            collective_id=5, has_side_effects=True, vmem_limit_bytes=LARGE_BYTES
        ),
        cost_estimate=cost(
            2 * peers * own * (size + inner.shape[2]) * width, 5 * peers * own * width
        ),
    )(
        grads, weight, tokens, hidden_grad, gain, second_grad, group_grad, inner, down, hidden, mask,
        summed, terms,
    )


def outputs_kernel(*refs):
    count = len(refs) // 2 - 2
    gains_ref, refs = refs[count], refs[:count] + refs[count + 1 :]
    for source, target in zip(refs[:count], refs[count : 2 * count]):
        target[...] = source[...].astype(target.dtype)
    first_ref, second_ref, group_ref = refs[2 * count :]
    group, half = lax.axis_index("fsdp"), LANES // 2
    row = group // 2
    for start, target in ((0, first_ref), (2, second_ref)):
        both = gains_ref[pl.ds(start + row, 1)]
        turned = pltpu.roll(both, half, 1)
        target[...] = jnp.where(lax.rem(group, 2) == 0, both, turned)[:, :half]
    group_ref[...] = gains_ref[pl.ds(8 + group, 1)]


def outputs(grads, rows, gains):
    arrays = [*grads, *rows]
    small = (LANES // 2, LANES // 2, LANES)
    return pl.pallas_call(
        outputs_kernel,
        in_specs=[vmem()] * (len(arrays) + 1),
        out_specs=[vmem()] * (len(arrays) + 3),
        out_shape=[jax.ShapeDtypeStruct(array.shape, FULL) for array in grads]
        + [jax.ShapeDtypeStruct(array.shape, HALF) for array in rows]
        + [jax.ShapeDtypeStruct((1, size), FULL) for size in small],
        compiler_params=pltpu.CompilerParams(vmem_limit_bytes=VMEM_BYTES),
    )(*arrays, gains)


def head_body(
    tokens,
    cotangent,
    lengths,
    block_order,
    log_decay,
    first_gain,
    query_weight,
    key_weight,
    value_weight,
    swish_weight,
    output_weight,
    group_gain,
    second_gain,
    feed_gate,
    feed_up,
    feed_down,
):
    peers, groups = lax.axis_size("seq"), lax.axis_size("fsdp")
    group = lax.axis_index("fsdp")
    batches, rows, width = tokens.shape
    own = batches * rows
    heads = log_decay.shape[0]
    key_size = query_weight.shape[1] // heads
    value_size = value_weight.shape[1] // heads
    part = feed_gate.shape[1] // peers
    slab = query_weight.shape[0]
    total = 2 * key_size + 2 * value_size

    def over_groups(local):
        return lax.all_gather(local, "fsdp", axis=0, tiled=True)

    def sum_groups(whole):
        return lax.psum_scatter(whole.astype(HALF), "fsdp", scatter_dimension=0, tiled=True)

    def gathered(cut):
        return over_groups(cut[None]).reshape(width, cut.shape[2])

    gains = jnp.concatenate(
        [
            group_gain.astype(FULL)[None],
            jnp.concatenate([first_gain, second_gain]).astype(FULL)[None],
            jnp.zeros((6, LANES), FULL),
        ],
        axis=0,
    )
    first_cut, rates, gains = first_swap(
        query_weight, key_weight, value_weight, swish_weight, log_decay, gains
    )
    out_weight = over_groups(output_weight)
    order = lax.dynamic_slice_in_dim(block_order, group * batches, batches, 0)
    numbers = jnp.arange(peers, dtype=jnp.int32)
    place = jnp.sum(
        numbers[None, None, :] * (order[:, None, :] == numbers[None, :, None]).astype(jnp.int32),
        axis=2,
    )
    live = lax.dynamic_slice_in_dim(lengths, group * batches, batches, 0)

    token_rows = tokens.reshape(own, width)
    outer_rows = cotangent.reshape(own, width)
    (
        entered, result_low, feed_cut, first_weight,
        mask, gain_one, gain_two, gain_group, decay, columns,
    ) = gather_inputs(
        lengths, block_order, token_rows, outer_rows, gains, rates, feed_gate, feed_up, first_cut,
        value_size,
    )
    first_weight = first_weight.reshape(width, total)
    entered, out_weight = lax.optimization_barrier((entered, out_weight))
    feed_weight = gathered(feed_cut)

    *saved, mixed = retention(
        entered.reshape(peers, batches, rows, width),
        first_weight,
        place,
        live,
        decay,
        columns,
        gain_group,
        key_size,
    )
    entered = entered.reshape(peers * own, width)
    mixed, feed_down = lax.optimization_barrier((mixed, feed_down))
    down_weight = over_groups(feed_down)
    mixed = mixed.reshape(peers * own, value_size)
    hidden, second = middle(mixed.reshape(peers, own, value_size), out_weight, token_rows, gain_two)
    second = second.reshape(peers * own, width)
    result_low = result_low.reshape(peers * own, width)
    inner_low, up_slope, gate_slope, down_term = feed(second, feed_weight, result_low)
    down_grad = sum_groups(down_term)
    both_grad = feed_back(result_low, down_weight, up_slope, gate_slope)
    both_term, both_grad = lax.optimization_barrier(
        (dot_tn(second, both_grad).astype(HALF), both_grad)
    )
    both_weight_grad = sum_groups(both_term).reshape(peers, slab, 2 * part)
    hidden_grad, second_gain_grad, branch_low = middle_back(
        both_grad.reshape(peers, own, 2 * part),
        feed_weight,
        hidden,
        outer_rows,
        mask,
        gain_two,
    )
    out_term, branch_low, down_grad = lax.optimization_barrier(
        (dot_tn(mixed, branch_low.reshape(peers * own, width)).astype(HALF), branch_low, down_grad)
    )
    out_grad = sum_groups(out_term)
    group_gain_grad, projected_grad = retention_back(
        branch_low.reshape(peers, batches, rows, width),
        out_weight,
        place,
        live,
        decay,
        columns,
        gain_group,
        saved,
    )
    flat_grad = projected_grad.reshape(peers * own, total)
    first_term = dot_tn(entered, flat_grad).astype(HALF)
    (
        input_rows, output_rows, small_grads,
        gate_back, up_back, query_back, key_back, value_back, swish_back,
    ) = last_rows(
        projected_grad.reshape(peers, own, total),
        first_weight,
        token_rows,
        hidden_grad,
        gain_one,
        second_gain_grad,
        group_gain_grad,
        inner_low.reshape(peers, own, part),
        down_weight,
        hidden,
        mask,
        both_weight_grad,
        (part, part),
        first_term.reshape(groups, peers, slab, total),
        (key_size, key_size, value_size, value_size),
    )
    (
        query_back, key_back, value_back, swish_back, out_back, gate_back, up_back, down_back,
        output_rows, input_rows, first_grad, second_grad, group_grad,
    ) = outputs(
        (query_back, key_back, value_back, swish_back, out_grad, gate_back, up_back, down_grad),
        (output_rows, input_rows),
        small_grads,
    )
    return (
        output_rows.reshape(batches, rows, width),
        input_rows.reshape(batches, rows, width),
        first_grad.reshape(slab),
        query_back,
        key_back,
        value_back,
        swish_back,
        out_back,
        group_grad.reshape(LANES),
        second_grad.reshape(slab),
        gate_back,
        up_back,
        down_back,
    )


def body(*arrays):
    peers, groups = lax.axis_size("seq"), lax.axis_size("fsdp")
    fits = peers == 8 and groups == 4 and arrays[4].shape[0] == peers and arrays[0].shape[0] == 2
    if fits:
        return head_body(*arrays)
    return general_body(*arrays)


def solution(mesh):
    placed = (
        P("fsdp", "seq", None),
        P("fsdp", "seq", None),
        P(),
        P(),
        P(None, "seq"),
        P(("seq", "fsdp")),
        P(("seq", "fsdp"), None),
        P(("seq", "fsdp"), None),
        P(("seq", "fsdp"), None),
        P(("seq", "fsdp"), None),
        P(("seq", "fsdp"), None),
        P(("seq", "fsdp")),
        P(("seq", "fsdp")),
        P(("seq", "fsdp"), None),
        P(("seq", "fsdp"), None),
        P(("seq", "fsdp"), None),
    )
    return jax.shard_map(
        body,
        mesh=mesh,
        in_specs=placed,
        out_specs=(
            P("fsdp", "seq", None),
            P("fsdp", "seq", None),
            P(("seq", "fsdp")),
            P(("seq", "fsdp"), None),
            P(("seq", "fsdp"), None),
            P(("seq", "fsdp"), None),
            P(("seq", "fsdp"), None),
            P(("seq", "fsdp"), None),
            P(("seq", "fsdp")),
            P(("seq", "fsdp")),
            P(("seq", "fsdp"), None),
            P(("seq", "fsdp"), None),
            P(("seq", "fsdp"), None),
        ),
        check_vma=False,
    )
```

```python
from functools import partial, reduce

import jax
import jax.numpy as jnp
from jax import lax
from jax.experimental import pallas as pl
from jax.experimental.pallas import tpu as pltpu
from jax.sharding import PartitionSpec as P

EPSILON = 1e-05
HIGHEST = lax.Precision.HIGHEST


def carried_in(value, axis, combine, identity, reverse):
    peers, index = (lax.axis_size(axis), lax.axis_index(axis))
    everything = jax.tree.map(
        lambda part, kind: lax.all_gather(part.astype(kind), axis),
        value,
        (jnp.bfloat16, jnp.bfloat16),
    )
    start = jax.tree.map(
        lambda part, zero: jnp.broadcast_to(jnp.asarray(zero, part.dtype), part.shape),
        value,
        identity,
    )

    def turn(k, before):
        at = peers - 1 - k if reverse else k
        reached = at > index if reverse else at < index
        new = combine(
            before, jax.tree.map(lambda part, own: part[at].astype(own.dtype), everything, value)
        )
        return jax.tree.map(lambda a, b: jnp.where(reached, a, b), new, before)

    return lax.fori_loop(0, peers, turn, start)


def norm_rows(values, gain):
    average = jnp.mean(values, axis=-1, keepdims=True)
    centered = values - average
    variance = jnp.mean(centered * centered, axis=-1, keepdims=True)
    return centered * lax.rsqrt(variance + EPSILON) * gain


def gated_swish(swish_in, grouped):
    return jax.nn.silu(swish_in) * grouped


def gated_gelu(gate_in, upward):
    return jax.nn.gelu(gate_in) * upward


def chain_states(earlier, later):
    return (earlier[0] * later[0], later[0][:, None, None] * earlier[1] + later[1])


def transposed(left_rows, weight):
    return jnp.einsum("ie,fe->if", left_rows, weight, preferred_element_type=jnp.float32)


def plain_dot(left_rows, weight):
    return jnp.dot(left_rows, weight, preferred_element_type=jnp.float32)


def outer_term(left_rows, right_rows):
    return jnp.einsum("ni,no->io", left_rows, right_rows, preferred_element_type=jnp.float32)


def spread_sum(matrix_pairs, vectors):
    terms = tuple((outer_term(left_rows, right_rows) for left_rows, right_rows in matrix_pairs))
    pieces = lax.psum_scatter(
        terms + tuple(vectors), ("seq", "fsdp"), scatter_dimension=0, tiled=True
    )
    return list(pieces)


def join_terms(collected):
    matrix_pairs = []
    for member in range(len(collected[0][0])):
        lefts = jnp.concatenate([entry[0][member][0] for entry in collected], axis=0)
        rights = jnp.concatenate([entry[0][member][1] for entry in collected], axis=0)
        matrix_pairs.append((lefts, rights))
    vectors = [
        reduce(jnp.add, [entry[1][member] for entry in collected])
        for member in range(len(collected[0][1]))
    ]
    return (matrix_pairs, vectors)


def layer_step(gathered, inputs, cot_rows, live_mask, log_rates):
    (
        first_gain,
        query_weight,
        key_weight,
        value_weight,
        swish_weight,
        output_weight,
        group_gain,
        second_gain,
        feed_gate,
        feed_up,
        feed_down,
    ) = gathered
    floats = jnp.float32
    halves = jnp.bfloat16
    head_count = log_rates.shape[0]
    token_rows = inputs.shape[0]
    key_size = query_weight.shape[1] // head_count
    value_size = value_weight.shape[1] // head_count
    start_values = inputs.astype(floats)
    normed_one, pull_one = jax.vjp(norm_rows, start_values, first_gain.astype(floats))
    normed = normed_one.astype(halves)
    queries = plain_dot(normed, query_weight).astype(halves)
    keys_in = plain_dot(normed, key_weight).astype(halves) * live_mask[:, None].astype(halves)
    values_in = plain_dot(normed, value_weight).astype(halves)
    swish_in = plain_dot(normed, swish_weight)
    queries3 = queries.reshape(token_rows, head_count, key_size)
    keys3 = keys_in.reshape(token_rows, head_count, key_size)
    values3 = values_in.reshape(token_rows, head_count, value_size)
    cumulative = jnp.cumsum(log_rates, axis=1)
    slot_index = jnp.arange(token_rows)
    lower_mask = slot_index[:, None] >= slot_index[None, :]
    spread = cumulative[:, :, None] - cumulative[:, None, :]
    decay_matrix = jnp.where(lower_mask, jnp.exp(jnp.where(lower_mask, spread, 0.0)), 0.0)
    block_decay = jnp.exp(cumulative[:, -1])
    end_weight = jnp.exp(cumulative[:, -1:] - cumulative).T[:, :, None]
    entry_decay = jnp.exp(cumulative).T[:, :, None]
    query_wide = queries3.astype(floats)
    key_wide = keys3.astype(floats)
    value_wide = values3.astype(floats)
    state_term = jnp.einsum("jhd,jhe->hde", key_wide * end_weight, value_wide, precision=HIGHEST)
    state_identity = (jnp.ones_like(block_decay), jnp.zeros_like(state_term))
    _, start_state = carried_in(
        (block_decay, state_term), "seq", chain_states, state_identity, False
    )
    scores = jnp.einsum("ihd,jhd->hij", queries3, keys3, preferred_element_type=floats)
    weights = (scores * decay_matrix).astype(halves)
    intra_term = jnp.einsum("hij,jhe->ihe", weights, values3, preferred_element_type=floats)
    carried = entry_decay * jnp.einsum("ihd,hde->ihe", query_wide, start_state, precision=HIGHEST)
    retained = intra_term + carried
    grouped, pull_group = jax.vjp(
        norm_rows, retained, group_gain.astype(floats).reshape(head_count, value_size)
    )
    grouped_flat = grouped.reshape(token_rows, head_count * value_size)
    mixed_float, pull_mixed = jax.vjp(gated_swish, swish_in, grouped_flat)
    mixed_low = mixed_float.astype(halves)
    hidden = start_values + plain_dot(mixed_low, output_weight)
    normed_two, pull_two = jax.vjp(norm_rows, hidden, second_gain.astype(floats))
    second = normed_two.astype(halves)
    gate_two = plain_dot(second, feed_gate)
    upward = plain_dot(second, feed_up)
    inner_float, pull_inner = jax.vjp(gated_gelu, gate_two, upward)
    inner_low = inner_float.astype(halves)
    result = plain_dot(inner_low, feed_down)
    output_rows = ((hidden + result) * live_mask[:, None]).astype(halves)
    outer_grad = cot_rows.astype(floats) * live_mask[:, None]
    result_low = outer_grad.astype(halves)
    inner_grad = transposed(result_low, feed_down)
    gate_two_grad, upward_grad = pull_inner(inner_grad)
    gate_two_low = gate_two_grad.astype(halves)
    upward_low = upward_grad.astype(halves)
    second_grad = transposed(gate_two_low, feed_gate) + transposed(upward_low, feed_up)
    hidden_part, second_gain_grad = pull_two(second_grad)
    hidden_grad = outer_grad + hidden_part
    branch_low = hidden_grad.astype(halves)
    mixed_grad = transposed(branch_low, output_weight)
    swish_grad, grouped_grad = pull_mixed(mixed_grad)
    swish_low = swish_grad.astype(halves)
    retained_grad, group_gain_grad = pull_group(
        grouped_grad.reshape(token_rows, head_count, value_size)
    )
    retained_low = retained_grad.astype(halves)
    weights_grad = jnp.einsum("ihe,jhe->hij", retained_low, values3, preferred_element_type=floats)
    scores_low = (weights_grad * decay_matrix).astype(halves)
    query_intra = jnp.einsum("hij,jhd->ihd", scores_low, keys3, preferred_element_type=floats)
    key_intra = jnp.einsum("hij,ihd->jhd", scores_low, queries3, preferred_element_type=floats)
    value_intra = jnp.einsum("hij,ihe->jhe", weights, retained_low, preferred_element_type=floats)
    retained_wide = retained_low.astype(floats)
    query_carried = entry_decay * jnp.einsum(
        "ihe,hde->ihd", retained_wide, start_state, precision=HIGHEST
    )
    local_grad = jnp.einsum(
        "ihd,ihe->hde", query_wide * entry_decay, retained_wide, precision=HIGHEST
    )
    _, end_grad = carried_in((block_decay, local_grad), "seq", chain_states, state_identity, True)
    key_state = end_weight * jnp.einsum("jhe,hde->jhd", value_wide, end_grad, precision=HIGHEST)
    value_state = end_weight * jnp.einsum("jhd,hde->jhe", key_wide, end_grad, precision=HIGHEST)
    query_low = (
        (query_intra + query_carried).astype(halves).reshape(token_rows, head_count * key_size)
    )
    key_low = (
        ((key_intra + key_state) * live_mask[:, None, None])
        .astype(halves)
        .reshape(token_rows, head_count * key_size)
    )
    value_low = (
        (value_intra + value_state).astype(halves).reshape(token_rows, head_count * value_size)
    )
    normed_grad = (
        transposed(query_low, query_weight)
        + transposed(key_low, key_weight)
        + transposed(value_low, value_weight)
        + transposed(swish_low, swish_weight)
    )
    input_part, first_gain_grad = pull_one(normed_grad)
    grad_rows = (hidden_grad + input_part).astype(halves)
    matrix_pairs = [
        (normed, query_low),
        (normed, key_low),
        (normed, value_low),
        (normed, swish_low),
        (mixed_low, branch_low),
        (second, gate_two_low),
        (second, upward_low),
        (inner_low, result_low),
    ]
    vectors = [first_gain_grad, group_gain_grad.reshape(-1), second_gain_grad]
    return (output_rows, grad_rows, matrix_pairs, vectors)


def general_body(
    tokens,
    cotangent,
    lengths,
    block_order,
    log_decay,
    first_gain,
    query_weight,
    key_weight,
    value_weight,
    swish_weight,
    output_weight,
    group_gain,
    second_gain,
    feed_gate,
    feed_up,
    feed_down,
):
    batches = tokens.shape[0]
    block_rows = tokens.shape[1]
    selected_locations = lax.axis_size("seq")
    position = lax.axis_index("seq")
    group_index = lax.axis_index("fsdp")
    place_numbers = jnp.arange(selected_locations, dtype=jnp.int32)
    arrived_tokens, arrived_cotangent = (
        lax.all_gather(tokens, "seq", axis=1, tiled=True),
        lax.all_gather(cotangent, "seq", axis=1, tiled=True),
    )
    gathered = (
        lax.all_gather(first_gain, ("seq", "fsdp"), axis=0, tiled=True),
        lax.all_gather(query_weight, ("seq", "fsdp"), axis=0, tiled=True),
        lax.all_gather(key_weight, ("seq", "fsdp"), axis=0, tiled=True),
        lax.all_gather(value_weight, ("seq", "fsdp"), axis=0, tiled=True),
        lax.all_gather(swish_weight, ("seq", "fsdp"), axis=0, tiled=True),
        lax.all_gather(output_weight, ("seq", "fsdp"), axis=0, tiled=True),
        lax.all_gather(group_gain, ("seq", "fsdp"), axis=0, tiled=True),
        lax.all_gather(second_gain, ("seq", "fsdp"), axis=0, tiled=True),
        lax.all_gather(feed_gate, ("seq", "fsdp"), axis=0, tiled=True),
        lax.all_gather(feed_up, ("seq", "fsdp"), axis=0, tiled=True),
        lax.all_gather(feed_down, ("seq", "fsdp"), axis=0, tiled=True),
    )
    outputs = []
    input_grads = []
    collected = []
    order_rows = []
    for batch_number in range(batches):
        sequence = group_index * batches + batch_number
        order_row = lax.dynamic_index_in_dim(block_order, sequence, 0, keepdims=False)
        order_rows.append(order_row)
        source = jnp.sum(place_numbers * (order_row == position).astype(jnp.int32))
        token_rows = lax.dynamic_slice_in_dim(
            arrived_tokens[batch_number], source * block_rows, block_rows, 0
        )
        cot_rows = lax.dynamic_slice_in_dim(
            arrived_cotangent[batch_number], source * block_rows, block_rows, 0
        )
        live_length = lax.dynamic_index_in_dim(lengths, sequence, 0, keepdims=False)
        location_number = position * block_rows + jnp.arange(block_rows, dtype=jnp.int32)
        live_mask = (location_number < live_length).astype(jnp.float32)
        output_rows, grad_rows, matrix_pairs, vectors = layer_step(
            gathered, token_rows, cot_rows, live_mask, log_decay
        )
        outputs.append(output_rows)
        input_grads.append(grad_rows)
        collected.append((matrix_pairs, vectors))
    joined_pairs, joined_vectors = join_terms(collected)
    shards = spread_sum(joined_pairs, joined_vectors)
    every_output, every_grad = (
        lax.all_gather(jnp.stack(outputs), "seq", axis=1, tiled=True),
        lax.all_gather(jnp.stack(input_grads), "seq", axis=1, tiled=True),
    )
    returned = []
    returned_grads = []
    for batch_number in range(batches):
        target = lax.dynamic_index_in_dim(order_rows[batch_number], position, 0, keepdims=False)
        returned.append(
            lax.dynamic_slice_in_dim(every_output[batch_number], target * block_rows, block_rows, 0)
        )
        returned_grads.append(
            lax.dynamic_slice_in_dim(every_grad[batch_number], target * block_rows, block_rows, 0)
        )
    return (
        jnp.stack(returned),
        jnp.stack(returned_grads),
        shards[8],
        shards[0],
        shards[1],
        shards[2],
        shards[3],
        shards[4],
        shards[9],
        shards[10],
        shards[5],
        shards[6],
        shards[7],
    )


FULL = jnp.float32
HALF = jnp.bfloat16
MESH = pl.DeviceIdType.MESH
VMEM_BYTES = 56 * 1024 * 1024
LARGE_BYTES = 63 * 1024 * 1024
LANES = 128


def dot_nn(left, right):
    return jnp.dot(left, right, preferred_element_type=FULL)


def dot_nt(left, right):
    return lax.dot_general(left, right, (((1,), (1,)), ((), ())), preferred_element_type=FULL)


def dot_tn(left, right):
    return lax.dot_general(left, right, (((0,), (0,)), ((), ())), preferred_element_type=FULL)


def plane_peers():
    me = lax.axis_index("seq")
    core = lax.rem(me, 2)
    across = 2 - 4 * lax.rem(me // 2, 2)
    down = 4 - 8 * (me // 4)
    return me, me + 1 - 2 * core, me + across, me + down, me + across + down


def to_peer(source, target, send, receive, peer):
    return pltpu.make_async_remote_copy(
        src_ref=source,
        dst_ref=target,
        send_sem=send,
        recv_sem=receive,
        device_id={"seq": peer},
        device_id_type=MESH,
    )


def greet_neighbours():
    _, other, near, below, _ = plane_peers()
    barrier = pltpu.get_barrier_semaphore()
    for peer in (other, near, below):
        pl.semaphore_signal(barrier, inc=1, device_id={"seq": peer}, device_id_type=MESH)
    pl.semaphore_wait(barrier, 3)


GATHER_COPIES = 14


def gather_plan():
    me, other, near, below, far = plane_peers()
    flip = other - me
    return (
        (me, 0, near, near),
        (me, 1, below, below),
        (me, 0, other, other),
        (me, 1, other, other),
        (me, 1, near, near),
        (me, 0, below, below),
        (near, 0, below, far),
        (below, 1, near, far),
        (near, 0, other, near + flip),
        (below, 1, other, below + flip),
        (near, 1, other, near + flip),
        (below, 0, other, below + flip),
        (far, 0, other, far + flip),
        (far, 1, other, far + flip),
    )


class PlaneGather:
    def __init__(self, own, out, keeps, sends, receives, window=0, windows=1):
        self.own, self.out = own, out
        self.keep = None if keeps is None else keeps.at[window]
        self.sends, self.receives = sends, receives
        self.size = own.shape[0] // windows
        self.window, self.start = window, window * self.size
        self.half = self.size // 2

    def rows(self, which):
        return pl.ds(self.start + which * self.half, self.half)

    def kept(self):
        me = lax.axis_index("seq")
        rows = pl.ds(self.start, self.size)
        return pltpu.make_async_copy(self.own.at[rows], self.out.at[me, rows], self.keep)

    def sent(self, source, target, number, peer):
        at = (self.window, number)
        return to_peer(source, target, self.sends.at[at], self.receives.at[at], peer)

    def copy(self, number):
        block, which, peer, _ = gather_plan()[number]
        target = self.out.at[block, self.rows(which)]
        source = self.own.at[self.rows(which)] if number < 6 else target
        return self.sent(source, target, number, peer)

    def landed(self, number):
        _, which, peer, landing = gather_plan()[number]
        target = self.out.at[landing, self.rows(which)]
        self.sent(target, target, number, peer).wait_recv()

    def begin(self):
        if self.keep is not None:
            self.kept().start()
        for number in range(6):
            self.copy(number).start()

    def relay(self):
        for arrived, onward in ((0, (6, 8)), (1, (7, 9)), (4, (10,)), (5, (11,))):
            self.landed(arrived)
            for number in onward:
                self.copy(number).start()

    def relay_far(self):
        for arrived, onward in ((6, 12), (7, 13)):
            self.landed(arrived)
            self.copy(onward).start()

    def expect(self, *numbers):
        for number in numbers:
            self.landed(number)

    def drain(self):
        for number in range(GATHER_COPIES):
            self.copy(number).wait_send()
        if self.keep is not None:
            self.kept().wait()

    def finish(self):
        self.relay_far()
        self.expect(2, 3, 8, 9, 10, 11, 12, 13)
        self.drain()


def gather_scratch(windows=1):
    return [
        pltpu.SemaphoreType.DMA((windows,)),
        pltpu.SemaphoreType.DMA((windows, GATHER_COPIES)),
        pltpu.SemaphoreType.DMA((windows, GATHER_COPIES)),
    ]


SCATTER_COPIES = 10
WINDOWS = 2
CHUNK = 32


def by_chunks(rows, work):
    def step(number, carry):
        work(pl.ds(pl.multiple_of(number * CHUNK, CHUNK), CHUNK))
        return carry

    lax.fori_loop(0, rows // CHUNK, step, 0)


class PlaneScatter:
    def __init__(self, window, others, terms, cores, nears, belows, sends, receives):
        self.window = window
        self.others, self.terms, self.cores = others, terms, cores
        self.nears, self.belows = nears, belows
        self.sends, self.receives = sends, receives
        self.size = terms.shape[1] // WINDOWS
        self.half = self.size // 2
        self.start = window * self.size

    def copy(self, number):
        _, other, near, below, _ = plane_peers()
        whole = pl.ds(self.start, self.size)
        upper, lower = (pl.ds(self.start + at * self.half, self.half) for at in (0, 1))
        if number < 4:
            source, target, peer = (
                self.others.at[number, whole],
                self.cores.at[number, whole],
                other,
            )
        else:
            slot, rows, landing, place, peer = (
                (0, upper, self.nears, 0, near),
                (0, lower, self.belows, 0, below),
                (1, upper, self.nears, 1, near),
                (2, lower, self.belows, 1, below),
                (1, lower, self.nears, 2, near),
                (2, upper, self.belows, 2, below),
            )[number - 4]
            source, target = self.terms.at[slot, rows], landing.at[self.window, place]
        at = (self.window, number)
        return to_peer(source, target, self.sends.at[at], self.receives.at[at], peer)

    def fold(self, slot):
        def work(rows):
            here = pl.ds(pl.multiple_of(self.start + rows.start, CHUNK), CHUNK)
            self.terms[slot, here] = (
                self.terms[slot, here].astype(FULL) + self.cores[slot, here].astype(FULL)
            ).astype(HALF)

        by_chunks(self.size, work)

    def fold_half(self, slot, which, landed):
        def work(rows):
            at = self.start + which * self.half
            here = pl.ds(pl.multiple_of(at + rows.start, CHUNK), CHUNK)
            self.terms[slot, here] = (
                self.terms[slot, here].astype(FULL) + landed[self.window, 0, rows].astype(FULL)
            ).astype(HALF)

        by_chunks(self.half, work)

    def advance(self, slot):
        self.copy(slot).wait_recv()
        self.fold(slot)
        for number in ((4, 5), (6,), (7,), ())[slot]:
            self.copy(number).start()

    def relay(self):
        self.copy(4).wait_recv()
        self.fold_half(2, 0, self.nears)
        self.copy(9).start()
        self.copy(5).wait_recv()
        self.fold_half(1, 1, self.belows)
        self.copy(8).start()

    def finish(self):
        for number in (6, 7, 8, 9):
            self.copy(number).wait_recv()

    def drain(self, first=0):
        for number in range(first, SCATTER_COPIES):
            self.copy(number).wait_send()

    def total(self, at):
        upper = at < self.half
        rows = pl.ds(at if upper else at - self.half, CHUNK)
        near, below = (1, 2) if upper else (2, 1)
        return (
            self.terms[3, pl.ds(self.start + at, CHUNK)].astype(FULL)
            + self.nears[self.window, near, rows].astype(FULL)
            + self.belows[self.window, below, rows].astype(FULL)
        )


def block_order_of_plane():
    me, other, near, below, far = plane_peers()
    return [block + at for block in (far, near, below, me) for at in (other - me, 0)]


class Blocks:
    def __init__(self, source, target, sems):
        self.source, self.target, self.sems = source, target, sems
        self.blocks, self.taken = block_order_of_plane(), 0

    def load(self, number):
        slot = number % self.target.shape[0]
        return pltpu.make_async_copy(
            self.source.at[self.blocks[number]], self.target.at[slot], self.sems.at[slot]
        )

    def begin(self):
        for number in range(min(len(self.blocks), self.target.shape[0])):
            self.load(number).start()

    def take(self, work):
        number, slots = self.taken, self.target.shape[0]
        self.taken += 1
        self.load(number).wait()
        out = work(self.target[number % slots])
        if number + slots < len(self.blocks):
            self.load(number + slots).start()
        return out


def staged(sources, targets, sems):
    copies = [
        pltpu.make_async_copy(source, target, sems.at[number])
        for number, (source, target) in enumerate(zip(sources, targets))
    ]
    for copy in copies:
        copy.start()
    return copies


def stage_scratch(*arrays):
    return [pltpu.VMEM(array.shape, array.dtype) for array in arrays] + [
        pltpu.SemaphoreType.DMA((len(arrays),))
    ]


def block_scratch(count, array):
    return [
        pltpu.VMEM((count,) + array.shape[1:], array.dtype),
        pltpu.SemaphoreType.DMA((count,)),
    ]


def scatter_head(term, refs, earlier=(), relay_later=False):
    windows = [PlaneScatter(window, *refs) for window in range(WINDOWS)]
    others, terms = refs[:2]
    blocks = block_order_of_plane()

    def fill(slot):
        for window in earlier:
            window.copy(slot).wait_send()
        others[slot] = term(blocks[2 * slot])
        for window in windows:
            window.copy(slot).start()
        terms[slot] = term(blocks[2 * slot + 1])

    fill(0)
    for slot in range(4):
        if slot < 3:
            fill(slot + 1)
        windows[0].advance(slot)
    if not relay_later:
        windows[0].relay()
    for window in windows[1:]:
        for slot in range(4):
            window.advance(slot)
        if not relay_later:
            window.relay()
    return windows


def scatter_tail(windows, use, after=lambda window: None):
    for number, window in enumerate(windows):
        window.finish()
        for at in range(0, window.size, CHUNK):
            use(window.start + at, window.total(at))
        after(number)


def scatter_scratch(rows, width):
    half = rows // WINDOWS // 2
    return [
        pltpu.VMEM((4, rows, width), HALF),
        pltpu.VMEM((4, rows, width), HALF),
        pltpu.VMEM((4, rows, width), HALF),
        pltpu.VMEM((WINDOWS, 3, half, width), HALF),
        pltpu.VMEM((WINDOWS, 3, half, width), HALF),
        pltpu.SemaphoreType.DMA((WINDOWS, SCATTER_COPIES)),
        pltpu.SemaphoreType.DMA((WINDOWS, SCATTER_COPIES)),
    ]


def regroup(values, outer, inner):
    rows = values.shape[0]
    low_half = lax.broadcasted_iota(jnp.int32, (rows, LANES), 1) < LANES // 2

    def piece(p, q):
        at = (p * inner + q) // 2
        return values[:, at * LANES : (at + 1) * LANES]

    def turned(value):
        return pltpu.roll(value, LANES // 2, 1)

    groups = []
    for q in range(inner):
        for p in range(0, outer, 2):
            first, second = piece(p, q), piece(p + 1, q)
            if q % 2 == 0:
                groups.append(jnp.where(low_half, first, turned(second)))
            else:
                groups.append(jnp.where(low_half, turned(first), second))
    return jnp.concatenate(groups, axis=1)


def normalised(values):
    average = jnp.mean(values, axis=-1, keepdims=True)
    centered = values - average
    scale = lax.rsqrt(jnp.mean(centered * centered, axis=-1, keepdims=True) + EPSILON)
    return centered * scale, scale


def normalised_back(grad, normed, scale):
    average = jnp.mean(grad, axis=-1, keepdims=True)
    along = jnp.mean(grad * normed, axis=-1, keepdims=True)
    return (grad - average - normed * along) * scale


def vmem():
    return pl.BlockSpec(memory_space=pltpu.VMEM)


def in_hbm():
    return pl.BlockSpec(memory_space=pl.ANY)


def cost(flops, link_bytes):
    return pl.CostEstimate(flops=int(flops), bytes_accessed=int(link_bytes) * 16, transcendentals=0)


def linked(collective):
    return pltpu.CompilerParams(
        collective_id=collective, has_side_effects=True, vmem_limit_bytes=VMEM_BYTES
    )


class PlaneSwap:
    def __init__(self, weights, targets, keeps, sends, receives):
        self.weights, self.targets = weights, targets
        self.keeps, self.sends, self.receives = keeps, sends, receives
        self.peers = lax.axis_size("seq")

    def part(self, number, peer):
        weight, (target, start) = self.weights[number], self.targets[number]
        size = weight.shape[1] // self.peers
        return weight.at[:, pl.ds(pl.multiple_of(peer * size, LANES), size)]

    def place(self, number, peer):
        weight, (target, start) = self.weights[number], self.targets[number]
        return target.at[peer, :, pl.ds(start, weight.shape[1] // self.peers)]

    def copy(self, number, turn):
        me = lax.axis_index("seq")
        peer = lax.rem(me + turn, self.peers)
        return to_peer(
            self.part(number, peer),
            self.place(number, me),
            self.sends.at[number, turn],
            self.receives.at[number, turn],
            peer,
        )

    def landed(self, number, turn):
        me = lax.axis_index("seq")
        peer = lax.rem(me + self.peers - turn, self.peers)
        target = self.place(number, peer)
        to_peer(
            target, target, self.sends.at[number, turn], self.receives.at[number, turn], peer
        ).wait_recv()

    def kept(self, number):
        me = lax.axis_index("seq")
        return pltpu.make_async_copy(
            self.part(number, me), self.place(number, me), self.keeps.at[number]
        )

    def begin(self):
        for number in range(len(self.weights)):
            for turn in range(1, self.peers):
                self.copy(number, turn).start()
            self.kept(number).start()

    def finish(self):
        for number in range(len(self.weights)):
            for turn in range(1, self.peers):
                self.landed(number, turn)
                self.copy(number, turn).wait_send()
            self.kept(number).wait()


def swap_scratch(count, peers):
    return [
        pltpu.SemaphoreType.DMA((count,)),
        pltpu.SemaphoreType.DMA((count, peers)),
        pltpu.SemaphoreType.DMA((count, peers)),
    ]


def greet_plane(with_groups):
    me, group = lax.axis_index("seq"), lax.axis_index("fsdp")
    peers, groups = lax.axis_size("seq"), lax.axis_size("fsdp")
    barrier = pltpu.get_barrier_semaphore()
    count = peers - 1
    for turn in range(1, peers):
        peer = lax.rem(me + turn, peers)
        pl.semaphore_signal(barrier, inc=1, device_id={"seq": peer}, device_id_type=MESH)
    if with_groups:
        count += groups - 1
        for turn in range(1, groups):
            peer = lax.rem(group + turn, groups)
            pl.semaphore_signal(barrier, inc=1, device_id={"fsdp": peer}, device_id_type=MESH)
    pl.semaphore_wait(barrier, count)


def all_to_each(source, out, axis, size, keep, sends, receives):
    me = lax.axis_index(axis)

    def copy(turn, slot):
        peer = lax.rem(me + turn, size)
        return pltpu.make_async_remote_copy(
            src_ref=source,
            dst_ref=out.at[slot],
            send_sem=sends.at[turn],
            recv_sem=receives.at[turn],
            device_id={axis: peer},
            device_id_type=MESH,
        )

    def begin():
        pltpu.make_async_copy(source, out.at[me], keep).start()
        for turn in range(1, size):
            copy(turn, me).start()

    def finish():
        for turn in range(1, size):
            copy(turn, lax.rem(me + size - turn, size)).wait_recv()
            copy(turn, me).wait_send()
        pltpu.make_async_copy(source, out.at[me], keep).wait()

    return begin, finish


def first_swap_kernel(
    query_ref, key_ref, value_ref, swish_ref, rates_ref, gains_ref,
    cut_out, rates_out, gains_out,
    column, keeps, sends, receives, rate_keep, rate_sends, rate_receives,
    group_keep, group_sends, group_receives, gain_keep, gain_sends, gain_receives,
):
    peers, groups = lax.axis_size("seq"), lax.axis_size("fsdp")
    size, wide = query_ref.shape[1] // peers, value_ref.shape[1] // peers
    greet_plane(True)
    begin_groups, finish_groups = all_to_each(
        gains_ref, column, "fsdp", groups, group_keep, group_sends, group_receives
    )
    begin_rates, finish_rates = all_to_each(
        rates_ref, rates_out, "seq", peers, rate_keep, rate_sends, rate_receives
    )
    begin_gains, finish_gains = all_to_each(
        column, gains_out, "seq", peers, gain_keep, gain_sends, gain_receives
    )
    swap = PlaneSwap(
        (query_ref, key_ref, value_ref, swish_ref),
        ((cut_out, 0), (cut_out, size), (cut_out, 2 * size), (cut_out, 2 * size + wide)),
        keeps,
        sends,
        receives,
    )
    begin_groups()
    begin_rates()
    swap.begin()
    finish_groups()
    begin_gains()
    finish_rates()
    finish_gains()
    swap.finish()


def first_swap(query, key, value, swish, rates, gains):
    peers, groups = lax.axis_size("seq"), lax.axis_size("fsdp")
    slab = query.shape[0]
    total = sum(weight.shape[1] for weight in (query, key, value, swish)) // peers
    return pl.pallas_call(
        first_swap_kernel,
        in_specs=[in_hbm()] * 4 + [vmem()] * 2,
        out_specs=[in_hbm()] + [vmem()] * 2,
        out_shape=[
            jax.ShapeDtypeStruct((peers, slab, total), HALF),
            jax.ShapeDtypeStruct((peers,) + rates.shape, FULL),
            jax.ShapeDtypeStruct((peers, groups) + gains.shape, FULL),
        ],
        scratch_shapes=[pltpu.VMEM((groups,) + gains.shape, FULL)]
        + swap_scratch(4, peers)
        + [pltpu.SemaphoreType.DMA] + [pltpu.SemaphoreType.DMA((peers,))] * 2
        + [pltpu.SemaphoreType.DMA] + [pltpu.SemaphoreType.DMA((groups,))] * 2
        + [pltpu.SemaphoreType.DMA] + [pltpu.SemaphoreType.DMA((peers,))] * 2,
        compiler_params=linked(0),
        cost_estimate=cost(0, 2 * slab * peers * total),
    )(query, key, value, swish, rates, gains)


class LineGather:
    def __init__(self, own, out, keep, sends, receives):
        self.own, self.out = own, out
        self.keep, self.sends, self.receives = keep, sends, receives
        self.me, self.last = lax.axis_index("fsdp"), lax.axis_size("fsdp") - 1
        self.pieces = own.shape[0]

    def block(self, way, depth):
        return self.me - depth if way == 0 else self.me + depth

    def holds(self, way, depth):
        return self.me >= depth if way == 0 else self.me + depth <= self.last

    def passes(self, way):
        return self.me < self.last if way == 0 else self.me > 0

    def sent(self, source, way, depth, piece, block):
        at = (way, depth, piece)
        return pltpu.make_async_remote_copy(
            src_ref=source,
            dst_ref=self.out.at[block, piece],
            send_sem=self.sends.at[at],
            recv_sem=self.receives.at[at],
            device_id={"fsdp": self.me + 1 if way == 0 else self.me - 1},
            device_id_type=MESH,
        )

    def copy(self, way, depth, piece):
        block = self.block(way, depth)
        source = self.own.at[piece] if depth == 0 else self.out.at[block, piece]
        return self.sent(source, way, depth, piece, block)

    def landed(self, way, depth, piece):
        block = self.block(way, depth)
        self.sent(self.out.at[block, piece], way, depth - 1, piece, block).wait_recv()

    def kept(self):
        return pltpu.make_async_copy(self.own, self.out.at[self.me], self.keep)

    def begin(self):
        for piece in range(self.pieces):
            for way in (0, 1):

                @pl.when(self.passes(way))
                def _():
                    self.copy(way, 0, piece).start()

        self.kept().start()

    def hand_on(self, depth):
        for piece in range(self.pieces):
            for way in (0, 1):

                @pl.when(self.holds(way, depth) & self.passes(way))
                def _():
                    self.landed(way, depth, piece)
                    self.copy(way, depth, piece).start()

    def finish(self):
        for depth in range(1, self.last + 1):
            for piece in range(self.pieces):
                for way in (0, 1):

                    @pl.when(self.holds(way, depth) & jnp.logical_not(self.passes(way)))
                    def _():
                        self.landed(way, depth, piece)

        for depth in range(self.last):
            for piece in range(self.pieces):
                for way in (0, 1):

                    @pl.when(self.holds(way, depth) & self.passes(way))
                    def _():
                        self.copy(way, depth, piece).wait_send()

        self.kept().wait()


def unpack_gains(gains_ref, one_ref, two_ref, group_ref):
    peers, groups = gains_ref.shape[:2]
    low_half = lax.broadcasted_iota(jnp.int32, (1, LANES), 1) < LANES // 2
    for peer in range(peers):
        for at in range(0, groups, 2):
            left, right = gains_ref[peer, at, 1:2], gains_ref[peer, at + 1, 1:2]
            lanes = pl.ds((peer * groups + at) * LANES // 2, LANES)
            one_ref[:, lanes] = jnp.where(low_half, left, pltpu.roll(right, LANES // 2, 1))
            two_ref[:, lanes] = jnp.where(low_half, pltpu.roll(left, LANES // 2, 1), right)
    me = lax.axis_index("seq")
    for at in range(groups):
        group_ref[:, at * LANES : (at + 1) * LANES] = gains_ref[me, at, 0:1]


def unpack_rates(rates_ref, decay_ref, column_ref):
    blocks, _, rows = rates_ref.shape
    me = lax.axis_index("seq")
    total = jnp.concatenate([rates_ref[block, pl.ds(me, 1)] for block in range(blocks)], axis=0)
    lane = lax.broadcasted_iota(jnp.int32, total.shape, 1)
    shift = 1
    while shift < rows:
        total += jnp.where(lane >= shift, pltpu.roll(total, shift, 1), 0.0)
        shift *= 2
    square = (rows, rows)
    lower = lax.broadcasted_iota(jnp.int32, square, 0) >= lax.broadcasted_iota(jnp.int32, square, 1)
    for block in range(blocks):
        along = jnp.broadcast_to(total[block : block + 1], square)
        down = along.T
        spread = jnp.where(lower, down - along, 0.0)
        decay_ref[block] = jnp.where(lower, jnp.exp(spread), 0.0)
        first = down[:, 0:1]
        column_ref[block, :, 0:1] = jnp.exp(first)
        column_ref[block, :, 1:2] = jnp.exp(first[rows - 1 : rows] - first)


def inputs_kernel(
    lengths_ref, order_ref, tokens_ref, grad_ref, gains_ref, rates_ref, gate_ref, up_ref, cut_ref,
    entered_out, grads_out, feed_out, weight_out,
    mask_ref, gain_ref, second_ref, group_ref, decay_ref, column_ref, place_ref, live_ref,
    own_entered, own_grad, keep_one, sends_one, receives_one, keep_two, sends_two, receives_two,
    keeps, sends, receives, line_keep, line_sends, line_receives,
):
    peers, groups = lax.axis_size("seq"), lax.axis_size("fsdp")
    greet_plane(True)
    line = LineGather(cut_ref, weight_out, line_keep, line_sends, line_receives)
    line.begin()
    size = gate_ref.shape[1] // peers
    me, group = lax.axis_index("seq"), lax.axis_index("fsdp")
    batches = lengths_ref.shape[0] // groups
    block = tokens_ref.shape[0] // batches
    for batch in range(batches):
        sequence = group * batches + batch
        numbers = order_ref[sequence, me] * block + lax.broadcasted_iota(jnp.int32, (block, 1), 0)
        live_ref[batch] = lengths_ref[sequence]
        live = (numbers < lengths_ref[sequence]).astype(FULL)
        mask_ref[batch * block : (batch + 1) * block] = live
        for position in range(peers):
            place = jnp.int32(0)
            for at in range(peers):
                place += jnp.where(order_ref[sequence, at] == position, at, 0)
            place_ref[batch, position] = place
    unpack_gains(gains_ref, gain_ref, second_ref, group_ref)
    gain = gain_ref[...]

    def work(rows):
        normed, _ = normalised(tokens_ref[rows].astype(FULL))
        own_entered[rows] = regroup(normed * gain, peers, groups).astype(HALF)
        own_grad[rows] = (grad_ref[rows].astype(FULL) * mask_ref[rows]).astype(HALF)

    by_chunks(tokens_ref.shape[0], work)
    one = PlaneGather(own_entered, entered_out, keep_one, sends_one, receives_one)
    two = PlaneGather(own_grad, grads_out, keep_two, sends_two, receives_two)
    swap = PlaneSwap((gate_ref, up_ref), ((feed_out, 0), (feed_out, size)), keeps, sends, receives)
    one.begin()
    one.relay()
    swap.begin()
    two.begin()
    unpack_rates(rates_ref, decay_ref, column_ref)
    line.hand_on(1)
    one.finish()
    two.relay()
    line.hand_on(2)
    swap.finish()
    two.finish()
    line.finish()


def gather_inputs(lengths, order, tokens, grad, gains, rates, gate, up, cut, value_size):
    peers, groups = lax.axis_size("seq"), lax.axis_size("fsdp")
    own, width = tokens.shape
    slab, columns = gate.shape
    part = columns // peers
    blocks, _, rows = rates.shape
    return pl.pallas_call(
        inputs_kernel,
        in_specs=[pl.BlockSpec(memory_space=pltpu.SMEM)] * 2 + [vmem()] * 4 + [in_hbm()] * 3,
        out_specs=[in_hbm()] * 4
        + [vmem()] * 6
        + [pl.BlockSpec(memory_space=pltpu.SMEM)] * 2,
        out_shape=[
            jax.ShapeDtypeStruct((peers, own, width), HALF),
            jax.ShapeDtypeStruct((peers, own, width), HALF),
            jax.ShapeDtypeStruct((peers, slab, 2 * part), HALF),
            jax.ShapeDtypeStruct((groups,) + cut.shape, HALF),
            jax.ShapeDtypeStruct((own, 1), FULL),
            jax.ShapeDtypeStruct((1, width), FULL),
            jax.ShapeDtypeStruct((1, width), FULL),
            jax.ShapeDtypeStruct((1, value_size), FULL),
            jax.ShapeDtypeStruct((blocks, rows, rows), FULL),
            jax.ShapeDtypeStruct((blocks, rows, 2), FULL),
            jax.ShapeDtypeStruct((own // rows, blocks), jnp.int32),
            jax.ShapeDtypeStruct((own // rows,), jnp.int32),
        ],
        scratch_shapes=[pltpu.VMEM((own, width), HALF)] * 2
        + gather_scratch()
        + gather_scratch()
        + swap_scratch(2, peers)
        + [
            pltpu.SemaphoreType.DMA,
            pltpu.SemaphoreType.DMA((2, groups - 1, peers)),
            pltpu.SemaphoreType.DMA((2, groups - 1, peers)),
        ],
        compiler_params=linked(1),
        cost_estimate=cost(0, 2 * peers * (2 * own * width + slab * 2 * part)),
    )(lengths, order, tokens, grad, gains, rates, gate, up, cut)


def feed_kernel(
    rows_ref, weight_ref, grads_ref, inner_ref, up_slope_ref, gate_slope_ref, down_ref, total
):
    step = pl.program_id(0)
    both = dot_nn(rows_ref[...], weight_ref[...])
    part = both.shape[1] // 2
    gate, upward = both[:, :part], both[:, part:]
    inside = 0.7978845608028654 * (gate + 0.044715 * (gate * gate * gate))
    bend = jnp.tanh(inside)
    share = 0.5 * (1.0 + bend)
    value = gate * share
    steep = 0.7978845608028654 * (1.0 + 3.0 * 0.044715 * (gate * gate))
    slope = share + 0.5 * gate * (1.0 - bend * bend) * steep
    inner_ref[...] = (value * upward).astype(HALF)
    up_slope_ref[...] = value.astype(HALF)
    gate_slope_ref[...] = (upward * slope).astype(HALF)
    term = dot_tn(inner_ref[...], grads_ref[...])

    @pl.when(step == 0)
    def _():
        total[...] = term

    @pl.when(step > 0)
    def _():
        total[...] += term

    @pl.when(step == pl.num_programs(0) - 1)
    def _():
        down_ref[...] = total[...].astype(HALF)


def feed(rows, weight, grads):
    count, width = rows.shape
    columns = weight.shape[1]
    part = columns // 2
    tile = 512
    tokens = pl.BlockSpec((tile, width), lambda i: (i, 0))
    out = pl.BlockSpec((tile, part), lambda i: (i, 0))
    return pl.pallas_call(
        feed_kernel,
        grid=(count // tile,),
        in_specs=[
            tokens,
            pl.BlockSpec((width, columns), lambda i: (0, 0), pipeline_mode=pl.Buffered(1)),
            tokens,
        ],
        out_specs=[out] * 3 + [pl.BlockSpec((part, width), lambda i: (0, 0))],
        out_shape=[jax.ShapeDtypeStruct((count, part), HALF)] * 3
        + [jax.ShapeDtypeStruct((part, width), HALF)],
        scratch_shapes=[pltpu.VMEM((part, width), FULL)],
        compiler_params=pltpu.CompilerParams(
            dimension_semantics=("arbitrary",), vmem_limit_bytes=VMEM_BYTES
        ),
        cost_estimate=pl.CostEstimate(
            flops=3 * count * width * columns,
            bytes_accessed=2 * (2 * count * width + width * columns + 2 * count * columns),
            transcendentals=0,
        ),
    )(rows, weight, grads)


def feed_back_kernel(rows_ref, weight_ref, up_slope_ref, gate_slope_ref, grad_ref):
    inner_grad = dot_nt(rows_ref[...], weight_ref[...])
    part = inner_grad.shape[1]
    grad_ref[:, :part] = (inner_grad * gate_slope_ref[...].astype(FULL)).astype(HALF)
    grad_ref[:, part:] = (inner_grad * up_slope_ref[...].astype(FULL)).astype(HALF)


def feed_back(rows, weight, up_slope, gate_slope):
    count, width = rows.shape
    part = weight.shape[0]
    tile = 512
    slope = pl.BlockSpec((tile, part), lambda i: (i, 0))
    return pl.pallas_call(
        feed_back_kernel,
        grid=(count // tile,),
        in_specs=[
            pl.BlockSpec((tile, width), lambda i: (i, 0)),
            pl.BlockSpec((part, width), lambda i: (0, 0), pipeline_mode=pl.Buffered(1)),
            slope,
            slope,
        ],
        out_specs=pl.BlockSpec((tile, 2 * part), lambda i: (i, 0)),
        out_shape=jax.ShapeDtypeStruct((count, 2 * part), HALF),
        compiler_params=pltpu.CompilerParams(
            dimension_semantics=("arbitrary",), vmem_limit_bytes=VMEM_BYTES
        ),
        cost_estimate=pl.CostEstimate(
            flops=2 * count * width * part,
            bytes_accessed=2 * (count * width + width * part + 4 * count * part),
            transcendentals=0,
        ),
    )(rows, weight, up_slope, gate_slope)


def retention_kernel(
    place_ref, live_ref, first_ref, second_ref, weight_ref, decay_ref, column_ref, gain_ref,
    qkv_ref, swish_ref, normed_ref, scale_ref, entry_ref, mixed_hbm, state, mixed_buffer, sems,
):
    step, steps = pl.program_id(0), pl.num_programs(0)
    rows = first_ref.shape[2]
    batches, key_size, value_size = state.shape
    total = 2 * key_size + value_size
    slot = lax.rem(step, 2)

    def sent(at, which, batch):
        return pltpu.make_async_copy(
            mixed_buffer.at[which, batch],
            mixed_hbm.at[place_ref[batch, at], batch],
            sems.at[which, batch],
        )

    @pl.when(step == 0)
    def _():
        state[...] = jnp.zeros_like(state)

    @pl.when(step >= 2)
    def _():
        for batch in range(batches):
            sent(step - 2, slot, batch).wait()

    rows_in = jnp.concatenate([first_ref[0, 0], second_ref[0, 0]], axis=0)
    projected = dot_nn(rows_in, weight_ref[...])
    decay = decay_ref[0]
    entry_decay = column_ref[0, :, 0:1]
    end_weight = column_ref[0, :, 1:2]
    block_decay = column_ref[0, rows - 1 : rows, 0:1]
    positions = step * rows + lax.broadcasted_iota(jnp.int32, (rows, 1), 0)
    for batch in range(batches):
        mine = slice(batch * rows, (batch + 1) * rows)
        live = (positions < live_ref[batch]).astype(FULL)
        query = projected[mine, :key_size].astype(HALF)
        key = (projected[mine, key_size : 2 * key_size] * live).astype(HALF)
        value = projected[mine, 2 * key_size : total].astype(HALF)
        swish = projected[mine, total:]
        before = state[batch]
        before_low = before.astype(HALF)
        weights = (dot_nt(query, key) * decay).astype(HALF)
        retained = dot_nn(weights, value) + entry_decay * dot_nn(query, before_low)
        key_ended = (key.astype(FULL) * end_weight).astype(HALF)
        state[batch] = block_decay * before + dot_tn(key_ended, value)
        normed, scale = normalised(retained)
        qkv_ref[batch, 0, :, :key_size] = query
        qkv_ref[batch, 0, :, key_size : 2 * key_size] = key
        qkv_ref[batch, 0, :, 2 * key_size :] = value
        scale_ref[batch, 0] = jnp.broadcast_to(scale, scale_ref.shape[2:])
        entry_ref[batch, 0] = before_low
        swish_ref[batch, 0] = swish.astype(HALF)
        normed_ref[batch, 0] = normed.astype(HALF)
        mixed = swish * jax.nn.sigmoid(swish) * (normed * gain_ref[...])
        mixed_buffer[slot, batch] = mixed.astype(HALF)
        sent(step, slot, batch).start()

    @pl.when(step == steps - 1)
    def _():
        for batch in range(batches):
            sent(step, slot, batch).wait()
            sent(step - 1, 1 - slot, batch).wait()


def retention(rows_in, weight, place, live, decay, columns, gain, key_size):
    blocks, batches, rows, width = rows_in.shape
    value_size = gain.shape[-1]
    total = 2 * key_size + value_size

    def arriving(batch):
        return pl.BlockSpec(
            (1, 1, rows, width), lambda i, place, live: (place[batch, i], batch, 0, 0)
        )

    def whole(shape):
        return pl.BlockSpec(
            shape, lambda i, place, live: (0,) * len(shape), pipeline_mode=pl.Buffered(1)
        )

    def here(*tail):
        return pl.BlockSpec((batches, 1) + tail, lambda i, place, live: (0, i, 0, 0))

    def along(*tail):
        return pl.BlockSpec((1,) + tail, lambda i, place, live: (i, 0, 0))

    return pl.pallas_call(
        retention_kernel,
        grid_spec=pltpu.PrefetchScalarGridSpec(
            num_scalar_prefetch=2,
            grid=(blocks,),
            in_specs=[
                arriving(0),
                arriving(1),
                whole((width, total + value_size)),
                along(rows, rows),
                along(rows, 2),
                whole((1, value_size)),
            ],
            out_specs=[
                here(rows, total),
                here(rows, value_size),
                here(rows, value_size),
                here(rows, LANES),
                here(key_size, value_size),
                in_hbm(),
            ],
            scratch_shapes=[
                pltpu.VMEM((batches, key_size, value_size), FULL),
                pltpu.VMEM((2, batches, rows, value_size), HALF),
                pltpu.SemaphoreType.DMA((2, batches)),
            ],
        ),
        out_shape=[
            jax.ShapeDtypeStruct((batches, blocks, rows, total), HALF),
            jax.ShapeDtypeStruct((batches, blocks, rows, value_size), HALF),
            jax.ShapeDtypeStruct((batches, blocks, rows, value_size), HALF),
            jax.ShapeDtypeStruct((batches, blocks, rows, LANES), FULL),
            jax.ShapeDtypeStruct((batches, blocks, key_size, value_size), HALF),
            jax.ShapeDtypeStruct((blocks, batches, rows, value_size), HALF),
        ],
        compiler_params=pltpu.CompilerParams(
            dimension_semantics=("arbitrary",), vmem_limit_bytes=VMEM_BYTES
        ),
        cost_estimate=pl.CostEstimate(
            flops=3 * blocks * batches * rows * width * total,
            bytes_accessed=2 * blocks * batches * rows * (width + 2 * total) + 4 * width * total,
            transcendentals=0,
        ),
    )(place, live, rows_in, rows_in, weight, decay, columns, gain)


def retention_back_kernel(
    place_ref, live_ref, first_ref, second_ref,
    weight_ref, decay_ref, column_ref, gain_ref, qkv_ref, swish_ref, normed_ref, scale_ref, entry_ref,
    gain_grad_ref, grads_hbm, state, grads_buffer, sems,
):
    step, steps = pl.program_id(0), pl.num_programs(0)
    rows = first_ref.shape[2]
    batches, key_size, value_size = state.shape
    slot = lax.rem(step, 2)

    def sent(at, which, batch):
        return pltpu.make_async_copy(
            grads_buffer.at[which, batch],
            grads_hbm.at[place_ref[batch, steps - 1 - at], batch],
            sems.at[which, batch],
        )

    @pl.when(step == 0)
    def _():
        state[...] = jnp.zeros_like(state)
        gain_grad_ref[...] = jnp.zeros_like(gain_grad_ref)

    @pl.when(step >= 2)
    def _():
        for batch in range(batches):
            sent(step - 2, slot, batch).wait()

    rows_in = jnp.concatenate([first_ref[0, 0], second_ref[0, 0]], axis=0)
    mixed_grads = dot_nt(rows_in, weight_ref[...])
    decay = decay_ref[0]
    entry_decay = column_ref[0, :, 0:1]
    end_weight = column_ref[0, :, 1:2]
    block_decay = column_ref[0, rows - 1 : rows, 0:1]
    positions = (steps - 1 - step) * rows + lax.broadcasted_iota(jnp.int32, (rows, 1), 0)
    gain = gain_ref[...]
    for batch in range(batches):
        live = (positions < live_ref[batch]).astype(FULL)
        mixed_grad = mixed_grads[batch * rows : (batch + 1) * rows]
        query = qkv_ref[batch, 0, :, :key_size]
        key = qkv_ref[batch, 0, :, key_size : 2 * key_size]
        value = qkv_ref[batch, 0, :, 2 * key_size :]
        swish = swish_ref[batch, 0].astype(FULL)
        normed = normed_ref[batch, 0].astype(FULL)
        scale = scale_ref[batch, 0, :, 0:1]
        entry = entry_ref[batch, 0]
        sigmoid = jax.nn.sigmoid(swish)
        silu = swish * sigmoid
        swish_grad = mixed_grad * (normed * gain) * (sigmoid * (1.0 + swish - silu))
        scaled_grad = mixed_grad * silu
        gain_grad_ref[...] += jnp.sum(scaled_grad * normed, axis=0, keepdims=True)
        retained_grad = normalised_back(scaled_grad * gain, normed, scale).astype(HALF)
        weights = (dot_nt(query, key) * decay).astype(HALF)
        scores_grad = (dot_nt(retained_grad, value) * decay).astype(HALF)
        after = state[batch]
        after_low = after.astype(HALF)
        query_grad = dot_nn(scores_grad, key) + entry_decay * dot_nt(retained_grad, entry)
        key_grad = dot_tn(scores_grad, query) + end_weight * dot_nt(value, after_low)
        value_grad = dot_tn(weights, retained_grad) + end_weight * dot_nn(key, after_low)
        query_entered = (query.astype(FULL) * entry_decay).astype(HALF)
        state[batch] = block_decay * after + dot_tn(query_entered, retained_grad)
        grads_buffer[slot, batch, :, :key_size] = query_grad.astype(HALF)
        grads_buffer[slot, batch, :, key_size : 2 * key_size] = (key_grad * live).astype(HALF)
        grads_buffer[slot, batch, :, 2 * key_size : 2 * key_size + value_size] = value_grad.astype(
            HALF
        )
        grads_buffer[slot, batch, :, 2 * key_size + value_size :] = swish_grad.astype(HALF)
        sent(step, slot, batch).start()

    @pl.when(step == steps - 1)
    def _():
        for batch in range(batches):
            sent(step, slot, batch).wait()
            sent(step - 1, 1 - slot, batch).wait()


def retention_back(rows_in, weight, place, live, decay, columns, gain, saved):
    blocks, batches, rows, width = rows_in.shape
    value_size = gain.shape[-1]
    key_size = saved[-1].shape[2]
    total = 2 * key_size + 2 * value_size

    def arriving(batch, size):
        return pl.BlockSpec(
            (1, 1, rows, size),
            lambda i, place, live: (place[batch, blocks - 1 - i], batch, 0, 0),
        )

    def whole(shape):
        return pl.BlockSpec(
            shape, lambda i, place, live: (0,) * len(shape), pipeline_mode=pl.Buffered(1)
        )

    def here(*tail):
        return pl.BlockSpec((batches, 1) + tail, lambda i, place, live: (0, blocks - 1 - i, 0, 0))

    def along(*tail):
        return pl.BlockSpec((1,) + tail, lambda i, place, live: (blocks - 1 - i, 0, 0))

    return pl.pallas_call(
        retention_back_kernel,
        grid_spec=pltpu.PrefetchScalarGridSpec(
            num_scalar_prefetch=2,
            grid=(blocks,),
            in_specs=[
                arriving(0, width),
                arriving(1, width),
                whole((value_size, width)),
                along(rows, rows),
                along(rows, 2),
                whole((1, value_size)),
                here(rows, 2 * key_size + value_size),
                here(rows, value_size),
                here(rows, value_size),
                here(rows, LANES),
                here(key_size, value_size),
            ],
            out_specs=[
                pl.BlockSpec((1, value_size), lambda i, place, live: (0, 0)),
                in_hbm(),
            ],
            scratch_shapes=[
                pltpu.VMEM((batches, key_size, value_size), FULL),
                pltpu.VMEM((2, batches, rows, total), HALF),
                pltpu.SemaphoreType.DMA((2, batches)),
            ],
        ),
        out_shape=[
            jax.ShapeDtypeStruct((1, value_size), FULL),
            jax.ShapeDtypeStruct((blocks, batches, rows, total), HALF),
        ],
        compiler_params=pltpu.CompilerParams(
            dimension_semantics=("arbitrary",), vmem_limit_bytes=VMEM_BYTES
        ),
        cost_estimate=pl.CostEstimate(
            flops=6 * blocks * batches * rows * width * value_size,
            bytes_accessed=2 * blocks * batches * rows * (width + 2 * total)
            + 2 * width * value_size,
            transcendentals=0,
        ),
    )(place, live, rows_in, rows_in, weight, decay, columns, gain, *saved)


def middle_kernel(
    mixed_hbm, weight_hbm, tokens_hbm, gain_ref, hidden_ref, second_out,
    *scratch,
):
    scatter = scratch[:7]
    own, keeps, gather_sends, gather_receives = scratch[7:11]
    weight_ref, tokens_ref, stage_sems, mixed, mixed_sems = scratch[11:]
    peers, groups = lax.axis_size("seq"), lax.axis_size("fsdp")
    sources, targets = (weight_hbm, tokens_hbm), (weight_ref, tokens_ref)
    weight_copy, tokens_copy = staged(sources, targets, stage_sems)
    blocks = Blocks(mixed_hbm, mixed, mixed_sems)
    blocks.begin()
    greet_neighbours()
    weight_copy.wait()

    def term(block):
        return blocks.take(lambda value: dot_nn(value, weight_ref[...]).astype(HALF))

    gain = gain_ref[...]

    def use(start, total):
        rows = pl.ds(start, CHUNK)
        hidden = tokens_ref[rows].astype(FULL) + total
        hidden_ref[rows] = hidden
        normed, _ = normalised(hidden)
        own[rows] = regroup(normed * gain, peers, groups).astype(HALF)

    gathers = [
        PlaneGather(own, second_out, keeps, gather_sends, gather_receives, window, WINDOWS)
        for window in range(WINDOWS)
    ]
    windows = scatter_head(term, scatter)
    tokens_copy.wait()
    scatter_tail(windows, use, lambda window: gathers[window].begin())
    for gather in gathers:
        gather.relay()
    for gather in gathers:
        gather.finish()
    for window in windows:
        window.drain()


def middle(mixed, weight, tokens, gain):
    peers, own, inner = mixed.shape
    width = weight.shape[1]
    return pl.pallas_call(
        middle_kernel,
        in_specs=[in_hbm()] * 3 + [vmem()],
        out_specs=[vmem(), in_hbm()],
        out_shape=[
            jax.ShapeDtypeStruct((own, width), FULL),
            jax.ShapeDtypeStruct((peers, own, width), HALF),
        ],
        scratch_shapes=scatter_scratch(own, width)
        + [pltpu.VMEM((own, width), HALF)]
        + gather_scratch(WINDOWS)
        + stage_scratch(weight, tokens)
        + block_scratch(peers, mixed),
        compiler_params=linked(2),
        cost_estimate=cost(2 * peers * own * inner * width, 4 * peers * own * width),
    )(mixed, weight, tokens, gain)


class LineSum:
    def __init__(self, terms, landed, own, final, loads, sends, receives):
        self.terms, self.landed, self.own, self.final = terms, landed, own, final
        self.loads, self.sends, self.receives = loads, sends, receives
        self.me, self.last = lax.axis_index("fsdp"), lax.axis_size("fsdp") - 1
        self.peers, self.place = lax.axis_size("seq"), lax.axis_index("seq")

    def piece(self, turn):
        return lax.rem(self.place + turn, self.peers)

    def depth(self, way):
        return self.me if way == 0 else self.last - self.me

    def block(self, way, order):
        return self.last - order if way == 0 else order

    def slot(self, way, order):
        return order if way == 0 else 2 * self.last - 2 - order

    def sent(self, source, way, order, turn):
        at = (way, order, turn)
        return pltpu.make_async_remote_copy(
            src_ref=source,
            dst_ref=self.landed.at[self.slot(way, order), self.piece(turn)],
            send_sem=self.sends.at[at],
            recv_sem=self.receives.at[at],
            device_id={"fsdp": self.me + 1 if way == 0 else self.me - 1},
            device_id_type=MESH,
        )

    def first(self, way, order, turn):
        source = self.terms.at[self.block(way, order), self.piece(turn)]
        return self.sent(source, way, order, turn)

    def onward(self, way, order, turn):
        source = self.landed.at[self.slot(way, order), self.piece(turn)]
        return self.sent(source, way, order, turn)

    def load(self, way, order):
        return pltpu.make_async_copy(
            self.terms.at[self.block(way, order)], self.own.at[way], self.loads.at[way]
        )

    def load_final(self):
        return pltpu.make_async_copy(self.terms.at[self.me], self.final, self.loads.at[2])

    def begin(self):
        for way in (0, 1):

            @pl.when(self.depth(way) == 0)
            def _():
                for order in range(self.last):
                    for turn in range(self.peers):
                        self.first(way, order, turn).start()

            self.load(way, 0).start()
        self.load_final().start()

    def loaded(self):
        for way in (0, 1):
            self.load(way, 0).wait()

    def load_next(self):
        for way in (0, 1):

            @pl.when(self.depth(way) == 1)
            def _():
                self.load(way, 1).start()

    def loaded_next(self):
        for way in (0, 1):

            @pl.when(self.depth(way) == 1)
            def _():
                self.load(way, 1).wait()

    def hand_on(self, order, depth, turns):
        for turn in turns:
            for way in (0, 1):

                @pl.when(self.depth(way) == depth)
                def _():
                    at, piece = self.slot(way, order), self.piece(turn)
                    self.onward(way, order, turn).wait_recv()
                    self.landed[at, piece] = (
                        self.landed[at, piece].astype(FULL) + self.own[way, piece].astype(FULL)
                    ).astype(HALF)
                    self.onward(way, order, turn).start()

    def finish(self, use):
        self.load_final().wait()
        for turn in range(self.peers):
            piece = self.piece(turn)
            for way in (0, 1):

                @pl.when(self.depth(way) > 0)
                def _():
                    order = self.last - self.depth(way)
                    self.onward(way, order, turn).wait_recv()
                    self.final[piece] = (
                        self.final[piece].astype(FULL)
                        + self.landed[self.slot(way, order), piece].astype(FULL)
                    ).astype(HALF)

            use(turn)

    def drain(self):
        for way in (0, 1):
            for order in range(self.last):
                for turn in range(self.peers):

                    @pl.when(self.depth(way) == 0)
                    def _():
                        self.first(way, order, turn).wait_send()

                    @pl.when((self.depth(way) > 0) & (self.depth(way) < self.last - order))
                    def _():
                        self.onward(way, order, turn).wait_send()


def line_scratch(groups, peers, slab, columns):
    block = (peers, slab, columns)
    return [
        pltpu.VMEM((2 * groups - 3,) + block, HALF),
        pltpu.VMEM((2,) + block, HALF),
        pltpu.VMEM(block, HALF),
        pltpu.SemaphoreType.DMA((3,)),
        pltpu.SemaphoreType.DMA((2, groups - 1, peers)),
        pltpu.SemaphoreType.DMA((2, groups - 1, peers)),
    ]


def middle_back_kernel(
    grads_hbm, weight_hbm, hidden_hbm, outer_hbm, mask_ref, gain_ref, mixed_hbm,
    hidden_grad_ref, gain_grad_ref, branch_out, out_grad_ref,
    *scratch,
):
    scatter = scratch[:7]
    own, gather_sends, gather_receives = scratch[7:10]
    weight_ref, hidden_ref, outer_ref, mixed_ref, stage_sems, grads, grad_sems = scratch[10:17]
    branch, total, out_sems = scratch[17:]
    peers, groups = lax.axis_size("seq"), lax.axis_size("fsdp")
    me, other, near, below, far = plane_peers()
    flip = other - me
    blocks = Blocks(grads_hbm, grads, grad_sems)
    weight_copy, *later = staged(
        (weight_hbm, hidden_hbm, outer_hbm, mixed_hbm),
        (weight_ref, hidden_ref, outer_ref, mixed_ref),
        stage_sems,
    )
    blocks.begin()
    greet_neighbours()
    weight_copy.wait()

    def term(block):
        return blocks.take(lambda value: dot_nt(value, weight_ref[...]).astype(HALF))

    gain = gain_ref[...]
    gain_grad_ref[...] = jnp.zeros_like(gain_grad_ref)

    def use(start, total):
        rows = pl.ds(start, CHUNK)
        grad = regroup(total, groups, peers)
        normed, scale = normalised(hidden_ref[rows])
        gain_grad_ref[...] += jnp.sum(grad * normed, axis=0, keepdims=True)
        outer = outer_ref[rows].astype(FULL) * mask_ref[rows]
        hidden_grad = outer + normalised_back(grad * gain, normed, scale)
        hidden_grad_ref[rows] = hidden_grad
        own[rows] = hidden_grad.astype(HALF)

    gathers = [
        PlaneGather(own, branch, None, gather_sends, gather_receives, window, WINDOWS)
        for window in range(WINDOWS)
    ]
    width, stored = own.shape[1], []

    def add(block, rows):
        copy = pltpu.make_async_copy(rows, branch_out.at[block], out_sems.at[len(stored)])
        copy.start()
        for start in range(0, width, 512):
            columns = pl.ds(start, 512)
            product = dot_tn(mixed_ref[block], rows[:, columns])
            total[:, columns] = total[:, columns] + product if stored else product
        stored.append(copy)

    windows = scatter_head(term, scatter)
    for copy in later:
        copy.wait()
    scatter_tail(windows, use, lambda window: gathers[window].begin())
    add(me, own)
    for gather in gathers:
        gather.expect(2, 3)
    add(other, branch.at[other])
    for gather in gathers:
        gather.relay()
    for block in (near, below):
        add(block, branch.at[block])
    for gather in gathers:
        gather.expect(8, 9, 10, 11)
    add(near + flip, branch.at[near + flip])
    for gather in gathers:
        gather.relay_far()
    add(below + flip, branch.at[below + flip])
    add(far, branch.at[far])
    for gather in gathers:
        gather.expect(12, 13)
    add(far + flip, branch.at[far + flip])
    out_grad_ref[...] = total[...].astype(HALF)
    for copy in stored:
        copy.wait()
    for gather in gathers:
        gather.drain()
    for window in windows:
        window.drain()


def middle_back(grads, weight, hidden, outer, mask, gain, mixed):
    peers, own, inner = grads.shape
    width = weight.shape[0]
    return pl.pallas_call(
        middle_back_kernel,
        in_specs=[in_hbm()] * 4 + [vmem()] * 2 + [in_hbm()],
        out_specs=[vmem(), vmem(), in_hbm(), vmem()],
        out_shape=[
            jax.ShapeDtypeStruct((own, width), FULL),
            jax.ShapeDtypeStruct((1, width), FULL),
            jax.ShapeDtypeStruct((peers, own, width), HALF),
            jax.ShapeDtypeStruct((mixed.shape[2], width), HALF),
        ],
        scratch_shapes=scatter_scratch(own, width)
        + [pltpu.VMEM((own, width), HALF)]
        + gather_scratch(WINDOWS)[1:]
        + stage_scratch(weight, hidden, outer, mixed)
        + block_scratch(2, grads)
        + [
            pltpu.VMEM((peers, own, width), HALF),
            pltpu.VMEM((mixed.shape[2], width), FULL),
            pltpu.SemaphoreType.DMA((peers,)),
        ],
        compiler_params=pltpu.CompilerParams(
            collective_id=3, has_side_effects=True, vmem_limit_bytes=LARGE_BYTES
        ),
        cost_estimate=cost(2 * peers * own * inner * width, 4 * peers * own * width),
    )(grads, weight, hidden, outer, mask, gain, mixed)


class PlaneReturn:
    def __init__(self, cuts, source, targets, keeps, sends, receives):
        self.cuts, self.source, self.targets = cuts, source, targets
        self.keeps, self.sends, self.receives = keeps, sends, receives
        self.peers, self.me = lax.axis_size("seq"), lax.axis_index("seq")

    def part(self, number, peer):
        start, size = self.cuts[number]
        return self.source.at[peer, :, pl.ds(start, size)]

    def place(self, number, peer):
        size = self.cuts[number][1]
        return self.targets[number].at[:, pl.ds(pl.multiple_of(peer * size, LANES), size)]

    def sent(self, source, target, number, turn, peer):
        at = (number, turn)
        return to_peer(source, target, self.sends.at[at], self.receives.at[at], peer)

    def copy(self, number, turn):
        peer = lax.rem(self.me + turn, self.peers)
        return self.sent(
            self.part(number, peer), self.place(number, self.me), number, turn, peer
        )

    def landed(self, number, turn):
        peer = lax.rem(self.me + self.peers - turn, self.peers)
        target = self.place(number, peer)
        return self.sent(target, target, number, turn, peer)

    def kept(self, number):
        return pltpu.make_async_copy(
            self.part(number, self.me), self.place(number, self.me), self.keeps.at[number]
        )

    def begin(self, turn):
        for number in range(len(self.cuts)):
            if turn > 0:
                self.copy(number, turn).start()
            else:
                self.kept(number).start()

    def finish(self):
        for number in range(len(self.cuts)):
            for turn in range(1, self.peers):
                self.landed(number, turn).wait_recv()
                self.copy(number, turn).wait_send()
            self.kept(number).wait()


def last_kernel(
    cuts, line_cuts, grads_hbm, weight_hbm, tokens_hbm, hidden_grad_hbm, gain_ref, second_grad_ref,
    group_grad_ref, inner_hbm, down_hbm, hidden_hbm, mask_ref, summed_ref, terms_ref,
    *refs,
):
    count, line_count = len(cuts), len(line_cuts)
    input_ref, output_ref, gains_ref = refs[:3]
    returned, refs = refs[3 : 3 + count], refs[3 + count :]
    line_returned, scratch = refs[:line_count], refs[line_count:]
    scatter, result = scratch[:7], scratch[:1] + scratch[7:13]
    (
        sums, parts, across, totals, first_grad, keep, part_sends, part_receives,
        group_keep, group_sends, group_receives,
    ) = scratch[13:24]
    peers, groups = lax.axis_size("seq"), lax.axis_size("fsdp")
    me = lax.axis_index("seq")
    grads, grad_sems = scratch[36:38]
    inner_ref = scratch[38]
    weight_ref, down_ref, hidden_ref, tokens_ref, hidden_grad_ref, stage_sems = scratch[39:]
    blocks = Blocks(grads_hbm, grads, grad_sems)
    weight_copy, inner_copy, down_copy, *later = staged(
        (weight_hbm, inner_hbm, down_hbm, hidden_hbm, tokens_hbm, hidden_grad_hbm),
        (weight_ref, inner_ref, down_ref, hidden_ref, tokens_ref, hidden_grad_ref),
        stage_sems,
    )
    blocks.begin()
    greet_plane(True)
    back = PlaneReturn(cuts, summed_ref, returned, *scratch[24:27])
    line_back = PlaneReturn(line_cuts, scratch[32], line_returned, *scratch[27:30])
    line = LineSum(terms_ref, *scratch[30:36])

    def term(block):
        return blocks.take(lambda value: dot_nt(value, weight_ref[...]).astype(HALF))

    def result_term(block):
        return dot_nn(inner_ref[block], down_ref[...]).astype(HALF)

    gain = gain_ref[...]
    first_grad[...] = jnp.zeros_like(first_grad)

    def use(start, total):
        rows = pl.ds(start, CHUNK)
        grad = regroup(total, groups, peers)
        normed, scale = normalised(tokens_ref[rows].astype(FULL))
        first_grad[...] += jnp.sum(grad * normed, axis=0, keepdims=True)
        input_ref[rows] = (
            hidden_grad_ref[rows] + normalised_back(grad * gain, normed, scale)
        ).astype(HALF)

    def use_result(start, total):
        rows = pl.ds(start, CHUNK)
        output_ref[rows] = ((hidden_ref[rows] + total) * mask_ref[rows]).astype(HALF)

    line.begin()
    weight_copy.wait()
    every, early, late = range(peers), range(peers // 2), range(peers // 2, peers)
    windows = scatter_head(term, scatter, (), True)
    windows[0].relay()
    line.loaded()
    line.hand_on(0, 1, every)
    line.load_next()
    windows[1].relay()
    inner_copy.wait()
    down_copy.wait()
    result_windows = scatter_head(result_term, result, windows, True)
    for turn in every:
        back.begin(turn)
    result_windows[0].relay()
    line.hand_on(0, 2, every)
    for copy in later:
        copy.wait()
    scatter_tail(windows, use)
    line.loaded_next()
    line.hand_on(1, 1, early)
    result_windows[1].relay()
    tile = LANES * 2
    for peer in range(peers):
        for row in range(tile // LANES):
            at = peer * tile + row * LANES
            sums[peer, row : row + 1] = first_grad[:, at : at + LANES]
            sums[peer, 2 + row : 3 + row] = second_grad_ref[:, at : at + LANES]
        sums[peer, 4:8] = jnp.zeros((4, LANES), FULL)

    def copy(turn):
        peer = lax.rem(me + turn, peers)
        return to_peer(
            sums.at[peer], parts.at[turn], part_sends.at[turn], part_receives.at[turn], peer
        )

    kept = pltpu.make_async_copy(sums.at[me], parts.at[0], keep)
    kept.start()
    for turn in range(1, peers):
        copy(turn).start()
    line.hand_on(1, 1, late)
    scatter_tail(result_windows, use_result)
    kept.wait()
    for turn in range(1, peers):
        copy(turn).wait_recv()
        copy(turn).wait_send()
    total = parts[0]
    for turn in range(1, peers):
        total += parts[turn]
    across[0:8] = total
    for row in range(4):
        across[8 + row : 9 + row] = group_grad_ref[:, row * LANES : (row + 1) * LANES]
    across[12:16] = jnp.zeros((4, LANES), FULL)
    begin, finish = all_to_each(
        across, totals, "fsdp", groups, group_keep, group_sends, group_receives
    )
    begin()
    line.finish(line_back.begin)
    back.finish()
    line_back.finish()
    line.drain()
    for window in windows:
        window.drain(4)
    for window in result_windows:
        window.drain()
    finish()
    summed = totals[0]
    for turn in range(1, groups):
        summed += totals[turn]
    gains_ref[...] = summed


def last_rows(
    grads, weight, tokens, hidden_grad, gain, second_grad, group_grad, inner, down, hidden, mask,
    summed, sizes, terms, line_sizes,
):
    peers, own, size = grads.shape
    groups = lax.axis_size("fsdp")
    width = weight.shape[0]
    slab = summed.shape[1]

    def cuts_of(sizes):
        return tuple((sum(sizes[:number]), sizes[number]) for number in range(len(sizes)))

    return pl.pallas_call(
        partial(last_kernel, cuts_of(sizes), cuts_of(line_sizes)),
        in_specs=[in_hbm()] * 4 + [vmem()] * 3 + [in_hbm()] * 3 + [vmem()] + [in_hbm()] * 2,
        out_specs=[vmem()] * 3 + [in_hbm()] * len(sizes + line_sizes),
        out_shape=[
            jax.ShapeDtypeStruct((own, width), HALF),
            jax.ShapeDtypeStruct((own, width), HALF),
            jax.ShapeDtypeStruct((16, LANES), FULL),
        ]
        + [jax.ShapeDtypeStruct((slab, peers * part), HALF) for part in sizes + line_sizes],
        scratch_shapes=scatter_scratch(own, width)
        + scatter_scratch(own, width)[1:]
        + [
            pltpu.VMEM((peers, 8, LANES), FULL),
            pltpu.VMEM((peers, 8, LANES), FULL),
            pltpu.VMEM((16, LANES), FULL),
            pltpu.VMEM((groups, 16, LANES), FULL),
            pltpu.VMEM((1, width), FULL),
            pltpu.SemaphoreType.DMA,
            pltpu.SemaphoreType.DMA((peers,)),
            pltpu.SemaphoreType.DMA((peers,)),
            pltpu.SemaphoreType.DMA,
            pltpu.SemaphoreType.DMA((groups,)),
            pltpu.SemaphoreType.DMA((groups,)),
        ]
        + swap_scratch(len(sizes), peers)
        + swap_scratch(len(line_sizes), peers)
        + line_scratch(groups, peers, slab, terms.shape[3])
        + block_scratch(2, grads)
        + [pltpu.VMEM(inner.shape, HALF)]
        + stage_scratch(weight, down, hidden, tokens, hidden_grad, inner)[:5]
        + [pltpu.SemaphoreType.DMA((6,))],
        compiler_params=pltpu.CompilerParams(
            collective_id=5, has_side_effects=True, vmem_limit_bytes=LARGE_BYTES
        ),
        cost_estimate=cost(
            2 * peers * own * (size + inner.shape[2]) * width, 5 * peers * own * width
        ),
    )(
        grads, weight, tokens, hidden_grad, gain, second_grad, group_grad, inner, down, hidden, mask,
        summed, terms,
    )


def outputs_kernel(*refs):
    count = len(refs) // 2 - 2
    gains_ref, refs = refs[count], refs[:count] + refs[count + 1 :]
    for source, target in zip(refs[:count], refs[count : 2 * count]):
        target[...] = source[...].astype(target.dtype)
    first_ref, second_ref, group_ref = refs[2 * count :]
    group, half = lax.axis_index("fsdp"), LANES // 2
    row = group // 2
    for start, target in ((0, first_ref), (2, second_ref)):
        both = gains_ref[pl.ds(start + row, 1)]
        turned = pltpu.roll(both, half, 1)
        target[...] = jnp.where(lax.rem(group, 2) == 0, both, turned)[:, :half]
    group_ref[...] = gains_ref[pl.ds(8 + group, 1)]


def outputs(grads, rows, gains):
    arrays = [*grads, *rows]
    small = (LANES // 2, LANES // 2, LANES)
    return pl.pallas_call(
        outputs_kernel,
        in_specs=[vmem()] * (len(arrays) + 1),
        out_specs=[vmem()] * (len(arrays) + 3),
        out_shape=[jax.ShapeDtypeStruct(array.shape, FULL) for array in grads]
        + [jax.ShapeDtypeStruct(array.shape, HALF) for array in rows]
        + [jax.ShapeDtypeStruct((1, size), FULL) for size in small],
        compiler_params=pltpu.CompilerParams(vmem_limit_bytes=VMEM_BYTES),
    )(*arrays, gains)


def head_body(
    tokens,
    cotangent,
    lengths,
    block_order,
    log_decay,
    first_gain,
    query_weight,
    key_weight,
    value_weight,
    swish_weight,
    output_weight,
    group_gain,
    second_gain,
    feed_gate,
    feed_up,
    feed_down,
):
    peers, groups = lax.axis_size("seq"), lax.axis_size("fsdp")
    batches, rows, width = tokens.shape
    own = batches * rows
    heads = log_decay.shape[0]
    key_size = query_weight.shape[1] // heads
    value_size = value_weight.shape[1] // heads
    part = feed_gate.shape[1] // peers
    slab = query_weight.shape[0]
    total = 2 * key_size + 2 * value_size

    def over_groups(local):
        return lax.all_gather(local, "fsdp", axis=0, tiled=True)

    def sum_groups(whole):
        return lax.psum_scatter(whole.astype(HALF), "fsdp", scatter_dimension=0, tiled=True)

    def gathered(cut):
        return over_groups(cut[None]).reshape(width, cut.shape[2])

    gains = jnp.concatenate(
        [
            group_gain.astype(FULL)[None],
            jnp.concatenate([first_gain, second_gain]).astype(FULL)[None],
            jnp.zeros((6, LANES), FULL),
        ],
        axis=0,
    )
    first_cut, rates, gains = first_swap(
        query_weight, key_weight, value_weight, swish_weight, log_decay, gains
    )
    out_weight = over_groups(output_weight)
    token_rows = tokens.reshape(own, width)
    outer_rows = cotangent.reshape(own, width)
    (
        entered, result_low, feed_cut, first_weight,
        mask, gain_one, gain_two, gain_group, decay, columns, place, live,
    ) = gather_inputs(
        lengths, block_order, token_rows, outer_rows, gains, rates, feed_gate, feed_up, first_cut,
        value_size,
    )
    first_weight = first_weight.reshape(width, total)
    entered, out_weight = lax.optimization_barrier((entered, out_weight))
    feed_weight = gathered(feed_cut)

    *saved, mixed = retention(
        entered.reshape(peers, batches, rows, width),
        first_weight,
        place,
        live,
        decay,
        columns,
        gain_group,
        key_size,
    )
    entered = entered.reshape(peers * own, width)
    mixed, feed_down = lax.optimization_barrier((mixed, feed_down))
    down_weight = over_groups(feed_down)
    mixed = mixed.reshape(peers * own, value_size)
    hidden, second = middle(mixed.reshape(peers, own, value_size), out_weight, token_rows, gain_two)
    second = second.reshape(peers * own, width)
    result_low = result_low.reshape(peers * own, width)
    inner_low, up_slope, gate_slope, down_term = feed(second, feed_weight, result_low)
    down_grad = sum_groups(down_term)
    both_grad = feed_back(result_low, down_weight, up_slope, gate_slope)
    both_term, both_grad = lax.optimization_barrier(
        (dot_tn(second, both_grad).astype(HALF), both_grad)
    )
    both_weight_grad = sum_groups(both_term).reshape(peers, slab, 2 * part)
    hidden_grad, second_gain_grad, branch_low, out_term = middle_back(
        both_grad.reshape(peers, own, 2 * part),
        feed_weight,
        hidden,
        outer_rows,
        mask,
        gain_two,
        mixed.reshape(peers, own, value_size),
    )
    branch_low, down_grad = lax.optimization_barrier((branch_low, down_grad))
    out_grad = sum_groups(out_term)
    group_gain_grad, projected_grad = retention_back(
        branch_low.reshape(peers, batches, rows, width),
        out_weight,
        place,
        live,
        decay,
        columns,
        gain_group,
        saved,
    )
    flat_grad = projected_grad.reshape(peers * own, total)
    first_term = dot_tn(entered, flat_grad).astype(HALF)
    (
        input_rows, output_rows, small_grads,
        gate_back, up_back, query_back, key_back, value_back, swish_back,
    ) = last_rows(
        projected_grad.reshape(peers, own, total),
        first_weight,
        token_rows,
        hidden_grad,
        gain_one,
        second_gain_grad,
        group_gain_grad,
        inner_low.reshape(peers, own, part),
        down_weight,
        hidden,
        mask,
        both_weight_grad,
        (part, part),
        first_term.reshape(groups, peers, slab, total),
        (key_size, key_size, value_size, value_size),
    )
    (
        query_back, key_back, value_back, swish_back, out_back, gate_back, up_back, down_back,
        output_rows, input_rows, first_grad, second_grad, group_grad,
    ) = outputs(
        (query_back, key_back, value_back, swish_back, out_grad, gate_back, up_back, down_grad),
        (output_rows, input_rows),
        small_grads,
    )
    return (
        output_rows.reshape(batches, rows, width),
        input_rows.reshape(batches, rows, width),
        first_grad.reshape(slab),
        query_back,
        key_back,
        value_back,
        swish_back,
        out_back,
        group_grad.reshape(LANES),
        second_grad.reshape(slab),
        gate_back,
        up_back,
        down_back,
    )


def body(*arrays):
    peers, groups = lax.axis_size("seq"), lax.axis_size("fsdp")
    fits = peers == 8 and groups == 4 and arrays[4].shape[0] == peers and arrays[0].shape[0] == 2
    if fits:
        return head_body(*arrays)
    return general_body(*arrays)


def solution(mesh):
    placed = (
        P("fsdp", "seq", None),
        P("fsdp", "seq", None),
        P(),
        P(),
        P(None, "seq"),
        P(("seq", "fsdp")),
        P(("seq", "fsdp"), None),
        P(("seq", "fsdp"), None),
        P(("seq", "fsdp"), None),
        P(("seq", "fsdp"), None),
        P(("seq", "fsdp"), None),
        P(("seq", "fsdp")),
        P(("seq", "fsdp")),
        P(("seq", "fsdp"), None),
        P(("seq", "fsdp"), None),
        P(("seq", "fsdp"), None),
    )
    return jax.shard_map(
        body,
        mesh=mesh,
        in_specs=placed,
        out_specs=(
            P("fsdp", "seq", None),
            P("fsdp", "seq", None),
            P(("seq", "fsdp")),
            P(("seq", "fsdp"), None),
            P(("seq", "fsdp"), None),
            P(("seq", "fsdp"), None),
            P(("seq", "fsdp"), None),
            P(("seq", "fsdp"), None),
            P(("seq", "fsdp")),
            P(("seq", "fsdp")),
            P(("seq", "fsdp"), None),
            P(("seq", "fsdp"), None),
            P(("seq", "fsdp"), None),
        ),
        check_vma=False,
    )
```

```python
from functools import partial, reduce

import jax
import jax.numpy as jnp
from jax import lax
from jax.experimental import pallas as pl
from jax.experimental.pallas import tpu as pltpu
from jax.sharding import PartitionSpec as P

EPSILON = 1e-05
HIGHEST = lax.Precision.HIGHEST


def carried_in(value, axis, combine, identity, reverse):
    peers, index = (lax.axis_size(axis), lax.axis_index(axis))
    everything = jax.tree.map(
        lambda part, kind: lax.all_gather(part.astype(kind), axis),
        value,
        (jnp.bfloat16, jnp.bfloat16),
    )
    start = jax.tree.map(
        lambda part, zero: jnp.broadcast_to(jnp.asarray(zero, part.dtype), part.shape),
        value,
        identity,
    )

    def turn(k, before):
        at = peers - 1 - k if reverse else k
        reached = at > index if reverse else at < index
        new = combine(
            before, jax.tree.map(lambda part, own: part[at].astype(own.dtype), everything, value)
        )
        return jax.tree.map(lambda a, b: jnp.where(reached, a, b), new, before)

    return lax.fori_loop(0, peers, turn, start)


def norm_rows(values, gain):
    average = jnp.mean(values, axis=-1, keepdims=True)
    centered = values - average
    variance = jnp.mean(centered * centered, axis=-1, keepdims=True)
    return centered * lax.rsqrt(variance + EPSILON) * gain


def gated_swish(swish_in, grouped):
    return jax.nn.silu(swish_in) * grouped


def gated_gelu(gate_in, upward):
    return jax.nn.gelu(gate_in) * upward


def chain_states(earlier, later):
    return (earlier[0] * later[0], later[0][:, None, None] * earlier[1] + later[1])


def transposed(left_rows, weight):
    return jnp.einsum("ie,fe->if", left_rows, weight, preferred_element_type=jnp.float32)


def plain_dot(left_rows, weight):
    return jnp.dot(left_rows, weight, preferred_element_type=jnp.float32)


def outer_term(left_rows, right_rows):
    return jnp.einsum("ni,no->io", left_rows, right_rows, preferred_element_type=jnp.float32)


def spread_sum(matrix_pairs, vectors):
    terms = tuple((outer_term(left_rows, right_rows) for left_rows, right_rows in matrix_pairs))
    pieces = lax.psum_scatter(
        terms + tuple(vectors), ("seq", "fsdp"), scatter_dimension=0, tiled=True
    )
    return list(pieces)


def join_terms(collected):
    matrix_pairs = []
    for member in range(len(collected[0][0])):
        lefts = jnp.concatenate([entry[0][member][0] for entry in collected], axis=0)
        rights = jnp.concatenate([entry[0][member][1] for entry in collected], axis=0)
        matrix_pairs.append((lefts, rights))
    vectors = [
        reduce(jnp.add, [entry[1][member] for entry in collected])
        for member in range(len(collected[0][1]))
    ]
    return (matrix_pairs, vectors)


def layer_step(gathered, inputs, cot_rows, live_mask, log_rates):
    (
        first_gain,
        query_weight,
        key_weight,
        value_weight,
        swish_weight,
        output_weight,
        group_gain,
        second_gain,
        feed_gate,
        feed_up,
        feed_down,
    ) = gathered
    floats = jnp.float32
    halves = jnp.bfloat16
    head_count = log_rates.shape[0]
    token_rows = inputs.shape[0]
    key_size = query_weight.shape[1] // head_count
    value_size = value_weight.shape[1] // head_count
    start_values = inputs.astype(floats)
    normed_one, pull_one = jax.vjp(norm_rows, start_values, first_gain.astype(floats))
    normed = normed_one.astype(halves)
    queries = plain_dot(normed, query_weight).astype(halves)
    keys_in = plain_dot(normed, key_weight).astype(halves) * live_mask[:, None].astype(halves)
    values_in = plain_dot(normed, value_weight).astype(halves)
    swish_in = plain_dot(normed, swish_weight)
    queries3 = queries.reshape(token_rows, head_count, key_size)
    keys3 = keys_in.reshape(token_rows, head_count, key_size)
    values3 = values_in.reshape(token_rows, head_count, value_size)
    cumulative = jnp.cumsum(log_rates, axis=1)
    slot_index = jnp.arange(token_rows)
    lower_mask = slot_index[:, None] >= slot_index[None, :]
    spread = cumulative[:, :, None] - cumulative[:, None, :]
    decay_matrix = jnp.where(lower_mask, jnp.exp(jnp.where(lower_mask, spread, 0.0)), 0.0)
    block_decay = jnp.exp(cumulative[:, -1])
    end_weight = jnp.exp(cumulative[:, -1:] - cumulative).T[:, :, None]
    entry_decay = jnp.exp(cumulative).T[:, :, None]
    query_wide = queries3.astype(floats)
    key_wide = keys3.astype(floats)
    value_wide = values3.astype(floats)
    state_term = jnp.einsum("jhd,jhe->hde", key_wide * end_weight, value_wide, precision=HIGHEST)
    state_identity = (jnp.ones_like(block_decay), jnp.zeros_like(state_term))
    _, start_state = carried_in(
        (block_decay, state_term), "seq", chain_states, state_identity, False
    )
    scores = jnp.einsum("ihd,jhd->hij", queries3, keys3, preferred_element_type=floats)
    weights = (scores * decay_matrix).astype(halves)
    intra_term = jnp.einsum("hij,jhe->ihe", weights, values3, preferred_element_type=floats)
    carried = entry_decay * jnp.einsum("ihd,hde->ihe", query_wide, start_state, precision=HIGHEST)
    retained = intra_term + carried
    grouped, pull_group = jax.vjp(
        norm_rows, retained, group_gain.astype(floats).reshape(head_count, value_size)
    )
    grouped_flat = grouped.reshape(token_rows, head_count * value_size)
    mixed_float, pull_mixed = jax.vjp(gated_swish, swish_in, grouped_flat)
    mixed_low = mixed_float.astype(halves)
    hidden = start_values + plain_dot(mixed_low, output_weight)
    normed_two, pull_two = jax.vjp(norm_rows, hidden, second_gain.astype(floats))
    second = normed_two.astype(halves)
    gate_two = plain_dot(second, feed_gate)
    upward = plain_dot(second, feed_up)
    inner_float, pull_inner = jax.vjp(gated_gelu, gate_two, upward)
    inner_low = inner_float.astype(halves)
    result = plain_dot(inner_low, feed_down)
    output_rows = ((hidden + result) * live_mask[:, None]).astype(halves)
    outer_grad = cot_rows.astype(floats) * live_mask[:, None]
    result_low = outer_grad.astype(halves)
    inner_grad = transposed(result_low, feed_down)
    gate_two_grad, upward_grad = pull_inner(inner_grad)
    gate_two_low = gate_two_grad.astype(halves)
    upward_low = upward_grad.astype(halves)
    second_grad = transposed(gate_two_low, feed_gate) + transposed(upward_low, feed_up)
    hidden_part, second_gain_grad = pull_two(second_grad)
    hidden_grad = outer_grad + hidden_part
    branch_low = hidden_grad.astype(halves)
    mixed_grad = transposed(branch_low, output_weight)
    swish_grad, grouped_grad = pull_mixed(mixed_grad)
    swish_low = swish_grad.astype(halves)
    retained_grad, group_gain_grad = pull_group(
        grouped_grad.reshape(token_rows, head_count, value_size)
    )
    retained_low = retained_grad.astype(halves)
    weights_grad = jnp.einsum("ihe,jhe->hij", retained_low, values3, preferred_element_type=floats)
    scores_low = (weights_grad * decay_matrix).astype(halves)
    query_intra = jnp.einsum("hij,jhd->ihd", scores_low, keys3, preferred_element_type=floats)
    key_intra = jnp.einsum("hij,ihd->jhd", scores_low, queries3, preferred_element_type=floats)
    value_intra = jnp.einsum("hij,ihe->jhe", weights, retained_low, preferred_element_type=floats)
    retained_wide = retained_low.astype(floats)
    query_carried = entry_decay * jnp.einsum(
        "ihe,hde->ihd", retained_wide, start_state, precision=HIGHEST
    )
    local_grad = jnp.einsum(
        "ihd,ihe->hde", query_wide * entry_decay, retained_wide, precision=HIGHEST
    )
    _, end_grad = carried_in((block_decay, local_grad), "seq", chain_states, state_identity, True)
    key_state = end_weight * jnp.einsum("jhe,hde->jhd", value_wide, end_grad, precision=HIGHEST)
    value_state = end_weight * jnp.einsum("jhd,hde->jhe", key_wide, end_grad, precision=HIGHEST)
    query_low = (
        (query_intra + query_carried).astype(halves).reshape(token_rows, head_count * key_size)
    )
    key_low = (
        ((key_intra + key_state) * live_mask[:, None, None])
        .astype(halves)
        .reshape(token_rows, head_count * key_size)
    )
    value_low = (
        (value_intra + value_state).astype(halves).reshape(token_rows, head_count * value_size)
    )
    normed_grad = (
        transposed(query_low, query_weight)
        + transposed(key_low, key_weight)
        + transposed(value_low, value_weight)
        + transposed(swish_low, swish_weight)
    )
    input_part, first_gain_grad = pull_one(normed_grad)
    grad_rows = (hidden_grad + input_part).astype(halves)
    matrix_pairs = [
        (normed, query_low),
        (normed, key_low),
        (normed, value_low),
        (normed, swish_low),
        (mixed_low, branch_low),
        (second, gate_two_low),
        (second, upward_low),
        (inner_low, result_low),
    ]
    vectors = [first_gain_grad, group_gain_grad.reshape(-1), second_gain_grad]
    return (output_rows, grad_rows, matrix_pairs, vectors)


def general_body(
    tokens,
    cotangent,
    lengths,
    block_order,
    log_decay,
    first_gain,
    query_weight,
    key_weight,
    value_weight,
    swish_weight,
    output_weight,
    group_gain,
    second_gain,
    feed_gate,
    feed_up,
    feed_down,
):
    batches = tokens.shape[0]
    block_rows = tokens.shape[1]
    selected_locations = lax.axis_size("seq")
    position = lax.axis_index("seq")
    group_index = lax.axis_index("fsdp")
    place_numbers = jnp.arange(selected_locations, dtype=jnp.int32)
    arrived_tokens, arrived_cotangent = (
        lax.all_gather(tokens, "seq", axis=1, tiled=True),
        lax.all_gather(cotangent, "seq", axis=1, tiled=True),
    )
    gathered = (
        lax.all_gather(first_gain, ("seq", "fsdp"), axis=0, tiled=True),
        lax.all_gather(query_weight, ("seq", "fsdp"), axis=0, tiled=True),
        lax.all_gather(key_weight, ("seq", "fsdp"), axis=0, tiled=True),
        lax.all_gather(value_weight, ("seq", "fsdp"), axis=0, tiled=True),
        lax.all_gather(swish_weight, ("seq", "fsdp"), axis=0, tiled=True),
        lax.all_gather(output_weight, ("seq", "fsdp"), axis=0, tiled=True),
        lax.all_gather(group_gain, ("seq", "fsdp"), axis=0, tiled=True),
        lax.all_gather(second_gain, ("seq", "fsdp"), axis=0, tiled=True),
        lax.all_gather(feed_gate, ("seq", "fsdp"), axis=0, tiled=True),
        lax.all_gather(feed_up, ("seq", "fsdp"), axis=0, tiled=True),
        lax.all_gather(feed_down, ("seq", "fsdp"), axis=0, tiled=True),
    )
    outputs = []
    input_grads = []
    collected = []
    order_rows = []
    for batch_number in range(batches):
        sequence = group_index * batches + batch_number
        order_row = lax.dynamic_index_in_dim(block_order, sequence, 0, keepdims=False)
        order_rows.append(order_row)
        source = jnp.sum(place_numbers * (order_row == position).astype(jnp.int32))
        token_rows = lax.dynamic_slice_in_dim(
            arrived_tokens[batch_number], source * block_rows, block_rows, 0
        )
        cot_rows = lax.dynamic_slice_in_dim(
            arrived_cotangent[batch_number], source * block_rows, block_rows, 0
        )
        live_length = lax.dynamic_index_in_dim(lengths, sequence, 0, keepdims=False)
        location_number = position * block_rows + jnp.arange(block_rows, dtype=jnp.int32)
        live_mask = (location_number < live_length).astype(jnp.float32)
        output_rows, grad_rows, matrix_pairs, vectors = layer_step(
            gathered, token_rows, cot_rows, live_mask, log_decay
        )
        outputs.append(output_rows)
        input_grads.append(grad_rows)
        collected.append((matrix_pairs, vectors))
    joined_pairs, joined_vectors = join_terms(collected)
    shards = spread_sum(joined_pairs, joined_vectors)
    every_output, every_grad = (
        lax.all_gather(jnp.stack(outputs), "seq", axis=1, tiled=True),
        lax.all_gather(jnp.stack(input_grads), "seq", axis=1, tiled=True),
    )
    returned = []
    returned_grads = []
    for batch_number in range(batches):
        target = lax.dynamic_index_in_dim(order_rows[batch_number], position, 0, keepdims=False)
        returned.append(
            lax.dynamic_slice_in_dim(every_output[batch_number], target * block_rows, block_rows, 0)
        )
        returned_grads.append(
            lax.dynamic_slice_in_dim(every_grad[batch_number], target * block_rows, block_rows, 0)
        )
    return (
        jnp.stack(returned),
        jnp.stack(returned_grads),
        shards[8],
        shards[0],
        shards[1],
        shards[2],
        shards[3],
        shards[4],
        shards[9],
        shards[10],
        shards[5],
        shards[6],
        shards[7],
    )


FULL = jnp.float32
HALF = jnp.bfloat16
MESH = pl.DeviceIdType.MESH
VMEM_BYTES = 56 * 1024 * 1024
LARGE_BYTES = 63 * 1024 * 1024
LANES = 128


def dot_nn(left, right):
    return jnp.dot(left, right, preferred_element_type=FULL)


def dot_nt(left, right):
    return lax.dot_general(left, right, (((1,), (1,)), ((), ())), preferred_element_type=FULL)


def dot_tn(left, right):
    return lax.dot_general(left, right, (((0,), (0,)), ((), ())), preferred_element_type=FULL)


def plane_peers():
    me = lax.axis_index("seq")
    core = lax.rem(me, 2)
    across = 2 - 4 * lax.rem(me // 2, 2)
    down = 4 - 8 * (me // 4)
    return me, me + 1 - 2 * core, me + across, me + down, me + across + down


def to_peer(source, target, send, receive, peer):
    return pltpu.make_async_remote_copy(
        src_ref=source,
        dst_ref=target,
        send_sem=send,
        recv_sem=receive,
        device_id={"seq": peer},
        device_id_type=MESH,
    )


def greet_neighbours():
    _, other, near, below, _ = plane_peers()
    barrier = pltpu.get_barrier_semaphore()
    for peer in (other, near, below):
        pl.semaphore_signal(barrier, inc=1, device_id={"seq": peer}, device_id_type=MESH)
    pl.semaphore_wait(barrier, 3)


GATHER_COPIES = 14


def gather_plan():
    me, other, near, below, far = plane_peers()
    flip = other - me
    return (
        (me, 0, near, near),
        (me, 1, below, below),
        (me, 0, other, other),
        (me, 1, other, other),
        (me, 1, near, near),
        (me, 0, below, below),
        (near, 0, below, far),
        (below, 1, near, far),
        (near, 0, other, near + flip),
        (below, 1, other, below + flip),
        (near, 1, other, near + flip),
        (below, 0, other, below + flip),
        (far, 0, other, far + flip),
        (far, 1, other, far + flip),
    )


class PlaneGather:
    def __init__(self, own, out, keeps, sends, receives, window=0, windows=1):
        self.own, self.out = own, out
        self.keep = None if keeps is None else keeps.at[window]
        self.sends, self.receives = sends, receives
        self.size = own.shape[0] // windows
        self.window, self.start = window, window * self.size
        self.half = self.size // 2

    def rows(self, which):
        return pl.ds(self.start + which * self.half, self.half)

    def kept(self):
        me = lax.axis_index("seq")
        rows = pl.ds(self.start, self.size)
        return pltpu.make_async_copy(self.own.at[rows], self.out.at[me, rows], self.keep)

    def sent(self, source, target, number, peer):
        at = (self.window, number)
        return to_peer(source, target, self.sends.at[at], self.receives.at[at], peer)

    def copy(self, number):
        block, which, peer, _ = gather_plan()[number]
        target = self.out.at[block, self.rows(which)]
        source = self.own.at[self.rows(which)] if number < 6 else target
        return self.sent(source, target, number, peer)

    def landed(self, number):
        _, which, peer, landing = gather_plan()[number]
        target = self.out.at[landing, self.rows(which)]
        self.sent(target, target, number, peer).wait_recv()

    def begin(self):
        if self.keep is not None:
            self.kept().start()
        for number in range(6):
            self.copy(number).start()

    def relay(self):
        for arrived, onward in ((0, (6, 8)), (1, (7, 9)), (4, (10,)), (5, (11,))):
            self.landed(arrived)
            for number in onward:
                self.copy(number).start()

    def relay_far(self):
        for arrived, onward in ((6, 12), (7, 13)):
            self.landed(arrived)
            self.copy(onward).start()

    def expect(self, *numbers):
        for number in numbers:
            self.landed(number)

    def drain(self):
        for number in range(GATHER_COPIES):
            self.copy(number).wait_send()
        if self.keep is not None:
            self.kept().wait()

    def finish(self):
        self.relay_far()
        self.expect(2, 3, 8, 9, 10, 11, 12, 13)
        self.drain()


def gather_scratch(windows=1):
    return [
        pltpu.SemaphoreType.DMA((windows,)),
        pltpu.SemaphoreType.DMA((windows, GATHER_COPIES)),
        pltpu.SemaphoreType.DMA((windows, GATHER_COPIES)),
    ]


SCATTER_COPIES = 10
WINDOWS = 2
CHUNK = 32


def by_chunks(rows, work):
    def step(number, carry):
        work(pl.ds(pl.multiple_of(number * CHUNK, CHUNK), CHUNK))
        return carry

    lax.fori_loop(0, rows // CHUNK, step, 0)


class PlaneScatter:
    def __init__(self, window, others, terms, cores, nears, belows, sends, receives):
        self.window = window
        self.others, self.terms, self.cores = others, terms, cores
        self.nears, self.belows = nears, belows
        self.sends, self.receives = sends, receives
        self.size = terms.shape[1] // WINDOWS
        self.half = self.size // 2
        self.start = window * self.size

    def copy(self, number):
        _, other, near, below, _ = plane_peers()
        whole = pl.ds(self.start, self.size)
        upper, lower = (pl.ds(self.start + at * self.half, self.half) for at in (0, 1))
        if number < 4:
            source, target, peer = (
                self.others.at[number, whole],
                self.cores.at[number, whole],
                other,
            )
        else:
            slot, rows, landing, place, peer = (
                (0, upper, self.nears, 0, near),
                (0, lower, self.belows, 0, below),
                (1, upper, self.nears, 1, near),
                (2, lower, self.belows, 1, below),
                (1, lower, self.nears, 2, near),
                (2, upper, self.belows, 2, below),
            )[number - 4]
            source, target = self.terms.at[slot, rows], landing.at[self.window, place]
        at = (self.window, number)
        return to_peer(source, target, self.sends.at[at], self.receives.at[at], peer)

    def fold(self, slot):
        def work(rows):
            here = pl.ds(pl.multiple_of(self.start + rows.start, CHUNK), CHUNK)
            self.terms[slot, here] = (
                self.terms[slot, here].astype(FULL) + self.cores[slot, here].astype(FULL)
            ).astype(HALF)

        by_chunks(self.size, work)

    def fold_half(self, slot, which, landed):
        def work(rows):
            at = self.start + which * self.half
            here = pl.ds(pl.multiple_of(at + rows.start, CHUNK), CHUNK)
            self.terms[slot, here] = (
                self.terms[slot, here].astype(FULL) + landed[self.window, 0, rows].astype(FULL)
            ).astype(HALF)

        by_chunks(self.half, work)

    def advance(self, slot):
        self.copy(slot).wait_recv()
        self.fold(slot)
        for number in ((4, 5), (6,), (7,), ())[slot]:
            self.copy(number).start()

    def relay(self):
        self.copy(4).wait_recv()
        self.fold_half(2, 0, self.nears)
        self.copy(9).start()
        self.copy(5).wait_recv()
        self.fold_half(1, 1, self.belows)
        self.copy(8).start()

    def finish(self):
        for number in (6, 7, 8, 9):
            self.copy(number).wait_recv()

    def drain(self, first=0):
        for number in range(first, SCATTER_COPIES):
            self.copy(number).wait_send()

    def total(self, at):
        upper = at < self.half
        rows = pl.ds(at if upper else at - self.half, CHUNK)
        near, below = (1, 2) if upper else (2, 1)
        return (
            self.terms[3, pl.ds(self.start + at, CHUNK)].astype(FULL)
            + self.nears[self.window, near, rows].astype(FULL)
            + self.belows[self.window, below, rows].astype(FULL)
        )


def block_order_of_plane():
    me, other, near, below, far = plane_peers()
    return [block + at for block in (far, near, below, me) for at in (other - me, 0)]


class Blocks:
    def __init__(self, source, target, sems):
        self.source, self.target, self.sems = source, target, sems
        self.blocks, self.taken = block_order_of_plane(), 0

    def load(self, number):
        slot = number % self.target.shape[0]
        return pltpu.make_async_copy(
            self.source.at[self.blocks[number]], self.target.at[slot], self.sems.at[slot]
        )

    def begin(self):
        for number in range(min(len(self.blocks), self.target.shape[0])):
            self.load(number).start()

    def take(self, work):
        number, slots = self.taken, self.target.shape[0]
        self.taken += 1
        self.load(number).wait()
        out = work(self.target[number % slots])
        if number + slots < len(self.blocks):
            self.load(number + slots).start()
        return out


def staged(sources, targets, sems):
    copies = [
        pltpu.make_async_copy(source, target, sems.at[number])
        for number, (source, target) in enumerate(zip(sources, targets))
    ]
    for copy in copies:
        copy.start()
    return copies


def stage_scratch(*arrays):
    return [pltpu.VMEM(array.shape, array.dtype) for array in arrays] + [
        pltpu.SemaphoreType.DMA((len(arrays),))
    ]


def block_scratch(count, array):
    return [
        pltpu.VMEM((count,) + array.shape[1:], array.dtype),
        pltpu.SemaphoreType.DMA((count,)),
    ]


def scatter_head(term, refs, earlier=(), relay_later=False):
    windows = [PlaneScatter(window, *refs) for window in range(WINDOWS)]
    others, terms = refs[:2]
    blocks = block_order_of_plane()

    def fill(slot):
        for window in earlier:
            window.copy(slot).wait_send()
        others[slot] = term(blocks[2 * slot])
        for window in windows:
            window.copy(slot).start()
        terms[slot] = term(blocks[2 * slot + 1])

    fill(0)
    for slot in range(4):
        if slot < 3:
            fill(slot + 1)
        windows[0].advance(slot)
    if not relay_later:
        windows[0].relay()
    for window in windows[1:]:
        for slot in range(4):
            window.advance(slot)
        if not relay_later:
            window.relay()
    return windows


def scatter_tail(windows, use, after=lambda window: None):
    for number, window in enumerate(windows):
        window.finish()
        for at in range(0, window.size, CHUNK):
            use(window.start + at, window.total(at))
        after(number)


def scatter_scratch(rows, width):
    half = rows // WINDOWS // 2
    return [
        pltpu.VMEM((4, rows, width), HALF),
        pltpu.VMEM((4, rows, width), HALF),
        pltpu.VMEM((4, rows, width), HALF),
        pltpu.VMEM((WINDOWS, 3, half, width), HALF),
        pltpu.VMEM((WINDOWS, 3, half, width), HALF),
        pltpu.SemaphoreType.DMA((WINDOWS, SCATTER_COPIES)),
        pltpu.SemaphoreType.DMA((WINDOWS, SCATTER_COPIES)),
    ]


def regroup(values, outer, inner):
    rows = values.shape[0]
    low_half = lax.broadcasted_iota(jnp.int32, (rows, LANES), 1) < LANES // 2

    def piece(p, q):
        at = (p * inner + q) // 2
        return values[:, at * LANES : (at + 1) * LANES]

    def turned(value):
        return pltpu.roll(value, LANES // 2, 1)

    groups = []
    for q in range(inner):
        for p in range(0, outer, 2):
            first, second = piece(p, q), piece(p + 1, q)
            if q % 2 == 0:
                groups.append(jnp.where(low_half, first, turned(second)))
            else:
                groups.append(jnp.where(low_half, turned(first), second))
    return jnp.concatenate(groups, axis=1)


def normalised(values):
    average = jnp.mean(values, axis=-1, keepdims=True)
    centered = values - average
    scale = lax.rsqrt(jnp.mean(centered * centered, axis=-1, keepdims=True) + EPSILON)
    return centered * scale, scale


def normalised_back(grad, normed, scale):
    average = jnp.mean(grad, axis=-1, keepdims=True)
    along = jnp.mean(grad * normed, axis=-1, keepdims=True)
    return (grad - average - normed * along) * scale


def vmem():
    return pl.BlockSpec(memory_space=pltpu.VMEM)


def in_hbm():
    return pl.BlockSpec(memory_space=pl.ANY)


def cost(flops, link_bytes):
    return pl.CostEstimate(flops=int(flops), bytes_accessed=int(link_bytes) * 16, transcendentals=0)


def linked(collective):
    return pltpu.CompilerParams(
        collective_id=collective, has_side_effects=True, vmem_limit_bytes=VMEM_BYTES
    )


class PlaneSwap:
    def __init__(self, weights, targets, keeps, sends, receives):
        self.weights, self.targets = weights, targets
        self.keeps, self.sends, self.receives = keeps, sends, receives
        self.peers = lax.axis_size("seq")

    def part(self, number, peer):
        weight, (target, start) = self.weights[number], self.targets[number]
        size = weight.shape[1] // self.peers
        return weight.at[:, pl.ds(pl.multiple_of(peer * size, LANES), size)]

    def place(self, number, peer):
        weight, (target, start) = self.weights[number], self.targets[number]
        return target.at[peer, :, pl.ds(start, weight.shape[1] // self.peers)]

    def copy(self, number, turn):
        me = lax.axis_index("seq")
        peer = lax.rem(me + turn, self.peers)
        return to_peer(
            self.part(number, peer),
            self.place(number, me),
            self.sends.at[number, turn],
            self.receives.at[number, turn],
            peer,
        )

    def landed(self, number, turn):
        me = lax.axis_index("seq")
        peer = lax.rem(me + self.peers - turn, self.peers)
        target = self.place(number, peer)
        to_peer(
            target, target, self.sends.at[number, turn], self.receives.at[number, turn], peer
        ).wait_recv()

    def kept(self, number):
        me = lax.axis_index("seq")
        return pltpu.make_async_copy(
            self.part(number, me), self.place(number, me), self.keeps.at[number]
        )

    def begin(self):
        for number in range(len(self.weights)):
            for turn in range(1, self.peers):
                self.copy(number, turn).start()
            self.kept(number).start()

    def finish(self):
        for number in range(len(self.weights)):
            for turn in range(1, self.peers):
                self.landed(number, turn)
                self.copy(number, turn).wait_send()
            self.kept(number).wait()


def swap_scratch(count, peers):
    return [
        pltpu.SemaphoreType.DMA((count,)),
        pltpu.SemaphoreType.DMA((count, peers)),
        pltpu.SemaphoreType.DMA((count, peers)),
    ]


def greet_plane(with_groups):
    me, group = lax.axis_index("seq"), lax.axis_index("fsdp")
    peers, groups = lax.axis_size("seq"), lax.axis_size("fsdp")
    barrier = pltpu.get_barrier_semaphore()
    count = peers - 1
    for turn in range(1, peers):
        peer = lax.rem(me + turn, peers)
        pl.semaphore_signal(barrier, inc=1, device_id={"seq": peer}, device_id_type=MESH)
    if with_groups:
        count += groups - 1
        for turn in range(1, groups):
            peer = lax.rem(group + turn, groups)
            pl.semaphore_signal(barrier, inc=1, device_id={"fsdp": peer}, device_id_type=MESH)
    pl.semaphore_wait(barrier, count)


def all_to_each(source, out, axis, size, keep, sends, receives):
    me = lax.axis_index(axis)

    def copy(turn, slot):
        peer = lax.rem(me + turn, size)
        return pltpu.make_async_remote_copy(
            src_ref=source,
            dst_ref=out.at[slot],
            send_sem=sends.at[turn],
            recv_sem=receives.at[turn],
            device_id={axis: peer},
            device_id_type=MESH,
        )

    def begin():
        pltpu.make_async_copy(source, out.at[me], keep).start()
        for turn in range(1, size):
            copy(turn, me).start()

    def finish():
        for turn in range(1, size):
            copy(turn, lax.rem(me + size - turn, size)).wait_recv()
            copy(turn, me).wait_send()
        pltpu.make_async_copy(source, out.at[me], keep).wait()

    return begin, finish


def first_swap_kernel(
    query_ref, key_ref, value_ref, swish_ref, rates_ref, gains_ref,
    cut_out, rates_out, gains_out,
    column, keeps, sends, receives, rate_keep, rate_sends, rate_receives,
    group_keep, group_sends, group_receives, gain_keep, gain_sends, gain_receives,
):
    peers, groups = lax.axis_size("seq"), lax.axis_size("fsdp")
    size, wide = query_ref.shape[1] // peers, value_ref.shape[1] // peers
    greet_plane(True)
    begin_groups, finish_groups = all_to_each(
        gains_ref, column, "fsdp", groups, group_keep, group_sends, group_receives
    )
    begin_rates, finish_rates = all_to_each(
        rates_ref, rates_out, "seq", peers, rate_keep, rate_sends, rate_receives
    )
    begin_gains, finish_gains = all_to_each(
        column, gains_out, "seq", peers, gain_keep, gain_sends, gain_receives
    )
    swap = PlaneSwap(
        (query_ref, key_ref, value_ref, swish_ref),
        ((cut_out, 0), (cut_out, size), (cut_out, 2 * size), (cut_out, 2 * size + wide)),
        keeps,
        sends,
        receives,
    )
    begin_groups()
    begin_rates()
    finish_groups()
    begin_gains()
    swap.begin()
    finish_rates()
    finish_gains()
    swap.finish()


def first_swap(query, key, value, swish, rates, gains):
    peers, groups = lax.axis_size("seq"), lax.axis_size("fsdp")
    slab = query.shape[0]
    total = sum(weight.shape[1] for weight in (query, key, value, swish)) // peers
    return pl.pallas_call(
        first_swap_kernel,
        in_specs=[in_hbm()] * 4 + [vmem()] * 2,
        out_specs=[in_hbm()] + [vmem()] * 2,
        out_shape=[
            jax.ShapeDtypeStruct((peers, slab, total), HALF),
            jax.ShapeDtypeStruct((peers,) + rates.shape, FULL),
            jax.ShapeDtypeStruct((peers, groups) + gains.shape, FULL),
        ],
        scratch_shapes=[pltpu.VMEM((groups,) + gains.shape, FULL)]
        + swap_scratch(4, peers)
        + [pltpu.SemaphoreType.DMA] + [pltpu.SemaphoreType.DMA((peers,))] * 2
        + [pltpu.SemaphoreType.DMA] + [pltpu.SemaphoreType.DMA((groups,))] * 2
        + [pltpu.SemaphoreType.DMA] + [pltpu.SemaphoreType.DMA((peers,))] * 2,
        compiler_params=linked(0),
        cost_estimate=cost(0, 2 * slab * peers * total),
    )(query, key, value, swish, rates, gains)


class LineGather:
    def __init__(self, own, out, keep, sends, receives):
        self.own, self.out = own, out
        self.keep, self.sends, self.receives = keep, sends, receives
        self.me, self.last = lax.axis_index("fsdp"), lax.axis_size("fsdp") - 1
        self.pieces = own.shape[0]

    def block(self, way, depth):
        return self.me - depth if way == 0 else self.me + depth

    def holds(self, way, depth):
        return self.me >= depth if way == 0 else self.me + depth <= self.last

    def passes(self, way):
        return self.me < self.last if way == 0 else self.me > 0

    def sent(self, source, way, depth, piece, block):
        at = (way, depth, piece)
        return pltpu.make_async_remote_copy(
            src_ref=source,
            dst_ref=self.out.at[block, piece],
            send_sem=self.sends.at[at],
            recv_sem=self.receives.at[at],
            device_id={"fsdp": self.me + 1 if way == 0 else self.me - 1},
            device_id_type=MESH,
        )

    def copy(self, way, depth, piece):
        block = self.block(way, depth)
        source = self.own.at[piece] if depth == 0 else self.out.at[block, piece]
        return self.sent(source, way, depth, piece, block)

    def landed(self, way, depth, piece):
        block = self.block(way, depth)
        self.sent(self.out.at[block, piece], way, depth - 1, piece, block).wait_recv()

    def kept(self):
        return pltpu.make_async_copy(self.own, self.out.at[self.me], self.keep)

    def begin(self):
        for piece in range(self.pieces):
            for way in (0, 1):

                @pl.when(self.passes(way))
                def _():
                    self.copy(way, 0, piece).start()

        self.kept().start()

    def hand_on(self, depth):
        for piece in range(self.pieces):
            for way in (0, 1):

                @pl.when(self.holds(way, depth) & self.passes(way))
                def _():
                    self.landed(way, depth, piece)
                    self.copy(way, depth, piece).start()

    def finish(self):
        for depth in range(1, self.last + 1):
            for piece in range(self.pieces):
                for way in (0, 1):

                    @pl.when(self.holds(way, depth) & jnp.logical_not(self.passes(way)))
                    def _():
                        self.landed(way, depth, piece)

        for depth in range(self.last):
            for piece in range(self.pieces):
                for way in (0, 1):

                    @pl.when(self.holds(way, depth) & self.passes(way))
                    def _():
                        self.copy(way, depth, piece).wait_send()

        self.kept().wait()


def unpack_gains(gains_ref, one_ref, two_ref, group_ref):
    peers, groups = gains_ref.shape[:2]
    low_half = lax.broadcasted_iota(jnp.int32, (1, LANES), 1) < LANES // 2
    for peer in range(peers):
        for at in range(0, groups, 2):
            left, right = gains_ref[peer, at, 1:2], gains_ref[peer, at + 1, 1:2]
            lanes = pl.ds((peer * groups + at) * LANES // 2, LANES)
            one_ref[:, lanes] = jnp.where(low_half, left, pltpu.roll(right, LANES // 2, 1))
            two_ref[:, lanes] = jnp.where(low_half, pltpu.roll(left, LANES // 2, 1), right)
    me = lax.axis_index("seq")
    for at in range(groups):
        group_ref[:, at * LANES : (at + 1) * LANES] = gains_ref[me, at, 0:1]


def unpack_rates(rates_ref, decay_ref, column_ref):
    blocks, _, rows = rates_ref.shape
    me = lax.axis_index("seq")
    total = jnp.concatenate([rates_ref[block, pl.ds(me, 1)] for block in range(blocks)], axis=0)
    lane = lax.broadcasted_iota(jnp.int32, total.shape, 1)
    shift = 1
    while shift < rows:
        total += jnp.where(lane >= shift, pltpu.roll(total, shift, 1), 0.0)
        shift *= 2
    square = (rows, rows)
    lower = lax.broadcasted_iota(jnp.int32, square, 0) >= lax.broadcasted_iota(jnp.int32, square, 1)
    for block in range(blocks):
        along = jnp.broadcast_to(total[block : block + 1], square)
        down = along.T
        spread = jnp.where(lower, down - along, 0.0)
        decay_ref[block] = jnp.where(lower, jnp.exp(spread), 0.0)
        first = down[:, 0:1]
        column_ref[block, :, 0:1] = jnp.exp(first)
        column_ref[block, :, 1:2] = jnp.exp(first[rows - 1 : rows] - first)


def inputs_kernel(
    lengths_ref, order_ref, tokens_ref, grad_ref, gains_ref, rates_ref, gate_ref, up_ref, cut_ref,
    entered_out, grads_out, feed_out, weight_out,
    mask_ref, gain_ref, second_ref, group_ref, decay_ref, column_ref,
    own_entered, own_grad, keep_one, sends_one, receives_one, keep_two, sends_two, receives_two,
    keeps, sends, receives, line_keep, line_sends, line_receives,
):
    peers, groups = lax.axis_size("seq"), lax.axis_size("fsdp")
    greet_plane(True)
    line = LineGather(cut_ref, weight_out, line_keep, line_sends, line_receives)
    line.begin()
    size = gate_ref.shape[1] // peers
    me, group = lax.axis_index("seq"), lax.axis_index("fsdp")
    batches = lengths_ref.shape[0] // groups
    block = tokens_ref.shape[0] // batches
    for batch in range(batches):
        sequence = group * batches + batch
        numbers = order_ref[sequence, me] * block + lax.broadcasted_iota(jnp.int32, (block, 1), 0)
        live = (numbers < lengths_ref[sequence]).astype(FULL)
        mask_ref[batch * block : (batch + 1) * block] = live
    unpack_gains(gains_ref, gain_ref, second_ref, group_ref)
    gain = gain_ref[...]

    def work(rows):
        normed, _ = normalised(tokens_ref[rows].astype(FULL))
        own_entered[rows] = regroup(normed * gain, peers, groups).astype(HALF)
        own_grad[rows] = (grad_ref[rows].astype(FULL) * mask_ref[rows]).astype(HALF)

    by_chunks(tokens_ref.shape[0], work)
    one = PlaneGather(own_entered, entered_out, keep_one, sends_one, receives_one)
    two = PlaneGather(own_grad, grads_out, keep_two, sends_two, receives_two)
    swap = PlaneSwap((gate_ref, up_ref), ((feed_out, 0), (feed_out, size)), keeps, sends, receives)
    one.begin()
    one.relay()
    swap.begin()
    two.begin()
    unpack_rates(rates_ref, decay_ref, column_ref)
    line.hand_on(1)
    one.finish()
    two.relay()
    line.hand_on(2)
    swap.finish()
    two.finish()
    line.finish()


def gather_inputs(lengths, order, tokens, grad, gains, rates, gate, up, cut, value_size):
    peers, groups = lax.axis_size("seq"), lax.axis_size("fsdp")
    own, width = tokens.shape
    slab, columns = gate.shape
    part = columns // peers
    blocks, _, rows = rates.shape
    return pl.pallas_call(
        inputs_kernel,
        in_specs=[pl.BlockSpec(memory_space=pltpu.SMEM)] * 2 + [vmem()] * 4 + [in_hbm()] * 3,
        out_specs=[in_hbm()] * 4 + [vmem()] * 6,
        out_shape=[
            jax.ShapeDtypeStruct((peers, own, width), HALF),
            jax.ShapeDtypeStruct((peers, own, width), HALF),
            jax.ShapeDtypeStruct((peers, slab, 2 * part), HALF),
            jax.ShapeDtypeStruct((groups,) + cut.shape, HALF),
            jax.ShapeDtypeStruct((own, 1), FULL),
            jax.ShapeDtypeStruct((1, width), FULL),
            jax.ShapeDtypeStruct((1, width), FULL),
            jax.ShapeDtypeStruct((1, value_size), FULL),
            jax.ShapeDtypeStruct((blocks, rows, rows), FULL),
            jax.ShapeDtypeStruct((blocks, rows, 2), FULL),
        ],
        scratch_shapes=[pltpu.VMEM((own, width), HALF)] * 2
        + gather_scratch()
        + gather_scratch()
        + swap_scratch(2, peers)
        + [
            pltpu.SemaphoreType.DMA,
            pltpu.SemaphoreType.DMA((2, groups - 1, peers)),
            pltpu.SemaphoreType.DMA((2, groups - 1, peers)),
        ],
        compiler_params=linked(1),
        cost_estimate=cost(0, 2 * peers * (2 * own * width + slab * 2 * part)),
    )(lengths, order, tokens, grad, gains, rates, gate, up, cut)


def feed_kernel(
    rows_ref, weight_ref, grads_ref, inner_ref, up_slope_ref, gate_slope_ref, down_ref, total
):
    step = pl.program_id(0)
    both = dot_nn(rows_ref[...], weight_ref[...])
    part = both.shape[1] // 2
    gate, upward = both[:, :part], both[:, part:]
    inside = 0.7978845608028654 * (gate + 0.044715 * (gate * gate * gate))
    bend = jnp.tanh(inside)
    share = 0.5 * (1.0 + bend)
    value = gate * share
    steep = 0.7978845608028654 * (1.0 + 3.0 * 0.044715 * (gate * gate))
    slope = share + 0.5 * gate * (1.0 - bend * bend) * steep
    inner_ref[...] = (value * upward).astype(HALF)
    up_slope_ref[...] = value.astype(HALF)
    gate_slope_ref[...] = (upward * slope).astype(HALF)
    term = dot_tn(inner_ref[...], grads_ref[...])

    @pl.when(step == 0)
    def _():
        total[...] = term

    @pl.when(step > 0)
    def _():
        total[...] += term

    @pl.when(step == pl.num_programs(0) - 1)
    def _():
        down_ref[...] = total[...].astype(HALF)


def feed(rows, weight, grads):
    count, width = rows.shape
    columns = weight.shape[1]
    part = columns // 2
    tile = 512
    tokens = pl.BlockSpec((tile, width), lambda i: (i, 0))
    out = pl.BlockSpec((tile, part), lambda i: (i, 0))
    return pl.pallas_call(
        feed_kernel,
        grid=(count // tile,),
        in_specs=[
            tokens,
            pl.BlockSpec((width, columns), lambda i: (0, 0), pipeline_mode=pl.Buffered(1)),
            tokens,
        ],
        out_specs=[out] * 3 + [pl.BlockSpec((part, width), lambda i: (0, 0))],
        out_shape=[jax.ShapeDtypeStruct((count, part), HALF)] * 3
        + [jax.ShapeDtypeStruct((part, width), HALF)],
        scratch_shapes=[pltpu.VMEM((part, width), FULL)],
        compiler_params=pltpu.CompilerParams(
            dimension_semantics=("arbitrary",), vmem_limit_bytes=VMEM_BYTES
        ),
        cost_estimate=pl.CostEstimate(
            flops=3 * count * width * columns,
            bytes_accessed=2 * (2 * count * width + width * columns + 2 * count * columns),
            transcendentals=0,
        ),
    )(rows, weight, grads)


def feed_back_kernel(rows_ref, weight_ref, up_slope_ref, gate_slope_ref, grad_ref):
    inner_grad = dot_nt(rows_ref[...], weight_ref[...])
    part = inner_grad.shape[1]
    grad_ref[:, :part] = (inner_grad * gate_slope_ref[...].astype(FULL)).astype(HALF)
    grad_ref[:, part:] = (inner_grad * up_slope_ref[...].astype(FULL)).astype(HALF)


def feed_back(rows, weight, up_slope, gate_slope):
    count, width = rows.shape
    part = weight.shape[0]
    tile = 512
    slope = pl.BlockSpec((tile, part), lambda i: (i, 0))
    return pl.pallas_call(
        feed_back_kernel,
        grid=(count // tile,),
        in_specs=[
            pl.BlockSpec((tile, width), lambda i: (i, 0)),
            pl.BlockSpec((part, width), lambda i: (0, 0), pipeline_mode=pl.Buffered(1)),
            slope,
            slope,
        ],
        out_specs=pl.BlockSpec((tile, 2 * part), lambda i: (i, 0)),
        out_shape=jax.ShapeDtypeStruct((count, 2 * part), HALF),
        compiler_params=pltpu.CompilerParams(
            dimension_semantics=("arbitrary",), vmem_limit_bytes=VMEM_BYTES
        ),
        cost_estimate=pl.CostEstimate(
            flops=2 * count * width * part,
            bytes_accessed=2 * (count * width + width * part + 4 * count * part),
            transcendentals=0,
        ),
    )(rows, weight, up_slope, gate_slope)


def retention_kernel(
    place_ref, live_ref, first_ref, second_ref, weight_ref, decay_ref, column_ref, gain_ref,
    qkv_ref, swish_ref, normed_ref, scale_ref, entry_ref, mixed_hbm, state, mixed_buffer, sems,
):
    step, steps = pl.program_id(0), pl.num_programs(0)
    rows = first_ref.shape[2]
    batches, key_size, value_size = state.shape
    total = 2 * key_size + value_size
    slot = lax.rem(step, 2)

    def sent(at, which, batch):
        return pltpu.make_async_copy(
            mixed_buffer.at[which, batch],
            mixed_hbm.at[place_ref[batch, at], batch],
            sems.at[which, batch],
        )

    @pl.when(step == 0)
    def _():
        state[...] = jnp.zeros_like(state)

    @pl.when(step >= 2)
    def _():
        for batch in range(batches):
            sent(step - 2, slot, batch).wait()

    rows_in = jnp.concatenate([first_ref[0, 0], second_ref[0, 0]], axis=0)
    projected = dot_nn(rows_in, weight_ref[...])
    decay = decay_ref[0]
    entry_decay = column_ref[0, :, 0:1]
    end_weight = column_ref[0, :, 1:2]
    block_decay = column_ref[0, rows - 1 : rows, 0:1]
    positions = step * rows + lax.broadcasted_iota(jnp.int32, (rows, 1), 0)
    for batch in range(batches):
        mine = slice(batch * rows, (batch + 1) * rows)
        live = (positions < live_ref[batch]).astype(FULL)
        query = projected[mine, :key_size].astype(HALF)
        key = (projected[mine, key_size : 2 * key_size] * live).astype(HALF)
        value = projected[mine, 2 * key_size : total].astype(HALF)
        swish = projected[mine, total:]
        before = state[batch]
        before_low = before.astype(HALF)
        weights = (dot_nt(query, key) * decay).astype(HALF)
        retained = dot_nn(weights, value) + entry_decay * dot_nn(query, before_low)
        key_ended = (key.astype(FULL) * end_weight).astype(HALF)
        state[batch] = block_decay * before + dot_tn(key_ended, value)
        normed, scale = normalised(retained)
        qkv_ref[batch, 0, :, :key_size] = query
        qkv_ref[batch, 0, :, key_size : 2 * key_size] = key
        qkv_ref[batch, 0, :, 2 * key_size :] = value
        scale_ref[batch, 0] = jnp.broadcast_to(scale, scale_ref.shape[2:])
        entry_ref[batch, 0] = before_low
        swish_ref[batch, 0] = swish.astype(HALF)
        normed_ref[batch, 0] = normed.astype(HALF)
        mixed = swish * jax.nn.sigmoid(swish) * (normed * gain_ref[...])
        mixed_buffer[slot, batch] = mixed.astype(HALF)
        sent(step, slot, batch).start()

    @pl.when(step == steps - 1)
    def _():
        for batch in range(batches):
            sent(step, slot, batch).wait()
            sent(step - 1, 1 - slot, batch).wait()


def retention(rows_in, weight, place, live, decay, columns, gain, key_size):
    blocks, batches, rows, width = rows_in.shape
    value_size = gain.shape[-1]
    total = 2 * key_size + value_size

    def arriving(batch):
        return pl.BlockSpec(
            (1, 1, rows, width), lambda i, place, live: (place[batch, i], batch, 0, 0)
        )

    def whole(shape):
        return pl.BlockSpec(
            shape, lambda i, place, live: (0,) * len(shape), pipeline_mode=pl.Buffered(1)
        )

    def here(*tail):
        return pl.BlockSpec((batches, 1) + tail, lambda i, place, live: (0, i, 0, 0))

    def along(*tail):
        return pl.BlockSpec((1,) + tail, lambda i, place, live: (i, 0, 0))

    return pl.pallas_call(
        retention_kernel,
        grid_spec=pltpu.PrefetchScalarGridSpec(
            num_scalar_prefetch=2,
            grid=(blocks,),
            in_specs=[
                arriving(0),
                arriving(1),
                whole((width, total + value_size)),
                along(rows, rows),
                along(rows, 2),
                whole((1, value_size)),
            ],
            out_specs=[
                here(rows, total),
                here(rows, value_size),
                here(rows, value_size),
                here(rows, LANES),
                here(key_size, value_size),
                in_hbm(),
            ],
            scratch_shapes=[
                pltpu.VMEM((batches, key_size, value_size), FULL),
                pltpu.VMEM((2, batches, rows, value_size), HALF),
                pltpu.SemaphoreType.DMA((2, batches)),
            ],
        ),
        out_shape=[
            jax.ShapeDtypeStruct((batches, blocks, rows, total), HALF),
            jax.ShapeDtypeStruct((batches, blocks, rows, value_size), HALF),
            jax.ShapeDtypeStruct((batches, blocks, rows, value_size), HALF),
            jax.ShapeDtypeStruct((batches, blocks, rows, LANES), FULL),
            jax.ShapeDtypeStruct((batches, blocks, key_size, value_size), HALF),
            jax.ShapeDtypeStruct((blocks, batches, rows, value_size), HALF),
        ],
        compiler_params=pltpu.CompilerParams(
            dimension_semantics=("arbitrary",), vmem_limit_bytes=VMEM_BYTES
        ),
        cost_estimate=pl.CostEstimate(
            flops=3 * blocks * batches * rows * width * total,
            bytes_accessed=2 * blocks * batches * rows * (width + 2 * total) + 4 * width * total,
            transcendentals=0,
        ),
    )(place, live, rows_in, rows_in, weight, decay, columns, gain)


def retention_back_kernel(
    place_ref, live_ref, first_ref, second_ref,
    weight_ref, decay_ref, column_ref, gain_ref, qkv_ref, swish_ref, normed_ref, scale_ref, entry_ref,
    gain_grad_ref, grads_hbm, state, grads_buffer, sems,
):
    step, steps = pl.program_id(0), pl.num_programs(0)
    rows = first_ref.shape[2]
    batches, key_size, value_size = state.shape
    slot = lax.rem(step, 2)

    def sent(at, which, batch):
        return pltpu.make_async_copy(
            grads_buffer.at[which, batch],
            grads_hbm.at[place_ref[batch, steps - 1 - at], batch],
            sems.at[which, batch],
        )

    @pl.when(step == 0)
    def _():
        state[...] = jnp.zeros_like(state)
        gain_grad_ref[...] = jnp.zeros_like(gain_grad_ref)

    @pl.when(step >= 2)
    def _():
        for batch in range(batches):
            sent(step - 2, slot, batch).wait()

    rows_in = jnp.concatenate([first_ref[0, 0], second_ref[0, 0]], axis=0)
    mixed_grads = dot_nt(rows_in, weight_ref[...])
    decay = decay_ref[0]
    entry_decay = column_ref[0, :, 0:1]
    end_weight = column_ref[0, :, 1:2]
    block_decay = column_ref[0, rows - 1 : rows, 0:1]
    positions = (steps - 1 - step) * rows + lax.broadcasted_iota(jnp.int32, (rows, 1), 0)
    gain = gain_ref[...]
    for batch in range(batches):
        live = (positions < live_ref[batch]).astype(FULL)
        mixed_grad = mixed_grads[batch * rows : (batch + 1) * rows]
        query = qkv_ref[batch, 0, :, :key_size]
        key = qkv_ref[batch, 0, :, key_size : 2 * key_size]
        value = qkv_ref[batch, 0, :, 2 * key_size :]
        swish = swish_ref[batch, 0].astype(FULL)
        normed = normed_ref[batch, 0].astype(FULL)
        scale = scale_ref[batch, 0, :, 0:1]
        entry = entry_ref[batch, 0]
        sigmoid = jax.nn.sigmoid(swish)
        silu = swish * sigmoid
        swish_grad = mixed_grad * (normed * gain) * (sigmoid * (1.0 + swish - silu))
        scaled_grad = mixed_grad * silu
        gain_grad_ref[...] += jnp.sum(scaled_grad * normed, axis=0, keepdims=True)
        retained_grad = normalised_back(scaled_grad * gain, normed, scale).astype(HALF)
        weights = (dot_nt(query, key) * decay).astype(HALF)
        scores_grad = (dot_nt(retained_grad, value) * decay).astype(HALF)
        after = state[batch]
        after_low = after.astype(HALF)
        query_grad = dot_nn(scores_grad, key) + entry_decay * dot_nt(retained_grad, entry)
        key_grad = dot_tn(scores_grad, query) + end_weight * dot_nt(value, after_low)
        value_grad = dot_tn(weights, retained_grad) + end_weight * dot_nn(key, after_low)
        query_entered = (query.astype(FULL) * entry_decay).astype(HALF)
        state[batch] = block_decay * after + dot_tn(query_entered, retained_grad)
        grads_buffer[slot, batch, :, :key_size] = query_grad.astype(HALF)
        grads_buffer[slot, batch, :, key_size : 2 * key_size] = (key_grad * live).astype(HALF)
        grads_buffer[slot, batch, :, 2 * key_size : 2 * key_size + value_size] = value_grad.astype(
            HALF
        )
        grads_buffer[slot, batch, :, 2 * key_size + value_size :] = swish_grad.astype(HALF)
        sent(step, slot, batch).start()

    @pl.when(step == steps - 1)
    def _():
        for batch in range(batches):
            sent(step, slot, batch).wait()
            sent(step - 1, 1 - slot, batch).wait()


def retention_back(rows_in, weight, place, live, decay, columns, gain, saved):
    blocks, batches, rows, width = rows_in.shape
    value_size = gain.shape[-1]
    key_size = saved[-1].shape[2]
    total = 2 * key_size + 2 * value_size

    def arriving(batch, size):
        return pl.BlockSpec(
            (1, 1, rows, size),
            lambda i, place, live: (place[batch, blocks - 1 - i], batch, 0, 0),
        )

    def whole(shape):
        return pl.BlockSpec(
            shape, lambda i, place, live: (0,) * len(shape), pipeline_mode=pl.Buffered(1)
        )

    def here(*tail):
        return pl.BlockSpec((batches, 1) + tail, lambda i, place, live: (0, blocks - 1 - i, 0, 0))

    def along(*tail):
        return pl.BlockSpec((1,) + tail, lambda i, place, live: (blocks - 1 - i, 0, 0))

    return pl.pallas_call(
        retention_back_kernel,
        grid_spec=pltpu.PrefetchScalarGridSpec(
            num_scalar_prefetch=2,
            grid=(blocks,),
            in_specs=[
                arriving(0, width),
                arriving(1, width),
                whole((value_size, width)),
                along(rows, rows),
                along(rows, 2),
                whole((1, value_size)),
                here(rows, 2 * key_size + value_size),
                here(rows, value_size),
                here(rows, value_size),
                here(rows, LANES),
                here(key_size, value_size),
            ],
            out_specs=[
                pl.BlockSpec((1, value_size), lambda i, place, live: (0, 0)),
                in_hbm(),
            ],
            scratch_shapes=[
                pltpu.VMEM((batches, key_size, value_size), FULL),
                pltpu.VMEM((2, batches, rows, total), HALF),
                pltpu.SemaphoreType.DMA((2, batches)),
            ],
        ),
        out_shape=[
            jax.ShapeDtypeStruct((1, value_size), FULL),
            jax.ShapeDtypeStruct((blocks, batches, rows, total), HALF),
        ],
        compiler_params=pltpu.CompilerParams(
            dimension_semantics=("arbitrary",), vmem_limit_bytes=VMEM_BYTES
        ),
        cost_estimate=pl.CostEstimate(
            flops=6 * blocks * batches * rows * width * value_size,
            bytes_accessed=2 * blocks * batches * rows * (width + 2 * total)
            + 2 * width * value_size,
            transcendentals=0,
        ),
    )(place, live, rows_in, rows_in, weight, decay, columns, gain, *saved)


def middle_kernel(
    mixed_hbm, weight_hbm, tokens_hbm, gain_ref, hidden_ref, second_out,
    *scratch,
):
    scatter = scratch[:7]
    own, keeps, gather_sends, gather_receives = scratch[7:11]
    weight_ref, tokens_ref, stage_sems, mixed, mixed_sems = scratch[11:]
    peers, groups = lax.axis_size("seq"), lax.axis_size("fsdp")
    sources, targets = (weight_hbm, tokens_hbm), (weight_ref, tokens_ref)
    weight_copy, tokens_copy = staged(sources, targets, stage_sems)
    blocks = Blocks(mixed_hbm, mixed, mixed_sems)
    blocks.begin()
    greet_neighbours()
    weight_copy.wait()

    def term(block):
        return blocks.take(lambda value: dot_nn(value, weight_ref[...]).astype(HALF))

    gain = gain_ref[...]

    def use(start, total):
        rows = pl.ds(start, CHUNK)
        hidden = tokens_ref[rows].astype(FULL) + total
        hidden_ref[rows] = hidden
        normed, _ = normalised(hidden)
        own[rows] = regroup(normed * gain, peers, groups).astype(HALF)

    gathers = [
        PlaneGather(own, second_out, keeps, gather_sends, gather_receives, window, WINDOWS)
        for window in range(WINDOWS)
    ]
    windows = scatter_head(term, scatter)
    tokens_copy.wait()
    scatter_tail(windows, use, lambda window: gathers[window].begin())
    for gather in gathers:
        gather.relay()
    for gather in gathers:
        gather.finish()
    for window in windows:
        window.drain()


def middle(mixed, weight, tokens, gain):
    peers, own, inner = mixed.shape
    width = weight.shape[1]
    return pl.pallas_call(
        middle_kernel,
        in_specs=[in_hbm()] * 3 + [vmem()],
        out_specs=[vmem(), in_hbm()],
        out_shape=[
            jax.ShapeDtypeStruct((own, width), FULL),
            jax.ShapeDtypeStruct((peers, own, width), HALF),
        ],
        scratch_shapes=scatter_scratch(own, width)
        + [pltpu.VMEM((own, width), HALF)]
        + gather_scratch(WINDOWS)
        + stage_scratch(weight, tokens)
        + block_scratch(peers, mixed),
        compiler_params=linked(2),
        cost_estimate=cost(2 * peers * own * inner * width, 4 * peers * own * width),
    )(mixed, weight, tokens, gain)


class LineSum:
    def __init__(self, terms, landed, own, final, loads, sends, receives):
        self.terms, self.landed, self.own, self.final = terms, landed, own, final
        self.loads, self.sends, self.receives = loads, sends, receives
        self.me, self.last = lax.axis_index("fsdp"), lax.axis_size("fsdp") - 1
        self.peers, self.place = lax.axis_size("seq"), lax.axis_index("seq")

    def piece(self, turn):
        return lax.rem(self.place + turn, self.peers)

    def depth(self, way):
        return self.me if way == 0 else self.last - self.me

    def block(self, way, order):
        return self.last - order if way == 0 else order

    def slot(self, way, order):
        return order if way == 0 else 2 * self.last - 2 - order

    def sent(self, source, way, order, turn):
        at = (way, order, turn)
        return pltpu.make_async_remote_copy(
            src_ref=source,
            dst_ref=self.landed.at[self.slot(way, order), self.piece(turn)],
            send_sem=self.sends.at[at],
            recv_sem=self.receives.at[at],
            device_id={"fsdp": self.me + 1 if way == 0 else self.me - 1},
            device_id_type=MESH,
        )

    def first(self, way, order, turn):
        source = self.terms.at[self.block(way, order), self.piece(turn)]
        return self.sent(source, way, order, turn)

    def onward(self, way, order, turn):
        source = self.landed.at[self.slot(way, order), self.piece(turn)]
        return self.sent(source, way, order, turn)

    def load(self, way, order):
        return pltpu.make_async_copy(
            self.terms.at[self.block(way, order)], self.own.at[way], self.loads.at[way]
        )

    def load_final(self):
        return pltpu.make_async_copy(self.terms.at[self.me], self.final, self.loads.at[2])

    def begin(self):
        for way in (0, 1):

            @pl.when(self.depth(way) == 0)
            def _():
                for order in range(self.last):
                    for turn in range(self.peers):
                        self.first(way, order, turn).start()

            self.load(way, 0).start()
        self.load_final().start()

    def loaded(self):
        for way in (0, 1):
            self.load(way, 0).wait()

    def load_next(self):
        for way in (0, 1):

            @pl.when(self.depth(way) == 1)
            def _():
                self.load(way, 1).start()

    def loaded_next(self):
        for way in (0, 1):

            @pl.when(self.depth(way) == 1)
            def _():
                self.load(way, 1).wait()

    def hand_on(self, order, depth, turns):
        for turn in turns:
            for way in (0, 1):

                @pl.when(self.depth(way) == depth)
                def _():
                    at, piece = self.slot(way, order), self.piece(turn)
                    self.onward(way, order, turn).wait_recv()
                    self.landed[at, piece] = (
                        self.landed[at, piece].astype(FULL) + self.own[way, piece].astype(FULL)
                    ).astype(HALF)
                    self.onward(way, order, turn).start()

    def finish(self, use):
        self.load_final().wait()
        for turn in range(self.peers):
            piece = self.piece(turn)
            for way in (0, 1):

                @pl.when(self.depth(way) > 0)
                def _():
                    order = self.last - self.depth(way)
                    self.onward(way, order, turn).wait_recv()
                    self.final[piece] = (
                        self.final[piece].astype(FULL)
                        + self.landed[self.slot(way, order), piece].astype(FULL)
                    ).astype(HALF)

            use(turn)

    def drain(self):
        for way in (0, 1):
            for order in range(self.last):
                for turn in range(self.peers):

                    @pl.when(self.depth(way) == 0)
                    def _():
                        self.first(way, order, turn).wait_send()

                    @pl.when((self.depth(way) > 0) & (self.depth(way) < self.last - order))
                    def _():
                        self.onward(way, order, turn).wait_send()


def line_scratch(groups, peers, slab, columns):
    block = (peers, slab, columns)
    return [
        pltpu.VMEM((2 * groups - 3,) + block, HALF),
        pltpu.VMEM((2,) + block, HALF),
        pltpu.VMEM(block, HALF),
        pltpu.SemaphoreType.DMA((3,)),
        pltpu.SemaphoreType.DMA((2, groups - 1, peers)),
        pltpu.SemaphoreType.DMA((2, groups - 1, peers)),
    ]


def middle_back_kernel(
    grads_hbm, weight_hbm, hidden_hbm, outer_hbm, mask_ref, gain_ref, mixed_hbm,
    hidden_grad_ref, gain_grad_ref, branch_out, out_grad_ref,
    *scratch,
):
    scatter = scratch[:7]
    own, gather_sends, gather_receives = scratch[7:10]
    weight_ref, hidden_ref, outer_ref, mixed_ref, stage_sems, grads, grad_sems = scratch[10:17]
    branch, total, out_sems = scratch[17:]
    peers, groups = lax.axis_size("seq"), lax.axis_size("fsdp")
    me, other, near, below, far = plane_peers()
    flip = other - me
    blocks = Blocks(grads_hbm, grads, grad_sems)
    weight_copy, *later = staged(
        (weight_hbm, hidden_hbm, outer_hbm, mixed_hbm),
        (weight_ref, hidden_ref, outer_ref, mixed_ref),
        stage_sems,
    )
    blocks.begin()
    greet_neighbours()
    weight_copy.wait()

    def term(block):
        return blocks.take(lambda value: dot_nt(value, weight_ref[...]).astype(HALF))

    gain = gain_ref[...]
    gain_grad_ref[...] = jnp.zeros_like(gain_grad_ref)

    def use(start, total):
        rows = pl.ds(start, CHUNK)
        grad = regroup(total, groups, peers)
        normed, scale = normalised(hidden_ref[rows])
        gain_grad_ref[...] += jnp.sum(grad * normed, axis=0, keepdims=True)
        outer = outer_ref[rows].astype(FULL) * mask_ref[rows]
        hidden_grad = outer + normalised_back(grad * gain, normed, scale)
        hidden_grad_ref[rows] = hidden_grad
        own[rows] = hidden_grad.astype(HALF)

    gathers = [
        PlaneGather(own, branch, None, gather_sends, gather_receives, window, WINDOWS)
        for window in range(WINDOWS)
    ]
    width, stored = own.shape[1], []

    def add(block, rows):
        copy = pltpu.make_async_copy(rows, branch_out.at[block], out_sems.at[len(stored)])
        copy.start()
        for start in range(0, width, 512):
            columns = pl.ds(start, 512)
            product = dot_tn(mixed_ref[block], rows[:, columns])
            total[:, columns] = total[:, columns] + product if stored else product
        stored.append(copy)

    windows = scatter_head(term, scatter)
    for copy in later:
        copy.wait()
    scatter_tail(windows, use, lambda window: gathers[window].begin())
    add(me, own)
    for gather in gathers:
        gather.expect(2, 3)
    add(other, branch.at[other])
    for gather in gathers:
        gather.relay()
    for block in (near, below):
        add(block, branch.at[block])
    for gather in gathers:
        gather.expect(8, 9, 10, 11)
    add(near + flip, branch.at[near + flip])
    for gather in gathers:
        gather.relay_far()
    add(below + flip, branch.at[below + flip])
    add(far, branch.at[far])
    for gather in gathers:
        gather.expect(12, 13)
    add(far + flip, branch.at[far + flip])
    out_grad_ref[...] = total[...].astype(HALF)
    for copy in stored:
        copy.wait()
    for gather in gathers:
        gather.drain()
    for window in windows:
        window.drain()


def middle_back(grads, weight, hidden, outer, mask, gain, mixed):
    peers, own, inner = grads.shape
    width = weight.shape[0]
    return pl.pallas_call(
        middle_back_kernel,
        in_specs=[in_hbm()] * 4 + [vmem()] * 2 + [in_hbm()],
        out_specs=[vmem(), vmem(), in_hbm(), vmem()],
        out_shape=[
            jax.ShapeDtypeStruct((own, width), FULL),
            jax.ShapeDtypeStruct((1, width), FULL),
            jax.ShapeDtypeStruct((peers, own, width), HALF),
            jax.ShapeDtypeStruct((mixed.shape[2], width), HALF),
        ],
        scratch_shapes=scatter_scratch(own, width)
        + [pltpu.VMEM((own, width), HALF)]
        + gather_scratch(WINDOWS)[1:]
        + stage_scratch(weight, hidden, outer, mixed)
        + block_scratch(2, grads)
        + [
            pltpu.VMEM((peers, own, width), HALF),
            pltpu.VMEM((mixed.shape[2], width), FULL),
            pltpu.SemaphoreType.DMA((peers,)),
        ],
        compiler_params=pltpu.CompilerParams(
            collective_id=3, has_side_effects=True, vmem_limit_bytes=LARGE_BYTES
        ),
        cost_estimate=cost(2 * peers * own * inner * width, 4 * peers * own * width),
    )(grads, weight, hidden, outer, mask, gain, mixed)


class PlaneReturn:
    def __init__(self, cuts, source, targets, keeps, sends, receives):
        self.cuts, self.source, self.targets = cuts, source, targets
        self.keeps, self.sends, self.receives = keeps, sends, receives
        self.peers, self.me = lax.axis_size("seq"), lax.axis_index("seq")

    def part(self, number, peer):
        start, size = self.cuts[number]
        return self.source.at[peer, :, pl.ds(start, size)]

    def place(self, number, peer):
        size = self.cuts[number][1]
        return self.targets[number].at[:, pl.ds(pl.multiple_of(peer * size, LANES), size)]

    def sent(self, source, target, number, turn, peer):
        at = (number, turn)
        return to_peer(source, target, self.sends.at[at], self.receives.at[at], peer)

    def copy(self, number, turn):
        peer = lax.rem(self.me + turn, self.peers)
        return self.sent(
            self.part(number, peer), self.place(number, self.me), number, turn, peer
        )

    def landed(self, number, turn):
        peer = lax.rem(self.me + self.peers - turn, self.peers)
        target = self.place(number, peer)
        return self.sent(target, target, number, turn, peer)

    def kept(self, number):
        return pltpu.make_async_copy(
            self.part(number, self.me), self.place(number, self.me), self.keeps.at[number]
        )

    def begin(self, turn):
        for number in range(len(self.cuts)):
            if turn > 0:
                self.copy(number, turn).start()
            else:
                self.kept(number).start()

    def finish(self):
        for number in range(len(self.cuts)):
            for turn in range(1, self.peers):
                self.landed(number, turn).wait_recv()
                self.copy(number, turn).wait_send()
            self.kept(number).wait()


def last_kernel(
    cuts, line_cuts, grads_hbm, weight_hbm, tokens_hbm, hidden_grad_hbm, gain_ref, second_grad_ref,
    group_grad_ref, inner_hbm, down_hbm, hidden_hbm, mask_ref, summed_ref, terms_ref,
    *refs,
):
    count, line_count = len(cuts), len(line_cuts)
    input_ref, output_ref, gains_ref = refs[:3]
    returned, refs = refs[3 : 3 + count], refs[3 + count :]
    line_returned, scratch = refs[:line_count], refs[line_count:]
    scatter, result = scratch[:7], scratch[:1] + scratch[7:13]
    (
        sums, parts, across, totals, first_grad, keep, part_sends, part_receives,
        group_keep, group_sends, group_receives,
    ) = scratch[13:24]
    peers, groups = lax.axis_size("seq"), lax.axis_size("fsdp")
    me = lax.axis_index("seq")
    grads, grad_sems = scratch[36:38]
    inner_ref = scratch[38]
    weight_ref, down_ref, hidden_ref, tokens_ref, hidden_grad_ref, stage_sems = scratch[39:]
    blocks = Blocks(grads_hbm, grads, grad_sems)
    weight_copy, inner_copy, down_copy, *later = staged(
        (weight_hbm, inner_hbm, down_hbm, hidden_hbm, tokens_hbm, hidden_grad_hbm),
        (weight_ref, inner_ref, down_ref, hidden_ref, tokens_ref, hidden_grad_ref),
        stage_sems,
    )
    blocks.begin()
    greet_plane(True)
    back = PlaneReturn(cuts, summed_ref, returned, *scratch[24:27])
    line_back = PlaneReturn(line_cuts, scratch[32], line_returned, *scratch[27:30])
    line = LineSum(terms_ref, *scratch[30:36])

    def term(block):
        return blocks.take(lambda value: dot_nt(value, weight_ref[...]).astype(HALF))

    def result_term(block):
        return dot_nn(inner_ref[block], down_ref[...]).astype(HALF)

    gain = gain_ref[...]
    first_grad[...] = jnp.zeros_like(first_grad)

    def use(start, total):
        rows = pl.ds(start, CHUNK)
        grad = regroup(total, groups, peers)
        normed, scale = normalised(tokens_ref[rows].astype(FULL))
        first_grad[...] += jnp.sum(grad * normed, axis=0, keepdims=True)
        input_ref[rows] = (
            hidden_grad_ref[rows] + normalised_back(grad * gain, normed, scale)
        ).astype(HALF)

    def use_result(start, total):
        rows = pl.ds(start, CHUNK)
        output_ref[rows] = ((hidden_ref[rows] + total) * mask_ref[rows]).astype(HALF)

    line.begin()
    weight_copy.wait()
    every, early, late = range(peers), range(peers // 2), range(peers // 2, peers)
    windows = scatter_head(term, scatter, (), True)
    windows[0].relay()
    line.loaded()
    line.hand_on(0, 1, every)
    line.load_next()
    windows[1].relay()
    inner_copy.wait()
    down_copy.wait()
    result_windows = scatter_head(result_term, result, windows, True)
    for turn in every:
        back.begin(turn)
    result_windows[0].relay()
    line.hand_on(0, 2, every)
    for copy in later:
        copy.wait()
    scatter_tail(windows, use)
    line.loaded_next()
    line.hand_on(1, 1, early)
    result_windows[1].relay()
    tile = LANES * 2
    for peer in range(peers):
        for row in range(tile // LANES):
            at = peer * tile + row * LANES
            sums[peer, row : row + 1] = first_grad[:, at : at + LANES]
            sums[peer, 2 + row : 3 + row] = second_grad_ref[:, at : at + LANES]
        sums[peer, 4:8] = jnp.zeros((4, LANES), FULL)

    def copy(turn):
        peer = lax.rem(me + turn, peers)
        return to_peer(
            sums.at[peer], parts.at[turn], part_sends.at[turn], part_receives.at[turn], peer
        )

    kept = pltpu.make_async_copy(sums.at[me], parts.at[0], keep)
    kept.start()
    for turn in range(1, peers):
        copy(turn).start()
    line.hand_on(1, 1, late)
    scatter_tail(result_windows, use_result)
    kept.wait()
    for turn in range(1, peers):
        copy(turn).wait_recv()
        copy(turn).wait_send()
    total = parts[0]
    for turn in range(1, peers):
        total += parts[turn]
    across[0:8] = total
    for row in range(4):
        across[8 + row : 9 + row] = group_grad_ref[:, row * LANES : (row + 1) * LANES]
    across[12:16] = jnp.zeros((4, LANES), FULL)
    begin, finish = all_to_each(
        across, totals, "fsdp", groups, group_keep, group_sends, group_receives
    )
    begin()
    line.finish(line_back.begin)
    back.finish()
    line_back.finish()
    line.drain()
    for window in windows:
        window.drain(4)
    for window in result_windows:
        window.drain()
    finish()
    summed = totals[0]
    for turn in range(1, groups):
        summed += totals[turn]
    gains_ref[...] = summed


def last_rows(
    grads, weight, tokens, hidden_grad, gain, second_grad, group_grad, inner, down, hidden, mask,
    summed, sizes, terms, line_sizes,
):
    peers, own, size = grads.shape
    groups = lax.axis_size("fsdp")
    width = weight.shape[0]
    slab = summed.shape[1]

    def cuts_of(sizes):
        return tuple((sum(sizes[:number]), sizes[number]) for number in range(len(sizes)))

    return pl.pallas_call(
        partial(last_kernel, cuts_of(sizes), cuts_of(line_sizes)),
        in_specs=[in_hbm()] * 4 + [vmem()] * 3 + [in_hbm()] * 3 + [vmem()] + [in_hbm()] * 2,
        out_specs=[vmem()] * 3 + [in_hbm()] * len(sizes + line_sizes),
        out_shape=[
            jax.ShapeDtypeStruct((own, width), HALF),
            jax.ShapeDtypeStruct((own, width), HALF),
            jax.ShapeDtypeStruct((16, LANES), FULL),
        ]
        + [jax.ShapeDtypeStruct((slab, peers * part), HALF) for part in sizes + line_sizes],
        scratch_shapes=scatter_scratch(own, width)
        + scatter_scratch(own, width)[1:]
        + [
            pltpu.VMEM((peers, 8, LANES), FULL),
            pltpu.VMEM((peers, 8, LANES), FULL),
            pltpu.VMEM((16, LANES), FULL),
            pltpu.VMEM((groups, 16, LANES), FULL),
            pltpu.VMEM((1, width), FULL),
            pltpu.SemaphoreType.DMA,
            pltpu.SemaphoreType.DMA((peers,)),
            pltpu.SemaphoreType.DMA((peers,)),
            pltpu.SemaphoreType.DMA,
            pltpu.SemaphoreType.DMA((groups,)),
            pltpu.SemaphoreType.DMA((groups,)),
        ]
        + swap_scratch(len(sizes), peers)
        + swap_scratch(len(line_sizes), peers)
        + line_scratch(groups, peers, slab, terms.shape[3])
        + block_scratch(2, grads)
        + [pltpu.VMEM(inner.shape, HALF)]
        + stage_scratch(weight, down, hidden, tokens, hidden_grad, inner)[:5]
        + [pltpu.SemaphoreType.DMA((6,))],
        compiler_params=pltpu.CompilerParams(
            collective_id=5, has_side_effects=True, vmem_limit_bytes=LARGE_BYTES
        ),
        cost_estimate=cost(
            2 * peers * own * (size + inner.shape[2]) * width, 5 * peers * own * width
        ),
    )(
        grads, weight, tokens, hidden_grad, gain, second_grad, group_grad, inner, down, hidden, mask,
        summed, terms,
    )


def outputs_kernel(count, *refs):
    sources, gains_ref, refs = refs[:count], refs[count], refs[count + 1 :]
    targets, (first_ref, second_ref, group_ref), refs = refs[:count], refs[count : count + 3], refs[count + 3 :]
    taken, given, loads, stores = refs[:count], refs[count : 2 * count], refs[-2], refs[-1]

    def load(number):
        return pltpu.make_async_copy(sources[number], taken[number], loads.at[number])

    def store(number):
        return pltpu.make_async_copy(given[number], targets[number], stores.at[number])

    for number in range(count):
        load(number).start()
    group, half = lax.axis_index("fsdp"), LANES // 2
    row = group // 2
    for start, target in ((0, first_ref), (2, second_ref)):
        both = gains_ref[pl.ds(start + row, 1)]
        turned = pltpu.roll(both, half, 1)
        target[...] = jnp.where(lax.rem(group, 2) == 0, both, turned)[:, :half]
    group_ref[...] = gains_ref[pl.ds(8 + group, 1)]
    for number in range(count):
        load(number).wait()
        given[number][...] = taken[number][...].astype(given[number].dtype)
        store(number).start()
    for number in range(count):
        store(number).wait()


def outputs(grads, rows, gains):
    arrays = [*grads, *rows]
    count = len(arrays)
    small = (LANES // 2, LANES // 2, LANES)
    shapes = [jax.ShapeDtypeStruct(array.shape, FULL) for array in grads] + [
        jax.ShapeDtypeStruct(array.shape, HALF) for array in rows
    ]
    return pl.pallas_call(
        partial(outputs_kernel, count),
        in_specs=[in_hbm()] * count + [vmem()],
        out_specs=[in_hbm()] * count + [vmem()] * 3,
        out_shape=shapes + [jax.ShapeDtypeStruct((1, size), FULL) for size in small],
        scratch_shapes=[pltpu.VMEM(array.shape, array.dtype) for array in arrays]
        + [pltpu.VMEM(shape.shape, shape.dtype) for shape in shapes]
        + [pltpu.SemaphoreType.DMA((count,))] * 2,
        compiler_params=pltpu.CompilerParams(vmem_limit_bytes=VMEM_BYTES),
    )(*arrays, gains)


def head_body(
    tokens,
    cotangent,
    lengths,
    block_order,
    log_decay,
    first_gain,
    query_weight,
    key_weight,
    value_weight,
    swish_weight,
    output_weight,
    group_gain,
    second_gain,
    feed_gate,
    feed_up,
    feed_down,
):
    peers, groups = lax.axis_size("seq"), lax.axis_size("fsdp")
    group = lax.axis_index("fsdp")
    batches, rows, width = tokens.shape
    own = batches * rows
    heads = log_decay.shape[0]
    key_size = query_weight.shape[1] // heads
    value_size = value_weight.shape[1] // heads
    part = feed_gate.shape[1] // peers
    slab = query_weight.shape[0]
    total = 2 * key_size + 2 * value_size

    def over_groups(local):
        return lax.all_gather(local, "fsdp", axis=0, tiled=True)

    def sum_groups(whole):
        return lax.psum_scatter(whole.astype(HALF), "fsdp", scatter_dimension=0, tiled=True)

    def gathered(cut):
        return over_groups(cut[None]).reshape(width, cut.shape[2])

    gains = jnp.concatenate(
        [
            group_gain.astype(FULL)[None],
            jnp.concatenate([first_gain, second_gain]).astype(FULL)[None],
            jnp.zeros((6, LANES), FULL),
        ],
        axis=0,
    )
    first_cut, rates, gains = first_swap(
        query_weight, key_weight, value_weight, swish_weight, log_decay, gains
    )
    out_weight = over_groups(output_weight)
    order = lax.dynamic_slice_in_dim(block_order, group * batches, batches, 0)
    numbers = jnp.arange(peers, dtype=jnp.int32)
    place = jnp.sum(
        numbers[None, None, :] * (order[:, None, :] == numbers[None, :, None]).astype(jnp.int32),
        axis=2,
    )
    live = lax.dynamic_slice_in_dim(lengths, group * batches, batches, 0)

    token_rows = tokens.reshape(own, width)
    outer_rows = cotangent.reshape(own, width)
    (
        entered, result_low, feed_cut, first_weight,
        mask, gain_one, gain_two, gain_group, decay, columns,
    ) = gather_inputs(
        lengths, block_order, token_rows, outer_rows, gains, rates, feed_gate, feed_up, first_cut,
        value_size,
    )
    first_weight = first_weight.reshape(width, total)
    entered, out_weight = lax.optimization_barrier((entered, out_weight))
    feed_weight = gathered(feed_cut)

    *saved, mixed = retention(
        entered.reshape(peers, batches, rows, width),
        first_weight,
        place,
        live,
        decay,
        columns,
        gain_group,
        key_size,
    )
    entered = entered.reshape(peers * own, width)
    mixed, feed_down = lax.optimization_barrier((mixed, feed_down))
    down_weight = over_groups(feed_down)
    mixed = mixed.reshape(peers * own, value_size)
    hidden, second = middle(mixed.reshape(peers, own, value_size), out_weight, token_rows, gain_two)
    second = second.reshape(peers * own, width)
    result_low = result_low.reshape(peers * own, width)
    inner_low, up_slope, gate_slope, down_term = feed(second, feed_weight, result_low)
    down_grad = sum_groups(down_term)
    both_grad = feed_back(result_low, down_weight, up_slope, gate_slope)
    both_term, both_grad = lax.optimization_barrier(
        (dot_tn(second, both_grad).astype(HALF), both_grad)
    )
    both_weight_grad = sum_groups(both_term).reshape(peers, slab, 2 * part)
    hidden_grad, second_gain_grad, branch_low, out_term = middle_back(
        both_grad.reshape(peers, own, 2 * part),
        feed_weight,
        hidden,
        outer_rows,
        mask,
        gain_two,
        mixed.reshape(peers, own, value_size),
    )
    branch_low, down_grad = lax.optimization_barrier((branch_low, down_grad))
    out_grad = sum_groups(out_term)
    group_gain_grad, projected_grad = retention_back(
        branch_low.reshape(peers, batches, rows, width),
        out_weight,
        place,
        live,
        decay,
        columns,
        gain_group,
        saved,
    )
    flat_grad = projected_grad.reshape(peers * own, total)
    first_term = dot_tn(entered, flat_grad).astype(HALF)
    (
        input_rows, output_rows, small_grads,
        gate_back, up_back, query_back, key_back, value_back, swish_back,
    ) = last_rows(
        projected_grad.reshape(peers, own, total),
        first_weight,
        token_rows,
        hidden_grad,
        gain_one,
        second_gain_grad,
        group_gain_grad,
        inner_low.reshape(peers, own, part),
        down_weight,
        hidden,
        mask,
        both_weight_grad,
        (part, part),
        first_term.reshape(groups, peers, slab, total),
        (key_size, key_size, value_size, value_size),
    )
    (
        query_back, key_back, value_back, swish_back, out_back, gate_back, up_back, down_back,
        output_rows, input_rows, first_grad, second_grad, group_grad,
    ) = outputs(
        (query_back, key_back, value_back, swish_back, out_grad, gate_back, up_back, down_grad),
        (output_rows, input_rows),
        small_grads,
    )
    return (
        output_rows.reshape(batches, rows, width),
        input_rows.reshape(batches, rows, width),
        first_grad.reshape(slab),
        query_back,
        key_back,
        value_back,
        swish_back,
        out_back,
        group_grad.reshape(LANES),
        second_grad.reshape(slab),
        gate_back,
        up_back,
        down_back,
    )


def body(*arrays):
    peers, groups = lax.axis_size("seq"), lax.axis_size("fsdp")
    fits = peers == 8 and groups == 4 and arrays[4].shape[0] == peers and arrays[0].shape[0] == 2
    if fits:
        return head_body(*arrays)
    return general_body(*arrays)


def solution(mesh):
    placed = (
        P("fsdp", "seq", None),
        P("fsdp", "seq", None),
        P(),
        P(),
        P(None, "seq"),
        P(("seq", "fsdp")),
        P(("seq", "fsdp"), None),
        P(("seq", "fsdp"), None),
        P(("seq", "fsdp"), None),
        P(("seq", "fsdp"), None),
        P(("seq", "fsdp"), None),
        P(("seq", "fsdp")),
        P(("seq", "fsdp")),
        P(("seq", "fsdp"), None),
        P(("seq", "fsdp"), None),
        P(("seq", "fsdp"), None),
    )
    return jax.shard_map(
        body,
        mesh=mesh,
        in_specs=placed,
        out_specs=(
            P("fsdp", "seq", None),
            P("fsdp", "seq", None),
            P(("seq", "fsdp")),
            P(("seq", "fsdp"), None),
            P(("seq", "fsdp"), None),
            P(("seq", "fsdp"), None),
            P(("seq", "fsdp"), None),
            P(("seq", "fsdp"), None),
            P(("seq", "fsdp")),
            P(("seq", "fsdp")),
            P(("seq", "fsdp"), None),
            P(("seq", "fsdp"), None),
            P(("seq", "fsdp"), None),
        ),
        check_vma=False,
    )
```

```python
from functools import partial, reduce

import jax
import jax.numpy as jnp
from jax import lax
from jax.experimental import pallas as pl
from jax.experimental.pallas import tpu as pltpu
from jax.sharding import PartitionSpec as P

EPSILON = 1e-05
HIGHEST = lax.Precision.HIGHEST


def carried_in(value, axis, combine, identity, reverse):
    peers, index = (lax.axis_size(axis), lax.axis_index(axis))
    everything = jax.tree.map(
        lambda part, kind: lax.all_gather(part.astype(kind), axis),
        value,
        (jnp.bfloat16, jnp.bfloat16),
    )
    start = jax.tree.map(
        lambda part, zero: jnp.broadcast_to(jnp.asarray(zero, part.dtype), part.shape),
        value,
        identity,
    )

    def turn(k, before):
        at = peers - 1 - k if reverse else k
        reached = at > index if reverse else at < index
        new = combine(
            before, jax.tree.map(lambda part, own: part[at].astype(own.dtype), everything, value)
        )
        return jax.tree.map(lambda a, b: jnp.where(reached, a, b), new, before)

    return lax.fori_loop(0, peers, turn, start)


def norm_rows(values, gain):
    average = jnp.mean(values, axis=-1, keepdims=True)
    centered = values - average
    variance = jnp.mean(centered * centered, axis=-1, keepdims=True)
    return centered * lax.rsqrt(variance + EPSILON) * gain


def gated_swish(swish_in, grouped):
    return jax.nn.silu(swish_in) * grouped


def gated_gelu(gate_in, upward):
    return jax.nn.gelu(gate_in) * upward


def chain_states(earlier, later):
    return (earlier[0] * later[0], later[0][:, None, None] * earlier[1] + later[1])


def transposed(left_rows, weight):
    return jnp.einsum("ie,fe->if", left_rows, weight, preferred_element_type=jnp.float32)


def plain_dot(left_rows, weight):
    return jnp.dot(left_rows, weight, preferred_element_type=jnp.float32)


def outer_term(left_rows, right_rows):
    return jnp.einsum("ni,no->io", left_rows, right_rows, preferred_element_type=jnp.float32)


def spread_sum(matrix_pairs, vectors):
    terms = tuple((outer_term(left_rows, right_rows) for left_rows, right_rows in matrix_pairs))
    pieces = lax.psum_scatter(
        terms + tuple(vectors), ("seq", "fsdp"), scatter_dimension=0, tiled=True
    )
    return list(pieces)


def join_terms(collected):
    matrix_pairs = []
    for member in range(len(collected[0][0])):
        lefts = jnp.concatenate([entry[0][member][0] for entry in collected], axis=0)
        rights = jnp.concatenate([entry[0][member][1] for entry in collected], axis=0)
        matrix_pairs.append((lefts, rights))
    vectors = [
        reduce(jnp.add, [entry[1][member] for entry in collected])
        for member in range(len(collected[0][1]))
    ]
    return (matrix_pairs, vectors)


def layer_step(gathered, inputs, cot_rows, live_mask, log_rates):
    (
        first_gain,
        query_weight,
        key_weight,
        value_weight,
        swish_weight,
        output_weight,
        group_gain,
        second_gain,
        feed_gate,
        feed_up,
        feed_down,
    ) = gathered
    floats = jnp.float32
    halves = jnp.bfloat16
    head_count = log_rates.shape[0]
    token_rows = inputs.shape[0]
    key_size = query_weight.shape[1] // head_count
    value_size = value_weight.shape[1] // head_count
    start_values = inputs.astype(floats)
    normed_one, pull_one = jax.vjp(norm_rows, start_values, first_gain.astype(floats))
    normed = normed_one.astype(halves)
    queries = plain_dot(normed, query_weight).astype(halves)
    keys_in = plain_dot(normed, key_weight).astype(halves) * live_mask[:, None].astype(halves)
    values_in = plain_dot(normed, value_weight).astype(halves)
    swish_in = plain_dot(normed, swish_weight)
    queries3 = queries.reshape(token_rows, head_count, key_size)
    keys3 = keys_in.reshape(token_rows, head_count, key_size)
    values3 = values_in.reshape(token_rows, head_count, value_size)
    cumulative = jnp.cumsum(log_rates, axis=1)
    slot_index = jnp.arange(token_rows)
    lower_mask = slot_index[:, None] >= slot_index[None, :]
    spread = cumulative[:, :, None] - cumulative[:, None, :]
    decay_matrix = jnp.where(lower_mask, jnp.exp(jnp.where(lower_mask, spread, 0.0)), 0.0)
    block_decay = jnp.exp(cumulative[:, -1])
    end_weight = jnp.exp(cumulative[:, -1:] - cumulative).T[:, :, None]
    entry_decay = jnp.exp(cumulative).T[:, :, None]
    query_wide = queries3.astype(floats)
    key_wide = keys3.astype(floats)
    value_wide = values3.astype(floats)
    state_term = jnp.einsum("jhd,jhe->hde", key_wide * end_weight, value_wide, precision=HIGHEST)
    state_identity = (jnp.ones_like(block_decay), jnp.zeros_like(state_term))
    _, start_state = carried_in(
        (block_decay, state_term), "seq", chain_states, state_identity, False
    )
    scores = jnp.einsum("ihd,jhd->hij", queries3, keys3, preferred_element_type=floats)
    weights = (scores * decay_matrix).astype(halves)
    intra_term = jnp.einsum("hij,jhe->ihe", weights, values3, preferred_element_type=floats)
    carried = entry_decay * jnp.einsum("ihd,hde->ihe", query_wide, start_state, precision=HIGHEST)
    retained = intra_term + carried
    grouped, pull_group = jax.vjp(
        norm_rows, retained, group_gain.astype(floats).reshape(head_count, value_size)
    )
    grouped_flat = grouped.reshape(token_rows, head_count * value_size)
    mixed_float, pull_mixed = jax.vjp(gated_swish, swish_in, grouped_flat)
    mixed_low = mixed_float.astype(halves)
    hidden = start_values + plain_dot(mixed_low, output_weight)
    normed_two, pull_two = jax.vjp(norm_rows, hidden, second_gain.astype(floats))
    second = normed_two.astype(halves)
    gate_two = plain_dot(second, feed_gate)
    upward = plain_dot(second, feed_up)
    inner_float, pull_inner = jax.vjp(gated_gelu, gate_two, upward)
    inner_low = inner_float.astype(halves)
    result = plain_dot(inner_low, feed_down)
    output_rows = ((hidden + result) * live_mask[:, None]).astype(halves)
    outer_grad = cot_rows.astype(floats) * live_mask[:, None]
    result_low = outer_grad.astype(halves)
    inner_grad = transposed(result_low, feed_down)
    gate_two_grad, upward_grad = pull_inner(inner_grad)
    gate_two_low = gate_two_grad.astype(halves)
    upward_low = upward_grad.astype(halves)
    second_grad = transposed(gate_two_low, feed_gate) + transposed(upward_low, feed_up)
    hidden_part, second_gain_grad = pull_two(second_grad)
    hidden_grad = outer_grad + hidden_part
    branch_low = hidden_grad.astype(halves)
    mixed_grad = transposed(branch_low, output_weight)
    swish_grad, grouped_grad = pull_mixed(mixed_grad)
    swish_low = swish_grad.astype(halves)
    retained_grad, group_gain_grad = pull_group(
        grouped_grad.reshape(token_rows, head_count, value_size)
    )
    retained_low = retained_grad.astype(halves)
    weights_grad = jnp.einsum("ihe,jhe->hij", retained_low, values3, preferred_element_type=floats)
    scores_low = (weights_grad * decay_matrix).astype(halves)
    query_intra = jnp.einsum("hij,jhd->ihd", scores_low, keys3, preferred_element_type=floats)
    key_intra = jnp.einsum("hij,ihd->jhd", scores_low, queries3, preferred_element_type=floats)
    value_intra = jnp.einsum("hij,ihe->jhe", weights, retained_low, preferred_element_type=floats)
    retained_wide = retained_low.astype(floats)
    query_carried = entry_decay * jnp.einsum(
        "ihe,hde->ihd", retained_wide, start_state, precision=HIGHEST
    )
    local_grad = jnp.einsum(
        "ihd,ihe->hde", query_wide * entry_decay, retained_wide, precision=HIGHEST
    )
    _, end_grad = carried_in((block_decay, local_grad), "seq", chain_states, state_identity, True)
    key_state = end_weight * jnp.einsum("jhe,hde->jhd", value_wide, end_grad, precision=HIGHEST)
    value_state = end_weight * jnp.einsum("jhd,hde->jhe", key_wide, end_grad, precision=HIGHEST)
    query_low = (
        (query_intra + query_carried).astype(halves).reshape(token_rows, head_count * key_size)
    )
    key_low = (
        ((key_intra + key_state) * live_mask[:, None, None])
        .astype(halves)
        .reshape(token_rows, head_count * key_size)
    )
    value_low = (
        (value_intra + value_state).astype(halves).reshape(token_rows, head_count * value_size)
    )
    normed_grad = (
        transposed(query_low, query_weight)
        + transposed(key_low, key_weight)
        + transposed(value_low, value_weight)
        + transposed(swish_low, swish_weight)
    )
    input_part, first_gain_grad = pull_one(normed_grad)
    grad_rows = (hidden_grad + input_part).astype(halves)
    matrix_pairs = [
        (normed, query_low),
        (normed, key_low),
        (normed, value_low),
        (normed, swish_low),
        (mixed_low, branch_low),
        (second, gate_two_low),
        (second, upward_low),
        (inner_low, result_low),
    ]
    vectors = [first_gain_grad, group_gain_grad.reshape(-1), second_gain_grad]
    return (output_rows, grad_rows, matrix_pairs, vectors)


def general_body(
    tokens,
    cotangent,
    lengths,
    block_order,
    log_decay,
    first_gain,
    query_weight,
    key_weight,
    value_weight,
    swish_weight,
    output_weight,
    group_gain,
    second_gain,
    feed_gate,
    feed_up,
    feed_down,
):
    batches = tokens.shape[0]
    block_rows = tokens.shape[1]
    selected_locations = lax.axis_size("seq")
    position = lax.axis_index("seq")
    group_index = lax.axis_index("fsdp")
    place_numbers = jnp.arange(selected_locations, dtype=jnp.int32)
    arrived_tokens, arrived_cotangent = (
        lax.all_gather(tokens, "seq", axis=1, tiled=True),
        lax.all_gather(cotangent, "seq", axis=1, tiled=True),
    )
    gathered = (
        lax.all_gather(first_gain, ("seq", "fsdp"), axis=0, tiled=True),
        lax.all_gather(query_weight, ("seq", "fsdp"), axis=0, tiled=True),
        lax.all_gather(key_weight, ("seq", "fsdp"), axis=0, tiled=True),
        lax.all_gather(value_weight, ("seq", "fsdp"), axis=0, tiled=True),
        lax.all_gather(swish_weight, ("seq", "fsdp"), axis=0, tiled=True),
        lax.all_gather(output_weight, ("seq", "fsdp"), axis=0, tiled=True),
        lax.all_gather(group_gain, ("seq", "fsdp"), axis=0, tiled=True),
        lax.all_gather(second_gain, ("seq", "fsdp"), axis=0, tiled=True),
        lax.all_gather(feed_gate, ("seq", "fsdp"), axis=0, tiled=True),
        lax.all_gather(feed_up, ("seq", "fsdp"), axis=0, tiled=True),
        lax.all_gather(feed_down, ("seq", "fsdp"), axis=0, tiled=True),
    )
    outputs = []
    input_grads = []
    collected = []
    order_rows = []
    for batch_number in range(batches):
        sequence = group_index * batches + batch_number
        order_row = lax.dynamic_index_in_dim(block_order, sequence, 0, keepdims=False)
        order_rows.append(order_row)
        source = jnp.sum(place_numbers * (order_row == position).astype(jnp.int32))
        token_rows = lax.dynamic_slice_in_dim(
            arrived_tokens[batch_number], source * block_rows, block_rows, 0
        )
        cot_rows = lax.dynamic_slice_in_dim(
            arrived_cotangent[batch_number], source * block_rows, block_rows, 0
        )
        live_length = lax.dynamic_index_in_dim(lengths, sequence, 0, keepdims=False)
        location_number = position * block_rows + jnp.arange(block_rows, dtype=jnp.int32)
        live_mask = (location_number < live_length).astype(jnp.float32)
        output_rows, grad_rows, matrix_pairs, vectors = layer_step(
            gathered, token_rows, cot_rows, live_mask, log_decay
        )
        outputs.append(output_rows)
        input_grads.append(grad_rows)
        collected.append((matrix_pairs, vectors))
    joined_pairs, joined_vectors = join_terms(collected)
    shards = spread_sum(joined_pairs, joined_vectors)
    every_output, every_grad = (
        lax.all_gather(jnp.stack(outputs), "seq", axis=1, tiled=True),
        lax.all_gather(jnp.stack(input_grads), "seq", axis=1, tiled=True),
    )
    returned = []
    returned_grads = []
    for batch_number in range(batches):
        target = lax.dynamic_index_in_dim(order_rows[batch_number], position, 0, keepdims=False)
        returned.append(
            lax.dynamic_slice_in_dim(every_output[batch_number], target * block_rows, block_rows, 0)
        )
        returned_grads.append(
            lax.dynamic_slice_in_dim(every_grad[batch_number], target * block_rows, block_rows, 0)
        )
    return (
        jnp.stack(returned),
        jnp.stack(returned_grads),
        shards[8],
        shards[0],
        shards[1],
        shards[2],
        shards[3],
        shards[4],
        shards[9],
        shards[10],
        shards[5],
        shards[6],
        shards[7],
    )


FULL = jnp.float32
HALF = jnp.bfloat16
MESH = pl.DeviceIdType.MESH
VMEM_BYTES = 56 * 1024 * 1024
LARGE_BYTES = 63 * 1024 * 1024
LANES = 128


def dot_nn(left, right):
    return jnp.dot(left, right, preferred_element_type=FULL)


def dot_nt(left, right):
    return lax.dot_general(left, right, (((1,), (1,)), ((), ())), preferred_element_type=FULL)


def dot_tn(left, right):
    return lax.dot_general(left, right, (((0,), (0,)), ((), ())), preferred_element_type=FULL)


def plane_peers():
    me = lax.axis_index("seq")
    core = lax.rem(me, 2)
    across = 2 - 4 * lax.rem(me // 2, 2)
    down = 4 - 8 * (me // 4)
    return me, me + 1 - 2 * core, me + across, me + down, me + across + down


def to_peer(source, target, send, receive, peer):
    return pltpu.make_async_remote_copy(
        src_ref=source,
        dst_ref=target,
        send_sem=send,
        recv_sem=receive,
        device_id={"seq": peer},
        device_id_type=MESH,
    )


def greet_neighbours():
    _, other, near, below, _ = plane_peers()
    barrier = pltpu.get_barrier_semaphore()
    for peer in (other, near, below):
        pl.semaphore_signal(barrier, inc=1, device_id={"seq": peer}, device_id_type=MESH)
    pl.semaphore_wait(barrier, 3)


GATHER_COPIES = 14


def gather_plan():
    me, other, near, below, far = plane_peers()
    flip = other - me
    return (
        (me, 0, near, near),
        (me, 1, below, below),
        (me, 0, other, other),
        (me, 1, other, other),
        (me, 1, near, near),
        (me, 0, below, below),
        (near, 0, below, far),
        (below, 1, near, far),
        (near, 0, other, near + flip),
        (below, 1, other, below + flip),
        (near, 1, other, near + flip),
        (below, 0, other, below + flip),
        (far, 0, other, far + flip),
        (far, 1, other, far + flip),
    )


class PlaneGather:
    def __init__(self, own, out, keeps, sends, receives, window=0, windows=1):
        self.own, self.out = own, out
        self.keep = None if keeps is None else keeps.at[window]
        self.sends, self.receives = sends, receives
        self.size = own.shape[0] // windows
        self.window, self.start = window, window * self.size
        self.half = self.size // 2

    def rows(self, which):
        return pl.ds(self.start + which * self.half, self.half)

    def kept(self):
        me = lax.axis_index("seq")
        rows = pl.ds(self.start, self.size)
        return pltpu.make_async_copy(self.own.at[rows], self.out.at[me, rows], self.keep)

    def sent(self, source, target, number, peer):
        at = (self.window, number)
        return to_peer(source, target, self.sends.at[at], self.receives.at[at], peer)

    def copy(self, number):
        block, which, peer, _ = gather_plan()[number]
        target = self.out.at[block, self.rows(which)]
        source = self.own.at[self.rows(which)] if number < 6 else target
        return self.sent(source, target, number, peer)

    def landed(self, number):
        _, which, peer, landing = gather_plan()[number]
        target = self.out.at[landing, self.rows(which)]
        self.sent(target, target, number, peer).wait_recv()

    def begin(self):
        if self.keep is not None:
            self.kept().start()
        for number in range(6):
            self.copy(number).start()

    def relay(self):
        for arrived, onward in ((0, (6, 8)), (1, (7, 9)), (4, (10,)), (5, (11,))):
            self.landed(arrived)
            for number in onward:
                self.copy(number).start()

    def relay_far(self):
        for arrived, onward in ((6, 12), (7, 13)):
            self.landed(arrived)
            self.copy(onward).start()

    def expect(self, *numbers):
        for number in numbers:
            self.landed(number)

    def drain(self):
        for number in range(GATHER_COPIES):
            self.copy(number).wait_send()
        if self.keep is not None:
            self.kept().wait()

    def finish(self):
        self.relay_far()
        self.expect(2, 3, 8, 9, 10, 11, 12, 13)
        self.drain()


def gather_scratch(windows=1):
    return [
        pltpu.SemaphoreType.DMA((windows,)),
        pltpu.SemaphoreType.DMA((windows, GATHER_COPIES)),
        pltpu.SemaphoreType.DMA((windows, GATHER_COPIES)),
    ]


SCATTER_COPIES = 10
WINDOWS = 2
CHUNK = 32


def by_chunks(rows, work):
    def step(number, carry):
        work(pl.ds(pl.multiple_of(number * CHUNK, CHUNK), CHUNK))
        return carry

    lax.fori_loop(0, rows // CHUNK, step, 0)


class PlaneScatter:
    def __init__(self, window, others, terms, cores, nears, belows, sends, receives):
        self.window = window
        self.others, self.terms, self.cores = others, terms, cores
        self.nears, self.belows = nears, belows
        self.sends, self.receives = sends, receives
        self.size = terms.shape[1] // WINDOWS
        self.half = self.size // 2
        self.start = window * self.size

    def copy(self, number):
        _, other, near, below, _ = plane_peers()
        whole = pl.ds(self.start, self.size)
        upper, lower = (pl.ds(self.start + at * self.half, self.half) for at in (0, 1))
        if number < 4:
            source, target, peer = (
                self.others.at[number, whole],
                self.cores.at[number, whole],
                other,
            )
        else:
            slot, rows, landing, place, peer = (
                (0, upper, self.nears, 0, near),
                (0, lower, self.belows, 0, below),
                (1, upper, self.nears, 1, near),
                (2, lower, self.belows, 1, below),
                (1, lower, self.nears, 2, near),
                (2, upper, self.belows, 2, below),
            )[number - 4]
            source, target = self.terms.at[slot, rows], landing.at[self.window, place]
        at = (self.window, number)
        return to_peer(source, target, self.sends.at[at], self.receives.at[at], peer)

    def fold(self, slot):
        def work(rows):
            here = pl.ds(pl.multiple_of(self.start + rows.start, CHUNK), CHUNK)
            self.terms[slot, here] = (
                self.terms[slot, here].astype(FULL) + self.cores[slot, here].astype(FULL)
            ).astype(HALF)

        by_chunks(self.size, work)

    def fold_half(self, slot, which, landed):
        def work(rows):
            at = self.start + which * self.half
            here = pl.ds(pl.multiple_of(at + rows.start, CHUNK), CHUNK)
            self.terms[slot, here] = (
                self.terms[slot, here].astype(FULL) + landed[self.window, 0, rows].astype(FULL)
            ).astype(HALF)

        by_chunks(self.half, work)

    def advance(self, slot):
        self.copy(slot).wait_recv()
        self.fold(slot)
        for number in ((4, 5), (6,), (7,), ())[slot]:
            self.copy(number).start()

    def relay(self):
        self.copy(4).wait_recv()
        self.fold_half(2, 0, self.nears)
        self.copy(9).start()
        self.copy(5).wait_recv()
        self.fold_half(1, 1, self.belows)
        self.copy(8).start()

    def finish(self):
        for number in (6, 7, 8, 9):
            self.copy(number).wait_recv()

    def drain(self, first=0):
        for number in range(first, SCATTER_COPIES):
            self.copy(number).wait_send()

    def total(self, at):
        upper = at < self.half
        rows = pl.ds(at if upper else at - self.half, CHUNK)
        near, below = (1, 2) if upper else (2, 1)
        return (
            self.terms[3, pl.ds(self.start + at, CHUNK)].astype(FULL)
            + self.nears[self.window, near, rows].astype(FULL)
            + self.belows[self.window, below, rows].astype(FULL)
        )


def block_order_of_plane():
    me, other, near, below, far = plane_peers()
    return [block + at for block in (far, near, below, me) for at in (other - me, 0)]


class Blocks:
    def __init__(self, source, target, sems):
        self.source, self.target, self.sems = source, target, sems
        self.blocks, self.taken = block_order_of_plane(), 0

    def load(self, number):
        slot = number % self.target.shape[0]
        return pltpu.make_async_copy(
            self.source.at[self.blocks[number]], self.target.at[slot], self.sems.at[slot]
        )

    def begin(self):
        for number in range(min(len(self.blocks), self.target.shape[0])):
            self.load(number).start()

    def take(self, work):
        number, slots = self.taken, self.target.shape[0]
        self.taken += 1
        self.load(number).wait()
        out = work(self.target[number % slots])
        if number + slots < len(self.blocks):
            self.load(number + slots).start()
        return out


def staged(sources, targets, sems):
    copies = [
        pltpu.make_async_copy(source, target, sems.at[number])
        for number, (source, target) in enumerate(zip(sources, targets))
    ]
    for copy in copies:
        copy.start()
    return copies


def stage_scratch(*arrays):
    return [pltpu.VMEM(array.shape, array.dtype) for array in arrays] + [
        pltpu.SemaphoreType.DMA((len(arrays),))
    ]


def block_scratch(count, array):
    return [
        pltpu.VMEM((count,) + array.shape[1:], array.dtype),
        pltpu.SemaphoreType.DMA((count,)),
    ]


def scatter_head(term, refs, earlier=(), relay_later=False):
    windows = [PlaneScatter(window, *refs) for window in range(WINDOWS)]
    others, terms = refs[:2]
    blocks = block_order_of_plane()

    def fill(slot):
        for window in earlier:
            window.copy(slot).wait_send()
        others[slot] = term(blocks[2 * slot])
        for window in windows:
            window.copy(slot).start()
        terms[slot] = term(blocks[2 * slot + 1])

    fill(0)
    for slot in range(4):
        if slot < 3:
            fill(slot + 1)
        windows[0].advance(slot)
    if not relay_later:
        windows[0].relay()
    for window in windows[1:]:
        for slot in range(4):
            window.advance(slot)
        if not relay_later:
            window.relay()
    return windows


def scatter_tail(windows, use, after=lambda window: None):
    for number, window in enumerate(windows):
        window.finish()
        for at in range(0, window.size, CHUNK):
            use(window.start + at, window.total(at))
        after(number)


def scatter_scratch(rows, width):
    half = rows // WINDOWS // 2
    return [
        pltpu.VMEM((4, rows, width), HALF),
        pltpu.VMEM((4, rows, width), HALF),
        pltpu.VMEM((4, rows, width), HALF),
        pltpu.VMEM((WINDOWS, 3, half, width), HALF),
        pltpu.VMEM((WINDOWS, 3, half, width), HALF),
        pltpu.SemaphoreType.DMA((WINDOWS, SCATTER_COPIES)),
        pltpu.SemaphoreType.DMA((WINDOWS, SCATTER_COPIES)),
    ]


def regroup(values, outer, inner):
    rows = values.shape[0]
    low_half = lax.broadcasted_iota(jnp.int32, (rows, LANES), 1) < LANES // 2

    def piece(p, q):
        at = (p * inner + q) // 2
        return values[:, at * LANES : (at + 1) * LANES]

    def turned(value):
        return pltpu.roll(value, LANES // 2, 1)

    groups = []
    for q in range(inner):
        for p in range(0, outer, 2):
            first, second = piece(p, q), piece(p + 1, q)
            if q % 2 == 0:
                groups.append(jnp.where(low_half, first, turned(second)))
            else:
                groups.append(jnp.where(low_half, turned(first), second))
    return jnp.concatenate(groups, axis=1)


def normalised(values):
    average = jnp.mean(values, axis=-1, keepdims=True)
    centered = values - average
    scale = lax.rsqrt(jnp.mean(centered * centered, axis=-1, keepdims=True) + EPSILON)
    return centered * scale, scale


def normalised_back(grad, normed, scale):
    average = jnp.mean(grad, axis=-1, keepdims=True)
    along = jnp.mean(grad * normed, axis=-1, keepdims=True)
    return (grad - average - normed * along) * scale


def vmem():
    return pl.BlockSpec(memory_space=pltpu.VMEM)


def in_hbm():
    return pl.BlockSpec(memory_space=pl.ANY)


def cost(flops, link_bytes):
    return pl.CostEstimate(flops=int(flops), bytes_accessed=int(link_bytes) * 16, transcendentals=0)


def linked(collective):
    return pltpu.CompilerParams(
        collective_id=collective, has_side_effects=True, vmem_limit_bytes=VMEM_BYTES
    )


class PlaneSwap:
    def __init__(self, weights, targets, keeps, sends, receives):
        self.weights, self.targets = weights, targets
        self.keeps, self.sends, self.receives = keeps, sends, receives
        self.peers = lax.axis_size("seq")

    def part(self, number, peer):
        weight, (target, start) = self.weights[number], self.targets[number]
        size = weight.shape[1] // self.peers
        return weight.at[:, pl.ds(pl.multiple_of(peer * size, LANES), size)]

    def place(self, number, peer):
        weight, (target, start) = self.weights[number], self.targets[number]
        return target.at[peer, :, pl.ds(start, weight.shape[1] // self.peers)]

    def copy(self, number, turn):
        me = lax.axis_index("seq")
        peer = lax.rem(me + turn, self.peers)
        return to_peer(
            self.part(number, peer),
            self.place(number, me),
            self.sends.at[number, turn],
            self.receives.at[number, turn],
            peer,
        )

    def landed(self, number, turn):
        me = lax.axis_index("seq")
        peer = lax.rem(me + self.peers - turn, self.peers)
        target = self.place(number, peer)
        to_peer(
            target, target, self.sends.at[number, turn], self.receives.at[number, turn], peer
        ).wait_recv()

    def kept(self, number):
        me = lax.axis_index("seq")
        return pltpu.make_async_copy(
            self.part(number, me), self.place(number, me), self.keeps.at[number]
        )

    def begin(self):
        for number in range(len(self.weights)):
            for turn in range(1, self.peers):
                self.copy(number, turn).start()
            self.kept(number).start()

    def finish(self):
        for number in range(len(self.weights)):
            for turn in range(1, self.peers):
                self.landed(number, turn)
                self.copy(number, turn).wait_send()
            self.kept(number).wait()


def swap_scratch(count, peers):
    return [
        pltpu.SemaphoreType.DMA((count,)),
        pltpu.SemaphoreType.DMA((count, peers)),
        pltpu.SemaphoreType.DMA((count, peers)),
    ]


def greet_plane(with_groups):
    me, group = lax.axis_index("seq"), lax.axis_index("fsdp")
    peers, groups = lax.axis_size("seq"), lax.axis_size("fsdp")
    barrier = pltpu.get_barrier_semaphore()
    count = peers - 1
    for turn in range(1, peers):
        peer = lax.rem(me + turn, peers)
        pl.semaphore_signal(barrier, inc=1, device_id={"seq": peer}, device_id_type=MESH)
    if with_groups:
        count += groups - 1
        for turn in range(1, groups):
            peer = lax.rem(group + turn, groups)
            pl.semaphore_signal(barrier, inc=1, device_id={"fsdp": peer}, device_id_type=MESH)
    pl.semaphore_wait(barrier, count)


def all_to_each(source, out, axis, size, keep, sends, receives):
    me = lax.axis_index(axis)

    def copy(turn, slot):
        peer = lax.rem(me + turn, size)
        return pltpu.make_async_remote_copy(
            src_ref=source,
            dst_ref=out.at[slot],
            send_sem=sends.at[turn],
            recv_sem=receives.at[turn],
            device_id={axis: peer},
            device_id_type=MESH,
        )

    def begin():
        pltpu.make_async_copy(source, out.at[me], keep).start()
        for turn in range(1, size):
            copy(turn, me).start()

    def finish():
        for turn in range(1, size):
            copy(turn, lax.rem(me + size - turn, size)).wait_recv()
            copy(turn, me).wait_send()
        pltpu.make_async_copy(source, out.at[me], keep).wait()

    return begin, finish


def first_swap_kernel(
    query_ref, key_ref, value_ref, swish_ref, rates_ref, gains_ref,
    cut_out, rates_out, gains_out,
    column, keeps, sends, receives, rate_keep, rate_sends, rate_receives,
    group_keep, group_sends, group_receives, gain_keep, gain_sends, gain_receives,
):
    peers, groups = lax.axis_size("seq"), lax.axis_size("fsdp")
    size, wide = query_ref.shape[1] // peers, value_ref.shape[1] // peers
    greet_plane(True)
    begin_groups, finish_groups = all_to_each(
        gains_ref, column, "fsdp", groups, group_keep, group_sends, group_receives
    )
    begin_rates, finish_rates = all_to_each(
        rates_ref, rates_out, "seq", peers, rate_keep, rate_sends, rate_receives
    )
    begin_gains, finish_gains = all_to_each(
        column, gains_out, "seq", peers, gain_keep, gain_sends, gain_receives
    )
    swap = PlaneSwap(
        (query_ref, key_ref, value_ref, swish_ref),
        ((cut_out, 0), (cut_out, size), (cut_out, 2 * size), (cut_out, 2 * size + wide)),
        keeps,
        sends,
        receives,
    )
    begin_groups()
    begin_rates()
    finish_groups()
    begin_gains()
    swap.begin()
    finish_rates()
    finish_gains()
    swap.finish()


def first_swap(query, key, value, swish, rates, gains):
    peers, groups = lax.axis_size("seq"), lax.axis_size("fsdp")
    slab = query.shape[0]
    total = sum(weight.shape[1] for weight in (query, key, value, swish)) // peers
    return pl.pallas_call(
        first_swap_kernel,
        in_specs=[in_hbm()] * 4 + [vmem()] * 2,
        out_specs=[in_hbm()] + [vmem()] * 2,
        out_shape=[
            jax.ShapeDtypeStruct((peers, slab, total), HALF),
            jax.ShapeDtypeStruct((peers,) + rates.shape, FULL),
            jax.ShapeDtypeStruct((peers, groups) + gains.shape, FULL),
        ],
        scratch_shapes=[pltpu.VMEM((groups,) + gains.shape, FULL)]
        + swap_scratch(4, peers)
        + [pltpu.SemaphoreType.DMA] + [pltpu.SemaphoreType.DMA((peers,))] * 2
        + [pltpu.SemaphoreType.DMA] + [pltpu.SemaphoreType.DMA((groups,))] * 2
        + [pltpu.SemaphoreType.DMA] + [pltpu.SemaphoreType.DMA((peers,))] * 2,
        compiler_params=linked(0),
        cost_estimate=cost(0, 2 * slab * peers * total),
    )(query, key, value, swish, rates, gains)


class LineGather:
    def __init__(self, own, out, keep, sends, receives):
        self.own, self.out = own, out
        self.keep, self.sends, self.receives = keep, sends, receives
        self.me, self.last = lax.axis_index("fsdp"), lax.axis_size("fsdp") - 1
        self.pieces = own.shape[0]

    def block(self, way, depth):
        return self.me - depth if way == 0 else self.me + depth

    def holds(self, way, depth):
        return self.me >= depth if way == 0 else self.me + depth <= self.last

    def passes(self, way):
        return self.me < self.last if way == 0 else self.me > 0

    def sent(self, source, way, depth, piece, block):
        at = (way, depth, piece)
        return pltpu.make_async_remote_copy(
            src_ref=source,
            dst_ref=self.out.at[block, piece],
            send_sem=self.sends.at[at],
            recv_sem=self.receives.at[at],
            device_id={"fsdp": self.me + 1 if way == 0 else self.me - 1},
            device_id_type=MESH,
        )

    def copy(self, way, depth, piece):
        block = self.block(way, depth)
        source = self.own.at[piece] if depth == 0 else self.out.at[block, piece]
        return self.sent(source, way, depth, piece, block)

    def landed(self, way, depth, piece):
        block = self.block(way, depth)
        self.sent(self.out.at[block, piece], way, depth - 1, piece, block).wait_recv()

    def kept(self):
        return pltpu.make_async_copy(self.own, self.out.at[self.me], self.keep)

    def begin(self):
        for piece in range(self.pieces):
            for way in (0, 1):

                @pl.when(self.passes(way))
                def _():
                    self.copy(way, 0, piece).start()

        self.kept().start()

    def hand_on(self, depth):
        for piece in range(self.pieces):
            for way in (0, 1):

                @pl.when(self.holds(way, depth) & self.passes(way))
                def _():
                    self.landed(way, depth, piece)
                    self.copy(way, depth, piece).start()

    def finish(self):
        for depth in range(1, self.last + 1):
            for piece in range(self.pieces):
                for way in (0, 1):

                    @pl.when(self.holds(way, depth) & jnp.logical_not(self.passes(way)))
                    def _():
                        self.landed(way, depth, piece)

        for depth in range(self.last):
            for piece in range(self.pieces):
                for way in (0, 1):

                    @pl.when(self.holds(way, depth) & self.passes(way))
                    def _():
                        self.copy(way, depth, piece).wait_send()

        self.kept().wait()


def unpack_gains(gains_ref, one_ref, two_ref, group_ref):
    peers, groups = gains_ref.shape[:2]
    low_half = lax.broadcasted_iota(jnp.int32, (1, LANES), 1) < LANES // 2
    for peer in range(peers):
        for at in range(0, groups, 2):
            left, right = gains_ref[peer, at, 1:2], gains_ref[peer, at + 1, 1:2]
            lanes = pl.ds((peer * groups + at) * LANES // 2, LANES)
            one_ref[:, lanes] = jnp.where(low_half, left, pltpu.roll(right, LANES // 2, 1))
            two_ref[:, lanes] = jnp.where(low_half, pltpu.roll(left, LANES // 2, 1), right)
    me = lax.axis_index("seq")
    for at in range(groups):
        group_ref[:, at * LANES : (at + 1) * LANES] = gains_ref[me, at, 0:1]


def unpack_rates(rates_ref, decay_ref, column_ref):
    blocks, _, rows = rates_ref.shape
    me = lax.axis_index("seq")
    total = jnp.concatenate([rates_ref[block, pl.ds(me, 1)] for block in range(blocks)], axis=0)
    lane = lax.broadcasted_iota(jnp.int32, total.shape, 1)
    shift = 1
    while shift < rows:
        total += jnp.where(lane >= shift, pltpu.roll(total, shift, 1), 0.0)
        shift *= 2
    square = (rows, rows)
    lower = lax.broadcasted_iota(jnp.int32, square, 0) >= lax.broadcasted_iota(jnp.int32, square, 1)
    for block in range(blocks):
        along = jnp.broadcast_to(total[block : block + 1], square)
        down = along.T
        spread = jnp.where(lower, down - along, 0.0)
        decay_ref[block] = jnp.where(lower, jnp.exp(spread), 0.0)
        first = down[:, 0:1]
        column_ref[block, :, 0:1] = jnp.exp(first)
        column_ref[block, :, 1:2] = jnp.exp(first[rows - 1 : rows] - first)


def inputs_kernel(
    lengths_ref, order_ref, tokens_ref, grad_ref, gains_ref, rates_ref, gate_ref, up_ref, cut_ref,
    entered_out, grads_out, feed_out, weight_out,
    mask_ref, gain_ref, second_ref, group_ref, decay_ref, column_ref,
    own_entered, own_grad, keep_one, sends_one, receives_one, keep_two, sends_two, receives_two,
    keeps, sends, receives, line_keep, line_sends, line_receives,
):
    peers, groups = lax.axis_size("seq"), lax.axis_size("fsdp")
    greet_plane(True)
    line = LineGather(cut_ref, weight_out, line_keep, line_sends, line_receives)
    line.begin()
    size = gate_ref.shape[1] // peers
    me, group = lax.axis_index("seq"), lax.axis_index("fsdp")
    batches = lengths_ref.shape[0] // groups
    block = tokens_ref.shape[0] // batches
    for batch in range(batches):
        sequence = group * batches + batch
        numbers = order_ref[sequence, me] * block + lax.broadcasted_iota(jnp.int32, (block, 1), 0)
        live = (numbers < lengths_ref[sequence]).astype(FULL)
        mask_ref[batch * block : (batch + 1) * block] = live
    unpack_gains(gains_ref, gain_ref, second_ref, group_ref)
    gain = gain_ref[...]

    def work(rows):
        normed, _ = normalised(tokens_ref[rows].astype(FULL))
        own_entered[rows] = regroup(normed * gain, peers, groups).astype(HALF)
        own_grad[rows] = (grad_ref[rows].astype(FULL) * mask_ref[rows]).astype(HALF)

    by_chunks(tokens_ref.shape[0], work)
    one = PlaneGather(own_entered, entered_out, keep_one, sends_one, receives_one)
    two = PlaneGather(own_grad, grads_out, keep_two, sends_two, receives_two)
    swap = PlaneSwap((gate_ref, up_ref), ((feed_out, 0), (feed_out, size)), keeps, sends, receives)
    one.begin()
    one.relay()
    swap.begin()
    two.begin()
    unpack_rates(rates_ref, decay_ref, column_ref)
    line.hand_on(1)
    one.finish()
    two.relay()
    line.hand_on(2)
    swap.finish()
    two.finish()
    line.finish()


def gather_inputs(lengths, order, tokens, grad, gains, rates, gate, up, cut, value_size):
    peers, groups = lax.axis_size("seq"), lax.axis_size("fsdp")
    own, width = tokens.shape
    slab, columns = gate.shape
    part = columns // peers
    blocks, _, rows = rates.shape
    return pl.pallas_call(
        inputs_kernel,
        in_specs=[pl.BlockSpec(memory_space=pltpu.SMEM)] * 2 + [vmem()] * 4 + [in_hbm()] * 3,
        out_specs=[in_hbm()] * 4 + [vmem()] * 6,
        out_shape=[
            jax.ShapeDtypeStruct((peers, own, width), HALF),
            jax.ShapeDtypeStruct((peers, own, width), HALF),
            jax.ShapeDtypeStruct((peers, slab, 2 * part), HALF),
            jax.ShapeDtypeStruct((groups,) + cut.shape, HALF),
            jax.ShapeDtypeStruct((own, 1), FULL),
            jax.ShapeDtypeStruct((1, width), FULL),
            jax.ShapeDtypeStruct((1, width), FULL),
            jax.ShapeDtypeStruct((1, value_size), FULL),
            jax.ShapeDtypeStruct((blocks, rows, rows), FULL),
            jax.ShapeDtypeStruct((blocks, rows, 2), FULL),
        ],
        scratch_shapes=[pltpu.VMEM((own, width), HALF)] * 2
        + gather_scratch()
        + gather_scratch()
        + swap_scratch(2, peers)
        + [
            pltpu.SemaphoreType.DMA,
            pltpu.SemaphoreType.DMA((2, groups - 1, peers)),
            pltpu.SemaphoreType.DMA((2, groups - 1, peers)),
        ],
        compiler_params=linked(1),
        cost_estimate=cost(0, 2 * peers * (2 * own * width + slab * 2 * part)),
    )(lengths, order, tokens, grad, gains, rates, gate, up, cut)


def feed_kernel(
    rows_ref, weight_ref, grads_ref, inner_ref, up_slope_ref, gate_slope_ref, down_ref, total
):
    step = pl.program_id(0)
    both = dot_nn(rows_ref[...], weight_ref[...])
    part = both.shape[1] // 2
    gate, upward = both[:, :part], both[:, part:]
    inside = 0.7978845608028654 * (gate + 0.044715 * (gate * gate * gate))
    bend = jnp.tanh(inside)
    share = 0.5 * (1.0 + bend)
    value = gate * share
    steep = 0.7978845608028654 * (1.0 + 3.0 * 0.044715 * (gate * gate))
    slope = share + 0.5 * gate * (1.0 - bend * bend) * steep
    inner_ref[...] = (value * upward).astype(HALF)
    up_slope_ref[...] = value.astype(HALF)
    gate_slope_ref[...] = (upward * slope).astype(HALF)
    term = dot_tn(inner_ref[...], grads_ref[...])

    @pl.when(step == 0)
    def _():
        total[...] = term

    @pl.when(step > 0)
    def _():
        total[...] += term

    @pl.when(step == pl.num_programs(0) - 1)
    def _():
        down_ref[...] = total[...].astype(HALF)


def feed(rows, weight, grads):
    count, width = rows.shape
    columns = weight.shape[1]
    part = columns // 2
    tile = 256
    tokens = pl.BlockSpec((tile, width), lambda i: (i, 0))
    out = pl.BlockSpec((tile, part), lambda i: (i, 0))
    return pl.pallas_call(
        feed_kernel,
        grid=(count // tile,),
        in_specs=[
            tokens,
            pl.BlockSpec((width, columns), lambda i: (0, 0), pipeline_mode=pl.Buffered(1)),
            tokens,
        ],
        out_specs=[out] * 3 + [pl.BlockSpec((part, width), lambda i: (0, 0))],
        out_shape=[jax.ShapeDtypeStruct((count, part), HALF)] * 3
        + [jax.ShapeDtypeStruct((part, width), HALF)],
        scratch_shapes=[pltpu.VMEM((part, width), FULL)],
        compiler_params=pltpu.CompilerParams(
            dimension_semantics=("arbitrary",), vmem_limit_bytes=VMEM_BYTES
        ),
        cost_estimate=pl.CostEstimate(
            flops=3 * count * width * columns,
            bytes_accessed=2 * (2 * count * width + width * columns + 2 * count * columns),
            transcendentals=0,
        ),
    )(rows, weight, grads)


def feed_back_kernel(rows_ref, weight_ref, up_slope_ref, gate_slope_ref, grad_ref):
    inner_grad = dot_nt(rows_ref[...], weight_ref[...])
    part = inner_grad.shape[1]
    grad_ref[:, :part] = (inner_grad * gate_slope_ref[...].astype(FULL)).astype(HALF)
    grad_ref[:, part:] = (inner_grad * up_slope_ref[...].astype(FULL)).astype(HALF)


def feed_back(rows, weight, up_slope, gate_slope):
    count, width = rows.shape
    part = weight.shape[0]
    tile = 512
    slope = pl.BlockSpec((tile, part), lambda i: (i, 0))
    return pl.pallas_call(
        feed_back_kernel,
        grid=(count // tile,),
        in_specs=[
            pl.BlockSpec((tile, width), lambda i: (i, 0)),
            pl.BlockSpec((part, width), lambda i: (0, 0), pipeline_mode=pl.Buffered(1)),
            slope,
            slope,
        ],
        out_specs=pl.BlockSpec((tile, 2 * part), lambda i: (i, 0)),
        out_shape=jax.ShapeDtypeStruct((count, 2 * part), HALF),
        compiler_params=pltpu.CompilerParams(
            dimension_semantics=("arbitrary",), vmem_limit_bytes=VMEM_BYTES
        ),
        cost_estimate=pl.CostEstimate(
            flops=2 * count * width * part,
            bytes_accessed=2 * (count * width + width * part + 4 * count * part),
            transcendentals=0,
        ),
    )(rows, weight, up_slope, gate_slope)


def retention_kernel(
    place_ref, live_ref, first_ref, second_ref, weight_ref, decay_ref, column_ref, gain_ref,
    qkv_ref, swish_ref, normed_ref, scale_ref, entry_ref, mixed_hbm, state, mixed_buffer, sems,
):
    step, steps = pl.program_id(0), pl.num_programs(0)
    rows = first_ref.shape[2]
    batches, key_size, value_size = state.shape
    total = 2 * key_size + value_size
    slot = lax.rem(step, 2)

    def sent(at, which, batch):
        return pltpu.make_async_copy(
            mixed_buffer.at[which, batch],
            mixed_hbm.at[place_ref[batch, at], batch],
            sems.at[which, batch],
        )

    @pl.when(step == 0)
    def _():
        state[...] = jnp.zeros_like(state)

    @pl.when(step >= 2)
    def _():
        for batch in range(batches):
            sent(step - 2, slot, batch).wait()

    rows_in = jnp.concatenate([first_ref[0, 0], second_ref[0, 0]], axis=0)
    projected = dot_nn(rows_in, weight_ref[...])
    decay = decay_ref[0]
    entry_decay = column_ref[0, :, 0:1]
    end_weight = column_ref[0, :, 1:2]
    block_decay = column_ref[0, rows - 1 : rows, 0:1]
    positions = step * rows + lax.broadcasted_iota(jnp.int32, (rows, 1), 0)
    for batch in range(batches):
        mine = slice(batch * rows, (batch + 1) * rows)
        live = (positions < live_ref[batch]).astype(FULL)
        query = projected[mine, :key_size].astype(HALF)
        key = (projected[mine, key_size : 2 * key_size] * live).astype(HALF)
        value = projected[mine, 2 * key_size : total].astype(HALF)
        swish = projected[mine, total:]
        before = state[batch]
        before_low = before.astype(HALF)
        weights = (dot_nt(query, key) * decay).astype(HALF)
        retained = dot_nn(weights, value) + entry_decay * dot_nn(query, before_low)
        key_ended = (key.astype(FULL) * end_weight).astype(HALF)
        state[batch] = block_decay * before + dot_tn(key_ended, value)
        normed, scale = normalised(retained)
        qkv_ref[batch, 0, :, :key_size] = query
        qkv_ref[batch, 0, :, key_size : 2 * key_size] = key
        qkv_ref[batch, 0, :, 2 * key_size :] = value
        scale_ref[batch, 0] = jnp.broadcast_to(scale, scale_ref.shape[2:])
        entry_ref[batch, 0] = before_low
        swish_ref[batch, 0] = swish.astype(HALF)
        normed_ref[batch, 0] = normed.astype(HALF)
        mixed = swish * jax.nn.sigmoid(swish) * (normed * gain_ref[...])
        mixed_buffer[slot, batch] = mixed.astype(HALF)
        sent(step, slot, batch).start()

    @pl.when(step == steps - 1)
    def _():
        for batch in range(batches):
            sent(step, slot, batch).wait()
            sent(step - 1, 1 - slot, batch).wait()


def retention(rows_in, weight, place, live, decay, columns, gain, key_size):
    blocks, batches, rows, width = rows_in.shape
    value_size = gain.shape[-1]
    total = 2 * key_size + value_size

    def arriving(batch):
        return pl.BlockSpec(
            (1, 1, rows, width), lambda i, place, live: (place[batch, i], batch, 0, 0)
        )

    def whole(shape):
        return pl.BlockSpec(
            shape, lambda i, place, live: (0,) * len(shape), pipeline_mode=pl.Buffered(1)
        )

    def here(*tail):
        return pl.BlockSpec((batches, 1) + tail, lambda i, place, live: (0, i, 0, 0))

    def along(*tail):
        return pl.BlockSpec((1,) + tail, lambda i, place, live: (i, 0, 0))

    return pl.pallas_call(
        retention_kernel,
        grid_spec=pltpu.PrefetchScalarGridSpec(
            num_scalar_prefetch=2,
            grid=(blocks,),
            in_specs=[
                arriving(0),
                arriving(1),
                whole((width, total + value_size)),
                along(rows, rows),
                along(rows, 2),
                whole((1, value_size)),
            ],
            out_specs=[
                here(rows, total),
                here(rows, value_size),
                here(rows, value_size),
                here(rows, LANES),
                here(key_size, value_size),
                in_hbm(),
            ],
            scratch_shapes=[
                pltpu.VMEM((batches, key_size, value_size), FULL),
                pltpu.VMEM((2, batches, rows, value_size), HALF),
                pltpu.SemaphoreType.DMA((2, batches)),
            ],
        ),
        out_shape=[
            jax.ShapeDtypeStruct((batches, blocks, rows, total), HALF),
            jax.ShapeDtypeStruct((batches, blocks, rows, value_size), HALF),
            jax.ShapeDtypeStruct((batches, blocks, rows, value_size), HALF),
            jax.ShapeDtypeStruct((batches, blocks, rows, LANES), FULL),
            jax.ShapeDtypeStruct((batches, blocks, key_size, value_size), HALF),
            jax.ShapeDtypeStruct((blocks, batches, rows, value_size), HALF),
        ],
        compiler_params=pltpu.CompilerParams(
            dimension_semantics=("arbitrary",), vmem_limit_bytes=VMEM_BYTES
        ),
        cost_estimate=pl.CostEstimate(
            flops=3 * blocks * batches * rows * width * total,
            bytes_accessed=2 * blocks * batches * rows * (width + 2 * total) + 4 * width * total,
            transcendentals=0,
        ),
    )(place, live, rows_in, rows_in, weight, decay, columns, gain)


def retention_back_kernel(
    place_ref, live_ref, first_ref, second_ref,
    weight_ref, decay_ref, column_ref, gain_ref, qkv_ref, swish_ref, normed_ref, scale_ref, entry_ref,
    gain_grad_ref, grads_hbm, state, grads_buffer, sems,
):
    step, steps = pl.program_id(0), pl.num_programs(0)
    rows = first_ref.shape[2]
    batches, key_size, value_size = state.shape
    slot = lax.rem(step, 2)

    def sent(at, which, batch):
        return pltpu.make_async_copy(
            grads_buffer.at[which, batch],
            grads_hbm.at[place_ref[batch, steps - 1 - at], batch],
            sems.at[which, batch],
        )

    @pl.when(step == 0)
    def _():
        state[...] = jnp.zeros_like(state)
        gain_grad_ref[...] = jnp.zeros_like(gain_grad_ref)

    @pl.when(step >= 2)
    def _():
        for batch in range(batches):
            sent(step - 2, slot, batch).wait()

    rows_in = jnp.concatenate([first_ref[0, 0], second_ref[0, 0]], axis=0)
    mixed_grads = dot_nt(rows_in, weight_ref[...])
    decay = decay_ref[0]
    entry_decay = column_ref[0, :, 0:1]
    end_weight = column_ref[0, :, 1:2]
    block_decay = column_ref[0, rows - 1 : rows, 0:1]
    positions = (steps - 1 - step) * rows + lax.broadcasted_iota(jnp.int32, (rows, 1), 0)
    gain = gain_ref[...]
    for batch in range(batches):
        live = (positions < live_ref[batch]).astype(FULL)
        mixed_grad = mixed_grads[batch * rows : (batch + 1) * rows]
        query = qkv_ref[batch, 0, :, :key_size]
        key = qkv_ref[batch, 0, :, key_size : 2 * key_size]
        value = qkv_ref[batch, 0, :, 2 * key_size :]
        swish = swish_ref[batch, 0].astype(FULL)
        normed = normed_ref[batch, 0].astype(FULL)
        scale = scale_ref[batch, 0, :, 0:1]
        entry = entry_ref[batch, 0]
        sigmoid = jax.nn.sigmoid(swish)
        silu = swish * sigmoid
        swish_grad = mixed_grad * (normed * gain) * (sigmoid * (1.0 + swish - silu))
        scaled_grad = mixed_grad * silu
        gain_grad_ref[...] += jnp.sum(scaled_grad * normed, axis=0, keepdims=True)
        retained_grad = normalised_back(scaled_grad * gain, normed, scale).astype(HALF)
        weights = (dot_nt(query, key) * decay).astype(HALF)
        scores_grad = (dot_nt(retained_grad, value) * decay).astype(HALF)
        after = state[batch]
        after_low = after.astype(HALF)
        query_grad = dot_nn(scores_grad, key) + entry_decay * dot_nt(retained_grad, entry)
        key_grad = dot_tn(scores_grad, query) + end_weight * dot_nt(value, after_low)
        value_grad = dot_tn(weights, retained_grad) + end_weight * dot_nn(key, after_low)
        query_entered = (query.astype(FULL) * entry_decay).astype(HALF)
        state[batch] = block_decay * after + dot_tn(query_entered, retained_grad)
        grads_buffer[slot, batch, :, :key_size] = query_grad.astype(HALF)
        grads_buffer[slot, batch, :, key_size : 2 * key_size] = (key_grad * live).astype(HALF)
        grads_buffer[slot, batch, :, 2 * key_size : 2 * key_size + value_size] = value_grad.astype(
            HALF
        )
        grads_buffer[slot, batch, :, 2 * key_size + value_size :] = swish_grad.astype(HALF)
        sent(step, slot, batch).start()

    @pl.when(step == steps - 1)
    def _():
        for batch in range(batches):
            sent(step, slot, batch).wait()
            sent(step - 1, 1 - slot, batch).wait()


def retention_back(rows_in, weight, place, live, decay, columns, gain, saved):
    blocks, batches, rows, width = rows_in.shape
    value_size = gain.shape[-1]
    key_size = saved[-1].shape[2]
    total = 2 * key_size + 2 * value_size

    def arriving(batch, size):
        return pl.BlockSpec(
            (1, 1, rows, size),
            lambda i, place, live: (place[batch, blocks - 1 - i], batch, 0, 0),
        )

    def whole(shape):
        return pl.BlockSpec(
            shape, lambda i, place, live: (0,) * len(shape), pipeline_mode=pl.Buffered(1)
        )

    def here(*tail):
        return pl.BlockSpec((batches, 1) + tail, lambda i, place, live: (0, blocks - 1 - i, 0, 0))

    def along(*tail):
        return pl.BlockSpec((1,) + tail, lambda i, place, live: (blocks - 1 - i, 0, 0))

    return pl.pallas_call(
        retention_back_kernel,
        grid_spec=pltpu.PrefetchScalarGridSpec(
            num_scalar_prefetch=2,
            grid=(blocks,),
            in_specs=[
                arriving(0, width),
                arriving(1, width),
                whole((value_size, width)),
                along(rows, rows),
                along(rows, 2),
                whole((1, value_size)),
                here(rows, 2 * key_size + value_size),
                here(rows, value_size),
                here(rows, value_size),
                here(rows, LANES),
                here(key_size, value_size),
            ],
            out_specs=[
                pl.BlockSpec((1, value_size), lambda i, place, live: (0, 0)),
                in_hbm(),
            ],
            scratch_shapes=[
                pltpu.VMEM((batches, key_size, value_size), FULL),
                pltpu.VMEM((2, batches, rows, total), HALF),
                pltpu.SemaphoreType.DMA((2, batches)),
            ],
        ),
        out_shape=[
            jax.ShapeDtypeStruct((1, value_size), FULL),
            jax.ShapeDtypeStruct((blocks, batches, rows, total), HALF),
        ],
        compiler_params=pltpu.CompilerParams(
            dimension_semantics=("arbitrary",), vmem_limit_bytes=VMEM_BYTES
        ),
        cost_estimate=pl.CostEstimate(
            flops=6 * blocks * batches * rows * width * value_size,
            bytes_accessed=2 * blocks * batches * rows * (width + 2 * total)
            + 2 * width * value_size,
            transcendentals=0,
        ),
    )(place, live, rows_in, rows_in, weight, decay, columns, gain, *saved)


def middle_kernel(
    mixed_hbm, weight_hbm, tokens_hbm, gain_ref, hidden_ref, second_out,
    *scratch,
):
    scatter = scratch[:7]
    own, keeps, gather_sends, gather_receives = scratch[7:11]
    weight_ref, tokens_ref, stage_sems, mixed, mixed_sems = scratch[11:]
    peers, groups = lax.axis_size("seq"), lax.axis_size("fsdp")
    sources, targets = (weight_hbm, tokens_hbm), (weight_ref, tokens_ref)
    weight_copy, tokens_copy = staged(sources, targets, stage_sems)
    blocks = Blocks(mixed_hbm, mixed, mixed_sems)
    blocks.begin()
    greet_neighbours()
    weight_copy.wait()

    def term(block):
        return blocks.take(lambda value: dot_nn(value, weight_ref[...]).astype(HALF))

    gain = gain_ref[...]

    def use(start, total):
        rows = pl.ds(start, CHUNK)
        hidden = tokens_ref[rows].astype(FULL) + total
        hidden_ref[rows] = hidden
        normed, _ = normalised(hidden)
        own[rows] = regroup(normed * gain, peers, groups).astype(HALF)

    gathers = [
        PlaneGather(own, second_out, keeps, gather_sends, gather_receives, window, WINDOWS)
        for window in range(WINDOWS)
    ]
    windows = scatter_head(term, scatter)
    tokens_copy.wait()
    scatter_tail(windows, use, lambda window: gathers[window].begin())
    for gather in gathers:
        gather.relay()
    for gather in gathers:
        gather.finish()
    for window in windows:
        window.drain()


def middle(mixed, weight, tokens, gain):
    peers, own, inner = mixed.shape
    width = weight.shape[1]
    return pl.pallas_call(
        middle_kernel,
        in_specs=[in_hbm()] * 3 + [vmem()],
        out_specs=[vmem(), in_hbm()],
        out_shape=[
            jax.ShapeDtypeStruct((own, width), FULL),
            jax.ShapeDtypeStruct((peers, own, width), HALF),
        ],
        scratch_shapes=scatter_scratch(own, width)
        + [pltpu.VMEM((own, width), HALF)]
        + gather_scratch(WINDOWS)
        + stage_scratch(weight, tokens)
        + block_scratch(peers, mixed),
        compiler_params=linked(2),
        cost_estimate=cost(2 * peers * own * inner * width, 4 * peers * own * width),
    )(mixed, weight, tokens, gain)


class LineSum:
    def __init__(self, terms, landed, own, final, loads, sends, receives):
        self.terms, self.landed, self.own, self.final = terms, landed, own, final
        self.loads, self.sends, self.receives = loads, sends, receives
        self.me, self.last = lax.axis_index("fsdp"), lax.axis_size("fsdp") - 1
        self.peers, self.place = lax.axis_size("seq"), lax.axis_index("seq")

    def piece(self, turn):
        return lax.rem(self.place + turn, self.peers)

    def depth(self, way):
        return self.me if way == 0 else self.last - self.me

    def block(self, way, order):
        return self.last - order if way == 0 else order

    def slot(self, way, order):
        return order if way == 0 else 2 * self.last - 2 - order

    def sent(self, source, way, order, turn):
        at = (way, order, turn)
        return pltpu.make_async_remote_copy(
            src_ref=source,
            dst_ref=self.landed.at[self.slot(way, order), self.piece(turn)],
            send_sem=self.sends.at[at],
            recv_sem=self.receives.at[at],
            device_id={"fsdp": self.me + 1 if way == 0 else self.me - 1},
            device_id_type=MESH,
        )

    def first(self, way, order, turn):
        source = self.terms.at[self.block(way, order), self.piece(turn)]
        return self.sent(source, way, order, turn)

    def onward(self, way, order, turn):
        source = self.landed.at[self.slot(way, order), self.piece(turn)]
        return self.sent(source, way, order, turn)

    def load(self, way, order):
        return pltpu.make_async_copy(
            self.terms.at[self.block(way, order)], self.own.at[way], self.loads.at[way]
        )

    def load_final(self):
        return pltpu.make_async_copy(self.terms.at[self.me], self.final, self.loads.at[2])

    def begin(self):
        for way in (0, 1):

            @pl.when(self.depth(way) == 0)
            def _():
                for order in range(self.last):
                    for turn in range(self.peers):
                        self.first(way, order, turn).start()

            self.load(way, 0).start()
        self.load_final().start()

    def loaded(self):
        for way in (0, 1):
            self.load(way, 0).wait()

    def load_next(self):
        for way in (0, 1):

            @pl.when(self.depth(way) == 1)
            def _():
                self.load(way, 1).start()

    def loaded_next(self):
        for way in (0, 1):

            @pl.when(self.depth(way) == 1)
            def _():
                self.load(way, 1).wait()

    def hand_on(self, order, depth, turns):
        for turn in turns:
            for way in (0, 1):

                @pl.when(self.depth(way) == depth)
                def _():
                    at, piece = self.slot(way, order), self.piece(turn)
                    self.onward(way, order, turn).wait_recv()
                    self.landed[at, piece] = (
                        self.landed[at, piece].astype(FULL) + self.own[way, piece].astype(FULL)
                    ).astype(HALF)
                    self.onward(way, order, turn).start()

    def finish(self, use):
        self.load_final().wait()
        for turn in range(self.peers):
            piece = self.piece(turn)
            for way in (0, 1):

                @pl.when(self.depth(way) > 0)
                def _():
                    order = self.last - self.depth(way)
                    self.onward(way, order, turn).wait_recv()
                    self.final[piece] = (
                        self.final[piece].astype(FULL)
                        + self.landed[self.slot(way, order), piece].astype(FULL)
                    ).astype(HALF)

            use(turn)

    def drain(self):
        for way in (0, 1):
            for order in range(self.last):
                for turn in range(self.peers):

                    @pl.when(self.depth(way) == 0)
                    def _():
                        self.first(way, order, turn).wait_send()

                    @pl.when((self.depth(way) > 0) & (self.depth(way) < self.last - order))
                    def _():
                        self.onward(way, order, turn).wait_send()


def line_scratch(groups, peers, slab, columns):
    block = (peers, slab, columns)
    return [
        pltpu.VMEM((2 * groups - 3,) + block, HALF),
        pltpu.VMEM((2,) + block, HALF),
        pltpu.VMEM(block, HALF),
        pltpu.SemaphoreType.DMA((3,)),
        pltpu.SemaphoreType.DMA((2, groups - 1, peers)),
        pltpu.SemaphoreType.DMA((2, groups - 1, peers)),
    ]


def middle_back_kernel(
    grads_hbm, weight_hbm, hidden_hbm, outer_hbm, mask_ref, gain_ref, mixed_hbm,
    hidden_grad_ref, gain_grad_ref, branch_out, out_grad_ref,
    *scratch,
):
    scatter = scratch[:7]
    own, gather_sends, gather_receives = scratch[7:10]
    weight_ref, hidden_ref, outer_ref, mixed_ref, stage_sems, grads, grad_sems = scratch[10:17]
    branch, total, out_sems = scratch[17:]
    peers, groups = lax.axis_size("seq"), lax.axis_size("fsdp")
    me, other, near, below, far = plane_peers()
    flip = other - me
    blocks = Blocks(grads_hbm, grads, grad_sems)
    weight_copy, *later = staged(
        (weight_hbm, hidden_hbm, outer_hbm, mixed_hbm),
        (weight_ref, hidden_ref, outer_ref, mixed_ref),
        stage_sems,
    )
    blocks.begin()
    greet_neighbours()
    weight_copy.wait()

    def term(block):
        return blocks.take(lambda value: dot_nt(value, weight_ref[...]).astype(HALF))

    gain = gain_ref[...]
    gain_grad_ref[...] = jnp.zeros_like(gain_grad_ref)

    def use(start, total):
        rows = pl.ds(start, CHUNK)
        grad = regroup(total, groups, peers)
        normed, scale = normalised(hidden_ref[rows])
        gain_grad_ref[...] += jnp.sum(grad * normed, axis=0, keepdims=True)
        outer = outer_ref[rows].astype(FULL) * mask_ref[rows]
        hidden_grad = outer + normalised_back(grad * gain, normed, scale)
        hidden_grad_ref[rows] = hidden_grad
        own[rows] = hidden_grad.astype(HALF)

    gathers = [
        PlaneGather(own, branch, None, gather_sends, gather_receives, window, WINDOWS)
        for window in range(WINDOWS)
    ]
    width, stored = own.shape[1], []

    def add(block, rows):
        copy = pltpu.make_async_copy(rows, branch_out.at[block], out_sems.at[len(stored)])
        copy.start()
        for start in range(0, width, 512):
            columns = pl.ds(start, 512)
            product = dot_tn(mixed_ref[block], rows[:, columns])
            total[:, columns] = total[:, columns] + product if stored else product
        stored.append(copy)

    windows = scatter_head(term, scatter)
    for copy in later:
        copy.wait()
    scatter_tail(windows, use, lambda window: gathers[window].begin())
    add(me, own)
    for gather in gathers:
        gather.expect(2, 3)
    add(other, branch.at[other])
    for gather in gathers:
        gather.relay()
    for block in (near, below):
        add(block, branch.at[block])
    for gather in gathers:
        gather.expect(8, 9, 10, 11)
    add(near + flip, branch.at[near + flip])
    for gather in gathers:
        gather.relay_far()
    add(below + flip, branch.at[below + flip])
    add(far, branch.at[far])
    for gather in gathers:
        gather.expect(12, 13)
    add(far + flip, branch.at[far + flip])
    out_grad_ref[...] = total[...].astype(HALF)
    for copy in stored:
        copy.wait()
    for gather in gathers:
        gather.drain()
    for window in windows:
        window.drain()


def middle_back(grads, weight, hidden, outer, mask, gain, mixed):
    peers, own, inner = grads.shape
    width = weight.shape[0]
    return pl.pallas_call(
        middle_back_kernel,
        in_specs=[in_hbm()] * 4 + [vmem()] * 2 + [in_hbm()],
        out_specs=[vmem(), vmem(), in_hbm(), vmem()],
        out_shape=[
            jax.ShapeDtypeStruct((own, width), FULL),
            jax.ShapeDtypeStruct((1, width), FULL),
            jax.ShapeDtypeStruct((peers, own, width), HALF),
            jax.ShapeDtypeStruct((mixed.shape[2], width), HALF),
        ],
        scratch_shapes=scatter_scratch(own, width)
        + [pltpu.VMEM((own, width), HALF)]
        + gather_scratch(WINDOWS)[1:]
        + stage_scratch(weight, hidden, outer, mixed)
        + block_scratch(2, grads)
        + [
            pltpu.VMEM((peers, own, width), HALF),
            pltpu.VMEM((mixed.shape[2], width), FULL),
            pltpu.SemaphoreType.DMA((peers,)),
        ],
        compiler_params=pltpu.CompilerParams(
            collective_id=3, has_side_effects=True, vmem_limit_bytes=LARGE_BYTES
        ),
        cost_estimate=cost(2 * peers * own * inner * width, 4 * peers * own * width),
    )(grads, weight, hidden, outer, mask, gain, mixed)


class PlaneReturn:
    def __init__(self, cuts, source, targets, keeps, sends, receives):
        self.cuts, self.source, self.targets = cuts, source, targets
        self.keeps, self.sends, self.receives = keeps, sends, receives
        self.peers, self.me = lax.axis_size("seq"), lax.axis_index("seq")

    def part(self, number, peer):
        start, size = self.cuts[number]
        return self.source.at[peer, :, pl.ds(start, size)]

    def place(self, number, peer):
        size = self.cuts[number][1]
        return self.targets[number].at[:, pl.ds(pl.multiple_of(peer * size, LANES), size)]

    def sent(self, source, target, number, turn, peer):
        at = (number, turn)
        return to_peer(source, target, self.sends.at[at], self.receives.at[at], peer)

    def copy(self, number, turn):
        peer = lax.rem(self.me + turn, self.peers)
        return self.sent(
            self.part(number, peer), self.place(number, self.me), number, turn, peer
        )

    def landed(self, number, turn):
        peer = lax.rem(self.me + self.peers - turn, self.peers)
        target = self.place(number, peer)
        return self.sent(target, target, number, turn, peer)

    def kept(self, number):
        return pltpu.make_async_copy(
            self.part(number, self.me), self.place(number, self.me), self.keeps.at[number]
        )

    def begin(self, turn):
        for number in range(len(self.cuts)):
            if turn > 0:
                self.copy(number, turn).start()
            else:
                self.kept(number).start()

    def finish(self):
        for number in range(len(self.cuts)):
            for turn in range(1, self.peers):
                self.landed(number, turn).wait_recv()
                self.copy(number, turn).wait_send()
            self.kept(number).wait()


def last_kernel(
    cuts, line_cuts, grads_hbm, weight_hbm, tokens_hbm, hidden_grad_hbm, gain_ref, second_grad_ref,
    group_grad_ref, inner_hbm, down_hbm, hidden_hbm, mask_ref, summed_ref, terms_ref,
    *refs,
):
    count, line_count = len(cuts), len(line_cuts)
    input_ref, output_ref, gains_ref = refs[:3]
    returned, refs = refs[3 : 3 + count], refs[3 + count :]
    line_returned, scratch = refs[:line_count], refs[line_count:]
    scatter, result = scratch[:7], scratch[:1] + scratch[7:13]
    (
        sums, parts, across, totals, first_grad, keep, part_sends, part_receives,
        group_keep, group_sends, group_receives,
    ) = scratch[13:24]
    peers, groups = lax.axis_size("seq"), lax.axis_size("fsdp")
    me = lax.axis_index("seq")
    grads, grad_sems = scratch[36:38]
    inner_ref = scratch[38]
    weight_ref, down_ref, hidden_ref, tokens_ref, hidden_grad_ref, stage_sems = scratch[39:]
    blocks = Blocks(grads_hbm, grads, grad_sems)
    weight_copy, inner_copy, down_copy, *later = staged(
        (weight_hbm, inner_hbm, down_hbm, hidden_hbm, tokens_hbm, hidden_grad_hbm),
        (weight_ref, inner_ref, down_ref, hidden_ref, tokens_ref, hidden_grad_ref),
        stage_sems,
    )
    blocks.begin()
    greet_plane(True)
    back = PlaneReturn(cuts, summed_ref, returned, *scratch[24:27])
    line_back = PlaneReturn(line_cuts, scratch[32], line_returned, *scratch[27:30])
    line = LineSum(terms_ref, *scratch[30:36])

    def term(block):
        return blocks.take(lambda value: dot_nt(value, weight_ref[...]).astype(HALF))

    def result_term(block):
        return dot_nn(inner_ref[block], down_ref[...]).astype(HALF)

    gain = gain_ref[...]
    first_grad[...] = jnp.zeros_like(first_grad)

    def use(start, total):
        rows = pl.ds(start, CHUNK)
        grad = regroup(total, groups, peers)
        normed, scale = normalised(tokens_ref[rows].astype(FULL))
        first_grad[...] += jnp.sum(grad * normed, axis=0, keepdims=True)
        input_ref[rows] = (
            hidden_grad_ref[rows] + normalised_back(grad * gain, normed, scale)
        ).astype(HALF)

    def use_result(start, total):
        rows = pl.ds(start, CHUNK)
        output_ref[rows] = ((hidden_ref[rows] + total) * mask_ref[rows]).astype(HALF)

    line.begin()
    weight_copy.wait()
    every, early, late = range(peers), range(peers // 2), range(peers // 2, peers)
    windows = scatter_head(term, scatter, (), True)
    windows[0].relay()
    line.loaded()
    line.hand_on(0, 1, every)
    line.load_next()
    windows[1].relay()
    inner_copy.wait()
    down_copy.wait()
    result_windows = scatter_head(result_term, result, windows, True)
    for turn in every:
        back.begin(turn)
    result_windows[0].relay()
    line.hand_on(0, 2, every)
    for copy in later:
        copy.wait()
    scatter_tail(windows, use)
    line.loaded_next()
    line.hand_on(1, 1, early)
    result_windows[1].relay()
    tile = LANES * 2
    for peer in range(peers):
        for row in range(tile // LANES):
            at = peer * tile + row * LANES
            sums[peer, row : row + 1] = first_grad[:, at : at + LANES]
            sums[peer, 2 + row : 3 + row] = second_grad_ref[:, at : at + LANES]
        sums[peer, 4:8] = jnp.zeros((4, LANES), FULL)

    def copy(turn):
        peer = lax.rem(me + turn, peers)
        return to_peer(
            sums.at[peer], parts.at[turn], part_sends.at[turn], part_receives.at[turn], peer
        )

    kept = pltpu.make_async_copy(sums.at[me], parts.at[0], keep)
    kept.start()
    for turn in range(1, peers):
        copy(turn).start()
    line.hand_on(1, 1, late)
    scatter_tail(result_windows, use_result)
    kept.wait()
    for turn in range(1, peers):
        copy(turn).wait_recv()
        copy(turn).wait_send()
    total = parts[0]
    for turn in range(1, peers):
        total += parts[turn]
    across[0:8] = total
    for row in range(4):
        across[8 + row : 9 + row] = group_grad_ref[:, row * LANES : (row + 1) * LANES]
    across[12:16] = jnp.zeros((4, LANES), FULL)
    begin, finish = all_to_each(
        across, totals, "fsdp", groups, group_keep, group_sends, group_receives
    )
    begin()
    line.finish(line_back.begin)
    back.finish()
    line_back.finish()
    line.drain()
    for window in windows:
        window.drain(4)
    for window in result_windows:
        window.drain()
    finish()
    summed = totals[0]
    for turn in range(1, groups):
        summed += totals[turn]
    gains_ref[...] = summed


def last_rows(
    grads, weight, tokens, hidden_grad, gain, second_grad, group_grad, inner, down, hidden, mask,
    summed, sizes, terms, line_sizes,
):
    peers, own, size = grads.shape
    groups = lax.axis_size("fsdp")
    width = weight.shape[0]
    slab = summed.shape[1]

    def cuts_of(sizes):
        return tuple((sum(sizes[:number]), sizes[number]) for number in range(len(sizes)))

    return pl.pallas_call(
        partial(last_kernel, cuts_of(sizes), cuts_of(line_sizes)),
        in_specs=[in_hbm()] * 4 + [vmem()] * 3 + [in_hbm()] * 3 + [vmem()] + [in_hbm()] * 2,
        out_specs=[vmem()] * 3 + [in_hbm()] * len(sizes + line_sizes),
        out_shape=[
            jax.ShapeDtypeStruct((own, width), HALF),
            jax.ShapeDtypeStruct((own, width), HALF),
            jax.ShapeDtypeStruct((16, LANES), FULL),
        ]
        + [jax.ShapeDtypeStruct((slab, peers * part), HALF) for part in sizes + line_sizes],
        scratch_shapes=scatter_scratch(own, width)
        + scatter_scratch(own, width)[1:]
        + [
            pltpu.VMEM((peers, 8, LANES), FULL),
            pltpu.VMEM((peers, 8, LANES), FULL),
            pltpu.VMEM((16, LANES), FULL),
            pltpu.VMEM((groups, 16, LANES), FULL),
            pltpu.VMEM((1, width), FULL),
            pltpu.SemaphoreType.DMA,
            pltpu.SemaphoreType.DMA((peers,)),
            pltpu.SemaphoreType.DMA((peers,)),
            pltpu.SemaphoreType.DMA,
            pltpu.SemaphoreType.DMA((groups,)),
            pltpu.SemaphoreType.DMA((groups,)),
        ]
        + swap_scratch(len(sizes), peers)
        + swap_scratch(len(line_sizes), peers)
        + line_scratch(groups, peers, slab, terms.shape[3])
        + block_scratch(2, grads)
        + [pltpu.VMEM(inner.shape, HALF)]
        + stage_scratch(weight, down, hidden, tokens, hidden_grad, inner)[:5]
        + [pltpu.SemaphoreType.DMA((6,))],
        compiler_params=pltpu.CompilerParams(
            collective_id=5, has_side_effects=True, vmem_limit_bytes=LARGE_BYTES
        ),
        cost_estimate=cost(
            2 * peers * own * (size + inner.shape[2]) * width, 5 * peers * own * width
        ),
    )(
        grads, weight, tokens, hidden_grad, gain, second_grad, group_grad, inner, down, hidden, mask,
        summed, terms,
    )


def outputs_kernel(count, *refs):
    sources, gains_ref, refs = refs[:count], refs[count], refs[count + 1 :]
    targets, (first_ref, second_ref, group_ref), refs = refs[:count], refs[count : count + 3], refs[count + 3 :]
    taken, given, loads, stores = refs[:count], refs[count : 2 * count], refs[-2], refs[-1]

    def load(number):
        return pltpu.make_async_copy(sources[number], taken[number], loads.at[number])

    def store(number):
        return pltpu.make_async_copy(given[number], targets[number], stores.at[number])

    for number in range(count):
        load(number).start()
    group, half = lax.axis_index("fsdp"), LANES // 2
    row = group // 2
    for start, target in ((0, first_ref), (2, second_ref)):
        both = gains_ref[pl.ds(start + row, 1)]
        turned = pltpu.roll(both, half, 1)
        target[...] = jnp.where(lax.rem(group, 2) == 0, both, turned)[:, :half]
    group_ref[...] = gains_ref[pl.ds(8 + group, 1)]
    for number in range(count):
        load(number).wait()
        given[number][...] = taken[number][...].astype(given[number].dtype)
        store(number).start()
    for number in range(count):
        store(number).wait()


def outputs(grads, rows, gains):
    arrays = [*grads, *rows]
    count = len(arrays)
    small = (LANES // 2, LANES // 2, LANES)
    shapes = [jax.ShapeDtypeStruct(array.shape, FULL) for array in grads] + [
        jax.ShapeDtypeStruct(array.shape, HALF) for array in rows
    ]
    return pl.pallas_call(
        partial(outputs_kernel, count),
        in_specs=[in_hbm()] * count + [vmem()],
        out_specs=[in_hbm()] * count + [vmem()] * 3,
        out_shape=shapes + [jax.ShapeDtypeStruct((1, size), FULL) for size in small],
        scratch_shapes=[pltpu.VMEM(array.shape, array.dtype) for array in arrays]
        + [pltpu.VMEM(shape.shape, shape.dtype) for shape in shapes]
        + [pltpu.SemaphoreType.DMA((count,))] * 2,
        compiler_params=pltpu.CompilerParams(vmem_limit_bytes=VMEM_BYTES),
    )(*arrays, gains)


def head_body(
    tokens,
    cotangent,
    lengths,
    block_order,
    log_decay,
    first_gain,
    query_weight,
    key_weight,
    value_weight,
    swish_weight,
    output_weight,
    group_gain,
    second_gain,
    feed_gate,
    feed_up,
    feed_down,
):
    peers, groups = lax.axis_size("seq"), lax.axis_size("fsdp")
    group = lax.axis_index("fsdp")
    batches, rows, width = tokens.shape
    own = batches * rows
    heads = log_decay.shape[0]
    key_size = query_weight.shape[1] // heads
    value_size = value_weight.shape[1] // heads
    part = feed_gate.shape[1] // peers
    slab = query_weight.shape[0]
    total = 2 * key_size + 2 * value_size

    def over_groups(local):
        return lax.all_gather(local, "fsdp", axis=0, tiled=True)

    def sum_groups(whole):
        return lax.psum_scatter(whole.astype(HALF), "fsdp", scatter_dimension=0, tiled=True)

    def gathered(cut):
        return over_groups(cut[None]).reshape(width, cut.shape[2])

    gains = jnp.concatenate(
        [
            group_gain.astype(FULL)[None],
            jnp.concatenate([first_gain, second_gain]).astype(FULL)[None],
            jnp.zeros((6, LANES), FULL),
        ],
        axis=0,
    )
    first_cut, rates, gains = first_swap(
        query_weight, key_weight, value_weight, swish_weight, log_decay, gains
    )
    out_weight = over_groups(output_weight)
    order = lax.dynamic_slice_in_dim(block_order, group * batches, batches, 0)
    numbers = jnp.arange(peers, dtype=jnp.int32)
    place = jnp.sum(
        numbers[None, None, :] * (order[:, None, :] == numbers[None, :, None]).astype(jnp.int32),
        axis=2,
    )
    live = lax.dynamic_slice_in_dim(lengths, group * batches, batches, 0)

    token_rows = tokens.reshape(own, width)
    outer_rows = cotangent.reshape(own, width)
    (
        entered, result_low, feed_cut, first_weight,
        mask, gain_one, gain_two, gain_group, decay, columns,
    ) = gather_inputs(
        lengths, block_order, token_rows, outer_rows, gains, rates, feed_gate, feed_up, first_cut,
        value_size,
    )
    first_weight = first_weight.reshape(width, total)
    entered, out_weight = lax.optimization_barrier((entered, out_weight))
    feed_weight = gathered(feed_cut)

    *saved, mixed = retention(
        entered.reshape(peers, batches, rows, width),
        first_weight,
        place,
        live,
        decay,
        columns,
        gain_group,
        key_size,
    )
    entered = entered.reshape(peers * own, width)
    mixed, feed_down = lax.optimization_barrier((mixed, feed_down))
    down_weight = over_groups(feed_down)
    mixed = mixed.reshape(peers * own, value_size)
    hidden, second = middle(mixed.reshape(peers, own, value_size), out_weight, token_rows, gain_two)
    second = second.reshape(peers * own, width)
    result_low = result_low.reshape(peers * own, width)
    inner_low, up_slope, gate_slope, down_term = feed(second, feed_weight, result_low)
    down_grad = sum_groups(down_term)
    both_grad = feed_back(result_low, down_weight, up_slope, gate_slope)
    both_term, both_grad = lax.optimization_barrier(
        (dot_tn(second, both_grad).astype(HALF), both_grad)
    )
    both_weight_grad = sum_groups(both_term).reshape(peers, slab, 2 * part)
    hidden_grad, second_gain_grad, branch_low, out_term = middle_back(
        both_grad.reshape(peers, own, 2 * part),
        feed_weight,
        hidden,
        outer_rows,
        mask,
        gain_two,
        mixed.reshape(peers, own, value_size),
    )
    branch_low, down_grad = lax.optimization_barrier((branch_low, down_grad))
    out_grad = sum_groups(out_term)
    group_gain_grad, projected_grad = retention_back(
        branch_low.reshape(peers, batches, rows, width),
        out_weight,
        place,
        live,
        decay,
        columns,
        gain_group,
        saved,
    )
    flat_grad = projected_grad.reshape(peers * own, total)
    first_term = dot_tn(entered, flat_grad).astype(HALF)
    (
        input_rows, output_rows, small_grads,
        gate_back, up_back, query_back, key_back, value_back, swish_back,
    ) = last_rows(
        projected_grad.reshape(peers, own, total),
        first_weight,
        token_rows,
        hidden_grad,
        gain_one,
        second_gain_grad,
        group_gain_grad,
        inner_low.reshape(peers, own, part),
        down_weight,
        hidden,
        mask,
        both_weight_grad,
        (part, part),
        first_term.reshape(groups, peers, slab, total),
        (key_size, key_size, value_size, value_size),
    )
    (
        query_back, key_back, value_back, swish_back, out_back, gate_back, up_back, down_back,
        output_rows, input_rows, first_grad, second_grad, group_grad,
    ) = outputs(
        (query_back, key_back, value_back, swish_back, out_grad, gate_back, up_back, down_grad),
        (output_rows, input_rows),
        small_grads,
    )
    return (
        output_rows.reshape(batches, rows, width),
        input_rows.reshape(batches, rows, width),
        first_grad.reshape(slab),
        query_back,
        key_back,
        value_back,
        swish_back,
        out_back,
        group_grad.reshape(LANES),
        second_grad.reshape(slab),
        gate_back,
        up_back,
        down_back,
    )


def body(*arrays):
    peers, groups = lax.axis_size("seq"), lax.axis_size("fsdp")
    fits = peers == 8 and groups == 4 and arrays[4].shape[0] == peers and arrays[0].shape[0] == 2
    if fits:
        return head_body(*arrays)
    return general_body(*arrays)


def solution(mesh):
    placed = (
        P("fsdp", "seq", None),
        P("fsdp", "seq", None),
        P(),
        P(),
        P(None, "seq"),
        P(("seq", "fsdp")),
        P(("seq", "fsdp"), None),
        P(("seq", "fsdp"), None),
        P(("seq", "fsdp"), None),
        P(("seq", "fsdp"), None),
        P(("seq", "fsdp"), None),
        P(("seq", "fsdp")),
        P(("seq", "fsdp")),
        P(("seq", "fsdp"), None),
        P(("seq", "fsdp"), None),
        P(("seq", "fsdp"), None),
    )
    return jax.shard_map(
        body,
        mesh=mesh,
        in_specs=placed,
        out_specs=(
            P("fsdp", "seq", None),
            P("fsdp", "seq", None),
            P(("seq", "fsdp")),
            P(("seq", "fsdp"), None),
            P(("seq", "fsdp"), None),
            P(("seq", "fsdp"), None),
            P(("seq", "fsdp"), None),
            P(("seq", "fsdp"), None),
            P(("seq", "fsdp")),
            P(("seq", "fsdp")),
            P(("seq", "fsdp"), None),
            P(("seq", "fsdp"), None),
            P(("seq", "fsdp"), None),
        ),
        check_vma=False,
    )
```

```python
from functools import partial, reduce

import jax
import jax.numpy as jnp
from jax import lax
from jax.experimental import pallas as pl
from jax.experimental.pallas import tpu as pltpu
from jax.sharding import PartitionSpec as P

EPSILON = 1e-05
HIGHEST = lax.Precision.HIGHEST


def carried_in(value, axis, combine, identity, reverse):
    peers, index = (lax.axis_size(axis), lax.axis_index(axis))
    everything = jax.tree.map(
        lambda part, kind: lax.all_gather(part.astype(kind), axis),
        value,
        (jnp.bfloat16, jnp.bfloat16),
    )
    start = jax.tree.map(
        lambda part, zero: jnp.broadcast_to(jnp.asarray(zero, part.dtype), part.shape),
        value,
        identity,
    )

    def turn(k, before):
        at = peers - 1 - k if reverse else k
        reached = at > index if reverse else at < index
        new = combine(
            before, jax.tree.map(lambda part, own: part[at].astype(own.dtype), everything, value)
        )
        return jax.tree.map(lambda a, b: jnp.where(reached, a, b), new, before)

    return lax.fori_loop(0, peers, turn, start)


def norm_rows(values, gain):
    average = jnp.mean(values, axis=-1, keepdims=True)
    centered = values - average
    variance = jnp.mean(centered * centered, axis=-1, keepdims=True)
    return centered * lax.rsqrt(variance + EPSILON) * gain


def gated_swish(swish_in, grouped):
    return jax.nn.silu(swish_in) * grouped


def gated_gelu(gate_in, upward):
    return jax.nn.gelu(gate_in) * upward


def chain_states(earlier, later):
    return (earlier[0] * later[0], later[0][:, None, None] * earlier[1] + later[1])


def transposed(left_rows, weight):
    return jnp.einsum("ie,fe->if", left_rows, weight, preferred_element_type=jnp.float32)


def plain_dot(left_rows, weight):
    return jnp.dot(left_rows, weight, preferred_element_type=jnp.float32)


def outer_term(left_rows, right_rows):
    return jnp.einsum("ni,no->io", left_rows, right_rows, preferred_element_type=jnp.float32)


def spread_sum(matrix_pairs, vectors):
    terms = tuple((outer_term(left_rows, right_rows) for left_rows, right_rows in matrix_pairs))
    pieces = lax.psum_scatter(
        terms + tuple(vectors), ("seq", "fsdp"), scatter_dimension=0, tiled=True
    )
    return list(pieces)


def join_terms(collected):
    matrix_pairs = []
    for member in range(len(collected[0][0])):
        lefts = jnp.concatenate([entry[0][member][0] for entry in collected], axis=0)
        rights = jnp.concatenate([entry[0][member][1] for entry in collected], axis=0)
        matrix_pairs.append((lefts, rights))
    vectors = [
        reduce(jnp.add, [entry[1][member] for entry in collected])
        for member in range(len(collected[0][1]))
    ]
    return (matrix_pairs, vectors)


def layer_step(gathered, inputs, cot_rows, live_mask, log_rates):
    (
        first_gain,
        query_weight,
        key_weight,
        value_weight,
        swish_weight,
        output_weight,
        group_gain,
        second_gain,
        feed_gate,
        feed_up,
        feed_down,
    ) = gathered
    floats = jnp.float32
    halves = jnp.bfloat16
    head_count = log_rates.shape[0]
    token_rows = inputs.shape[0]
    key_size = query_weight.shape[1] // head_count
    value_size = value_weight.shape[1] // head_count
    start_values = inputs.astype(floats)
    normed_one, pull_one = jax.vjp(norm_rows, start_values, first_gain.astype(floats))
    normed = normed_one.astype(halves)
    queries = plain_dot(normed, query_weight).astype(halves)
    keys_in = plain_dot(normed, key_weight).astype(halves) * live_mask[:, None].astype(halves)
    values_in = plain_dot(normed, value_weight).astype(halves)
    swish_in = plain_dot(normed, swish_weight)
    queries3 = queries.reshape(token_rows, head_count, key_size)
    keys3 = keys_in.reshape(token_rows, head_count, key_size)
    values3 = values_in.reshape(token_rows, head_count, value_size)
    cumulative = jnp.cumsum(log_rates, axis=1)
    slot_index = jnp.arange(token_rows)
    lower_mask = slot_index[:, None] >= slot_index[None, :]
    spread = cumulative[:, :, None] - cumulative[:, None, :]
    decay_matrix = jnp.where(lower_mask, jnp.exp(jnp.where(lower_mask, spread, 0.0)), 0.0)
    block_decay = jnp.exp(cumulative[:, -1])
    end_weight = jnp.exp(cumulative[:, -1:] - cumulative).T[:, :, None]
    entry_decay = jnp.exp(cumulative).T[:, :, None]
    query_wide = queries3.astype(floats)
    key_wide = keys3.astype(floats)
    value_wide = values3.astype(floats)
    state_term = jnp.einsum("jhd,jhe->hde", key_wide * end_weight, value_wide, precision=HIGHEST)
    state_identity = (jnp.ones_like(block_decay), jnp.zeros_like(state_term))
    _, start_state = carried_in(
        (block_decay, state_term), "seq", chain_states, state_identity, False
    )
    scores = jnp.einsum("ihd,jhd->hij", queries3, keys3, preferred_element_type=floats)
    weights = (scores * decay_matrix).astype(halves)
    intra_term = jnp.einsum("hij,jhe->ihe", weights, values3, preferred_element_type=floats)
    carried = entry_decay * jnp.einsum("ihd,hde->ihe", query_wide, start_state, precision=HIGHEST)
    retained = intra_term + carried
    grouped, pull_group = jax.vjp(
        norm_rows, retained, group_gain.astype(floats).reshape(head_count, value_size)
    )
    grouped_flat = grouped.reshape(token_rows, head_count * value_size)
    mixed_float, pull_mixed = jax.vjp(gated_swish, swish_in, grouped_flat)
    mixed_low = mixed_float.astype(halves)
    hidden = start_values + plain_dot(mixed_low, output_weight)
    normed_two, pull_two = jax.vjp(norm_rows, hidden, second_gain.astype(floats))
    second = normed_two.astype(halves)
    gate_two = plain_dot(second, feed_gate)
    upward = plain_dot(second, feed_up)
    inner_float, pull_inner = jax.vjp(gated_gelu, gate_two, upward)
    inner_low = inner_float.astype(halves)
    result = plain_dot(inner_low, feed_down)
    output_rows = ((hidden + result) * live_mask[:, None]).astype(halves)
    outer_grad = cot_rows.astype(floats) * live_mask[:, None]
    result_low = outer_grad.astype(halves)
    inner_grad = transposed(result_low, feed_down)
    gate_two_grad, upward_grad = pull_inner(inner_grad)
    gate_two_low = gate_two_grad.astype(halves)
    upward_low = upward_grad.astype(halves)
    second_grad = transposed(gate_two_low, feed_gate) + transposed(upward_low, feed_up)
    hidden_part, second_gain_grad = pull_two(second_grad)
    hidden_grad = outer_grad + hidden_part
    branch_low = hidden_grad.astype(halves)
    mixed_grad = transposed(branch_low, output_weight)
    swish_grad, grouped_grad = pull_mixed(mixed_grad)
    swish_low = swish_grad.astype(halves)
    retained_grad, group_gain_grad = pull_group(
        grouped_grad.reshape(token_rows, head_count, value_size)
    )
    retained_low = retained_grad.astype(halves)
    weights_grad = jnp.einsum("ihe,jhe->hij", retained_low, values3, preferred_element_type=floats)
    scores_low = (weights_grad * decay_matrix).astype(halves)
    query_intra = jnp.einsum("hij,jhd->ihd", scores_low, keys3, preferred_element_type=floats)
    key_intra = jnp.einsum("hij,ihd->jhd", scores_low, queries3, preferred_element_type=floats)
    value_intra = jnp.einsum("hij,ihe->jhe", weights, retained_low, preferred_element_type=floats)
    retained_wide = retained_low.astype(floats)
    query_carried = entry_decay * jnp.einsum(
        "ihe,hde->ihd", retained_wide, start_state, precision=HIGHEST
    )
    local_grad = jnp.einsum(
        "ihd,ihe->hde", query_wide * entry_decay, retained_wide, precision=HIGHEST
    )
    _, end_grad = carried_in((block_decay, local_grad), "seq", chain_states, state_identity, True)
    key_state = end_weight * jnp.einsum("jhe,hde->jhd", value_wide, end_grad, precision=HIGHEST)
    value_state = end_weight * jnp.einsum("jhd,hde->jhe", key_wide, end_grad, precision=HIGHEST)
    query_low = (
        (query_intra + query_carried).astype(halves).reshape(token_rows, head_count * key_size)
    )
    key_low = (
        ((key_intra + key_state) * live_mask[:, None, None])
        .astype(halves)
        .reshape(token_rows, head_count * key_size)
    )
    value_low = (
        (value_intra + value_state).astype(halves).reshape(token_rows, head_count * value_size)
    )
    normed_grad = (
        transposed(query_low, query_weight)
        + transposed(key_low, key_weight)
        + transposed(value_low, value_weight)
        + transposed(swish_low, swish_weight)
    )
    input_part, first_gain_grad = pull_one(normed_grad)
    grad_rows = (hidden_grad + input_part).astype(halves)
    matrix_pairs = [
        (normed, query_low),
        (normed, key_low),
        (normed, value_low),
        (normed, swish_low),
        (mixed_low, branch_low),
        (second, gate_two_low),
        (second, upward_low),
        (inner_low, result_low),
    ]
    vectors = [first_gain_grad, group_gain_grad.reshape(-1), second_gain_grad]
    return (output_rows, grad_rows, matrix_pairs, vectors)


def general_body(
    tokens,
    cotangent,
    lengths,
    block_order,
    log_decay,
    first_gain,
    query_weight,
    key_weight,
    value_weight,
    swish_weight,
    output_weight,
    group_gain,
    second_gain,
    feed_gate,
    feed_up,
    feed_down,
):
    batches = tokens.shape[0]
    block_rows = tokens.shape[1]
    selected_locations = lax.axis_size("seq")
    position = lax.axis_index("seq")
    group_index = lax.axis_index("fsdp")
    place_numbers = jnp.arange(selected_locations, dtype=jnp.int32)
    arrived_tokens, arrived_cotangent = (
        lax.all_gather(tokens, "seq", axis=1, tiled=True),
        lax.all_gather(cotangent, "seq", axis=1, tiled=True),
    )
    gathered = (
        lax.all_gather(first_gain, ("seq", "fsdp"), axis=0, tiled=True),
        lax.all_gather(query_weight, ("seq", "fsdp"), axis=0, tiled=True),
        lax.all_gather(key_weight, ("seq", "fsdp"), axis=0, tiled=True),
        lax.all_gather(value_weight, ("seq", "fsdp"), axis=0, tiled=True),
        lax.all_gather(swish_weight, ("seq", "fsdp"), axis=0, tiled=True),
        lax.all_gather(output_weight, ("seq", "fsdp"), axis=0, tiled=True),
        lax.all_gather(group_gain, ("seq", "fsdp"), axis=0, tiled=True),
        lax.all_gather(second_gain, ("seq", "fsdp"), axis=0, tiled=True),
        lax.all_gather(feed_gate, ("seq", "fsdp"), axis=0, tiled=True),
        lax.all_gather(feed_up, ("seq", "fsdp"), axis=0, tiled=True),
        lax.all_gather(feed_down, ("seq", "fsdp"), axis=0, tiled=True),
    )
    outputs = []
    input_grads = []
    collected = []
    order_rows = []
    for batch_number in range(batches):
        sequence = group_index * batches + batch_number
        order_row = lax.dynamic_index_in_dim(block_order, sequence, 0, keepdims=False)
        order_rows.append(order_row)
        source = jnp.sum(place_numbers * (order_row == position).astype(jnp.int32))
        token_rows = lax.dynamic_slice_in_dim(
            arrived_tokens[batch_number], source * block_rows, block_rows, 0
        )
        cot_rows = lax.dynamic_slice_in_dim(
            arrived_cotangent[batch_number], source * block_rows, block_rows, 0
        )
        live_length = lax.dynamic_index_in_dim(lengths, sequence, 0, keepdims=False)
        location_number = position * block_rows + jnp.arange(block_rows, dtype=jnp.int32)
        live_mask = (location_number < live_length).astype(jnp.float32)
        output_rows, grad_rows, matrix_pairs, vectors = layer_step(
            gathered, token_rows, cot_rows, live_mask, log_decay
        )
        outputs.append(output_rows)
        input_grads.append(grad_rows)
        collected.append((matrix_pairs, vectors))
    joined_pairs, joined_vectors = join_terms(collected)
    shards = spread_sum(joined_pairs, joined_vectors)
    every_output, every_grad = (
        lax.all_gather(jnp.stack(outputs), "seq", axis=1, tiled=True),
        lax.all_gather(jnp.stack(input_grads), "seq", axis=1, tiled=True),
    )
    returned = []
    returned_grads = []
    for batch_number in range(batches):
        target = lax.dynamic_index_in_dim(order_rows[batch_number], position, 0, keepdims=False)
        returned.append(
            lax.dynamic_slice_in_dim(every_output[batch_number], target * block_rows, block_rows, 0)
        )
        returned_grads.append(
            lax.dynamic_slice_in_dim(every_grad[batch_number], target * block_rows, block_rows, 0)
        )
    return (
        jnp.stack(returned),
        jnp.stack(returned_grads),
        shards[8],
        shards[0],
        shards[1],
        shards[2],
        shards[3],
        shards[4],
        shards[9],
        shards[10],
        shards[5],
        shards[6],
        shards[7],
    )


FULL = jnp.float32
HALF = jnp.bfloat16
MESH = pl.DeviceIdType.MESH
VMEM_BYTES = 56 * 1024 * 1024
LARGE_BYTES = 63 * 1024 * 1024
LANES = 128


def dot_nn(left, right):
    return jnp.dot(left, right, preferred_element_type=FULL)


def dot_nt(left, right):
    return lax.dot_general(left, right, (((1,), (1,)), ((), ())), preferred_element_type=FULL)


def dot_tn(left, right):
    return lax.dot_general(left, right, (((0,), (0,)), ((), ())), preferred_element_type=FULL)


def plane_peers():
    me = lax.axis_index("seq")
    core = lax.rem(me, 2)
    across = 2 - 4 * lax.rem(me // 2, 2)
    down = 4 - 8 * (me // 4)
    return me, me + 1 - 2 * core, me + across, me + down, me + across + down


def to_peer(source, target, send, receive, peer):
    return pltpu.make_async_remote_copy(
        src_ref=source,
        dst_ref=target,
        send_sem=send,
        recv_sem=receive,
        device_id={"seq": peer},
        device_id_type=MESH,
    )


def greet_neighbours():
    _, other, near, below, _ = plane_peers()
    barrier = pltpu.get_barrier_semaphore()
    for peer in (other, near, below):
        pl.semaphore_signal(barrier, inc=1, device_id={"seq": peer}, device_id_type=MESH)
    pl.semaphore_wait(barrier, 3)


GATHER_COPIES = 14


def gather_plan():
    me, other, near, below, far = plane_peers()
    flip = other - me
    return (
        (me, 0, near, near),
        (me, 1, below, below),
        (me, 0, other, other),
        (me, 1, other, other),
        (me, 1, near, near),
        (me, 0, below, below),
        (near, 0, below, far),
        (below, 1, near, far),
        (near, 0, other, near + flip),
        (below, 1, other, below + flip),
        (near, 1, other, near + flip),
        (below, 0, other, below + flip),
        (far, 0, other, far + flip),
        (far, 1, other, far + flip),
    )


class PlaneGather:
    def __init__(self, own, out, keeps, sends, receives, window=0, windows=1):
        self.own, self.out = own, out
        self.keep = None if keeps is None else keeps.at[window]
        self.sends, self.receives = sends, receives
        self.size = own.shape[0] // windows
        self.window, self.start = window, window * self.size
        self.half = self.size // 2

    def rows(self, which):
        return pl.ds(self.start + which * self.half, self.half)

    def kept(self):
        me = lax.axis_index("seq")
        rows = pl.ds(self.start, self.size)
        return pltpu.make_async_copy(self.own.at[rows], self.out.at[me, rows], self.keep)

    def sent(self, source, target, number, peer):
        at = (self.window, number)
        return to_peer(source, target, self.sends.at[at], self.receives.at[at], peer)

    def copy(self, number):
        block, which, peer, _ = gather_plan()[number]
        target = self.out.at[block, self.rows(which)]
        source = self.own.at[self.rows(which)] if number < 6 else target
        return self.sent(source, target, number, peer)

    def landed(self, number):
        _, which, peer, landing = gather_plan()[number]
        target = self.out.at[landing, self.rows(which)]
        self.sent(target, target, number, peer).wait_recv()

    def begin(self):
        if self.keep is not None:
            self.kept().start()
        for number in range(6):
            self.copy(number).start()

    def relay(self):
        for arrived, onward in ((0, (6, 8)), (1, (7, 9)), (4, (10,)), (5, (11,))):
            self.landed(arrived)
            for number in onward:
                self.copy(number).start()

    def relay_far(self):
        for arrived, onward in ((6, 12), (7, 13)):
            self.landed(arrived)
            self.copy(onward).start()

    def expect(self, *numbers):
        for number in numbers:
            self.landed(number)

    def drain(self):
        for number in range(GATHER_COPIES):
            self.copy(number).wait_send()
        if self.keep is not None:
            self.kept().wait()

    def finish(self):
        self.relay_far()
        self.expect(2, 3, 8, 9, 10, 11, 12, 13)
        self.drain()


def gather_scratch(windows=1):
    return [
        pltpu.SemaphoreType.DMA((windows,)),
        pltpu.SemaphoreType.DMA((windows, GATHER_COPIES)),
        pltpu.SemaphoreType.DMA((windows, GATHER_COPIES)),
    ]


SCATTER_COPIES = 10
WINDOWS = 2
CHUNK = 32


def by_chunks(rows, work):
    def step(number, carry):
        work(pl.ds(pl.multiple_of(number * CHUNK, CHUNK), CHUNK))
        return carry

    lax.fori_loop(0, rows // CHUNK, step, 0)


class PlaneScatter:
    def __init__(self, window, others, terms, cores, nears, belows, sends, receives):
        self.window = window
        self.others, self.terms, self.cores = others, terms, cores
        self.nears, self.belows = nears, belows
        self.sends, self.receives = sends, receives
        self.size = terms.shape[1] // WINDOWS
        self.half = self.size // 2
        self.start = window * self.size

    def copy(self, number):
        _, other, near, below, _ = plane_peers()
        whole = pl.ds(self.start, self.size)
        upper, lower = (pl.ds(self.start + at * self.half, self.half) for at in (0, 1))
        if number < 4:
            source, target, peer = (
                self.others.at[number, whole],
                self.cores.at[number, whole],
                other,
            )
        else:
            slot, rows, landing, place, peer = (
                (0, upper, self.nears, 0, near),
                (0, lower, self.belows, 0, below),
                (1, upper, self.nears, 1, near),
                (2, lower, self.belows, 1, below),
                (1, lower, self.nears, 2, near),
                (2, upper, self.belows, 2, below),
            )[number - 4]
            source, target = self.terms.at[slot, rows], landing.at[self.window, place]
        at = (self.window, number)
        return to_peer(source, target, self.sends.at[at], self.receives.at[at], peer)

    def fold(self, slot):
        def work(rows):
            here = pl.ds(pl.multiple_of(self.start + rows.start, CHUNK), CHUNK)
            self.terms[slot, here] = (
                self.terms[slot, here].astype(FULL) + self.cores[slot, here].astype(FULL)
            ).astype(HALF)

        by_chunks(self.size, work)

    def fold_half(self, slot, which, landed):
        def work(rows):
            at = self.start + which * self.half
            here = pl.ds(pl.multiple_of(at + rows.start, CHUNK), CHUNK)
            self.terms[slot, here] = (
                self.terms[slot, here].astype(FULL) + landed[self.window, 0, rows].astype(FULL)
            ).astype(HALF)

        by_chunks(self.half, work)

    def advance(self, slot):
        self.copy(slot).wait_recv()
        self.fold(slot)
        for number in ((4, 5), (6,), (7,), ())[slot]:
            self.copy(number).start()

    def relay(self):
        self.copy(4).wait_recv()
        self.fold_half(2, 0, self.nears)
        self.copy(9).start()
        self.copy(5).wait_recv()
        self.fold_half(1, 1, self.belows)
        self.copy(8).start()

    def finish(self):
        for number in (6, 7, 8, 9):
            self.copy(number).wait_recv()

    def drain(self, first=0):
        for number in range(first, SCATTER_COPIES):
            self.copy(number).wait_send()

    def total(self, at):
        upper = at < self.half
        rows = pl.ds(at if upper else at - self.half, CHUNK)
        near, below = (1, 2) if upper else (2, 1)
        return (
            self.terms[3, pl.ds(self.start + at, CHUNK)].astype(FULL)
            + self.nears[self.window, near, rows].astype(FULL)
            + self.belows[self.window, below, rows].astype(FULL)
        )


def block_order_of_plane():
    me, other, near, below, far = plane_peers()
    return [block + at for block in (far, near, below, me) for at in (other - me, 0)]


class Blocks:
    def __init__(self, source, target, sems):
        self.source, self.target, self.sems = source, target, sems
        self.blocks, self.taken = block_order_of_plane(), 0

    def load(self, number):
        slot = number % self.target.shape[0]
        return pltpu.make_async_copy(
            self.source.at[self.blocks[number]], self.target.at[slot], self.sems.at[slot]
        )

    def begin(self):
        for number in range(min(len(self.blocks), self.target.shape[0])):
            self.load(number).start()

    def take(self, work):
        number, slots = self.taken, self.target.shape[0]
        self.taken += 1
        self.load(number).wait()
        out = work(self.target[number % slots])
        if number + slots < len(self.blocks):
            self.load(number + slots).start()
        return out


def staged(sources, targets, sems):
    copies = [
        pltpu.make_async_copy(source, target, sems.at[number])
        for number, (source, target) in enumerate(zip(sources, targets))
    ]
    for copy in copies:
        copy.start()
    return copies


def stage_scratch(*arrays):
    return [pltpu.VMEM(array.shape, array.dtype) for array in arrays] + [
        pltpu.SemaphoreType.DMA((len(arrays),))
    ]


def block_scratch(count, array):
    return [
        pltpu.VMEM((count,) + array.shape[1:], array.dtype),
        pltpu.SemaphoreType.DMA((count,)),
    ]


def scatter_head(term, refs, earlier=(), relay_later=False):
    windows = [PlaneScatter(window, *refs) for window in range(WINDOWS)]
    others, terms = refs[:2]
    blocks = block_order_of_plane()

    def fill(slot):
        for window in earlier:
            window.copy(slot).wait_send()
        others[slot] = term(blocks[2 * slot])
        for window in windows:
            window.copy(slot).start()
        terms[slot] = term(blocks[2 * slot + 1])

    fill(0)
    for slot in range(4):
        if slot < 3:
            fill(slot + 1)
        windows[0].advance(slot)
    if not relay_later:
        windows[0].relay()
    for window in windows[1:]:
        for slot in range(4):
            window.advance(slot)
        if not relay_later:
            window.relay()
    return windows


def scatter_tail(windows, use, after=lambda window: None):
    for number, window in enumerate(windows):
        window.finish()
        for at in range(0, window.size, CHUNK):
            use(window.start + at, window.total(at))
        after(number)


def scatter_scratch(rows, width):
    half = rows // WINDOWS // 2
    return [
        pltpu.VMEM((4, rows, width), HALF),
        pltpu.VMEM((4, rows, width), HALF),
        pltpu.VMEM((4, rows, width), HALF),
        pltpu.VMEM((WINDOWS, 3, half, width), HALF),
        pltpu.VMEM((WINDOWS, 3, half, width), HALF),
        pltpu.SemaphoreType.DMA((WINDOWS, SCATTER_COPIES)),
        pltpu.SemaphoreType.DMA((WINDOWS, SCATTER_COPIES)),
    ]


def regroup(values, outer, inner):
    rows = values.shape[0]
    low_half = lax.broadcasted_iota(jnp.int32, (rows, LANES), 1) < LANES // 2

    def piece(p, q):
        at = (p * inner + q) // 2
        return values[:, at * LANES : (at + 1) * LANES]

    def turned(value):
        return pltpu.roll(value, LANES // 2, 1)

    groups = []
    for q in range(inner):
        for p in range(0, outer, 2):
            first, second = piece(p, q), piece(p + 1, q)
            if q % 2 == 0:
                groups.append(jnp.where(low_half, first, turned(second)))
            else:
                groups.append(jnp.where(low_half, turned(first), second))
    return jnp.concatenate(groups, axis=1)


def normalised(values):
    average = jnp.mean(values, axis=-1, keepdims=True)
    centered = values - average
    scale = lax.rsqrt(jnp.mean(centered * centered, axis=-1, keepdims=True) + EPSILON)
    return centered * scale, scale


def normalised_back(grad, normed, scale):
    average = jnp.mean(grad, axis=-1, keepdims=True)
    along = jnp.mean(grad * normed, axis=-1, keepdims=True)
    return (grad - average - normed * along) * scale


def vmem():
    return pl.BlockSpec(memory_space=pltpu.VMEM)


def in_hbm():
    return pl.BlockSpec(memory_space=pl.ANY)


def cost(flops, link_bytes):
    return pl.CostEstimate(flops=int(flops), bytes_accessed=int(link_bytes) * 16, transcendentals=0)


def linked(collective):
    return pltpu.CompilerParams(
        collective_id=collective, has_side_effects=True, vmem_limit_bytes=VMEM_BYTES
    )


class PlaneSwap:
    def __init__(self, weights, targets, keeps, sends, receives):
        self.weights, self.targets = weights, targets
        self.keeps, self.sends, self.receives = keeps, sends, receives
        self.peers = lax.axis_size("seq")

    def part(self, number, peer):
        weight, (target, start) = self.weights[number], self.targets[number]
        size = weight.shape[1] // self.peers
        return weight.at[:, pl.ds(pl.multiple_of(peer * size, LANES), size)]

    def place(self, number, peer):
        weight, (target, start) = self.weights[number], self.targets[number]
        return target.at[peer, :, pl.ds(start, weight.shape[1] // self.peers)]

    def copy(self, number, turn):
        me = lax.axis_index("seq")
        peer = lax.rem(me + turn, self.peers)
        return to_peer(
            self.part(number, peer),
            self.place(number, me),
            self.sends.at[number, turn],
            self.receives.at[number, turn],
            peer,
        )

    def landed(self, number, turn):
        me = lax.axis_index("seq")
        peer = lax.rem(me + self.peers - turn, self.peers)
        target = self.place(number, peer)
        to_peer(
            target, target, self.sends.at[number, turn], self.receives.at[number, turn], peer
        ).wait_recv()

    def kept(self, number):
        me = lax.axis_index("seq")
        return pltpu.make_async_copy(
            self.part(number, me), self.place(number, me), self.keeps.at[number]
        )

    def begin(self):
        for number in range(len(self.weights)):
            for turn in range(1, self.peers):
                self.copy(number, turn).start()
            self.kept(number).start()

    def finish(self):
        for number in range(len(self.weights)):
            for turn in range(1, self.peers):
                self.landed(number, turn)
                self.copy(number, turn).wait_send()
            self.kept(number).wait()


def swap_scratch(count, peers):
    return [
        pltpu.SemaphoreType.DMA((count,)),
        pltpu.SemaphoreType.DMA((count, peers)),
        pltpu.SemaphoreType.DMA((count, peers)),
    ]


def greet_plane(with_groups):
    me, group = lax.axis_index("seq"), lax.axis_index("fsdp")
    peers, groups = lax.axis_size("seq"), lax.axis_size("fsdp")
    barrier = pltpu.get_barrier_semaphore()
    count = peers - 1
    for turn in range(1, peers):
        peer = lax.rem(me + turn, peers)
        pl.semaphore_signal(barrier, inc=1, device_id={"seq": peer}, device_id_type=MESH)
    if with_groups:
        count += groups - 1
        for turn in range(1, groups):
            peer = lax.rem(group + turn, groups)
            pl.semaphore_signal(barrier, inc=1, device_id={"fsdp": peer}, device_id_type=MESH)
    pl.semaphore_wait(barrier, count)


def all_to_each(source, out, axis, size, keep, sends, receives):
    me = lax.axis_index(axis)

    def copy(turn, slot):
        peer = lax.rem(me + turn, size)
        return pltpu.make_async_remote_copy(
            src_ref=source,
            dst_ref=out.at[slot],
            send_sem=sends.at[turn],
            recv_sem=receives.at[turn],
            device_id={axis: peer},
            device_id_type=MESH,
        )

    def begin():
        pltpu.make_async_copy(source, out.at[me], keep).start()
        for turn in range(1, size):
            copy(turn, me).start()

    def finish():
        for turn in range(1, size):
            copy(turn, lax.rem(me + size - turn, size)).wait_recv()
            copy(turn, me).wait_send()
        pltpu.make_async_copy(source, out.at[me], keep).wait()

    return begin, finish


def first_swap_kernel(
    query_ref, key_ref, value_ref, swish_ref, rates_ref, gains_ref,
    cut_out, rates_out, gains_out,
    column, keeps, sends, receives, rate_keep, rate_sends, rate_receives,
    group_keep, group_sends, group_receives, gain_keep, gain_sends, gain_receives,
):
    peers, groups = lax.axis_size("seq"), lax.axis_size("fsdp")
    size, wide = query_ref.shape[1] // peers, value_ref.shape[1] // peers
    greet_plane(True)
    begin_groups, finish_groups = all_to_each(
        gains_ref, column, "fsdp", groups, group_keep, group_sends, group_receives
    )
    begin_rates, finish_rates = all_to_each(
        rates_ref, rates_out, "seq", peers, rate_keep, rate_sends, rate_receives
    )
    begin_gains, finish_gains = all_to_each(
        column, gains_out, "seq", peers, gain_keep, gain_sends, gain_receives
    )
    swap = PlaneSwap(
        (query_ref, key_ref, value_ref, swish_ref),
        ((cut_out, 0), (cut_out, size), (cut_out, 2 * size), (cut_out, 2 * size + wide)),
        keeps,
        sends,
        receives,
    )
    begin_groups()
    begin_rates()
    swap.begin()
    finish_groups()
    begin_gains()
    finish_rates()
    finish_gains()
    swap.finish()


def first_swap(query, key, value, swish, rates, gains):
    peers, groups = lax.axis_size("seq"), lax.axis_size("fsdp")
    slab = query.shape[0]
    total = sum(weight.shape[1] for weight in (query, key, value, swish)) // peers
    return pl.pallas_call(
        first_swap_kernel,
        in_specs=[in_hbm()] * 4 + [vmem()] * 2,
        out_specs=[in_hbm()] + [vmem()] * 2,
        out_shape=[
            jax.ShapeDtypeStruct((peers, slab, total), HALF),
            jax.ShapeDtypeStruct((peers,) + rates.shape, FULL),
            jax.ShapeDtypeStruct((peers, groups) + gains.shape, FULL),
        ],
        scratch_shapes=[pltpu.VMEM((groups,) + gains.shape, FULL)]
        + swap_scratch(4, peers)
        + [pltpu.SemaphoreType.DMA] + [pltpu.SemaphoreType.DMA((peers,))] * 2
        + [pltpu.SemaphoreType.DMA] + [pltpu.SemaphoreType.DMA((groups,))] * 2
        + [pltpu.SemaphoreType.DMA] + [pltpu.SemaphoreType.DMA((peers,))] * 2,
        compiler_params=linked(0),
        cost_estimate=cost(0, 2 * slab * peers * total),
    )(query, key, value, swish, rates, gains)


class LineGather:
    def __init__(self, own, out, keep, sends, receives):
        self.own, self.out = own, out
        self.keep, self.sends, self.receives = keep, sends, receives
        self.me, self.last = lax.axis_index("fsdp"), lax.axis_size("fsdp") - 1
        self.pieces = own.shape[0]

    def block(self, way, depth):
        return self.me - depth if way == 0 else self.me + depth

    def holds(self, way, depth):
        return self.me >= depth if way == 0 else self.me + depth <= self.last

    def passes(self, way):
        return self.me < self.last if way == 0 else self.me > 0

    def sent(self, source, way, depth, piece, block):
        at = (way, depth, piece)
        return pltpu.make_async_remote_copy(
            src_ref=source,
            dst_ref=self.out.at[block, piece],
            send_sem=self.sends.at[at],
            recv_sem=self.receives.at[at],
            device_id={"fsdp": self.me + 1 if way == 0 else self.me - 1},
            device_id_type=MESH,
        )

    def copy(self, way, depth, piece):
        block = self.block(way, depth)
        source = self.own.at[piece] if depth == 0 else self.out.at[block, piece]
        return self.sent(source, way, depth, piece, block)

    def landed(self, way, depth, piece):
        block = self.block(way, depth)
        self.sent(self.out.at[block, piece], way, depth - 1, piece, block).wait_recv()

    def kept(self):
        return pltpu.make_async_copy(self.own, self.out.at[self.me], self.keep)

    def begin(self):
        for piece in range(self.pieces):
            for way in (0, 1):

                @pl.when(self.passes(way))
                def _():
                    self.copy(way, 0, piece).start()

        self.kept().start()

    def hand_on(self, depth):
        for piece in range(self.pieces):
            for way in (0, 1):

                @pl.when(self.holds(way, depth) & self.passes(way))
                def _():
                    self.landed(way, depth, piece)
                    self.copy(way, depth, piece).start()

    def finish(self):
        for depth in range(1, self.last + 1):
            for piece in range(self.pieces):
                for way in (0, 1):

                    @pl.when(self.holds(way, depth) & jnp.logical_not(self.passes(way)))
                    def _():
                        self.landed(way, depth, piece)

        for depth in range(self.last):
            for piece in range(self.pieces):
                for way in (0, 1):

                    @pl.when(self.holds(way, depth) & self.passes(way))
                    def _():
                        self.copy(way, depth, piece).wait_send()

        self.kept().wait()


def unpack_gains(gains_ref, one_ref, two_ref, group_ref):
    peers, groups = gains_ref.shape[:2]
    low_half = lax.broadcasted_iota(jnp.int32, (1, LANES), 1) < LANES // 2
    for peer in range(peers):
        for at in range(0, groups, 2):
            left, right = gains_ref[peer, at, 1:2], gains_ref[peer, at + 1, 1:2]
            lanes = pl.ds((peer * groups + at) * LANES // 2, LANES)
            one_ref[:, lanes] = jnp.where(low_half, left, pltpu.roll(right, LANES // 2, 1))
            two_ref[:, lanes] = jnp.where(low_half, pltpu.roll(left, LANES // 2, 1), right)
    me = lax.axis_index("seq")
    for at in range(groups):
        group_ref[:, at * LANES : (at + 1) * LANES] = gains_ref[me, at, 0:1]


def unpack_rates(rates_ref, decay_ref, column_ref):
    blocks, _, rows = rates_ref.shape
    me = lax.axis_index("seq")
    total = jnp.concatenate([rates_ref[block, pl.ds(me, 1)] for block in range(blocks)], axis=0)
    lane = lax.broadcasted_iota(jnp.int32, total.shape, 1)
    shift = 1
    while shift < rows:
        total += jnp.where(lane >= shift, pltpu.roll(total, shift, 1), 0.0)
        shift *= 2
    square = (rows, rows)
    lower = lax.broadcasted_iota(jnp.int32, square, 0) >= lax.broadcasted_iota(jnp.int32, square, 1)
    for block in range(blocks):
        along = jnp.broadcast_to(total[block : block + 1], square)
        down = along.T
        spread = jnp.where(lower, down - along, 0.0)
        decay_ref[block] = jnp.where(lower, jnp.exp(spread), 0.0)
        first = down[:, 0:1]
        column_ref[block, :, 0:1] = jnp.exp(first)
        column_ref[block, :, 1:2] = jnp.exp(first[rows - 1 : rows] - first)


def inputs_kernel(
    lengths_ref, order_ref, tokens_ref, grad_ref, gains_ref, rates_ref, gate_ref, up_ref, cut_ref,
    entered_out, grads_out, feed_out, weight_out,
    mask_ref, gain_ref, second_ref, group_ref, decay_ref, column_ref, place_ref, live_ref,
    own_entered, own_grad, keep_one, sends_one, receives_one, keep_two, sends_two, receives_two,
    keeps, sends, receives, line_keep, line_sends, line_receives,
):
    peers, groups = lax.axis_size("seq"), lax.axis_size("fsdp")
    greet_plane(True)
    line = LineGather(cut_ref, weight_out, line_keep, line_sends, line_receives)
    line.begin()
    size = gate_ref.shape[1] // peers
    me, group = lax.axis_index("seq"), lax.axis_index("fsdp")
    batches = lengths_ref.shape[0] // groups
    block = tokens_ref.shape[0] // batches
    for batch in range(batches):
        sequence = group * batches + batch
        numbers = order_ref[sequence, me] * block + lax.broadcasted_iota(jnp.int32, (block, 1), 0)
        live_ref[batch] = lengths_ref[sequence]
        live = (numbers < lengths_ref[sequence]).astype(FULL)
        mask_ref[batch * block : (batch + 1) * block] = live
        for position in range(peers):
            place = jnp.int32(0)
            for at in range(peers):
                place += jnp.where(order_ref[sequence, at] == position, at, 0)
            place_ref[batch, position] = place
    unpack_gains(gains_ref, gain_ref, second_ref, group_ref)
    gain = gain_ref[...]

    def work(rows):
        normed, _ = normalised(tokens_ref[rows].astype(FULL))
        own_entered[rows] = regroup(normed * gain, peers, groups).astype(HALF)
        own_grad[rows] = (grad_ref[rows].astype(FULL) * mask_ref[rows]).astype(HALF)

    by_chunks(tokens_ref.shape[0], work)
    one = PlaneGather(own_entered, entered_out, keep_one, sends_one, receives_one)
    two = PlaneGather(own_grad, grads_out, keep_two, sends_two, receives_two)
    swap = PlaneSwap((gate_ref, up_ref), ((feed_out, 0), (feed_out, size)), keeps, sends, receives)
    one.begin()
    one.relay()
    swap.begin()
    two.begin()
    unpack_rates(rates_ref, decay_ref, column_ref)
    line.hand_on(1)
    one.finish()
    two.relay()
    line.hand_on(2)
    swap.finish()
    two.finish()
    line.finish()


def gather_inputs(lengths, order, tokens, grad, gains, rates, gate, up, cut, value_size):
    peers, groups = lax.axis_size("seq"), lax.axis_size("fsdp")
    own, width = tokens.shape
    slab, columns = gate.shape
    part = columns // peers
    blocks, _, rows = rates.shape
    return pl.pallas_call(
        inputs_kernel,
        in_specs=[pl.BlockSpec(memory_space=pltpu.SMEM)] * 2 + [vmem()] * 4 + [in_hbm()] * 3,
        out_specs=[in_hbm()] * 4
        + [vmem()] * 6
        + [pl.BlockSpec(memory_space=pltpu.SMEM)] * 2,
        out_shape=[
            jax.ShapeDtypeStruct((peers, own, width), HALF),
            jax.ShapeDtypeStruct((peers, own, width), HALF),
            jax.ShapeDtypeStruct((peers, slab, 2 * part), HALF),
            jax.ShapeDtypeStruct((groups,) + cut.shape, HALF),
            jax.ShapeDtypeStruct((own, 1), FULL),
            jax.ShapeDtypeStruct((1, width), FULL),
            jax.ShapeDtypeStruct((1, width), FULL),
            jax.ShapeDtypeStruct((1, value_size), FULL),
            jax.ShapeDtypeStruct((blocks, rows, rows), FULL),
            jax.ShapeDtypeStruct((blocks, rows, 2), FULL),
            jax.ShapeDtypeStruct((own // rows, blocks), jnp.int32),
            jax.ShapeDtypeStruct((own // rows,), jnp.int32),
        ],
        scratch_shapes=[pltpu.VMEM((own, width), HALF)] * 2
        + gather_scratch()
        + gather_scratch()
        + swap_scratch(2, peers)
        + [
            pltpu.SemaphoreType.DMA,
            pltpu.SemaphoreType.DMA((2, groups - 1, peers)),
            pltpu.SemaphoreType.DMA((2, groups - 1, peers)),
        ],
        compiler_params=linked(1),
        cost_estimate=cost(0, 2 * peers * (2 * own * width + slab * 2 * part)),
    )(lengths, order, tokens, grad, gains, rates, gate, up, cut)


def feed_kernel(
    rows_ref, weight_ref, grads_ref, inner_ref, up_slope_ref, gate_slope_ref, down_ref, total
):
    step = pl.program_id(0)
    both = dot_nn(rows_ref[...], weight_ref[...])
    part = both.shape[1] // 2
    gate, upward = both[:, :part], both[:, part:]
    inside = 0.7978845608028654 * (gate + 0.044715 * (gate * gate * gate))
    bend = jnp.tanh(inside)
    share = 0.5 * (1.0 + bend)
    value = gate * share
    steep = 0.7978845608028654 * (1.0 + 3.0 * 0.044715 * (gate * gate))
    slope = share + 0.5 * gate * (1.0 - bend * bend) * steep
    inner_ref[...] = (value * upward).astype(HALF)
    up_slope_ref[...] = value.astype(HALF)
    gate_slope_ref[...] = (upward * slope).astype(HALF)
    term = dot_tn(inner_ref[...], grads_ref[...])

    @pl.when(step == 0)
    def _():
        total[...] = term

    @pl.when(step > 0)
    def _():
        total[...] += term

    @pl.when(step == pl.num_programs(0) - 1)
    def _():
        down_ref[...] = total[...].astype(HALF)


def feed(rows, weight, grads):
    count, width = rows.shape
    columns = weight.shape[1]
    part = columns // 2
    tile = 256
    tokens = pl.BlockSpec((tile, width), lambda i: (i, 0))
    out = pl.BlockSpec((tile, part), lambda i: (i, 0))
    return pl.pallas_call(
        feed_kernel,
        grid=(count // tile,),
        in_specs=[
            tokens,
            pl.BlockSpec((width, columns), lambda i: (0, 0), pipeline_mode=pl.Buffered(1)),
            tokens,
        ],
        out_specs=[out] * 3 + [pl.BlockSpec((part, width), lambda i: (0, 0))],
        out_shape=[jax.ShapeDtypeStruct((count, part), HALF)] * 3
        + [jax.ShapeDtypeStruct((part, width), HALF)],
        scratch_shapes=[pltpu.VMEM((part, width), FULL)],
        compiler_params=pltpu.CompilerParams(
            dimension_semantics=("arbitrary",), vmem_limit_bytes=VMEM_BYTES
        ),
        cost_estimate=pl.CostEstimate(
            flops=3 * count * width * columns,
            bytes_accessed=2 * (2 * count * width + width * columns + 2 * count * columns),
            transcendentals=0,
        ),
    )(rows, weight, grads)


def feed_back_kernel(rows_ref, weight_ref, up_slope_ref, gate_slope_ref, grad_ref):
    inner_grad = dot_nt(rows_ref[...], weight_ref[...])
    part = inner_grad.shape[1]
    grad_ref[:, :part] = (inner_grad * gate_slope_ref[...].astype(FULL)).astype(HALF)
    grad_ref[:, part:] = (inner_grad * up_slope_ref[...].astype(FULL)).astype(HALF)


def feed_back(rows, weight, up_slope, gate_slope):
    count, width = rows.shape
    part = weight.shape[0]
    tile = 512
    slope = pl.BlockSpec((tile, part), lambda i: (i, 0))
    return pl.pallas_call(
        feed_back_kernel,
        grid=(count // tile,),
        in_specs=[
            pl.BlockSpec((tile, width), lambda i: (i, 0)),
            pl.BlockSpec((part, width), lambda i: (0, 0), pipeline_mode=pl.Buffered(1)),
            slope,
            slope,
        ],
        out_specs=pl.BlockSpec((tile, 2 * part), lambda i: (i, 0)),
        out_shape=jax.ShapeDtypeStruct((count, 2 * part), HALF),
        compiler_params=pltpu.CompilerParams(
            dimension_semantics=("arbitrary",), vmem_limit_bytes=VMEM_BYTES
        ),
        cost_estimate=pl.CostEstimate(
            flops=2 * count * width * part,
            bytes_accessed=2 * (count * width + width * part + 4 * count * part),
            transcendentals=0,
        ),
    )(rows, weight, up_slope, gate_slope)


def retention_kernel(
    place_ref, live_ref, first_ref, second_ref, weight_ref, decay_ref, column_ref, gain_ref,
    qkv_ref, swish_ref, normed_ref, scale_ref, entry_ref, mixed_hbm, state, mixed_buffer, sems,
):
    step, steps = pl.program_id(0), pl.num_programs(0)
    rows = first_ref.shape[2]
    batches, key_size, value_size = state.shape
    total = 2 * key_size + value_size
    slot = lax.rem(step, 2)

    def sent(at, which, batch):
        return pltpu.make_async_copy(
            mixed_buffer.at[which, batch],
            mixed_hbm.at[place_ref[batch, at], batch],
            sems.at[which, batch],
        )

    @pl.when(step == 0)
    def _():
        state[...] = jnp.zeros_like(state)

    @pl.when(step >= 2)
    def _():
        for batch in range(batches):
            sent(step - 2, slot, batch).wait()

    rows_in = jnp.concatenate([first_ref[0, 0], second_ref[0, 0]], axis=0)
    projected = dot_nn(rows_in, weight_ref[...])
    decay = decay_ref[0]
    entry_decay = column_ref[0, :, 0:1]
    end_weight = column_ref[0, :, 1:2]
    block_decay = column_ref[0, rows - 1 : rows, 0:1]
    positions = step * rows + lax.broadcasted_iota(jnp.int32, (rows, 1), 0)
    for batch in range(batches):
        mine = slice(batch * rows, (batch + 1) * rows)
        live = (positions < live_ref[batch]).astype(FULL)
        query = projected[mine, :key_size].astype(HALF)
        key = (projected[mine, key_size : 2 * key_size] * live).astype(HALF)
        value = projected[mine, 2 * key_size : total].astype(HALF)
        swish = projected[mine, total:]
        before = state[batch]
        before_low = before.astype(HALF)
        weights = (dot_nt(query, key) * decay).astype(HALF)
        retained = dot_nn(weights, value) + entry_decay * dot_nn(query, before_low)
        key_ended = (key.astype(FULL) * end_weight).astype(HALF)
        state[batch] = block_decay * before + dot_tn(key_ended, value)
        normed, scale = normalised(retained)
        qkv_ref[batch, 0, :, :key_size] = query
        qkv_ref[batch, 0, :, key_size : 2 * key_size] = key
        qkv_ref[batch, 0, :, 2 * key_size :] = value
        scale_ref[batch, 0] = jnp.broadcast_to(scale, scale_ref.shape[2:])
        entry_ref[batch, 0] = before_low
        swish_ref[batch, 0] = swish.astype(HALF)
        normed_ref[batch, 0] = normed.astype(HALF)
        mixed = swish * jax.nn.sigmoid(swish) * (normed * gain_ref[...])
        mixed_buffer[slot, batch] = mixed.astype(HALF)
        sent(step, slot, batch).start()

    @pl.when(step == steps - 1)
    def _():
        for batch in range(batches):
            sent(step, slot, batch).wait()
            sent(step - 1, 1 - slot, batch).wait()


def retention(rows_in, weight, place, live, decay, columns, gain, key_size):
    blocks, batches, rows, width = rows_in.shape
    value_size = gain.shape[-1]
    total = 2 * key_size + value_size

    def arriving(batch):
        return pl.BlockSpec(
            (1, 1, rows, width), lambda i, place, live: (place[batch, i], batch, 0, 0)
        )

    def whole(shape):
        return pl.BlockSpec(
            shape, lambda i, place, live: (0,) * len(shape), pipeline_mode=pl.Buffered(1)
        )

    def here(*tail):
        return pl.BlockSpec((batches, 1) + tail, lambda i, place, live: (0, i, 0, 0))

    def along(*tail):
        return pl.BlockSpec((1,) + tail, lambda i, place, live: (i, 0, 0))

    return pl.pallas_call(
        retention_kernel,
        grid_spec=pltpu.PrefetchScalarGridSpec(
            num_scalar_prefetch=2,
            grid=(blocks,),
            in_specs=[
                arriving(0),
                arriving(1),
                whole((width, total + value_size)),
                along(rows, rows),
                along(rows, 2),
                whole((1, value_size)),
            ],
            out_specs=[
                here(rows, total),
                here(rows, value_size),
                here(rows, value_size),
                here(rows, LANES),
                here(key_size, value_size),
                in_hbm(),
            ],
            scratch_shapes=[
                pltpu.VMEM((batches, key_size, value_size), FULL),
                pltpu.VMEM((2, batches, rows, value_size), HALF),
                pltpu.SemaphoreType.DMA((2, batches)),
            ],
        ),
        out_shape=[
            jax.ShapeDtypeStruct((batches, blocks, rows, total), HALF),
            jax.ShapeDtypeStruct((batches, blocks, rows, value_size), HALF),
            jax.ShapeDtypeStruct((batches, blocks, rows, value_size), HALF),
            jax.ShapeDtypeStruct((batches, blocks, rows, LANES), FULL),
            jax.ShapeDtypeStruct((batches, blocks, key_size, value_size), HALF),
            jax.ShapeDtypeStruct((blocks, batches, rows, value_size), HALF),
        ],
        compiler_params=pltpu.CompilerParams(
            dimension_semantics=("arbitrary",), vmem_limit_bytes=VMEM_BYTES
        ),
        cost_estimate=pl.CostEstimate(
            flops=3 * blocks * batches * rows * width * total,
            bytes_accessed=2 * blocks * batches * rows * (width + 2 * total) + 4 * width * total,
            transcendentals=0,
        ),
    )(place, live, rows_in, rows_in, weight, decay, columns, gain)


def retention_back_kernel(
    place_ref, live_ref, first_ref, second_ref,
    weight_ref, decay_ref, column_ref, gain_ref, qkv_ref, swish_ref, normed_ref, scale_ref, entry_ref,
    gain_grad_ref, grads_hbm, state, grads_buffer, sems,
):
    step, steps = pl.program_id(0), pl.num_programs(0)
    rows = first_ref.shape[2]
    batches, key_size, value_size = state.shape
    slot = lax.rem(step, 2)

    def sent(at, which, batch):
        return pltpu.make_async_copy(
            grads_buffer.at[which, batch],
            grads_hbm.at[place_ref[batch, steps - 1 - at], batch],
            sems.at[which, batch],
        )

    @pl.when(step == 0)
    def _():
        state[...] = jnp.zeros_like(state)
        gain_grad_ref[...] = jnp.zeros_like(gain_grad_ref)

    @pl.when(step >= 2)
    def _():
        for batch in range(batches):
            sent(step - 2, slot, batch).wait()

    rows_in = jnp.concatenate([first_ref[0, 0], second_ref[0, 0]], axis=0)
    mixed_grads = dot_nt(rows_in, weight_ref[...])
    decay = decay_ref[0]
    entry_decay = column_ref[0, :, 0:1]
    end_weight = column_ref[0, :, 1:2]
    block_decay = column_ref[0, rows - 1 : rows, 0:1]
    positions = (steps - 1 - step) * rows + lax.broadcasted_iota(jnp.int32, (rows, 1), 0)
    gain = gain_ref[...]
    for batch in range(batches):
        live = (positions < live_ref[batch]).astype(FULL)
        mixed_grad = mixed_grads[batch * rows : (batch + 1) * rows]
        query = qkv_ref[batch, 0, :, :key_size]
        key = qkv_ref[batch, 0, :, key_size : 2 * key_size]
        value = qkv_ref[batch, 0, :, 2 * key_size :]
        swish = swish_ref[batch, 0].astype(FULL)
        normed = normed_ref[batch, 0].astype(FULL)
        scale = scale_ref[batch, 0, :, 0:1]
        entry = entry_ref[batch, 0]
        sigmoid = jax.nn.sigmoid(swish)
        silu = swish * sigmoid
        swish_grad = mixed_grad * (normed * gain) * (sigmoid * (1.0 + swish - silu))
        scaled_grad = mixed_grad * silu
        gain_grad_ref[...] += jnp.sum(scaled_grad * normed, axis=0, keepdims=True)
        retained_grad = normalised_back(scaled_grad * gain, normed, scale).astype(HALF)
        weights = (dot_nt(query, key) * decay).astype(HALF)
        scores_grad = (dot_nt(retained_grad, value) * decay).astype(HALF)
        after = state[batch]
        after_low = after.astype(HALF)
        query_grad = dot_nn(scores_grad, key) + entry_decay * dot_nt(retained_grad, entry)
        key_grad = dot_tn(scores_grad, query) + end_weight * dot_nt(value, after_low)
        value_grad = dot_tn(weights, retained_grad) + end_weight * dot_nn(key, after_low)
        query_entered = (query.astype(FULL) * entry_decay).astype(HALF)
        state[batch] = block_decay * after + dot_tn(query_entered, retained_grad)
        grads_buffer[slot, batch, :, :key_size] = query_grad.astype(HALF)
        grads_buffer[slot, batch, :, key_size : 2 * key_size] = (key_grad * live).astype(HALF)
        grads_buffer[slot, batch, :, 2 * key_size : 2 * key_size + value_size] = value_grad.astype(
            HALF
        )
        grads_buffer[slot, batch, :, 2 * key_size + value_size :] = swish_grad.astype(HALF)
        sent(step, slot, batch).start()

    @pl.when(step == steps - 1)
    def _():
        for batch in range(batches):
            sent(step, slot, batch).wait()
            sent(step - 1, 1 - slot, batch).wait()


def retention_back(rows_in, weight, place, live, decay, columns, gain, saved):
    blocks, batches, rows, width = rows_in.shape
    value_size = gain.shape[-1]
    key_size = saved[-1].shape[2]
    total = 2 * key_size + 2 * value_size

    def arriving(batch, size):
        return pl.BlockSpec(
            (1, 1, rows, size),
            lambda i, place, live: (place[batch, blocks - 1 - i], batch, 0, 0),
        )

    def whole(shape):
        return pl.BlockSpec(
            shape, lambda i, place, live: (0,) * len(shape), pipeline_mode=pl.Buffered(1)
        )

    def here(*tail):
        return pl.BlockSpec((batches, 1) + tail, lambda i, place, live: (0, blocks - 1 - i, 0, 0))

    def along(*tail):
        return pl.BlockSpec((1,) + tail, lambda i, place, live: (blocks - 1 - i, 0, 0))

    return pl.pallas_call(
        retention_back_kernel,
        grid_spec=pltpu.PrefetchScalarGridSpec(
            num_scalar_prefetch=2,
            grid=(blocks,),
            in_specs=[
                arriving(0, width),
                arriving(1, width),
                whole((value_size, width)),
                along(rows, rows),
                along(rows, 2),
                whole((1, value_size)),
                here(rows, 2 * key_size + value_size),
                here(rows, value_size),
                here(rows, value_size),
                here(rows, LANES),
                here(key_size, value_size),
            ],
            out_specs=[
                pl.BlockSpec((1, value_size), lambda i, place, live: (0, 0)),
                in_hbm(),
            ],
            scratch_shapes=[
                pltpu.VMEM((batches, key_size, value_size), FULL),
                pltpu.VMEM((2, batches, rows, total), HALF),
                pltpu.SemaphoreType.DMA((2, batches)),
            ],
        ),
        out_shape=[
            jax.ShapeDtypeStruct((1, value_size), FULL),
            jax.ShapeDtypeStruct((blocks, batches, rows, total), HALF),
        ],
        compiler_params=pltpu.CompilerParams(
            dimension_semantics=("arbitrary",), vmem_limit_bytes=VMEM_BYTES
        ),
        cost_estimate=pl.CostEstimate(
            flops=6 * blocks * batches * rows * width * value_size,
            bytes_accessed=2 * blocks * batches * rows * (width + 2 * total)
            + 2 * width * value_size,
            transcendentals=0,
        ),
    )(place, live, rows_in, rows_in, weight, decay, columns, gain, *saved)


def middle_kernel(
    mixed_hbm, weight_hbm, tokens_hbm, gain_ref, hidden_ref, second_out,
    *scratch,
):
    scatter = scratch[:7]
    own, keeps, gather_sends, gather_receives = scratch[7:11]
    weight_ref, tokens_ref, stage_sems, mixed, mixed_sems = scratch[11:]
    peers, groups = lax.axis_size("seq"), lax.axis_size("fsdp")
    sources, targets = (weight_hbm, tokens_hbm), (weight_ref, tokens_ref)
    weight_copy, tokens_copy = staged(sources, targets, stage_sems)
    blocks = Blocks(mixed_hbm, mixed, mixed_sems)
    blocks.begin()
    greet_neighbours()
    weight_copy.wait()

    def term(block):
        return blocks.take(lambda value: dot_nn(value, weight_ref[...]).astype(HALF))

    gain = gain_ref[...]

    def use(start, total):
        rows = pl.ds(start, CHUNK)
        hidden = tokens_ref[rows].astype(FULL) + total
        hidden_ref[rows] = hidden
        normed, _ = normalised(hidden)
        own[rows] = regroup(normed * gain, peers, groups).astype(HALF)

    gathers = [
        PlaneGather(own, second_out, keeps, gather_sends, gather_receives, window, WINDOWS)
        for window in range(WINDOWS)
    ]
    windows = scatter_head(term, scatter)
    tokens_copy.wait()
    scatter_tail(windows, use, lambda window: gathers[window].begin())
    for gather in gathers:
        gather.relay()
    for gather in gathers:
        gather.finish()
    for window in windows:
        window.drain()


def middle(mixed, weight, tokens, gain):
    peers, own, inner = mixed.shape
    width = weight.shape[1]
    return pl.pallas_call(
        middle_kernel,
        in_specs=[in_hbm()] * 3 + [vmem()],
        out_specs=[vmem(), in_hbm()],
        out_shape=[
            jax.ShapeDtypeStruct((own, width), FULL),
            jax.ShapeDtypeStruct((peers, own, width), HALF),
        ],
        scratch_shapes=scatter_scratch(own, width)
        + [pltpu.VMEM((own, width), HALF)]
        + gather_scratch(WINDOWS)
        + stage_scratch(weight, tokens)
        + block_scratch(peers, mixed),
        compiler_params=linked(2),
        cost_estimate=cost(2 * peers * own * inner * width, 4 * peers * own * width),
    )(mixed, weight, tokens, gain)


class LineSum:
    def __init__(self, terms, landed, own, final, loads, sends, receives):
        self.terms, self.landed, self.own, self.final = terms, landed, own, final
        self.loads, self.sends, self.receives = loads, sends, receives
        self.me, self.last = lax.axis_index("fsdp"), lax.axis_size("fsdp") - 1
        self.peers, self.place = lax.axis_size("seq"), lax.axis_index("seq")

    def piece(self, turn):
        return lax.rem(self.place + turn, self.peers)

    def depth(self, way):
        return self.me if way == 0 else self.last - self.me

    def block(self, way, order):
        return self.last - order if way == 0 else order

    def slot(self, way, order):
        return order if way == 0 else 2 * self.last - 2 - order

    def sent(self, source, way, order, turn):
        at = (way, order, turn)
        return pltpu.make_async_remote_copy(
            src_ref=source,
            dst_ref=self.landed.at[self.slot(way, order), self.piece(turn)],
            send_sem=self.sends.at[at],
            recv_sem=self.receives.at[at],
            device_id={"fsdp": self.me + 1 if way == 0 else self.me - 1},
            device_id_type=MESH,
        )

    def first(self, way, order, turn):
        source = self.terms.at[self.block(way, order), self.piece(turn)]
        return self.sent(source, way, order, turn)

    def onward(self, way, order, turn):
        source = self.landed.at[self.slot(way, order), self.piece(turn)]
        return self.sent(source, way, order, turn)

    def load(self, way, order):
        return pltpu.make_async_copy(
            self.terms.at[self.block(way, order)], self.own.at[way], self.loads.at[way]
        )

    def load_final(self):
        return pltpu.make_async_copy(self.terms.at[self.me], self.final, self.loads.at[2])

    def begin(self):
        for way in (0, 1):

            @pl.when(self.depth(way) == 0)
            def _():
                for order in range(self.last):
                    for turn in range(self.peers):
                        self.first(way, order, turn).start()

            self.load(way, 0).start()
        self.load_final().start()

    def loaded(self):
        for way in (0, 1):
            self.load(way, 0).wait()

    def load_next(self):
        for way in (0, 1):

            @pl.when(self.depth(way) == 1)
            def _():
                self.load(way, 1).start()

    def loaded_next(self):
        for way in (0, 1):

            @pl.when(self.depth(way) == 1)
            def _():
                self.load(way, 1).wait()

    def hand_on(self, order, depth, turns):
        for turn in turns:
            for way in (0, 1):

                @pl.when(self.depth(way) == depth)
                def _():
                    at, piece = self.slot(way, order), self.piece(turn)
                    self.onward(way, order, turn).wait_recv()
                    self.landed[at, piece] = (
                        self.landed[at, piece].astype(FULL) + self.own[way, piece].astype(FULL)
                    ).astype(HALF)
                    self.onward(way, order, turn).start()

    def finish(self, use):
        self.load_final().wait()
        for turn in range(self.peers):
            piece = self.piece(turn)
            for way in (0, 1):

                @pl.when(self.depth(way) > 0)
                def _():
                    order = self.last - self.depth(way)
                    self.onward(way, order, turn).wait_recv()
                    self.final[piece] = (
                        self.final[piece].astype(FULL)
                        + self.landed[self.slot(way, order), piece].astype(FULL)
                    ).astype(HALF)

            use(turn)

    def drain(self):
        for way in (0, 1):
            for order in range(self.last):
                for turn in range(self.peers):

                    @pl.when(self.depth(way) == 0)
                    def _():
                        self.first(way, order, turn).wait_send()

                    @pl.when((self.depth(way) > 0) & (self.depth(way) < self.last - order))
                    def _():
                        self.onward(way, order, turn).wait_send()


def line_scratch(groups, peers, slab, columns):
    block = (peers, slab, columns)
    return [
        pltpu.VMEM((2 * groups - 3,) + block, HALF),
        pltpu.VMEM((2,) + block, HALF),
        pltpu.VMEM(block, HALF),
        pltpu.SemaphoreType.DMA((3,)),
        pltpu.SemaphoreType.DMA((2, groups - 1, peers)),
        pltpu.SemaphoreType.DMA((2, groups - 1, peers)),
    ]


def middle_back_kernel(
    grads_hbm, weight_hbm, hidden_hbm, outer_hbm, mask_ref, gain_ref, mixed_hbm,
    hidden_grad_ref, gain_grad_ref, branch_out, out_grad_ref,
    *scratch,
):
    scatter = scratch[:7]
    own, gather_sends, gather_receives = scratch[7:10]
    weight_ref, hidden_ref, outer_ref, mixed_ref, stage_sems, grads, grad_sems = scratch[10:17]
    branch, total, out_sems = scratch[17:]
    peers, groups = lax.axis_size("seq"), lax.axis_size("fsdp")
    me, other, near, below, far = plane_peers()
    flip = other - me
    blocks = Blocks(grads_hbm, grads, grad_sems)
    weight_copy, *later = staged(
        (weight_hbm, hidden_hbm, outer_hbm, mixed_hbm),
        (weight_ref, hidden_ref, outer_ref, mixed_ref),
        stage_sems,
    )
    blocks.begin()
    greet_neighbours()
    weight_copy.wait()

    def term(block):
        return blocks.take(lambda value: dot_nt(value, weight_ref[...]).astype(HALF))

    gain = gain_ref[...]
    gain_grad_ref[...] = jnp.zeros_like(gain_grad_ref)

    def use(start, total):
        rows = pl.ds(start, CHUNK)
        grad = regroup(total, groups, peers)
        normed, scale = normalised(hidden_ref[rows])
        gain_grad_ref[...] += jnp.sum(grad * normed, axis=0, keepdims=True)
        outer = outer_ref[rows].astype(FULL) * mask_ref[rows]
        hidden_grad = outer + normalised_back(grad * gain, normed, scale)
        hidden_grad_ref[rows] = hidden_grad
        own[rows] = hidden_grad.astype(HALF)

    gathers = [
        PlaneGather(own, branch, None, gather_sends, gather_receives, window, WINDOWS)
        for window in range(WINDOWS)
    ]
    width, stored = own.shape[1], []

    def add(block, rows):
        copy = pltpu.make_async_copy(rows, branch_out.at[block], out_sems.at[len(stored)])
        copy.start()
        for start in range(0, width, 512):
            columns = pl.ds(start, 512)
            product = dot_tn(mixed_ref[block], rows[:, columns])
            total[:, columns] = total[:, columns] + product if stored else product
        stored.append(copy)

    windows = scatter_head(term, scatter)
    for copy in later:
        copy.wait()
    scatter_tail(windows, use, lambda window: gathers[window].begin())
    add(me, own)
    for gather in gathers:
        gather.expect(2, 3)
    add(other, branch.at[other])
    for gather in gathers:
        gather.relay()
    for block in (near, below):
        add(block, branch.at[block])
    for gather in gathers:
        gather.expect(8, 9, 10, 11)
    add(near + flip, branch.at[near + flip])
    for gather in gathers:
        gather.relay_far()
    add(below + flip, branch.at[below + flip])
    add(far, branch.at[far])
    for gather in gathers:
        gather.expect(12, 13)
    add(far + flip, branch.at[far + flip])
    out_grad_ref[...] = total[...].astype(HALF)
    for copy in stored:
        copy.wait()
    for gather in gathers:
        gather.drain()
    for window in windows:
        window.drain()


def middle_back(grads, weight, hidden, outer, mask, gain, mixed):
    peers, own, inner = grads.shape
    width = weight.shape[0]
    return pl.pallas_call(
        middle_back_kernel,
        in_specs=[in_hbm()] * 4 + [vmem()] * 2 + [in_hbm()],
        out_specs=[vmem(), vmem(), in_hbm(), vmem()],
        out_shape=[
            jax.ShapeDtypeStruct((own, width), FULL),
            jax.ShapeDtypeStruct((1, width), FULL),
            jax.ShapeDtypeStruct((peers, own, width), HALF),
            jax.ShapeDtypeStruct((mixed.shape[2], width), HALF),
        ],
        scratch_shapes=scatter_scratch(own, width)
        + [pltpu.VMEM((own, width), HALF)]
        + gather_scratch(WINDOWS)[1:]
        + stage_scratch(weight, hidden, outer, mixed)
        + block_scratch(2, grads)
        + [
            pltpu.VMEM((peers, own, width), HALF),
            pltpu.VMEM((mixed.shape[2], width), FULL),
            pltpu.SemaphoreType.DMA((peers,)),
        ],
        compiler_params=pltpu.CompilerParams(
            collective_id=3, has_side_effects=True, vmem_limit_bytes=LARGE_BYTES
        ),
        cost_estimate=cost(2 * peers * own * inner * width, 4 * peers * own * width),
    )(grads, weight, hidden, outer, mask, gain, mixed)


class PlaneReturn:
    def __init__(self, cuts, source, targets, keeps, sends, receives):
        self.cuts, self.source, self.targets = cuts, source, targets
        self.keeps, self.sends, self.receives = keeps, sends, receives
        self.peers, self.me = lax.axis_size("seq"), lax.axis_index("seq")

    def part(self, number, peer):
        start, size = self.cuts[number]
        return self.source.at[peer, :, pl.ds(start, size)]

    def place(self, number, peer):
        size = self.cuts[number][1]
        return self.targets[number].at[:, pl.ds(pl.multiple_of(peer * size, LANES), size)]

    def sent(self, source, target, number, turn, peer):
        at = (number, turn)
        return to_peer(source, target, self.sends.at[at], self.receives.at[at], peer)

    def copy(self, number, turn):
        peer = lax.rem(self.me + turn, self.peers)
        return self.sent(
            self.part(number, peer), self.place(number, self.me), number, turn, peer
        )

    def landed(self, number, turn):
        peer = lax.rem(self.me + self.peers - turn, self.peers)
        target = self.place(number, peer)
        return self.sent(target, target, number, turn, peer)

    def kept(self, number):
        return pltpu.make_async_copy(
            self.part(number, self.me), self.place(number, self.me), self.keeps.at[number]
        )

    def begin(self, turn):
        for number in range(len(self.cuts)):
            if turn > 0:
                self.copy(number, turn).start()
            else:
                self.kept(number).start()

    def finish(self):
        for number in range(len(self.cuts)):
            for turn in range(1, self.peers):
                self.landed(number, turn).wait_recv()
                self.copy(number, turn).wait_send()
            self.kept(number).wait()


def last_kernel(
    cuts, line_cuts, grads_hbm, weight_hbm, tokens_hbm, hidden_grad_hbm, gain_ref, second_grad_ref,
    group_grad_ref, inner_hbm, down_hbm, hidden_hbm, mask_ref, summed_ref, terms_ref,
    *refs,
):
    count, line_count = len(cuts), len(line_cuts)
    input_ref, output_ref, gains_ref = refs[:3]
    returned, refs = refs[3 : 3 + count], refs[3 + count :]
    line_returned, scratch = refs[:line_count], refs[line_count:]
    scatter, result = scratch[:7], scratch[:1] + scratch[7:13]
    (
        sums, parts, across, totals, first_grad, keep, part_sends, part_receives,
        group_keep, group_sends, group_receives,
    ) = scratch[13:24]
    peers, groups = lax.axis_size("seq"), lax.axis_size("fsdp")
    me = lax.axis_index("seq")
    grads, grad_sems = scratch[36:38]
    inner_ref = scratch[38]
    weight_ref, down_ref, hidden_ref, tokens_ref, hidden_grad_ref, stage_sems = scratch[39:]
    blocks = Blocks(grads_hbm, grads, grad_sems)
    weight_copy, inner_copy, down_copy, *later = staged(
        (weight_hbm, inner_hbm, down_hbm, hidden_hbm, tokens_hbm, hidden_grad_hbm),
        (weight_ref, inner_ref, down_ref, hidden_ref, tokens_ref, hidden_grad_ref),
        stage_sems,
    )
    blocks.begin()
    greet_plane(True)
    back = PlaneReturn(cuts, summed_ref, returned, *scratch[24:27])
    line_back = PlaneReturn(line_cuts, scratch[32], line_returned, *scratch[27:30])
    line = LineSum(terms_ref, *scratch[30:36])

    def term(block):
        return blocks.take(lambda value: dot_nt(value, weight_ref[...]).astype(HALF))

    def result_term(block):
        return dot_nn(inner_ref[block], down_ref[...]).astype(HALF)

    gain = gain_ref[...]
    first_grad[...] = jnp.zeros_like(first_grad)

    def use(start, total):
        rows = pl.ds(start, CHUNK)
        grad = regroup(total, groups, peers)
        normed, scale = normalised(tokens_ref[rows].astype(FULL))
        first_grad[...] += jnp.sum(grad * normed, axis=0, keepdims=True)
        input_ref[rows] = (
            hidden_grad_ref[rows] + normalised_back(grad * gain, normed, scale)
        ).astype(HALF)

    def use_result(start, total):
        rows = pl.ds(start, CHUNK)
        output_ref[rows] = ((hidden_ref[rows] + total) * mask_ref[rows]).astype(HALF)

    line.begin()
    weight_copy.wait()
    every, early, late = range(peers), range(peers // 2), range(peers // 2, peers)
    windows = scatter_head(term, scatter, (), True)
    windows[0].relay()
    line.loaded()
    line.hand_on(0, 1, every)
    line.load_next()
    windows[1].relay()
    inner_copy.wait()
    down_copy.wait()
    result_windows = scatter_head(result_term, result, windows, True)
    for turn in every:
        back.begin(turn)
    result_windows[0].relay()
    line.hand_on(0, 2, every)
    for copy in later:
        copy.wait()
    scatter_tail(windows, use)
    line.loaded_next()
    line.hand_on(1, 1, early)
    result_windows[1].relay()
    tile = LANES * 2
    for peer in range(peers):
        for row in range(tile // LANES):
            at = peer * tile + row * LANES
            sums[peer, row : row + 1] = first_grad[:, at : at + LANES]
            sums[peer, 2 + row : 3 + row] = second_grad_ref[:, at : at + LANES]
        sums[peer, 4:8] = jnp.zeros((4, LANES), FULL)

    def copy(turn):
        peer = lax.rem(me + turn, peers)
        return to_peer(
            sums.at[peer], parts.at[turn], part_sends.at[turn], part_receives.at[turn], peer
        )

    kept = pltpu.make_async_copy(sums.at[me], parts.at[0], keep)
    kept.start()
    for turn in range(1, peers):
        copy(turn).start()
    line.hand_on(1, 1, late)
    scatter_tail(result_windows, use_result)
    kept.wait()
    for turn in range(1, peers):
        copy(turn).wait_recv()
        copy(turn).wait_send()
    total = parts[0]
    for turn in range(1, peers):
        total += parts[turn]
    across[0:8] = total
    for row in range(4):
        across[8 + row : 9 + row] = group_grad_ref[:, row * LANES : (row + 1) * LANES]
    across[12:16] = jnp.zeros((4, LANES), FULL)
    begin, finish = all_to_each(
        across, totals, "fsdp", groups, group_keep, group_sends, group_receives
    )
    begin()
    line.finish(line_back.begin)
    back.finish()
    line_back.finish()
    line.drain()
    for window in windows:
        window.drain(4)
    for window in result_windows:
        window.drain()
    finish()
    summed = totals[0]
    for turn in range(1, groups):
        summed += totals[turn]
    gains_ref[...] = summed


def last_rows(
    grads, weight, tokens, hidden_grad, gain, second_grad, group_grad, inner, down, hidden, mask,
    summed, sizes, terms, line_sizes,
):
    peers, own, size = grads.shape
    groups = lax.axis_size("fsdp")
    width = weight.shape[0]
    slab = summed.shape[1]

    def cuts_of(sizes):
        return tuple((sum(sizes[:number]), sizes[number]) for number in range(len(sizes)))

    return pl.pallas_call(
        partial(last_kernel, cuts_of(sizes), cuts_of(line_sizes)),
        in_specs=[in_hbm()] * 4 + [vmem()] * 3 + [in_hbm()] * 3 + [vmem()] + [in_hbm()] * 2,
        out_specs=[vmem()] * 3 + [in_hbm()] * len(sizes + line_sizes),
        out_shape=[
            jax.ShapeDtypeStruct((own, width), HALF),
            jax.ShapeDtypeStruct((own, width), HALF),
            jax.ShapeDtypeStruct((16, LANES), FULL),
        ]
        + [jax.ShapeDtypeStruct((slab, peers * part), HALF) for part in sizes + line_sizes],
        scratch_shapes=scatter_scratch(own, width)
        + scatter_scratch(own, width)[1:]
        + [
            pltpu.VMEM((peers, 8, LANES), FULL),
            pltpu.VMEM((peers, 8, LANES), FULL),
            pltpu.VMEM((16, LANES), FULL),
            pltpu.VMEM((groups, 16, LANES), FULL),
            pltpu.VMEM((1, width), FULL),
            pltpu.SemaphoreType.DMA,
            pltpu.SemaphoreType.DMA((peers,)),
            pltpu.SemaphoreType.DMA((peers,)),
            pltpu.SemaphoreType.DMA,
            pltpu.SemaphoreType.DMA((groups,)),
            pltpu.SemaphoreType.DMA((groups,)),
        ]
        + swap_scratch(len(sizes), peers)
        + swap_scratch(len(line_sizes), peers)
        + line_scratch(groups, peers, slab, terms.shape[3])
        + block_scratch(2, grads)
        + [pltpu.VMEM(inner.shape, HALF)]
        + stage_scratch(weight, down, hidden, tokens, hidden_grad, inner)[:5]
        + [pltpu.SemaphoreType.DMA((6,))],
        compiler_params=pltpu.CompilerParams(
            collective_id=5, has_side_effects=True, vmem_limit_bytes=LARGE_BYTES
        ),
        cost_estimate=cost(
            2 * peers * own * (size + inner.shape[2]) * width, 5 * peers * own * width
        ),
    )(
        grads, weight, tokens, hidden_grad, gain, second_grad, group_grad, inner, down, hidden, mask,
        summed, terms,
    )


def outputs_kernel(*refs):
    count = len(refs) // 2 - 2
    gains_ref, refs = refs[count], refs[:count] + refs[count + 1 :]
    for source, target in zip(refs[:count], refs[count : 2 * count]):
        target[...] = source[...].astype(target.dtype)
    first_ref, second_ref, group_ref = refs[2 * count :]
    group, half = lax.axis_index("fsdp"), LANES // 2
    row = group // 2
    for start, target in ((0, first_ref), (2, second_ref)):
        both = gains_ref[pl.ds(start + row, 1)]
        turned = pltpu.roll(both, half, 1)
        target[...] = jnp.where(lax.rem(group, 2) == 0, both, turned)[:, :half]
    group_ref[...] = gains_ref[pl.ds(8 + group, 1)]


def outputs(grads, rows, gains):
    arrays = [*grads, *rows]
    small = (LANES // 2, LANES // 2, LANES)
    return pl.pallas_call(
        outputs_kernel,
        in_specs=[vmem()] * (len(arrays) + 1),
        out_specs=[vmem()] * (len(arrays) + 3),
        out_shape=[jax.ShapeDtypeStruct(array.shape, FULL) for array in grads]
        + [jax.ShapeDtypeStruct(array.shape, HALF) for array in rows]
        + [jax.ShapeDtypeStruct((1, size), FULL) for size in small],
        compiler_params=pltpu.CompilerParams(vmem_limit_bytes=VMEM_BYTES),
    )(*arrays, gains)


def head_body(
    tokens,
    cotangent,
    lengths,
    block_order,
    log_decay,
    first_gain,
    query_weight,
    key_weight,
    value_weight,
    swish_weight,
    output_weight,
    group_gain,
    second_gain,
    feed_gate,
    feed_up,
    feed_down,
):
    peers, groups = lax.axis_size("seq"), lax.axis_size("fsdp")
    batches, rows, width = tokens.shape
    own = batches * rows
    heads = log_decay.shape[0]
    key_size = query_weight.shape[1] // heads
    value_size = value_weight.shape[1] // heads
    part = feed_gate.shape[1] // peers
    slab = query_weight.shape[0]
    total = 2 * key_size + 2 * value_size

    def over_groups(local):
        return lax.all_gather(local, "fsdp", axis=0, tiled=True)

    def sum_groups(whole):
        return lax.psum_scatter(whole.astype(HALF), "fsdp", scatter_dimension=0, tiled=True)

    def gathered(cut):
        return over_groups(cut[None]).reshape(width, cut.shape[2])

    gains = jnp.concatenate(
        [
            group_gain.astype(FULL)[None],
            jnp.concatenate([first_gain, second_gain]).astype(FULL)[None],
            jnp.zeros((6, LANES), FULL),
        ],
        axis=0,
    )
    first_cut, rates, gains = first_swap(
        query_weight, key_weight, value_weight, swish_weight, log_decay, gains
    )
    out_weight = over_groups(output_weight)
    token_rows = tokens.reshape(own, width)
    outer_rows = cotangent.reshape(own, width)
    (
        entered, result_low, feed_cut, first_weight,
        mask, gain_one, gain_two, gain_group, decay, columns, place, live,
    ) = gather_inputs(
        lengths, block_order, token_rows, outer_rows, gains, rates, feed_gate, feed_up, first_cut,
        value_size,
    )
    first_weight = first_weight.reshape(width, total)
    entered, out_weight = lax.optimization_barrier((entered, out_weight))
    feed_weight = gathered(feed_cut)

    *saved, mixed = retention(
        entered.reshape(peers, batches, rows, width),
        first_weight,
        place,
        live,
        decay,
        columns,
        gain_group,
        key_size,
    )
    entered = entered.reshape(peers * own, width)
    mixed, feed_down = lax.optimization_barrier((mixed, feed_down))
    down_weight = over_groups(feed_down)
    mixed = mixed.reshape(peers * own, value_size)
    hidden, second = middle(mixed.reshape(peers, own, value_size), out_weight, token_rows, gain_two)
    second = second.reshape(peers * own, width)
    result_low = result_low.reshape(peers * own, width)
    inner_low, up_slope, gate_slope, down_term = feed(second, feed_weight, result_low)
    down_grad = sum_groups(down_term)
    both_grad = feed_back(result_low, down_weight, up_slope, gate_slope)
    both_term, both_grad = lax.optimization_barrier(
        (dot_tn(second, both_grad).astype(HALF), both_grad)
    )
    both_weight_grad = sum_groups(both_term).reshape(peers, slab, 2 * part)
    hidden_grad, second_gain_grad, branch_low, out_term = middle_back(
        both_grad.reshape(peers, own, 2 * part),
        feed_weight,
        hidden,
        outer_rows,
        mask,
        gain_two,
        mixed.reshape(peers, own, value_size),
    )
    branch_low, down_grad = lax.optimization_barrier((branch_low, down_grad))
    out_grad = sum_groups(out_term)
    group_gain_grad, projected_grad = retention_back(
        branch_low.reshape(peers, batches, rows, width),
        out_weight,
        place,
        live,
        decay,
        columns,
        gain_group,
        saved,
    )
    flat_grad = projected_grad.reshape(peers * own, total)
    first_term = dot_tn(entered, flat_grad).astype(HALF)
    (
        input_rows, output_rows, small_grads,
        gate_back, up_back, query_back, key_back, value_back, swish_back,
    ) = last_rows(
        projected_grad.reshape(peers, own, total),
        first_weight,
        token_rows,
        hidden_grad,
        gain_one,
        second_gain_grad,
        group_gain_grad,
        inner_low.reshape(peers, own, part),
        down_weight,
        hidden,
        mask,
        both_weight_grad,
        (part, part),
        first_term.reshape(groups, peers, slab, total),
        (key_size, key_size, value_size, value_size),
    )
    (
        query_back, key_back, value_back, swish_back, out_back, gate_back, up_back, down_back,
        output_rows, input_rows, first_grad, second_grad, group_grad,
    ) = outputs(
        (query_back, key_back, value_back, swish_back, out_grad, gate_back, up_back, down_grad),
        (output_rows, input_rows),
        small_grads,
    )
    return (
        output_rows.reshape(batches, rows, width),
        input_rows.reshape(batches, rows, width),
        first_grad.reshape(slab),
        query_back,
        key_back,
        value_back,
        swish_back,
        out_back,
        group_grad.reshape(LANES),
        second_grad.reshape(slab),
        gate_back,
        up_back,
        down_back,
    )


def body(*arrays):
    peers, groups = lax.axis_size("seq"), lax.axis_size("fsdp")
    fits = peers == 8 and groups == 4 and arrays[4].shape[0] == peers and arrays[0].shape[0] == 2
    if fits:
        return head_body(*arrays)
    return general_body(*arrays)


def solution(mesh):
    placed = (
        P("fsdp", "seq", None),
        P("fsdp", "seq", None),
        P(),
        P(),
        P(None, "seq"),
        P(("seq", "fsdp")),
        P(("seq", "fsdp"), None),
        P(("seq", "fsdp"), None),
        P(("seq", "fsdp"), None),
        P(("seq", "fsdp"), None),
        P(("seq", "fsdp"), None),
        P(("seq", "fsdp")),
        P(("seq", "fsdp")),
        P(("seq", "fsdp"), None),
        P(("seq", "fsdp"), None),
        P(("seq", "fsdp"), None),
    )
    return jax.shard_map(
        body,
        mesh=mesh,
        in_specs=placed,
        out_specs=(
            P("fsdp", "seq", None),
            P("fsdp", "seq", None),
            P(("seq", "fsdp")),
            P(("seq", "fsdp"), None),
            P(("seq", "fsdp"), None),
            P(("seq", "fsdp"), None),
            P(("seq", "fsdp"), None),
            P(("seq", "fsdp"), None),
            P(("seq", "fsdp")),
            P(("seq", "fsdp")),
            P(("seq", "fsdp"), None),
            P(("seq", "fsdp"), None),
            P(("seq", "fsdp"), None),
        ),
        check_vma=False,
    )
```
